32 devices in a mesh: gx: 4 (over z), gy: 8 (over y, x, core).
Axes of the slice: x: 2, y: 2, z: 4, core: 2. Of those that a mesh axis runs over, the one named last changes fastest.
Arguments:
- x_in: bfloat16 [4096, 768], P(('gx', 'gy')), may hold values from -6 to 6
- norm1_gain: float32 [768], replicated, may hold values from 0.1 to 1.9
- w_query: bfloat16 [768, 768], P('gx', 'gy'), may hold values from -0.21875 to 0.21875
- w_key: bfloat16 [768, 768], P('gx', 'gy'), may hold values from -0.21875 to 0.21875
- w_value: bfloat16 [768, 768], P('gx', 'gy'), may hold values from -0.21875 to 0.21875
- relative_bias_table: float32 [32, 12], replicated, may hold values from -4 to 4
- w_out: bfloat16 [768, 768], P('gy', 'gx'), may hold values from -1.75 to 1.75
- norm2_gain: float32 [768], P('gx'), may hold values from 0.1 to 1.9
- w_router: float32 [768, 32], P('gx'), may hold values from -0.15625 to 0.15625
- w_hidden: bfloat16 [768, 98304], P('gx', 'gy'), may hold values from -0.21875 to 0.21875
- w_back: bfloat16 [768, 98304], P('gx', 'gy'), may hold values from -6 to 6
- expert_choice: int32 [4096], replicated, may hold values from 0 to 31
- doc_ids: int32 [4096], P('gx'), may hold values from 0 to 11, as said below
- grad_out: bfloat16 [4096, 768], P(('gx', 'gy')), may hold values from -6 to 6
Outputs:
- block_out: float32 [4096, 768], P(('gx', 'gy'))
- grad_input: float32 [4096, 768], P(('gx', 'gy'))
- grad_norm1: float32 [768], replicated
- grad_query: float32 [768, 768], P('gx', 'gy')
- grad_key: float32 [768, 768], P('gx', 'gy')
- grad_value: float32 [768, 768], P('gx', 'gy')
- grad_table: float32 [32, 12], replicated
- grad_out_proj: float32 [768, 768], P('gy', 'gx')
- grad_norm2: float32 [768], P('gx')
- grad_router: float32 [768, 32], P('gx')
- grad_hidden: float32 [768, 98304], P('gx', 'gy')
- grad_back: float32 [768, 98304], P('gx', 'gy')
The draws below stay inside these ranges and needn't reach their ends.
Inputs may be any that keep to these rules, and one draw needn't show every extreme that they name: doc_ids never fall along the tokens; each sequence of 1024 tokens holds three documents, the middle one starting within the sequence's first 128 tokens and ending within its last 128.
All inputs are finite; a program needn't handle non-finite values.
Results may differ from the reference program's by a relative error of at most 0.014.
Values may be sent and summed in bfloat16 or wider, within the bound.
A program may use at most 384 MiB of HBM per device.

```python
import math
from functools import partial
import jax
import jax.numpy as jnp
import numpy as np
from jax import lax

D = 768
HEADS = 12
HSIZE = 64
HD = 768
FF = 3072
EXPERTS = 32
BUCKETS = 32
WINDOW = 1024
TOK_DEV = 128
SEQ = 1024
TOKENS = 4096
CAPACITY = 160


def draw_doc_ids(key, part):
    key = jax.random.fold_in(key, 7)
    seq_count = TOKENS // SEQ
    first_key, last_key = jax.random.split(key)
    first_cut = jax.random.randint(first_key, (seq_count, 1), 1, TOK_DEV)
    last_cut = SEQ - jax.random.randint(last_key, (seq_count, 1), 1, TOK_DEV)
    position = jnp.arange(SEQ, dtype=jnp.int32)[None, :]
    inner_ids = (position >= first_cut).astype(jnp.int32) + (position >= last_cut).astype(jnp.int32)
    offsets = 3 * jnp.arange(seq_count, dtype=jnp.int32)[:, None]
    return (offsets + inner_ids).reshape(TOKENS).astype(jnp.int32)


def plant(entries, rng, least, largest):
    extent = entries.shape
    place = [jax.random.randint(jax.random.fold_in(rng, axis), (), 0, extent[axis]) for axis in range(len(extent))]
    entries = entries.at[tuple(place)].set(least)
    longest = extent.index(max(extent))
    place[longest] = (place[longest] + 1) % extent[longest]
    return entries.at[tuple(place)].set(largest)


def shard_levels(rng, shape, shards, smallest, high):
    gain, own = 1.0, jax.random.fold_in(rng, 6)
    for axis_at, blocks in shards:
        draws = jnp.exp(jax.random.uniform(jax.random.fold_in(own, axis_at), (blocks,), jnp.float32, smallest / len(shards), high / len(shards)))
        gain = gain * jnp.repeat(draws, shape[axis_at] // blocks).reshape([-1 if axis == axis_at else 1 for axis in range(len(shape))])
    return gain


def rank_table(amount, lean):
    weights = [(1 << 20) // math.isqrt(rank ** lean) + 1 for rank in range(1, amount + 1)]
    scale = 1 + sum(weights) // (1 << 30)
    return np.cumsum(np.array([max(1, weight // scale) for weight in weights]))


def ranked(rng, shape, count, slope):
    listing = rank_table(count, slope)
    pick = jax.random.randint(jax.random.fold_in(rng, 1), shape, 0, int(listing[count - 1]))
    rank = jnp.searchsorted(jnp.asarray(listing, jnp.int32), pick, side="right")
    return jax.random.permutation(jax.random.fold_in(rng, 2), count)[rank].astype(jnp.int32)


def centred(stream_key, shape, scale, bound, shards=(), held_as=jnp.bfloat16):
    array = scale * jax.random.normal(stream_key, shape, jnp.float32)
    if shards:
        array = array * shard_levels(stream_key, shape, shards, -0.22, 0.18)
    return jnp.clip(array, -bound, bound).astype(held_as)


def setup_inputs(seed: int = 0) -> dict:
    streams_of = jax.random.split(jax.random.key(seed), 15)
    x_in = centred(streams_of[0], (TOKENS, D), 1.0, 6.0, ((0, 32),))
    norm1_gain = jnp.clip(1.0 + 0.18 * jax.random.normal(streams_of[1], (D,), jnp.float32), 0.1, 1.9)
    w_query = centred(streams_of[2], (D, HD), D ** -0.5, 0.21875, ((0, 4), (1, 8)))
    w_key = centred(streams_of[3], (D, HD), D ** -0.5, 0.21875, ((0, 4), (1, 8)))
    w_value = centred(streams_of[4], (D, HD), D ** -0.5, 0.21875, ((0, 4), (1, 8)))
    relative_bias_table = centred(streams_of[5], (BUCKETS, HEADS), 1.0, 4.0, (), jnp.float32)
    w_out = centred(streams_of[6], (HD, D), (HD // 64) ** -0.5, 1.75, ((0, 8), (1, 4)))
    norm2_gain = jnp.clip(1.0 + 0.18 * jax.random.normal(streams_of[7], (D,), jnp.float32), 0.1, 1.9)
    w_router = centred(streams_of[8], (D, EXPERTS), (2 * D) ** -0.5, 0.15625, ((0, 4),), jnp.float32)
    w_hidden = centred(streams_of[9], (D, FF * EXPERTS), D ** -0.5, 0.21875, ((0, 4), (1, 8)))
    w_back = centred(streams_of[10], (D, FF * EXPERTS), (max(1, FF // 2400)) ** -0.5, 6.0, ((0, 4), (1, 8)))
    expert_choice = plant(ranked(streams_of[11], (TOKENS,), EXPERTS, 1), jax.random.fold_in(streams_of[11], 3), 0, EXPERTS - 1).astype(jnp.int32)
    doc_ids = draw_doc_ids(jax.random.fold_in(streams_of[14], 71), 0)
    grad_out = centred(streams_of[13], (TOKENS, D), 1.0, 6.0, ((0, 32),))
    return dict(x_in=x_in, norm1_gain=norm1_gain, w_query=w_query, w_key=w_key, w_value=w_value, relative_bias_table=relative_bias_table, w_out=w_out, norm2_gain=norm2_gain, w_router=w_router, w_hidden=w_hidden, w_back=w_back, expert_choice=expert_choice, doc_ids=doc_ids, grad_out=grad_out)


@jax.custom_vjp
def low(v):
    return lax.optimization_barrier(v.astype(jnp.bfloat16)).astype(jnp.float32)

@jax.custom_vjp
def low_back(v):
    return v

def low_keep(v):
    return (low(v), None)

def low_pass(kept, grad):
    return (grad,)

def back_keep(v):
    return (v, None)

def back_low(kept, grad):
    return (low(grad),)
low.defvjp(low_keep, low_pass)
low_back.defvjp(back_keep, back_low)
epsilon = 1e-06
far_steps = (12, 16, 23, 32, 46, 64, 91)
highest = lax.Precision.HIGHEST

def bucket_ids(offset):
    ahead_part = (offset > 0).astype(jnp.int32) * 16
    distance = jnp.abs(offset)
    far_part = 8 + sum(((distance >= threshold).astype(jnp.int32) for threshold in far_steps))
    return ahead_part + jnp.where(distance < 8, distance, far_part)

def rms_norm(values, gain_vector):
    mean_square = lax.optimization_barrier(jnp.mean(values * values, axis=-1, keepdims=True))
    return values * lax.rsqrt(mean_square + epsilon) * gain_vector

def attend_sequence(bias_table, inputs):
    query_seq, key_seq, value_seq, doc_seq = inputs
    block_rows = min(512, SEQ)
    block_count = SEQ // block_rows
    span = block_rows + 2 * WINDOW
    zero_rows = jnp.zeros((WINDOW, HD), jnp.float32)
    key_pad = jnp.concatenate([zero_rows, key_seq, zero_rows], axis=0)
    value_pad = jnp.concatenate([zero_rows, value_seq, zero_rows], axis=0)
    no_doc = jnp.full((WINDOW,), -1, jnp.int32)
    doc_pad = jnp.concatenate([no_doc, doc_seq.astype(jnp.int32), no_doc], axis=0)
    offset = jnp.arange(span, dtype=jnp.int32)[None, :] - WINDOW - jnp.arange(block_rows, dtype=jnp.int32)[:, None]
    bias_terms = jnp.take(jnp.transpose(bias_table), bucket_ids(offset), axis=1)
    inside = jnp.abs(offset) < WINDOW

    def one_block(block_inputs):
        query_blk, doc_blk, start = block_inputs
        key_blk = lax.dynamic_slice_in_dim(key_pad, start, span, 0).reshape(span, HEADS, HSIZE)
        value_blk = lax.dynamic_slice_in_dim(value_pad, start, span, 0).reshape(span, HEADS, HSIZE)
        doc_keys = lax.dynamic_slice_in_dim(doc_pad, start, span, 0)
        query_heads = query_blk.reshape(block_rows, HEADS, HSIZE)
        attention_scores = jnp.einsum('qhd,khd->hqk', query_heads, key_blk, precision=highest) * HSIZE ** (-0.5) + bias_terms
        allowed = inside & (doc_blk[:, None] == doc_keys[None, :])
        attention_scores = low_back(jnp.where(allowed[None], attention_scores, -1000000000.0))
        weights = low(jax.nn.softmax(attention_scores, axis=-1))
        attended = jnp.einsum('hqk,khd->qhd', weights, value_blk, precision=highest)
        return attended.reshape(block_rows, HD)
    starts = jnp.arange(block_count, dtype=jnp.int32) * block_rows
    result = lax.map(jax.checkpoint(one_block), (query_seq.reshape(block_count, block_rows, HD), doc_seq.astype(jnp.int32).reshape(block_count, block_rows), starts))
    return result.reshape(SEQ, HD)

def expert_apply(inputs):
    rows_in, first_weight, second_weight = inputs
    pre_act = low_back(jnp.dot(rows_in, first_weight, precision=highest))
    activated = low(jax.nn.gelu(pre_act))
    return jnp.dot(activated, second_weight, precision=highest)

def forward(expert_choice, doc_ids, x_in, norm1_gain, w_query, w_key, w_value, relative_bias_table, w_out, norm2_gain, w_router, w_hidden, w_back):
    normed_first = low(rms_norm(x_in, norm1_gain))
    query_all = low(low_back(jnp.dot(normed_first, w_query, precision=highest)))
    key_all = low(low_back(jnp.dot(normed_first, w_key, precision=highest)))
    value_all = low(low_back(jnp.dot(normed_first, w_value, precision=highest)))
    seq_count = TOKENS // SEQ
    stacked = (query_all.reshape(seq_count, SEQ, HD), key_all.reshape(seq_count, SEQ, HD), value_all.reshape(seq_count, SEQ, HD), doc_ids.reshape(seq_count, SEQ))

    def seq_step(carry_state, inputs):
        return (carry_state, attend_sequence(relative_bias_table, inputs))
    unused_state, attended = lax.scan(seq_step, None, stacked)
    attended = low(low_back(attended.reshape(TOKENS, HD)))
    attn_out = low(low_back(jnp.dot(attended, w_out, precision=highest)))
    hidden_first = x_in + attn_out
    normed_second = rms_norm(hidden_first, norm2_gain)
    router = jax.nn.softmax(jnp.dot(normed_second, w_router, precision=highest), axis=-1)
    chosen = expert_choice
    picked = chosen[:, None] == jnp.arange(EXPERTS, dtype=jnp.int32)[None, :]
    gate_value = lax.optimization_barrier(jnp.sum(jnp.where(picked, router, 0.0), axis=-1))
    running = jnp.cumsum(picked.astype(jnp.int32), axis=0) - 1
    position = lax.optimization_barrier(jnp.sum(jnp.where(picked, running, 0), axis=-1))
    kept_mask = position < CAPACITY
    slot_index = jnp.where(kept_mask, chosen * CAPACITY + position, EXPERTS * CAPACITY).astype(jnp.int32)
    source = jnp.full((EXPERTS * CAPACITY + 1,), TOKENS, jnp.int32).at[slot_index].set(jnp.arange(TOKENS, dtype=jnp.int32))[:EXPERTS * CAPACITY]
    padded = jnp.concatenate([low(normed_second), jnp.zeros((1, D), jnp.float32)], axis=0)
    slot_in = jnp.take(padded, source, axis=0).reshape(EXPERTS, CAPACITY, D)
    first_stack = jnp.transpose(w_hidden.reshape(D, FF, EXPERTS), (2, 0, 1))
    second_stack = jnp.transpose(w_back.reshape(D, FF, EXPERTS), (2, 1, 0))
    expert_out = lax.map(jax.checkpoint(expert_apply), (slot_in, first_stack, second_stack))
    flat_out = jnp.concatenate([expert_out.reshape(EXPERTS * CAPACITY, D), jnp.zeros((1, D), jnp.float32)], axis=0)
    routed = low_back(jnp.take(flat_out, slot_index, axis=0))
    return hidden_first + gate_value[:, None] * routed

def reference(x_in, norm1_gain, w_query, w_key, w_value, relative_bias_table, w_out, norm2_gain, w_router, w_hidden, w_back, expert_choice, doc_ids, grad_out):
    floats = (x_in.astype(jnp.float32), norm1_gain, w_query.astype(jnp.float32), w_key.astype(jnp.float32), w_value.astype(jnp.float32), relative_bias_table, w_out.astype(jnp.float32), norm2_gain, w_router, w_hidden.astype(jnp.float32), w_back.astype(jnp.float32))
    block_out, pullback = jax.vjp(partial(forward, expert_choice, doc_ids), *floats)
    gradients = pullback(grad_out.astype(jnp.float32))
    return (block_out, gradients[0], gradients[1], gradients[2], gradients[3], gradients[4], gradients[5], gradients[6], gradients[7], gradients[8], gradients[9], gradients[10])
```

```python
import functools
import math

import jax
import jax.numpy as jnp
from jax import lax
from jax.experimental import pallas as pl
from jax.experimental.pallas import tpu as pltpu
from jax.sharding import PartitionSpec as P

D = 768
HEADS = 12
HSIZE = 64
EXPERTS = 32
WINDOW = 1024


epsilon = 1e-06
far_steps = (12, 16, 23, 32, 46, 64, 91)
highest = lax.Precision.HIGHEST


def passed_along(value, axis, steps):
    count = lax.axis_size(axis)
    first, last = (max(0, -steps), min(count, count - steps))
    return lax.ppermute(value, axis, [(source, source + steps) for source in range(first, last)])


def bucket_ids(offset):
    ahead_part = (offset > 0).astype(jnp.int32) * 16
    distance = jnp.abs(offset)
    far_part = 8 + sum(((distance >= threshold).astype(jnp.int32) for threshold in far_steps))
    return ahead_part + jnp.where(distance < 8, distance, far_part)


def width_total(values):
    return lax.psum(values, "gx")


def token_rows(block_part):
    return lax.all_gather(block_part, "gy", axis=0, tiled=True)


def width_rows(block_part):
    return lax.all_gather(block_part, "gx", axis=0, tiled=True)


def width_sums(term_fn, row_number):
    return lax.psum_scatter(
        term_fn(jnp.int32(0), lax.axis_size("gx") * row_number),
        "gx",
        scatter_dimension=0,
        tiled=True,
    )


def token_sums(term_fn, row_number):
    return lax.psum_scatter(
        term_fn(jnp.int32(0), lax.axis_size("gy") * row_number),
        "gy",
        scatter_dimension=0,
        tiled=True,
    )


def collect_window(own_pair, reach):
    window_parts = []
    for offset_step in range(-reach, reach + 1):
        if offset_step == 0:
            window_parts.append(own_pair)
        else:
            window_parts.append(passed_along(own_pair, "gy", -offset_step))
    return jnp.concatenate(window_parts, axis=0)


def return_window(partials, reach, head_rows):
    combined = partials[reach * head_rows : (reach + 1) * head_rows]
    for offset_step in range(-reach, reach + 1):
        if offset_step != 0:
            start = (offset_step + reach) * head_rows
            combined = combined + passed_along(
                partials[start : start + head_rows], "gy", offset_step
            )
    return combined


def head_scores(query_heads, key_heads, bias_terms, allowed, score_scale):
    raw_scores = jnp.einsum(
        "qhd,khd->hqk", query_heads, key_heads, preferred_element_type=jnp.float32
    )
    return jnp.where(allowed[None], raw_scores * score_scale + bias_terms, -1000000000.0)


def rows_cols(blocks, width_devs, token_devs):
    grid = blocks.reshape(width_devs, token_devs, blocks.shape[1], blocks.shape[2])
    return jnp.transpose(grid, (0, 2, 1, 3)).reshape(
        width_devs * blocks.shape[1], token_devs * blocks.shape[2]
    )


def cols_rows(blocks, width_devs, token_devs):
    grid = blocks.reshape(width_devs, token_devs, blocks.shape[1], blocks.shape[2])
    return jnp.transpose(grid, (1, 2, 0, 3)).reshape(
        token_devs * blocks.shape[1], width_devs * blocks.shape[2]
    )


def grid_rows_cols(complete, width_devs, token_devs):
    row_total, col_total = complete.shape
    grid = complete.reshape(
        width_devs, row_total // width_devs, token_devs, col_total // token_devs
    )
    return jnp.transpose(grid, (0, 2, 1, 3)).reshape(
        width_devs * token_devs, row_total // width_devs, col_total // token_devs
    )


def grid_cols_rows(complete, width_devs, token_devs):
    row_total, col_total = complete.shape
    grid = complete.reshape(
        token_devs, row_total // token_devs, width_devs, col_total // width_devs
    )
    return jnp.transpose(grid, (2, 0, 1, 3)).reshape(
        width_devs * token_devs, row_total // token_devs, col_total // width_devs
    )


def spread_rows(partial_sum, column, group_count):
    picked_row = (jnp.arange(group_count, dtype=jnp.int32) == column).astype(jnp.float32)
    return picked_row.reshape((group_count,) + (1,) * partial_sum.ndim) * partial_sum[None]


def take_rows(table, index):
    return jnp.take(table, index, axis=0, mode="fill", fill_value=0)


def local(
    x_in,
    norm1_gain,
    w_query,
    w_key,
    w_value,
    relative_bias_table,
    w_out,
    norm2_gain,
    w_router,
    w_hidden,
    w_back,
    expert_choice,
    doc_ids,
    grad_out,
):
    token_devs = lax.axis_size("gy")
    width_devs = lax.axis_size("gx")
    member = lax.axis_index("gy")
    column = lax.axis_index("gx")
    local_count = x_in.shape[0]
    width_cols = w_router.shape[0]
    own_rows = local_count * width_devs
    all_tokens = own_rows * token_devs
    seq_len = local_count * token_devs
    experts = EXPERTS
    capacity = all_tokens * 5 // (4 * experts)
    score_scale = HSIZE ** (-0.5)
    reach = min((WINDOW + local_count - 2) // local_count, token_devs - 1)
    key_count = (2 * reach + 1) * local_count
    whole_weights = (
        lax.all_gather(w_query[None], ("gx", "gy"), axis=0, tiled=True),
        lax.all_gather(w_key[None], ("gx", "gy"), axis=0, tiled=True),
        lax.all_gather(w_value[None], ("gx", "gy"), axis=0, tiled=True),
        lax.all_gather(w_out[None], ("gx", "gy"), axis=0, tiled=True),
    )
    qkv_full = jnp.concatenate(
        [
            rows_cols(whole_weights[0], width_devs, token_devs),
            rows_cols(whole_weights[1], width_devs, token_devs),
            rows_cols(whole_weights[2], width_devs, token_devs),
        ],
        axis=1,
    )
    out_full = cols_rows(whole_weights[3], width_devs, token_devs)
    head_width = out_full.shape[0]
    inputs_row = x_in.astype(jnp.float32)
    scale_first = lax.rsqrt(jnp.mean(inputs_row * inputs_row, axis=-1, keepdims=True) + epsilon)
    normed_first = (inputs_row * scale_first * norm1_gain).astype(jnp.bfloat16)
    qkv_rows = jnp.dot(normed_first, qkv_full, preferred_element_type=jnp.float32).astype(
        jnp.bfloat16
    )
    query_heads = qkv_rows[:, :head_width].reshape(local_count, HEADS, HSIZE)
    pair_window = collect_window(
        qkv_rows[:, head_width:].reshape(local_count, 2, head_width), reach
    )
    key_heads = pair_window[:, 0].reshape(key_count, HEADS, HSIZE)
    value_heads = pair_window[:, 1].reshape(key_count, HEADS, HSIZE)
    query_pos = member * local_count + jnp.arange(local_count, dtype=jnp.int32)
    key_pos = (member - reach) * local_count + jnp.arange(key_count, dtype=jnp.int32)
    offset = key_pos[None, :] - query_pos[:, None]
    buckets = bucket_ids(offset)
    bias_terms = jnp.take(jnp.transpose(relative_bias_table), buckets, axis=1)
    no_doc = jnp.full((reach * local_count,), -1, jnp.int32)
    doc_padded = jnp.concatenate([no_doc, doc_ids, no_doc], axis=0)
    key_docs = lax.dynamic_slice_in_dim(doc_padded, member * local_count, key_count, 0)
    query_docs = lax.dynamic_slice_in_dim(doc_ids, member * local_count, local_count, 0)
    allowed = (jnp.abs(offset) < WINDOW) & (query_docs[:, None] == key_docs[None, :])
    attention_scores = head_scores(query_heads, key_heads, bias_terms, allowed, score_scale)
    row_peak = jnp.max(attention_scores, axis=-1, keepdims=True)
    shifted = jnp.exp(attention_scores - row_peak)
    row_sum = jnp.sum(shifted, axis=-1, keepdims=True)
    log_total = row_peak + jnp.log(row_sum)
    weights_reduced_precision = (shifted / row_sum).astype(jnp.bfloat16)
    attended = jnp.einsum(
        "hqk,khd->qhd", weights_reduced_precision, value_heads, preferred_element_type=jnp.float32
    )
    attended_low = attended.reshape(local_count, head_width).astype(jnp.bfloat16)
    attn_low = jnp.dot(attended_low, out_full, preferred_element_type=jnp.float32).astype(
        jnp.bfloat16
    )
    arrived = lax.all_to_all(
        jnp.stack([x_in, attn_low, grad_out], axis=1), "gx", split_axis=2, concat_axis=0, tiled=True
    )
    inputs = arrived[:, 0].astype(jnp.float32)
    grad_rows = arrived[:, 2].astype(jnp.float32)
    hidden_first = inputs + arrived[:, 1].astype(jnp.float32)
    scale_second = lax.rsqrt(
        width_total(jnp.sum(hidden_first * hidden_first, axis=-1)) / D + epsilon
    )[:, None]
    normed_second = hidden_first * scale_second * norm2_gain
    logits = width_total(jnp.dot(normed_second, w_router, precision=highest))
    router = jax.nn.softmax(logits, axis=-1)
    expert_iota = jnp.arange(experts, dtype=jnp.int32)
    tok_block = math.gcd(all_tokens, 128)
    block_count = all_tokens // tok_block
    chosen_rows = expert_iota[:, None] == expert_choice[None, :]
    chosen_low = chosen_rows.astype(jnp.bfloat16).reshape(experts, block_count, tok_block)
    block_iota = jnp.arange(tok_block, dtype=jnp.int32)
    upper = (block_iota[:, None] <= block_iota[None, :]).astype(jnp.bfloat16)
    inside_count = jnp.einsum("ebi,ij->ebj", chosen_low, upper, preferred_element_type=jnp.float32)
    block_totals = inside_count[:, :, tok_block - 1]
    earlier_blocks = jnp.cumsum(block_totals, axis=1) - block_totals
    counted = (inside_count + earlier_blocks[:, :, None]).reshape(experts, all_tokens)
    position = (jnp.sum(jnp.where(chosen_rows, counted, 0.0), axis=0) - 1.0).astype(jnp.int32)
    kept_all = position < capacity
    slot_all = jnp.where(kept_all, expert_choice * capacity + position, experts * capacity)
    source = (
        jnp.full((experts * capacity + 1,), all_tokens, jnp.int32)
        .at[slot_all]
        .set(jnp.arange(all_tokens, dtype=jnp.int32))[: experts * capacity]
    )
    source_seq = source // seq_len
    source_inner = source % seq_len
    source_rows = jnp.where(
        source < all_tokens,
        source_inner // local_count * own_rows
        + source_seq * local_count
        + source_inner % local_count,
        all_tokens,
    )
    row_iota = jnp.arange(all_tokens, dtype=jnp.int32)
    global_of_row = (
        row_iota // local_count % width_devs * seq_len
        + row_iota // own_rows * local_count
        + row_iota % local_count
    )
    slot_rows = jnp.take(slot_all, global_of_row)
    own_global = lax.dynamic_slice_in_dim(global_of_row, member * own_rows, own_rows, 0)
    picked_mine = jnp.take(expert_choice, own_global)[:, None] == expert_iota[None, :]
    gate_value = jnp.sum(jnp.where(picked_mine, router, 0.0), axis=-1)
    second_rows = token_rows(normed_second.astype(jnp.bfloat16))
    hidden_weight = jnp.transpose(w_hidden.reshape(width_cols, -1, experts), (2, 0, 1))
    back_weight = jnp.transpose(w_back.reshape(width_cols, -1, experts), (2, 1, 0))
    expert_rows = experts // width_devs
    slot_in = take_rows(second_rows, source_rows).reshape(experts, capacity, width_cols)

    def hidden_term(first_row, row_count):
        return jnp.einsum(
            "ecd,edf->ecf", slot_in, hidden_weight, preferred_element_type=jnp.float32
        )

    pre_block = width_sums(hidden_term, expert_rows)
    act_rows = width_rows(jax.nn.gelu(pre_block).astype(jnp.bfloat16))
    expert_out = jnp.einsum(
        "ecf,efd->ecd", act_rows, back_weight, preferred_element_type=jnp.float32
    ).reshape(experts * capacity, width_cols)

    def route_term(first_row, row_count):
        return take_rows(expert_out, slot_rows)

    routed = token_sums(route_term, own_rows)
    block_out = hidden_first + gate_value[:, None] * routed
    gate_grad = width_total(jnp.sum(grad_rows * routed, axis=-1))
    route_rows = token_rows((grad_rows * gate_value[:, None]).astype(jnp.bfloat16))
    gelu_pair = jax.vjp(jax.nn.gelu, pre_block)
    slot_grad = take_rows(route_rows, source_rows).reshape(experts, capacity, width_cols)
    back_grads = jnp.einsum("ecf,ecd->efd", act_rows, slot_grad, preferred_element_type=jnp.float32)

    def act_term(first_row, row_count):
        return jnp.einsum(
            "ecd,efd->ecf", slot_grad, back_weight, preferred_element_type=jnp.float32
        )

    act_grad = width_sums(act_term, expert_rows)
    pre_rows = width_rows(gelu_pair[1](act_grad)[0].astype(jnp.bfloat16))
    hidden_gradient_rows = jnp.einsum(
        "ecd,ecf->edf", slot_in, pre_rows, preferred_element_type=jnp.float32
    )
    slot_in_grad = jnp.einsum(
        "ecf,edf->ecd", pre_rows, hidden_weight, preferred_element_type=jnp.float32
    ).reshape(experts * capacity, width_cols)

    def back_route_term(first_row, row_count):
        return take_rows(slot_in_grad, slot_rows)

    back_routed = token_sums(back_route_term, own_rows)
    grad_hidden = jnp.transpose(hidden_gradient_rows, (1, 2, 0)).reshape(width_cols, -1)
    grad_back = jnp.transpose(back_grads, (2, 1, 0)).reshape(width_cols, -1)
    logit_grad = router * (
        gate_grad[:, None] * picked_mine.astype(jnp.float32) - (gate_value * gate_grad)[:, None]
    )
    second_grad = back_routed + jnp.einsum("re,de->rd", logit_grad, w_router, precision=highest)
    router_part = jnp.einsum("rd,re->de", normed_second, logit_grad, precision=highest)
    norm2_part = jnp.sum(second_grad * hidden_first * scale_second, axis=0)
    gained_second = second_grad * norm2_gain
    row_dot_second = width_total(jnp.sum(gained_second * hidden_first, axis=-1))[:, None]
    hidden_grad = (
        grad_rows
        + scale_second * gained_second
        - hidden_first * scale_second**3 * row_dot_second / D
    )
    out_rows, hidden_rows = (
        lax.all_to_all(block_out, "gx", split_axis=0, concat_axis=1, tiled=True),
        lax.all_to_all(hidden_grad, "gx", split_axis=0, concat_axis=1, tiled=True),
    )
    attn_grad = hidden_rows.astype(jnp.bfloat16)
    grad_out_full = jnp.einsum(
        "rf,rd->fd", attended_low, attn_grad, preferred_element_type=jnp.float32
    )
    attended_grad = (
        jnp.einsum("rd,fd->rf", attn_grad, out_full, preferred_element_type=jnp.float32)
        .astype(jnp.bfloat16)
        .reshape(local_count, HEADS, HSIZE)
    )
    scores_again = head_scores(query_heads, key_heads, bias_terms, allowed, score_scale)
    probs_again = jnp.exp(scores_again - log_total)
    value_grad = jnp.einsum(
        "hqk,qhd->khd",
        probs_again.astype(jnp.bfloat16),
        attended_grad,
        preferred_element_type=jnp.float32,
    )
    prob_grad = jnp.einsum(
        "qhd,khd->hqk", attended_grad, value_heads, preferred_element_type=jnp.float32
    )
    score_gradient = (
        probs_again * (prob_grad - jnp.sum(probs_again * prob_grad, axis=-1, keepdims=True))
    ).astype(jnp.bfloat16)
    query_grad = (
        jnp.einsum("hqk,khd->qhd", score_gradient, key_heads, preferred_element_type=jnp.float32)
        * score_scale
    ).astype(jnp.bfloat16)
    key_grad = (
        jnp.einsum("hqk,qhd->khd", score_gradient, query_heads, preferred_element_type=jnp.float32)
        * score_scale
    )
    band_low = max(0, reach * local_count - 90)
    band_high = min(key_count, reach * local_count + local_count + 90)
    bucket_iota = jnp.arange(relative_bias_table.shape[0], dtype=jnp.int32)
    band_onehot = (buckets[None, :, band_low:band_high] == bucket_iota[:, None, None]).astype(
        jnp.bfloat16
    )
    table_near = jnp.einsum(
        "ivt,zvt->zi",
        score_gradient[:, :, band_low:band_high],
        band_onehot,
        preferred_element_type=jnp.float32,
    )
    left_far = jnp.sum(score_gradient[:, :, :band_low].astype(jnp.float32), axis=(1, 2))
    right_far = jnp.sum(score_gradient[:, :, band_high:].astype(jnp.float32), axis=(1, 2))
    table_part = (
        table_near
        + (bucket_iota == 15).astype(jnp.float32)[:, None] * left_far[None, :]
        + (bucket_iota == 31).astype(jnp.float32)[:, None] * right_far[None, :]
    )
    pair_grads = return_window(
        jnp.stack(
            [key_grad.reshape(key_count, head_width), value_grad.reshape(key_count, head_width)],
            axis=1,
        ),
        reach,
        local_count,
    )
    qkv_grad = jnp.concatenate(
        [
            query_grad.reshape(local_count, head_width),
            pair_grads.astype(jnp.bfloat16).reshape(local_count, 2 * head_width),
        ],
        axis=1,
    )
    qkv_grads = jnp.einsum("rd,rc->dc", normed_first, qkv_grad, preferred_element_type=jnp.float32)
    first_grad = jnp.einsum("rc,dc->rd", qkv_grad, qkv_full, preferred_element_type=jnp.float32)
    norm1_part = jnp.sum(first_grad * inputs_row * scale_first, axis=0)
    gained_first = first_grad * norm1_gain
    row_dot_first = jnp.sum(gained_first * inputs_row, axis=-1, keepdims=True)
    input_rows = (
        hidden_rows + scale_first * gained_first - inputs_row * scale_first**3 * row_dot_first / D
    )
    summed = lax.psum(
        (
            norm1_part,
            table_part,
            spread_rows(norm2_part, column, width_devs),
            spread_rows(router_part, column, width_devs),
        ),
        ("gx", "gy"),
    )
    grad_norm1 = summed[0]
    grad_table = summed[1]
    grad_norm2 = lax.dynamic_index_in_dim(summed[2], column, 0, keepdims=False)
    grad_router = lax.dynamic_index_in_dim(summed[3], column, 0, keepdims=False)
    weight_parts = (
        lax.psum_scatter(
            grid_rows_cols(qkv_grads[:, :head_width], width_devs, token_devs),
            ("gx", "gy"),
            scatter_dimension=0,
            tiled=True,
        ),
        lax.psum_scatter(
            grid_rows_cols(qkv_grads[:, head_width : 2 * head_width], width_devs, token_devs),
            ("gx", "gy"),
            scatter_dimension=0,
            tiled=True,
        ),
        lax.psum_scatter(
            grid_rows_cols(qkv_grads[:, 2 * head_width :], width_devs, token_devs),
            ("gx", "gy"),
            scatter_dimension=0,
            tiled=True,
        ),
        lax.psum_scatter(
            grid_cols_rows(grad_out_full, width_devs, token_devs),
            ("gx", "gy"),
            scatter_dimension=0,
            tiled=True,
        ),
    )
    return (
        out_rows,
        input_rows,
        grad_norm1,
        weight_parts[0][0],
        weight_parts[1][0],
        weight_parts[2][0],
        grad_table,
        weight_parts[3][0],
        grad_norm2,
        grad_router,
        grad_hidden,
        grad_back,
    )


MESH = pl.DeviceIdType.MESH
GELU_C = math.sqrt(2.0 / math.pi)
f32, bf16 = jnp.float32, jnp.bfloat16


def nt(a, b):
    return lax.dot_general(a, b, (((1,), (1,)), ((), ())), preferred_element_type=f32)


def tn(a, b):
    return lax.dot_general(a, b, (((0,), (0,)), ((), ())), preferred_element_type=f32)


def remote(src, dst, send_sem, recv_sem, device):
    return pltpu.make_async_remote_copy(
        src_ref=src, dst_ref=dst, send_sem=send_sem, recv_sem=recv_sem,
        device_id=device, device_id_type=MESH)


def greet(devices):
    barrier = pltpu.get_barrier_semaphore()
    for device in devices:
        pl.semaphore_signal(barrier, inc=1, device_id=device, device_id_type=MESH)
    pl.semaphore_wait(barrier, len(devices))


RING = 8
GROUP = 8
LAG_B, LAG_C, LAG_D = 2, 4, 6


def moe_kernel(experts, capacity, width, units, tokens,
               r_ref, slot_row, slot_col, w1_ref, w2_ref,
               out_ref, gh_ref, gb_ref,
               x_sl, g_sl, p_ref, re_ref, rm_ref, c_ref, y_ref, gh_st, gb_st,
               pair_out, pair_in, chip_out, chip_in, line_out, line_in,
               p_sem, re_sem, rm_sem, t_sem, gh_sem, gb_sem,
               po_sem, pi_sem, co_sem, ci_sem, lo_sem, li_sem):
    gx, gy = lax.axis_index("gx"), lax.axis_index("gy")
    core, chip = lax.rem(gy, 2), gy // 2
    peer = gy + 1 - 2 * core
    is_mid = jnp.logical_and(gx > 0, gx < 3)
    is_end = jnp.logical_not(is_mid)
    mid_of = jnp.where(gx < 2, 1, 2)
    other_mid = 3 - mid_of
    end_of = jnp.where(gx < 2, 0, 3)
    line = [lax.rem(gx + k, 4) for k in (1, 2, 3)]
    chips = [lax.rem(chip + k, 4) for k in (1, 2, 3)]
    greet([(z, gy) for z in line] + [(gx, 2 * c + core) for c in chips] + [(gx, peer)])

    def send_p(e):
        return remote(p_ref.at[lax.rem(e, RING)], re_ref.at[e], p_sem.at[lax.rem(e, RING)], re_sem.at[e], (mid_of, gy))

    def send_s(e):
        return remote(p_ref.at[lax.rem(e, RING)], rm_ref.at[e], p_sem.at[lax.rem(e, RING)], rm_sem.at[e], (other_mid, gy))

    def send_t(e):
        return remote(re_ref.at[e], re_ref.at[e], t_sem.at[e], re_sem.at[e], (end_of, gy))

    def grad_copy(stage, target, sems, e):
        return pltpu.make_async_copy(stage.at[lax.rem(e, 2)], target.at[e], sems.at[lax.rem(e, 2)])

    kblock = 1024

    def step(i, carry):
        @pl.when(i < experts)
        def _():
            e = i
            sl = lax.rem(e, RING)

            @pl.when(e >= RING)
            def _():
                send_p(e - RING).wait_send()
            ids = lax.broadcasted_iota(jnp.int32, (capacity, kblock), 0) + e * capacity
            acc = jnp.zeros((capacity, 2 * width), f32)
            for kb in range(tokens // kblock):
                hot = (slot_row[:, kb * kblock:(kb + 1) * kblock] == ids).astype(f32).astype(bf16)
                acc = acc + jnp.dot(hot, r_ref[kb * kblock:(kb + 1) * kblock, :], preferred_element_type=f32)
            xs = acc[:, :width].astype(bf16)
            gs = acc[:, width:].astype(bf16)
            x_sl[sl] = xs
            g_sl[sl] = gs
            p_ref[sl, 0:capacity, :] = jnp.dot(xs, w1_ref[e], preferred_element_type=f32).astype(bf16)
            p_ref[sl, capacity:2 * capacity, :] = jnp.dot(gs, w2_ref[e], preferred_element_type=f32).astype(bf16)

            @pl.when(is_end)
            def _():
                send_p(e).start()

        eb = i - LAG_B

        @pl.when(jnp.logical_and(is_mid, jnp.logical_and(eb >= 0, eb < experts)))
        def _():
            sl = lax.rem(eb, RING)
            send_p(eb).wait_recv()
            p_ref[sl] = (p_ref[sl].astype(f32) + re_ref[eb].astype(f32)).astype(bf16)
            send_s(eb).start()

        ec = i - LAG_C

        @pl.when(jnp.logical_and(is_mid, jnp.logical_and(ec >= 0, ec < experts)))
        def _():
            sl = lax.rem(ec, RING)
            send_s(ec).wait_recv()
            re_ref[ec] = (p_ref[sl].astype(f32) + rm_ref[ec].astype(f32)).astype(bf16)
            send_t(ec).start()

        ed = i - LAG_D

        @pl.when(ed >= 0)
        def _():
            e = ed
            sl = lax.rem(e, RING)

            @pl.when(is_end)
            def _():
                send_t(e).wait_recv()
            u = re_ref[e, 0:capacity, :].astype(f32)
            ag = re_ref[e, capacity:2 * capacity, :].astype(f32)
            u2 = u * u
            th = jnp.tanh(GELU_C * (u + 0.044715 * (u2 * u)))
            half = 0.5 * (1.0 + th)
            act = (u * half).astype(bf16)
            dg = half + 0.5 * u * (1.0 - th * th) * (GELU_C * (1.0 + 3 * 0.044715 * u2))
            pg = (ag * dg).astype(bf16)
            y1 = nt(act, w2_ref[e])
            y2 = nt(pg, w1_ref[e])
            row = pl.multiple_of(lax.rem(e, GROUP) * capacity, 32)
            y_ref[pl.ds(row, capacity), :] = jnp.concatenate([y1, y2], axis=1).astype(bf16)

            @pl.when(e >= 2)
            def _():
                grad_copy(gh_st, gh_ref, gh_sem, e - 2).wait()
                grad_copy(gb_st, gb_ref, gb_sem, e - 2).wait()
            gh_st[lax.rem(e, 2)] = tn(x_sl[sl], pg)
            gb_st[lax.rem(e, 2)] = tn(g_sl[sl], act)
            grad_copy(gh_st, gh_ref, gh_sem, e).start()
            grad_copy(gb_st, gb_ref, gb_sem, e).start()

            @pl.when(lax.rem(e, GROUP) == GROUP - 1)
            def _():
                rows = 512
                base = (e - (GROUP - 1)) * capacity

                def block(b, c):
                    at = pl.ds(pl.multiple_of(b * rows, rows), rows)
                    cols = lax.broadcasted_iota(jnp.int32, (rows, GROUP * capacity), 1) + base
                    hot = (slot_col[at, :] == cols).astype(f32).astype(bf16)
                    add = jnp.dot(hot, y_ref[...], preferred_element_type=f32)

                    @pl.when(e == GROUP - 1)
                    def _():
                        c_ref[at, :] = add

                    @pl.when(e > GROUP - 1)
                    def _():
                        c_ref[at, :] = c_ref[at, :] + add
                    return c
                lax.fori_loop(0, tokens // rows, block, 0)
        return carry

    lax.fori_loop(0, experts + LAG_D, step, 0)

    def drain(e, carry):
        send_p(e).wait_send()
        return carry
    lax.fori_loop(experts - RING, experts, drain, 0)

    @pl.when(is_mid)
    def _():
        lax.fori_loop(0, experts, lambda e, c: (send_t(e).wait_send(), c)[1], 0)
    for e in (experts - 2, experts - 1):
        grad_copy(gh_st, gh_ref, gh_sem, e).wait()
        grad_copy(gb_st, gb_ref, gb_sem, e).wait()

    local = tokens // 32

    def c_block(z, c, k):
        return pl.ds(pl.multiple_of((z * 8 + 2 * c + k) * local, local), local)

    def pair_copy(z):
        return remote(pair_out.at[z], pair_in.at[z], po_sem.at[z], pi_sem.at[z], (gx, peer))

    def chip_copy(z, k):
        return remote(chip_out.at[z, k], chip_in.at[z, k], co_sem.at[z, k], ci_sem.at[z, k],
                      (gx, 2 * chips[k] + core))

    def line_copy(k):
        return remote(line_out.at[k], line_in.at[k], lo_sem.at[k], li_sem.at[k], (line[k], gy))

    order = [lax.rem(gx + 1 + k, 4) for k in range(4)]
    for k in range(4):
        z = order[k]
        for c in range(4):
            pair_out[k, c] = c_ref[c_block(z, c, 1 - core), :].astype(bf16)
        pair_copy(k).start()
    for k in range(4):
        z = order[k]
        pair_copy(k).wait_recv()
        for j in range(3):
            chip_out[k, j] = (c_ref[c_block(z, chips[j], core), :] + pair_in[k, chips[j]].astype(f32)).astype(bf16)
            chip_copy(k, j).start()
    for k in range(4):
        z = order[k]
        total = c_ref[c_block(z, chip, core), :] + pair_in[k, chip].astype(f32)
        for j in range(3):
            chip_copy(k, j).wait_recv()
            total = total + chip_in[k, j].astype(f32)
        if k < 3:
            line_out[k] = total.astype(bf16)
            line_copy(k).start()
        else:
            out_ref[gx] = total
    for k in range(3):
        line_copy(k).wait_recv()
        src = lax.rem(gx + 3 - k, 4)
        out_ref[src] = line_in[k].astype(f32)
    for k in range(4):
        pair_copy(k).wait_send()
        for j in range(3):
            chip_copy(k, j).wait_send()
    for k in range(3):
        line_copy(k).wait_send()


def moe(rows, slot_row, slot_col, w1, w2, collective_id):
    experts, width, units = w1.shape
    tokens = rows.shape[0]
    capacity = tokens * 5 // (4 * experts)
    local = tokens // 32
    vm = pl.BlockSpec(memory_space=pltpu.VMEM)
    hbm = pl.BlockSpec(memory_space=pl.ANY)
    dma = pltpu.SemaphoreType.DMA
    return pl.pallas_call(
        functools.partial(moe_kernel, experts, capacity, width, units, tokens),
        out_shape=(jax.ShapeDtypeStruct((4, local, 2 * width), f32),
                   jax.ShapeDtypeStruct((experts, width, units), f32),
                   jax.ShapeDtypeStruct((experts, width, units), f32)),
        in_specs=[vm] * 5,
        out_specs=(vm, hbm, hbm),
        scratch_shapes=[
            pltpu.VMEM((RING, capacity, width), bf16),
            pltpu.VMEM((RING, capacity, width), bf16),
            pltpu.VMEM((RING, 2 * capacity, units), bf16),
            pltpu.VMEM((experts, 2 * capacity, units), bf16),
            pltpu.VMEM((experts, 2 * capacity, units), bf16),
            pltpu.VMEM((tokens, 2 * width), f32),
            pltpu.VMEM((GROUP * capacity, 2 * width), bf16),
            pltpu.VMEM((2, width, units), f32),
            pltpu.VMEM((2, width, units), f32),
            pltpu.VMEM((4, 4, local, 2 * width), bf16),
            pltpu.VMEM((4, 4, local, 2 * width), bf16),
            pltpu.VMEM((4, 3, local, 2 * width), bf16),
            pltpu.VMEM((4, 3, local, 2 * width), bf16),
            pltpu.VMEM((3, local, 2 * width), bf16),
            pltpu.VMEM((3, local, 2 * width), bf16),
            dma((RING,)), dma((experts,)), dma((experts,)), dma((experts,)), dma((2,)), dma((2,)),
            dma((4,)), dma((4,)), dma((4, 3)), dma((4, 3)), dma((3,)), dma((3,)),
        ],
        compiler_params=pltpu.CompilerParams(
            collective_id=collective_id, has_side_effects=True, vmem_limit_bytes=62 * 2**20),
        cost_estimate=pl.CostEstimate(flops=20 * 10**9, bytes_accessed=50 * 10**6, transcendentals=2 * 10**6),
    )(rows, slot_row, slot_col, w1, w2)


def fits(mesh):
    return mesh.shape["gx"] == 4 and mesh.shape["gy"] == 8


def expert_slots(expert_choice, experts, capacity):
    all_tokens = expert_choice.shape[0]
    tok_block = 128
    chosen_rows = jnp.arange(experts, dtype=jnp.int32)[:, None] == expert_choice[None, :]
    chosen_low = chosen_rows.astype(jnp.bfloat16).reshape(experts, all_tokens // tok_block, tok_block)
    block_iota = jnp.arange(tok_block, dtype=jnp.int32)
    upper = (block_iota[:, None] <= block_iota[None, :]).astype(jnp.bfloat16)
    inside_count = jnp.einsum("ebi,ij->ebj", chosen_low, upper, preferred_element_type=jnp.float32)
    block_totals = inside_count[:, :, tok_block - 1]
    earlier_blocks = jnp.cumsum(block_totals, axis=1) - block_totals
    counted = (inside_count + earlier_blocks[:, :, None]).reshape(experts, all_tokens)
    position = (jnp.sum(jnp.where(chosen_rows, counted, 0.0), axis=0) - 1.0).astype(jnp.int32)
    return jnp.where(position < capacity, expert_choice * capacity + position, -1)


def fast(
    x_in,
    norm1_gain,
    w_query,
    w_key,
    w_value,
    relative_bias_table,
    w_out,
    norm2_gain,
    w_router,
    w_hidden,
    w_back,
    expert_choice,
    doc_ids,
    grad_out,
):
    token_devs = lax.axis_size("gy")
    width_devs = lax.axis_size("gx")
    member = lax.axis_index("gy")
    column = lax.axis_index("gx")
    local_count = x_in.shape[0]
    width_cols = w_router.shape[0]
    own_rows = local_count * width_devs
    all_tokens = own_rows * token_devs
    seq_len = local_count * token_devs
    experts = EXPERTS
    capacity = all_tokens * 5 // (4 * experts)
    score_scale = HSIZE ** (-0.5)
    reach = min((WINDOW + local_count - 2) // local_count, token_devs - 1)
    key_count = (2 * reach + 1) * local_count
    all_weights = lax.all_gather(
        jnp.concatenate([w_query, w_key, w_value, w_out.reshape(w_query.shape)], axis=1)[None],
        ("gx", "gy"),
        axis=0,
        tiled=True,
    )
    head_cols = w_query.shape[1]
    qkv_full = jnp.concatenate(
        [
            rows_cols(all_weights[:, :, k * head_cols : (k + 1) * head_cols], width_devs, token_devs)
            for k in range(3)
        ],
        axis=1,
    )
    out_full = cols_rows(
        all_weights[:, :, 3 * head_cols :].reshape(-1, *w_out.shape), width_devs, token_devs
    )
    head_width = out_full.shape[0]
    inputs_row = x_in.astype(jnp.float32)
    scale_first = lax.rsqrt(jnp.mean(inputs_row * inputs_row, axis=-1, keepdims=True) + epsilon)
    normed_first = (inputs_row * scale_first * norm1_gain).astype(jnp.bfloat16)
    qkv_rows = jnp.dot(normed_first, qkv_full, preferred_element_type=jnp.float32).astype(
        jnp.bfloat16
    )
    query_heads = qkv_rows[:, :head_width].reshape(local_count, HEADS, HSIZE)
    pair_window = collect_window(
        qkv_rows[:, head_width:].reshape(local_count, 2, head_width), reach
    )
    key_heads = pair_window[:, 0].reshape(key_count, HEADS, HSIZE)
    value_heads = pair_window[:, 1].reshape(key_count, HEADS, HSIZE)
    query_pos = member * local_count + jnp.arange(local_count, dtype=jnp.int32)
    key_pos = (member - reach) * local_count + jnp.arange(key_count, dtype=jnp.int32)
    offset = key_pos[None, :] - query_pos[:, None]
    buckets = bucket_ids(offset)
    bias_terms = sum(
        jnp.where(buckets[None] == b, relative_bias_table[b][:, None, None], 0.0)
        for b in range(relative_bias_table.shape[0])
    )
    no_doc = jnp.full((reach * local_count,), -1, jnp.int32)
    doc_padded = jnp.concatenate([no_doc, doc_ids, no_doc], axis=0)
    key_docs = lax.dynamic_slice_in_dim(doc_padded, member * local_count, key_count, 0)
    query_docs = lax.dynamic_slice_in_dim(doc_ids, member * local_count, local_count, 0)
    allowed = (jnp.abs(offset) < WINDOW) & (query_docs[:, None] == key_docs[None, :])
    attention_scores = head_scores(query_heads, key_heads, bias_terms, allowed, score_scale)
    row_peak = jnp.max(attention_scores, axis=-1, keepdims=True)
    shifted = jnp.exp(attention_scores - row_peak)
    row_sum = jnp.sum(shifted, axis=-1, keepdims=True)
    log_total = row_peak + jnp.log(row_sum)
    weights_reduced_precision = (shifted / row_sum).astype(jnp.bfloat16)
    attended = jnp.einsum(
        "hqk,khd->qhd", weights_reduced_precision, value_heads, preferred_element_type=jnp.float32
    )
    attended_low = attended.reshape(local_count, head_width).astype(jnp.bfloat16)
    attn_low = jnp.dot(attended_low, out_full, preferred_element_type=jnp.float32).astype(
        jnp.bfloat16
    )

    hidden_first = inputs_row + attn_low.astype(jnp.float32)
    grad_rows = grad_out.astype(jnp.float32)
    scale_second = lax.rsqrt(
        jnp.mean(hidden_first * hidden_first, axis=-1, keepdims=True) + epsilon
    )
    gain_second = lax.all_gather(norm2_gain, "gx", axis=0, tiled=True)
    router_full = lax.all_gather(w_router, "gx", axis=0, tiled=True)
    normed_second = hidden_first * scale_second * gain_second
    logits = jnp.dot(normed_second, router_full, precision=highest)
    router = jax.nn.softmax(logits, axis=-1)
    own_choice = lax.dynamic_slice_in_dim(
        expert_choice, (column * token_devs + member) * local_count, local_count, 0
    )
    picked = (own_choice[:, None] == jnp.arange(experts, dtype=jnp.int32)[None, :]).astype(
        jnp.float32
    )
    gate_value = jnp.sum(picked * router, axis=-1, keepdims=True)
    slot_all = expert_slots(expert_choice, experts, capacity)
    pair_rows = jnp.stack(
        [normed_second.astype(jnp.bfloat16), (grad_rows * gate_value).astype(jnp.bfloat16)], axis=1
    ).reshape(local_count, 2, width_devs, width_cols)
    pair_rows = jnp.transpose(pair_rows, (2, 0, 1, 3)).reshape(
        width_devs, local_count, 2 * width_cols
    )
    moved = lax.all_to_all(pair_rows, "gx", split_axis=0, concat_axis=0, tiled=True)
    everyone = lax.all_gather(moved[:, None], "gy", axis=1, tiled=True)
    dispatch_rows = everyone.reshape(all_tokens, 2 * width_cols)
    hidden_weight = jnp.transpose(w_hidden.reshape(width_cols, -1, experts), (2, 0, 1))
    back_weight = jnp.transpose(w_back.reshape(width_cols, -1, experts), (2, 0, 1))
    returned, hidden_grads, back_grads = moe(
        dispatch_rows, slot_all[None, :], slot_all[:, None], hidden_weight, back_weight, 1
    )
    grad_hidden = jnp.transpose(hidden_grads, (1, 2, 0)).reshape(width_cols, -1)
    grad_back = jnp.transpose(back_grads, (1, 2, 0)).reshape(width_cols, -1)
    returned = jnp.transpose(
        returned.reshape(width_devs, local_count, 2, width_cols), (2, 1, 0, 3)
    ).reshape(2, local_count, width_devs * width_cols)
    routed, back_routed = returned[0], returned[1]
    out_rows = hidden_first + gate_value * routed
    gate_grad = jnp.sum(grad_rows * routed, axis=-1, keepdims=True)
    logit_grad = router * (gate_grad * picked - gate_value * gate_grad)
    second_grad = back_routed + jnp.einsum("re,de->rd", logit_grad, router_full, precision=highest)
    router_part = jnp.einsum("rd,re->de", normed_second, logit_grad, precision=highest)
    norm2_part = jnp.sum(second_grad * hidden_first * scale_second, axis=0)
    gained_second = second_grad * gain_second
    row_dot_second = jnp.sum(gained_second * hidden_first, axis=-1, keepdims=True)
    hidden_rows = (
        grad_rows
        + scale_second * gained_second
        - hidden_first * scale_second**3 * row_dot_second / D
    )
    attn_grad = hidden_rows.astype(jnp.bfloat16)
    grad_out_full = jnp.einsum(
        "rf,rd->fd", attended_low, attn_grad, preferred_element_type=jnp.float32
    )
    attended_grad = (
        jnp.einsum("rd,fd->rf", attn_grad, out_full, preferred_element_type=jnp.float32)
        .astype(jnp.bfloat16)
        .reshape(local_count, HEADS, HSIZE)
    )
    scores_again = head_scores(query_heads, key_heads, bias_terms, allowed, score_scale)
    probs_again = jnp.exp(scores_again - log_total)
    value_grad = jnp.einsum(
        "hqk,qhd->khd",
        probs_again.astype(jnp.bfloat16),
        attended_grad,
        preferred_element_type=jnp.float32,
    )
    prob_grad = jnp.einsum(
        "qhd,khd->hqk", attended_grad, value_heads, preferred_element_type=jnp.float32
    )
    score_gradient = (
        probs_again * (prob_grad - jnp.sum(probs_again * prob_grad, axis=-1, keepdims=True))
    ).astype(jnp.bfloat16)
    query_grad = (
        jnp.einsum("hqk,khd->qhd", score_gradient, key_heads, preferred_element_type=jnp.float32)
        * score_scale
    ).astype(jnp.bfloat16)
    key_grad = (
        jnp.einsum("hqk,qhd->khd", score_gradient, query_heads, preferred_element_type=jnp.float32)
        * score_scale
    )
    band_low = max(0, reach * local_count - 90)
    band_high = min(key_count, reach * local_count + local_count + 90)
    bucket_iota = jnp.arange(relative_bias_table.shape[0], dtype=jnp.int32)
    band_onehot = (buckets[None, :, band_low:band_high] == bucket_iota[:, None, None]).astype(
        jnp.bfloat16
    )
    table_near = jnp.einsum(
        "ivt,zvt->zi",
        score_gradient[:, :, band_low:band_high],
        band_onehot,
        preferred_element_type=jnp.float32,
    )
    left_far = jnp.sum(score_gradient[:, :, :band_low].astype(jnp.float32), axis=(1, 2))
    right_far = jnp.sum(score_gradient[:, :, band_high:].astype(jnp.float32), axis=(1, 2))
    table_part = (
        table_near
        + (bucket_iota == 15).astype(jnp.float32)[:, None] * left_far[None, :]
        + (bucket_iota == 31).astype(jnp.float32)[:, None] * right_far[None, :]
    )
    pair_grads = return_window(
        jnp.stack(
            [key_grad.reshape(key_count, head_width), value_grad.reshape(key_count, head_width)],
            axis=1,
        ),
        reach,
        local_count,
    )
    qkv_grad = jnp.concatenate(
        [
            query_grad.reshape(local_count, head_width),
            pair_grads.astype(jnp.bfloat16).reshape(local_count, 2 * head_width),
        ],
        axis=1,
    )
    qkv_grads = jnp.einsum("rd,rc->dc", normed_first, qkv_grad, preferred_element_type=jnp.float32)
    first_grad = jnp.einsum("rc,dc->rd", qkv_grad, qkv_full, preferred_element_type=jnp.float32)
    norm1_part = jnp.sum(first_grad * inputs_row * scale_first, axis=0)
    gained_first = first_grad * norm1_gain
    row_dot_first = jnp.sum(gained_first * inputs_row, axis=-1, keepdims=True)
    input_rows = (
        hidden_rows + scale_first * gained_first - inputs_row * scale_first**3 * row_dot_first / D
    )
    summed = lax.psum((norm1_part, table_part, norm2_part, router_part), ("gx", "gy"))
    grad_norm2 = lax.dynamic_slice_in_dim(summed[2], column * width_cols, width_cols, 0)
    grad_router = lax.dynamic_slice_in_dim(summed[3], column * width_cols, width_cols, 0)
    weight_blocks = jnp.concatenate(
        [
            grid_rows_cols(qkv_grads[:, k * head_width : (k + 1) * head_width], width_devs, token_devs)
            for k in range(3)
        ]
        + [grid_cols_rows(grad_out_full, width_devs, token_devs).reshape(-1, *w_query.shape)],
        axis=2,
    )
    weight_part = lax.psum_scatter(
        weight_blocks, ("gx", "gy"), scatter_dimension=0, tiled=True
    )[0]
    return (
        out_rows,
        input_rows,
        summed[0],
        weight_part[:, :head_cols],
        weight_part[:, head_cols : 2 * head_cols],
        weight_part[:, 2 * head_cols : 3 * head_cols],
        summed[1],
        weight_part[:, 3 * head_cols :].reshape(w_out.shape),
        grad_norm2,
        grad_router,
        grad_hidden,
        grad_back,
    )


def solution(mesh):
    return jax.shard_map(
        fast if fits(mesh) else local,
        mesh=mesh,
        in_specs=(
            P(("gx", "gy"), None),
            P(),
            P("gx", "gy"),
            P("gx", "gy"),
            P("gx", "gy"),
            P(),
            P("gy", "gx"),
            P("gx"),
            P("gx", None),
            P("gx", "gy"),
            P("gx", "gy"),
            P(),
            P("gx"),
            P(("gx", "gy"), None),
        ),
        out_specs=(
            P(("gx", "gy"), None),
            P(("gx", "gy"), None),
            P(),
            P("gx", "gy"),
            P("gx", "gy"),
            P("gx", "gy"),
            P(),
            P("gy", "gx"),
            P("gx"),
            P("gx", None),
            P("gx", "gy"),
            P("gx", "gy"),
        ),
        check_vma=False,
    )
```

```python
import functools
import math

import jax
import jax.numpy as jnp
from jax import lax
from jax.experimental import pallas as pl
from jax.experimental.pallas import tpu as pltpu
from jax.sharding import PartitionSpec as P

D = 768
HEADS = 12
HSIZE = 64
EXPERTS = 32
WINDOW = 1024


epsilon = 1e-06
far_steps = (12, 16, 23, 32, 46, 64, 91)
highest = lax.Precision.HIGHEST


def passed_along(value, axis, steps):
    count = lax.axis_size(axis)
    first, last = (max(0, -steps), min(count, count - steps))
    return lax.ppermute(value, axis, [(source, source + steps) for source in range(first, last)])


def bucket_ids(offset):
    ahead_part = (offset > 0).astype(jnp.int32) * 16
    distance = jnp.abs(offset)
    far_part = 8 + sum(((distance >= threshold).astype(jnp.int32) for threshold in far_steps))
    return ahead_part + jnp.where(distance < 8, distance, far_part)


def width_total(values):
    return lax.psum(values, "gx")


def token_rows(block_part):
    return lax.all_gather(block_part, "gy", axis=0, tiled=True)


def width_rows(block_part):
    return lax.all_gather(block_part, "gx", axis=0, tiled=True)


def width_sums(term_fn, row_number):
    return lax.psum_scatter(
        term_fn(jnp.int32(0), lax.axis_size("gx") * row_number),
        "gx",
        scatter_dimension=0,
        tiled=True,
    )


def token_sums(term_fn, row_number):
    return lax.psum_scatter(
        term_fn(jnp.int32(0), lax.axis_size("gy") * row_number),
        "gy",
        scatter_dimension=0,
        tiled=True,
    )


def collect_window(own_pair, reach):
    window_parts = []
    for offset_step in range(-reach, reach + 1):
        if offset_step == 0:
            window_parts.append(own_pair)
        else:
            window_parts.append(passed_along(own_pair, "gy", -offset_step))
    return jnp.concatenate(window_parts, axis=0)


def return_window(partials, reach, head_rows):
    combined = partials[reach * head_rows : (reach + 1) * head_rows]
    for offset_step in range(-reach, reach + 1):
        if offset_step != 0:
            start = (offset_step + reach) * head_rows
            combined = combined + passed_along(
                partials[start : start + head_rows], "gy", offset_step
            )
    return combined


def head_scores(query_heads, key_heads, bias_terms, allowed, score_scale):
    raw_scores = jnp.einsum(
        "qhd,khd->hqk", query_heads, key_heads, preferred_element_type=jnp.float32
    )
    return jnp.where(allowed[None], raw_scores * score_scale + bias_terms, -1000000000.0)


def rows_cols(blocks, width_devs, token_devs):
    grid = blocks.reshape(width_devs, token_devs, blocks.shape[1], blocks.shape[2])
    return jnp.transpose(grid, (0, 2, 1, 3)).reshape(
        width_devs * blocks.shape[1], token_devs * blocks.shape[2]
    )


def cols_rows(blocks, width_devs, token_devs):
    grid = blocks.reshape(width_devs, token_devs, blocks.shape[1], blocks.shape[2])
    return jnp.transpose(grid, (1, 2, 0, 3)).reshape(
        token_devs * blocks.shape[1], width_devs * blocks.shape[2]
    )


def grid_rows_cols(complete, width_devs, token_devs):
    row_total, col_total = complete.shape
    grid = complete.reshape(
        width_devs, row_total // width_devs, token_devs, col_total // token_devs
    )
    return jnp.transpose(grid, (0, 2, 1, 3)).reshape(
        width_devs * token_devs, row_total // width_devs, col_total // token_devs
    )


def grid_cols_rows(complete, width_devs, token_devs):
    row_total, col_total = complete.shape
    grid = complete.reshape(
        token_devs, row_total // token_devs, width_devs, col_total // width_devs
    )
    return jnp.transpose(grid, (2, 0, 1, 3)).reshape(
        width_devs * token_devs, row_total // token_devs, col_total // width_devs
    )


def spread_rows(partial_sum, column, group_count):
    picked_row = (jnp.arange(group_count, dtype=jnp.int32) == column).astype(jnp.float32)
    return picked_row.reshape((group_count,) + (1,) * partial_sum.ndim) * partial_sum[None]


def take_rows(table, index):
    return jnp.take(table, index, axis=0, mode="fill", fill_value=0)


def local(
    x_in,
    norm1_gain,
    w_query,
    w_key,
    w_value,
    relative_bias_table,
    w_out,
    norm2_gain,
    w_router,
    w_hidden,
    w_back,
    expert_choice,
    doc_ids,
    grad_out,
):
    token_devs = lax.axis_size("gy")
    width_devs = lax.axis_size("gx")
    member = lax.axis_index("gy")
    column = lax.axis_index("gx")
    local_count = x_in.shape[0]
    width_cols = w_router.shape[0]
    own_rows = local_count * width_devs
    all_tokens = own_rows * token_devs
    seq_len = local_count * token_devs
    experts = EXPERTS
    capacity = all_tokens * 5 // (4 * experts)
    score_scale = HSIZE ** (-0.5)
    reach = min((WINDOW + local_count - 2) // local_count, token_devs - 1)
    key_count = (2 * reach + 1) * local_count
    whole_weights = (
        lax.all_gather(w_query[None], ("gx", "gy"), axis=0, tiled=True),
        lax.all_gather(w_key[None], ("gx", "gy"), axis=0, tiled=True),
        lax.all_gather(w_value[None], ("gx", "gy"), axis=0, tiled=True),
        lax.all_gather(w_out[None], ("gx", "gy"), axis=0, tiled=True),
    )
    qkv_full = jnp.concatenate(
        [
            rows_cols(whole_weights[0], width_devs, token_devs),
            rows_cols(whole_weights[1], width_devs, token_devs),
            rows_cols(whole_weights[2], width_devs, token_devs),
        ],
        axis=1,
    )
    out_full = cols_rows(whole_weights[3], width_devs, token_devs)
    head_width = out_full.shape[0]
    inputs_row = x_in.astype(jnp.float32)
    scale_first = lax.rsqrt(jnp.mean(inputs_row * inputs_row, axis=-1, keepdims=True) + epsilon)
    normed_first = (inputs_row * scale_first * norm1_gain).astype(jnp.bfloat16)
    qkv_rows = jnp.dot(normed_first, qkv_full, preferred_element_type=jnp.float32).astype(
        jnp.bfloat16
    )
    query_heads = qkv_rows[:, :head_width].reshape(local_count, HEADS, HSIZE)
    pair_window = collect_window(
        qkv_rows[:, head_width:].reshape(local_count, 2, head_width), reach
    )
    key_heads = pair_window[:, 0].reshape(key_count, HEADS, HSIZE)
    value_heads = pair_window[:, 1].reshape(key_count, HEADS, HSIZE)
    query_pos = member * local_count + jnp.arange(local_count, dtype=jnp.int32)
    key_pos = (member - reach) * local_count + jnp.arange(key_count, dtype=jnp.int32)
    offset = key_pos[None, :] - query_pos[:, None]
    buckets = bucket_ids(offset)
    bias_terms = jnp.take(jnp.transpose(relative_bias_table), buckets, axis=1)
    no_doc = jnp.full((reach * local_count,), -1, jnp.int32)
    doc_padded = jnp.concatenate([no_doc, doc_ids, no_doc], axis=0)
    key_docs = lax.dynamic_slice_in_dim(doc_padded, member * local_count, key_count, 0)
    query_docs = lax.dynamic_slice_in_dim(doc_ids, member * local_count, local_count, 0)
    allowed = (jnp.abs(offset) < WINDOW) & (query_docs[:, None] == key_docs[None, :])
    attention_scores = head_scores(query_heads, key_heads, bias_terms, allowed, score_scale)
    row_peak = jnp.max(attention_scores, axis=-1, keepdims=True)
    shifted = jnp.exp(attention_scores - row_peak)
    row_sum = jnp.sum(shifted, axis=-1, keepdims=True)
    log_total = row_peak + jnp.log(row_sum)
    weights_reduced_precision = (shifted / row_sum).astype(jnp.bfloat16)
    attended = jnp.einsum(
        "hqk,khd->qhd", weights_reduced_precision, value_heads, preferred_element_type=jnp.float32
    )
    attended_low = attended.reshape(local_count, head_width).astype(jnp.bfloat16)
    attn_low = jnp.dot(attended_low, out_full, preferred_element_type=jnp.float32).astype(
        jnp.bfloat16
    )
    arrived = lax.all_to_all(
        jnp.stack([x_in, attn_low, grad_out], axis=1), "gx", split_axis=2, concat_axis=0, tiled=True
    )
    inputs = arrived[:, 0].astype(jnp.float32)
    grad_rows = arrived[:, 2].astype(jnp.float32)
    hidden_first = inputs + arrived[:, 1].astype(jnp.float32)
    scale_second = lax.rsqrt(
        width_total(jnp.sum(hidden_first * hidden_first, axis=-1)) / D + epsilon
    )[:, None]
    normed_second = hidden_first * scale_second * norm2_gain
    logits = width_total(jnp.dot(normed_second, w_router, precision=highest))
    router = jax.nn.softmax(logits, axis=-1)
    expert_iota = jnp.arange(experts, dtype=jnp.int32)
    tok_block = math.gcd(all_tokens, 128)
    block_count = all_tokens // tok_block
    chosen_rows = expert_iota[:, None] == expert_choice[None, :]
    chosen_low = chosen_rows.astype(jnp.bfloat16).reshape(experts, block_count, tok_block)
    block_iota = jnp.arange(tok_block, dtype=jnp.int32)
    upper = (block_iota[:, None] <= block_iota[None, :]).astype(jnp.bfloat16)
    inside_count = jnp.einsum("ebi,ij->ebj", chosen_low, upper, preferred_element_type=jnp.float32)
    block_totals = inside_count[:, :, tok_block - 1]
    earlier_blocks = jnp.cumsum(block_totals, axis=1) - block_totals
    counted = (inside_count + earlier_blocks[:, :, None]).reshape(experts, all_tokens)
    position = (jnp.sum(jnp.where(chosen_rows, counted, 0.0), axis=0) - 1.0).astype(jnp.int32)
    kept_all = position < capacity
    slot_all = jnp.where(kept_all, expert_choice * capacity + position, experts * capacity)
    source = (
        jnp.full((experts * capacity + 1,), all_tokens, jnp.int32)
        .at[slot_all]
        .set(jnp.arange(all_tokens, dtype=jnp.int32))[: experts * capacity]
    )
    source_seq = source // seq_len
    source_inner = source % seq_len
    source_rows = jnp.where(
        source < all_tokens,
        source_inner // local_count * own_rows
        + source_seq * local_count
        + source_inner % local_count,
        all_tokens,
    )
    row_iota = jnp.arange(all_tokens, dtype=jnp.int32)
    global_of_row = (
        row_iota // local_count % width_devs * seq_len
        + row_iota // own_rows * local_count
        + row_iota % local_count
    )
    slot_rows = jnp.take(slot_all, global_of_row)
    own_global = lax.dynamic_slice_in_dim(global_of_row, member * own_rows, own_rows, 0)
    picked_mine = jnp.take(expert_choice, own_global)[:, None] == expert_iota[None, :]
    gate_value = jnp.sum(jnp.where(picked_mine, router, 0.0), axis=-1)
    second_rows = token_rows(normed_second.astype(jnp.bfloat16))
    hidden_weight = jnp.transpose(w_hidden.reshape(width_cols, -1, experts), (2, 0, 1))
    back_weight = jnp.transpose(w_back.reshape(width_cols, -1, experts), (2, 1, 0))
    expert_rows = experts // width_devs
    slot_in = take_rows(second_rows, source_rows).reshape(experts, capacity, width_cols)

    def hidden_term(first_row, row_count):
        return jnp.einsum(
            "ecd,edf->ecf", slot_in, hidden_weight, preferred_element_type=jnp.float32
        )

    pre_block = width_sums(hidden_term, expert_rows)
    act_rows = width_rows(jax.nn.gelu(pre_block).astype(jnp.bfloat16))
    expert_out = jnp.einsum(
        "ecf,efd->ecd", act_rows, back_weight, preferred_element_type=jnp.float32
    ).reshape(experts * capacity, width_cols)

    def route_term(first_row, row_count):
        return take_rows(expert_out, slot_rows)

    routed = token_sums(route_term, own_rows)
    block_out = hidden_first + gate_value[:, None] * routed
    gate_grad = width_total(jnp.sum(grad_rows * routed, axis=-1))
    route_rows = token_rows((grad_rows * gate_value[:, None]).astype(jnp.bfloat16))
    gelu_pair = jax.vjp(jax.nn.gelu, pre_block)
    slot_grad = take_rows(route_rows, source_rows).reshape(experts, capacity, width_cols)
    back_grads = jnp.einsum("ecf,ecd->efd", act_rows, slot_grad, preferred_element_type=jnp.float32)

    def act_term(first_row, row_count):
        return jnp.einsum(
            "ecd,efd->ecf", slot_grad, back_weight, preferred_element_type=jnp.float32
        )

    act_grad = width_sums(act_term, expert_rows)
    pre_rows = width_rows(gelu_pair[1](act_grad)[0].astype(jnp.bfloat16))
    hidden_gradient_rows = jnp.einsum(
        "ecd,ecf->edf", slot_in, pre_rows, preferred_element_type=jnp.float32
    )
    slot_in_grad = jnp.einsum(
        "ecf,edf->ecd", pre_rows, hidden_weight, preferred_element_type=jnp.float32
    ).reshape(experts * capacity, width_cols)

    def back_route_term(first_row, row_count):
        return take_rows(slot_in_grad, slot_rows)

    back_routed = token_sums(back_route_term, own_rows)
    grad_hidden = jnp.transpose(hidden_gradient_rows, (1, 2, 0)).reshape(width_cols, -1)
    grad_back = jnp.transpose(back_grads, (2, 1, 0)).reshape(width_cols, -1)
    logit_grad = router * (
        gate_grad[:, None] * picked_mine.astype(jnp.float32) - (gate_value * gate_grad)[:, None]
    )
    second_grad = back_routed + jnp.einsum("re,de->rd", logit_grad, w_router, precision=highest)
    router_part = jnp.einsum("rd,re->de", normed_second, logit_grad, precision=highest)
    norm2_part = jnp.sum(second_grad * hidden_first * scale_second, axis=0)
    gained_second = second_grad * norm2_gain
    row_dot_second = width_total(jnp.sum(gained_second * hidden_first, axis=-1))[:, None]
    hidden_grad = (
        grad_rows
        + scale_second * gained_second
        - hidden_first * scale_second**3 * row_dot_second / D
    )
    out_rows, hidden_rows = (
        lax.all_to_all(block_out, "gx", split_axis=0, concat_axis=1, tiled=True),
        lax.all_to_all(hidden_grad, "gx", split_axis=0, concat_axis=1, tiled=True),
    )
    attn_grad = hidden_rows.astype(jnp.bfloat16)
    grad_out_full = jnp.einsum(
        "rf,rd->fd", attended_low, attn_grad, preferred_element_type=jnp.float32
    )
    attended_grad = (
        jnp.einsum("rd,fd->rf", attn_grad, out_full, preferred_element_type=jnp.float32)
        .astype(jnp.bfloat16)
        .reshape(local_count, HEADS, HSIZE)
    )
    scores_again = head_scores(query_heads, key_heads, bias_terms, allowed, score_scale)
    probs_again = jnp.exp(scores_again - log_total)
    value_grad = jnp.einsum(
        "hqk,qhd->khd",
        probs_again.astype(jnp.bfloat16),
        attended_grad,
        preferred_element_type=jnp.float32,
    )
    prob_grad = jnp.einsum(
        "qhd,khd->hqk", attended_grad, value_heads, preferred_element_type=jnp.float32
    )
    score_gradient = (
        probs_again * (prob_grad - jnp.sum(probs_again * prob_grad, axis=-1, keepdims=True))
    ).astype(jnp.bfloat16)
    query_grad = (
        jnp.einsum("hqk,khd->qhd", score_gradient, key_heads, preferred_element_type=jnp.float32)
        * score_scale
    ).astype(jnp.bfloat16)
    key_grad = (
        jnp.einsum("hqk,qhd->khd", score_gradient, query_heads, preferred_element_type=jnp.float32)
        * score_scale
    )
    band_low = max(0, reach * local_count - 90)
    band_high = min(key_count, reach * local_count + local_count + 90)
    bucket_iota = jnp.arange(relative_bias_table.shape[0], dtype=jnp.int32)
    band_onehot = (buckets[None, :, band_low:band_high] == bucket_iota[:, None, None]).astype(
        jnp.bfloat16
    )
    table_near = jnp.einsum(
        "ivt,zvt->zi",
        score_gradient[:, :, band_low:band_high],
        band_onehot,
        preferred_element_type=jnp.float32,
    )
    left_far = jnp.sum(score_gradient[:, :, :band_low].astype(jnp.float32), axis=(1, 2))
    right_far = jnp.sum(score_gradient[:, :, band_high:].astype(jnp.float32), axis=(1, 2))
    table_part = (
        table_near
        + (bucket_iota == 15).astype(jnp.float32)[:, None] * left_far[None, :]
        + (bucket_iota == 31).astype(jnp.float32)[:, None] * right_far[None, :]
    )
    pair_grads = return_window(
        jnp.stack(
            [key_grad.reshape(key_count, head_width), value_grad.reshape(key_count, head_width)],
            axis=1,
        ),
        reach,
        local_count,
    )
    qkv_grad = jnp.concatenate(
        [
            query_grad.reshape(local_count, head_width),
            pair_grads.astype(jnp.bfloat16).reshape(local_count, 2 * head_width),
        ],
        axis=1,
    )
    qkv_grads = jnp.einsum("rd,rc->dc", normed_first, qkv_grad, preferred_element_type=jnp.float32)
    first_grad = jnp.einsum("rc,dc->rd", qkv_grad, qkv_full, preferred_element_type=jnp.float32)
    norm1_part = jnp.sum(first_grad * inputs_row * scale_first, axis=0)
    gained_first = first_grad * norm1_gain
    row_dot_first = jnp.sum(gained_first * inputs_row, axis=-1, keepdims=True)
    input_rows = (
        hidden_rows + scale_first * gained_first - inputs_row * scale_first**3 * row_dot_first / D
    )
    summed = lax.psum(
        (
            norm1_part,
            table_part,
            spread_rows(norm2_part, column, width_devs),
            spread_rows(router_part, column, width_devs),
        ),
        ("gx", "gy"),
    )
    grad_norm1 = summed[0]
    grad_table = summed[1]
    grad_norm2 = lax.dynamic_index_in_dim(summed[2], column, 0, keepdims=False)
    grad_router = lax.dynamic_index_in_dim(summed[3], column, 0, keepdims=False)
    weight_parts = (
        lax.psum_scatter(
            grid_rows_cols(qkv_grads[:, :head_width], width_devs, token_devs),
            ("gx", "gy"),
            scatter_dimension=0,
            tiled=True,
        ),
        lax.psum_scatter(
            grid_rows_cols(qkv_grads[:, head_width : 2 * head_width], width_devs, token_devs),
            ("gx", "gy"),
            scatter_dimension=0,
            tiled=True,
        ),
        lax.psum_scatter(
            grid_rows_cols(qkv_grads[:, 2 * head_width :], width_devs, token_devs),
            ("gx", "gy"),
            scatter_dimension=0,
            tiled=True,
        ),
        lax.psum_scatter(
            grid_cols_rows(grad_out_full, width_devs, token_devs),
            ("gx", "gy"),
            scatter_dimension=0,
            tiled=True,
        ),
    )
    return (
        out_rows,
        input_rows,
        grad_norm1,
        weight_parts[0][0],
        weight_parts[1][0],
        weight_parts[2][0],
        grad_table,
        weight_parts[3][0],
        grad_norm2,
        grad_router,
        grad_hidden,
        grad_back,
    )


MESH = pl.DeviceIdType.MESH
GELU_C = math.sqrt(2.0 / math.pi)
f32, bf16 = jnp.float32, jnp.bfloat16


def nt(a, b):
    return lax.dot_general(a, b, (((1,), (1,)), ((), ())), preferred_element_type=f32)


def tn(a, b):
    return lax.dot_general(a, b, (((0,), (0,)), ((), ())), preferred_element_type=f32)


def remote(src, dst, send_sem, recv_sem, device):
    return pltpu.make_async_remote_copy(
        src_ref=src, dst_ref=dst, send_sem=send_sem, recv_sem=recv_sem,
        device_id=device, device_id_type=MESH)


def greet(devices):
    barrier = pltpu.get_barrier_semaphore()
    for device in devices:
        pl.semaphore_signal(barrier, inc=1, device_id=device, device_id_type=MESH)
    pl.semaphore_wait(barrier, len(devices))


RING = 8
GROUP = 8
LAG_B, LAG_C, LAG_D = 2, 4, 6


def moe_kernel(experts, capacity, width, units, tokens,
               r_ref, slot_row, slot_col, w1_ref, w2_ref,
               out_ref, gh_ref, gb_ref,
               x_sl, g_sl, p_ref, re_ref, rm_ref, c_ref, y_ref, gh_st, gb_st,
               pair_out, pair_in, chip_out, chip_in, line_out, line_in,
               p_sem, re_sem, rm_sem, t_sem, gh_sem, gb_sem,
               po_sem, pi_sem, co_sem, ci_sem, lo_sem, li_sem):
    gx, gy = lax.axis_index("gx"), lax.axis_index("gy")
    core, chip = lax.rem(gy, 2), gy // 2
    peer = gy + 1 - 2 * core
    is_mid = jnp.logical_and(gx > 0, gx < 3)
    is_end = jnp.logical_not(is_mid)
    mid_of = jnp.where(gx < 2, 1, 2)
    other_mid = 3 - mid_of
    end_of = jnp.where(gx < 2, 0, 3)
    line = [lax.rem(gx + k, 4) for k in (1, 2, 3)]
    chips = [lax.rem(chip + k, 4) for k in (1, 2, 3)]
    greet([(z, gy) for z in line] + [(gx, 2 * c + core) for c in chips] + [(gx, peer)])

    def send_p(e):
        return remote(p_ref.at[lax.rem(e, RING)], re_ref.at[e], p_sem.at[lax.rem(e, RING)], re_sem.at[e], (mid_of, gy))

    def send_s(e):
        return remote(p_ref.at[lax.rem(e, RING)], rm_ref.at[e], p_sem.at[lax.rem(e, RING)], rm_sem.at[e], (other_mid, gy))

    def send_t(e):
        return remote(re_ref.at[e], re_ref.at[e], t_sem.at[e], re_sem.at[e], (end_of, gy))

    def grad_copy(stage, target, sems, e):
        return pltpu.make_async_copy(stage.at[lax.rem(e, 2)], target.at[e], sems.at[lax.rem(e, 2)])

    kblock = 1024

    def step(i, carry):
        @pl.when(i < experts)
        def _():
            e = i
            sl = lax.rem(e, RING)

            @pl.when(e >= RING)
            def _():
                send_p(e - RING).wait_send()
            ids = lax.broadcasted_iota(jnp.int32, (capacity, kblock), 0) + e * capacity
            acc = jnp.zeros((capacity, 2 * width), f32)
            for kb in range(tokens // kblock):
                hot = (slot_row[:, kb * kblock:(kb + 1) * kblock] == ids).astype(f32).astype(bf16)
                acc = acc + jnp.dot(hot, r_ref[kb * kblock:(kb + 1) * kblock, :], preferred_element_type=f32)
            xs = acc[:, :width].astype(bf16)
            gs = acc[:, width:].astype(bf16)
            x_sl[sl] = xs
            g_sl[sl] = gs
            p_ref[sl, 0:capacity, :] = jnp.dot(xs, w1_ref[e], preferred_element_type=f32).astype(bf16)
            p_ref[sl, capacity:2 * capacity, :] = jnp.dot(gs, w2_ref[e], preferred_element_type=f32).astype(bf16)

            @pl.when(is_end)
            def _():
                send_p(e).start()

        eb = i - LAG_B

        @pl.when(jnp.logical_and(is_mid, jnp.logical_and(eb >= 0, eb < experts)))
        def _():
            sl = lax.rem(eb, RING)
            send_p(eb).wait_recv()
            p_ref[sl] = (p_ref[sl].astype(f32) + re_ref[eb].astype(f32)).astype(bf16)
            send_s(eb).start()

        ec = i - LAG_C

        @pl.when(jnp.logical_and(is_mid, jnp.logical_and(ec >= 0, ec < experts)))
        def _():
            sl = lax.rem(ec, RING)
            send_s(ec).wait_recv()
            re_ref[ec] = (p_ref[sl].astype(f32) + rm_ref[ec].astype(f32)).astype(bf16)
            send_t(ec).start()

        ed = i - LAG_D

        @pl.when(ed >= 0)
        def _():
            e = ed
            sl = lax.rem(e, RING)

            @pl.when(is_end)
            def _():
                send_t(e).wait_recv()
            u = re_ref[e, 0:capacity, :].astype(f32)
            ag = re_ref[e, capacity:2 * capacity, :].astype(f32)
            u2 = u * u
            th = jnp.tanh(GELU_C * (u + 0.044715 * (u2 * u)))
            half = 0.5 * (1.0 + th)
            act = (u * half).astype(bf16)
            dg = half + 0.5 * u * (1.0 - th * th) * (GELU_C * (1.0 + 3 * 0.044715 * u2))
            pg = (ag * dg).astype(bf16)
            y1 = nt(act, w2_ref[e])
            y2 = nt(pg, w1_ref[e])
            row = pl.multiple_of(lax.rem(e, GROUP) * capacity, 32)
            y_ref[pl.ds(row, capacity), :] = jnp.concatenate([y1, y2], axis=1).astype(bf16)

            @pl.when(e >= 2)
            def _():
                grad_copy(gh_st, gh_ref, gh_sem, e - 2).wait()
                grad_copy(gb_st, gb_ref, gb_sem, e - 2).wait()
            gh_st[lax.rem(e, 2)] = tn(x_sl[sl], pg)
            gb_st[lax.rem(e, 2)] = tn(g_sl[sl], act)
            grad_copy(gh_st, gh_ref, gh_sem, e).start()
            grad_copy(gb_st, gb_ref, gb_sem, e).start()

            @pl.when(lax.rem(e, GROUP) == GROUP - 1)
            def _():
                rows = 512
                base = (e - (GROUP - 1)) * capacity

                def block(b, c):
                    at = pl.ds(pl.multiple_of(b * rows, rows), rows)
                    cols = lax.broadcasted_iota(jnp.int32, (rows, GROUP * capacity), 1) + base
                    hot = (slot_col[at, :] == cols).astype(f32).astype(bf16)
                    add = jnp.dot(hot, y_ref[...], preferred_element_type=f32)

                    @pl.when(e == GROUP - 1)
                    def _():
                        c_ref[at, :] = add

                    @pl.when(e > GROUP - 1)
                    def _():
                        c_ref[at, :] = c_ref[at, :] + add
                    return c
                lax.fori_loop(0, tokens // rows, block, 0)
        return carry

    lax.fori_loop(0, experts + LAG_D, step, 0)

    def drain(e, carry):
        send_p(e).wait_send()
        return carry
    lax.fori_loop(experts - RING, experts, drain, 0)

    @pl.when(is_mid)
    def _():
        lax.fori_loop(0, experts, lambda e, c: (send_t(e).wait_send(), c)[1], 0)
    for e in (experts - 2, experts - 1):
        grad_copy(gh_st, gh_ref, gh_sem, e).wait()
        grad_copy(gb_st, gb_ref, gb_sem, e).wait()

    local = tokens // 32

    def c_block(z, c, k):
        return pl.ds(pl.multiple_of((z * 8 + 2 * c + k) * local, local), local)

    def pair_copy(z):
        return remote(pair_out.at[z], pair_in.at[z], po_sem.at[z], pi_sem.at[z], (gx, peer))

    def chip_copy(z, k):
        return remote(chip_out.at[z, k], chip_in.at[z, k], co_sem.at[z, k], ci_sem.at[z, k],
                      (gx, 2 * chips[k] + core))

    def line_copy(k):
        return remote(line_out.at[k], line_in.at[k], lo_sem.at[k], li_sem.at[k], (line[k], gy))

    order = [lax.rem(gx + 1 + k, 4) for k in range(4)]
    for k in range(4):
        z = order[k]
        for c in range(4):
            pair_out[k, c] = c_ref[c_block(z, c, 1 - core), :].astype(bf16)
        pair_copy(k).start()
    for k in range(4):
        z = order[k]
        pair_copy(k).wait_recv()
        for j in range(3):
            chip_out[k, j] = (c_ref[c_block(z, chips[j], core), :] + pair_in[k, chips[j]].astype(f32)).astype(bf16)
            chip_copy(k, j).start()
    for k in range(4):
        z = order[k]
        total = c_ref[c_block(z, chip, core), :] + pair_in[k, chip].astype(f32)
        for j in range(3):
            chip_copy(k, j).wait_recv()
            total = total + chip_in[k, j].astype(f32)
        if k < 3:
            line_out[k] = total.astype(bf16)
            line_copy(k).start()
        else:
            out_ref[gx] = total
    for k in range(3):
        line_copy(k).wait_recv()
        src = lax.rem(gx + 3 - k, 4)
        out_ref[src] = line_in[k].astype(f32)
    for k in range(4):
        pair_copy(k).wait_send()
        for j in range(3):
            chip_copy(k, j).wait_send()
    for k in range(3):
        line_copy(k).wait_send()


def moe(rows, slot_row, slot_col, w1, w2, collective_id):
    experts, width, units = w1.shape
    tokens = rows.shape[0]
    capacity = tokens * 5 // (4 * experts)
    local = tokens // 32
    vm = pl.BlockSpec(memory_space=pltpu.VMEM)
    hbm = pl.BlockSpec(memory_space=pl.ANY)
    dma = pltpu.SemaphoreType.DMA
    return pl.pallas_call(
        functools.partial(moe_kernel, experts, capacity, width, units, tokens),
        out_shape=(jax.ShapeDtypeStruct((4, local, 2 * width), f32),
                   jax.ShapeDtypeStruct((experts, width, units), f32),
                   jax.ShapeDtypeStruct((experts, width, units), f32)),
        in_specs=[vm] * 5,
        out_specs=(vm, hbm, hbm),
        scratch_shapes=[
            pltpu.VMEM((RING, capacity, width), bf16),
            pltpu.VMEM((RING, capacity, width), bf16),
            pltpu.VMEM((RING, 2 * capacity, units), bf16),
            pltpu.VMEM((experts, 2 * capacity, units), bf16),
            pltpu.VMEM((experts, 2 * capacity, units), bf16),
            pltpu.VMEM((tokens, 2 * width), f32),
            pltpu.VMEM((GROUP * capacity, 2 * width), bf16),
            pltpu.VMEM((2, width, units), f32),
            pltpu.VMEM((2, width, units), f32),
            pltpu.VMEM((4, 4, local, 2 * width), bf16),
            pltpu.VMEM((4, 4, local, 2 * width), bf16),
            pltpu.VMEM((4, 3, local, 2 * width), bf16),
            pltpu.VMEM((4, 3, local, 2 * width), bf16),
            pltpu.VMEM((3, local, 2 * width), bf16),
            pltpu.VMEM((3, local, 2 * width), bf16),
            dma((RING,)), dma((experts,)), dma((experts,)), dma((experts,)), dma((2,)), dma((2,)),
            dma((4,)), dma((4,)), dma((4, 3)), dma((4, 3)), dma((3,)), dma((3,)),
        ],
        compiler_params=pltpu.CompilerParams(
            collective_id=collective_id, has_side_effects=True, vmem_limit_bytes=62 * 2**20),
        cost_estimate=pl.CostEstimate(flops=20 * 10**9, bytes_accessed=50 * 10**6, transcendentals=2 * 10**6),
    )(rows, slot_row, slot_col, w1, w2)


def nn(a, b):
    return jnp.dot(a, b, preferred_element_type=f32)


class Place:
    def __init__(self):
        self.gx, self.gy = lax.axis_index("gx"), lax.axis_index("gy")
        self.core, self.chip = lax.rem(self.gy, 2), self.gy // 2
        self.pair = (self.gx, self.gy + 1 - 2 * self.core)
        self.line = [lax.rem(self.gx + k, 4) for k in (1, 2, 3)]
        self.chips = [lax.rem(self.chip + k, 4) for k in (1, 2, 3)]
        self.line_from = [lax.rem(self.gx + 4 - k, 4) for k in (1, 2, 3)]
        self.chips_from = [lax.rem(self.chip + 4 - k, 4) for k in (1, 2, 3)]

    def on_line(self, k):
        return (self.line[k], self.gy)

    def on_plane(self, k):
        return (self.gx, 2 * self.chips[k] + self.core)

    def greet_all(self):
        greet([self.on_line(k) for k in range(3)] + [self.on_plane(k) for k in range(3)] + [self.pair])


def near_buckets(rows):
    offset = (
        lax.broadcasted_iota(jnp.int32, (rows, 3 * rows), 1)
        - rows
        - lax.broadcasted_iota(jnp.int32, (rows, 3 * rows), 0)
    )
    return bucket_ids(offset)


def fill_bias(bias_ref, table_ref, chip, heads):
    rows = bias_ref.shape[1]
    span = bias_ref.shape[2]
    mid = span // 2
    buckets = near_buckets(rows)
    for h in range(heads):
        column = chip * heads + h
        near = jnp.zeros(buckets.shape, f32)
        for b in range(table_ref.shape[0]):
            near = jnp.where(buckets == b, table_ref[b, column], near)
        bias_ref[h, :, 0:mid - rows] = jnp.full((rows, mid - rows), table_ref[15, column], f32)
        bias_ref[h, :, mid - rows:mid + 2 * rows] = near
        bias_ref[h, :, mid + 2 * rows:] = jnp.full((rows, span - mid - 2 * rows), table_ref[31, column], f32)


def unit_scores(q_block, keys, bias_ref, h, block_at, allowed):
    rows = q_block.shape[0]
    seq = keys.shape[0]
    lanes = lax.broadcasted_iota(jnp.int32, q_block.shape, 1) // HSIZE
    masked = jnp.where(lanes == h, q_block, jnp.zeros_like(q_block))
    start = pl.multiple_of(seq - rows * block_at, rows)
    return jnp.where(allowed, nt(masked, keys) + bias_ref[h, :, pl.ds(start, seq)], -1000000000.0)


def front_kernel(heads, experts,
                 x_ref, gain1_ref, wqkv_ref, wout_ref, table_ref, small_ref, doc_row, doc_col, choice_ref, grad_ref,
                 rows_ref, hidden_ref, normed_ref, router_ref, gate_ref, at_ref, q_ref, kv_ref, lse_ref, xn_ref,
                 wqkv_all, wout_all, small_all, bias_ref,
                 wq_st, wo_st, sm_st, at_in, rows_out,
                 xn_s, xn_r, wq_s, wq_r, wqp_s, wqp_r, sm_s, sm_r, wo_s, wo_r, woc_s, woc_r, wop_s, wop_r,
                 kv_s, kv_r, at_s, at_r, rz_s, rz_r, rc_s, rc_r, rp_s, rp_r):
    me = Place()
    gx, gy, core, chip = me.gx, me.gy, me.core, me.chip
    width = wqkv_ref.shape[0]
    cols = wqkv_ref.shape[1] // 3
    local = x_ref.shape[0]
    x = x_ref[...].astype(f32)
    r1 = lax.rsqrt(jnp.mean(x * x, axis=-1, keepdims=True) + epsilon)
    xn_ref[chip] = (x * r1 * gain1_ref[...]).astype(bf16)
    me.greet_all()

    def wq_line(k):
        return remote(wqkv_ref, wq_st.at[core, gx], wq_s.at[k], wq_r.at[k], me.on_line(k))

    def xn_plane(k):
        return remote(xn_ref.at[chip], xn_ref.at[chip], xn_s.at[k], xn_r.at[k], me.on_plane(k))

    def sm_line(k):
        return remote(small_ref, sm_st.at[gx], sm_s.at[k], sm_r.at[k], me.on_line(k))

    def wo_line(k):
        return remote(wout_ref, wo_st.at[gy, gx], wo_s.at[k], wo_r.at[k], me.on_line(k))

    def wq_pair(k):
        src = wqkv_ref if k == 0 else wq_st.at[core, me.line_from[k - 1]]
        z = gx if k == 0 else me.line_from[k - 1]
        return remote(src, wq_st.at[core, z], wqp_s.at[k], wqp_r.at[k], me.pair)

    def wo_plane(k):
        return remote(wo_st.at[gy], wo_st.at[gy], woc_s.at[k], woc_r.at[k], me.on_plane(k))

    def wo_pair(k):
        c = chip if k == 0 else me.chips_from[k - 1]
        return remote(wo_st.at[2 * c + core], wo_st.at[2 * c + core], wop_s.at[k], wop_r.at[k], me.pair)

    for k in range(3):
        wq_line(k).start()
        xn_plane(k).start()
    wq_pair(0).start()
    for k in range(3):
        wo_line(k).start()
        sm_line(k).start()
    wq_st[core, gx] = wqkv_ref[...]
    wo_st[gy, gx] = wout_ref[...]
    sm_st[gx] = small_ref[...]
    fill_bias(bias_ref, table_ref, chip, heads)
    for k in range(3):
        wq_line(k).wait_recv()
        wq_pair(k + 1).start()
    for k in range(3):
        wo_line(k).wait_recv()
    for k in range(3):
        wo_plane(k).start()
    wo_pair(0).start()
    for k in range(4):
        wq_pair(k).wait_recv()
    for z in range(4):
        parts = [wq_st[0, z], wq_st[1, z]]
        wqkv_all[z * width:(z + 1) * width, :] = jnp.concatenate(
            [parts[j][:, n * cols:(n + 1) * cols] for n in range(3) for j in range(2)], axis=1)

    def kv_pair(c):
        return remote(kv_ref.at[2 * c + core], kv_ref.at[2 * c + core], kv_s.at[c], kv_r.at[c], me.pair)

    scale = HSIZE ** (-0.5)
    hd = 2 * cols
    for k in range(4):
        c = chip if k == 0 else me.chips_from[k - 1]
        if k > 0:
            xn_plane(k - 1).wait_recv()
        made = nn(xn_ref[c], wqkv_all[...])
        q_ref[c] = (made[:, :hd].astype(bf16).astype(f32) * scale).astype(bf16)
        kv_ref[2 * c + core] = made[:, hd:].astype(bf16)
        kv_pair(c).start()
    for k in range(3):
        wo_plane(k).wait_recv()
        wo_pair(k + 1).start()
    for c in range(4):
        kv_pair(c).wait_recv()
    seq = 8 * local
    lanes = lax.broadcasted_iota(jnp.int32, (local, hd), 1) // HSIZE

    def at_plane(k):
        return remote(at_ref.at[me.chips[k]], at_in.at[chip], at_s.at[k], at_r.at[k], me.on_plane(k))

    for k in range(4):
        c = me.chips[k] if k < 3 else chip
        block_at = 2 * c + core
        allowed = doc_col[pl.ds(pl.multiple_of(block_at * local, local), local), :] == doc_row[...]
        keys = kv_ref[:, :, :hd].reshape(seq, hd)
        values = kv_ref[:, :, hd:].reshape(seq, hd)
        total = jnp.zeros((local, hd), f32)
        for h in range(heads):
            scores = unit_scores(q_ref[c], keys, bias_ref, h, block_at, allowed)
            peak = jnp.max(scores, axis=-1, keepdims=True)
            shifted = jnp.exp(scores - peak)
            summed = jnp.sum(shifted, axis=-1, keepdims=True)
            lse_ref[c, h] = jnp.broadcast_to(peak + jnp.log(summed), (local, 128))
            low = (shifted * (1.0 / summed)).astype(bf16)
            total = jnp.where(lanes == h, nn(low, values), total)
        at_ref[c] = total.astype(bf16)
        if k < 3:
            at_plane(k).start()
        else:
            at_in[chip] = total.astype(bf16)
    for k in range(3):
        sm_line(k).wait_recv()
    small_all[...] = jnp.concatenate([sm_st[z] for z in range(4)], axis=1)
    for k in range(4):
        wo_pair(k).wait_recv()
    for g in range(8):
        wout_all[g * cols:(g + 1) * cols, :] = jnp.concatenate([wo_st[g, z] for z in range(4)], axis=1)
    for k in range(3):
        at_plane(k).wait_recv()
    attended = jnp.concatenate([at_in[c] for c in range(4)], axis=1)
    hidden = x + nn(attended, wout_all[...]).astype(bf16).astype(f32)
    hidden_ref[...] = hidden
    r2 = lax.rsqrt(jnp.mean(hidden * hidden, axis=-1, keepdims=True) + epsilon)
    normed = hidden * r2 * small_all[experts:experts + 1, :]
    normed_ref[...] = normed
    logits = lax.dot_general(normed, small_all[:experts, :], (((1,), (1,)), ((), ())),
                             precision=lax.Precision.HIGHEST, preferred_element_type=f32)
    lifted = jnp.exp(logits - jnp.max(logits, axis=-1, keepdims=True))
    router = lifted / jnp.sum(lifted, axis=-1, keepdims=True)
    router_ref[...] = router
    picked = choice_ref[...] == lax.broadcasted_iota(jnp.int32, router.shape, 1)
    gate = jnp.sum(jnp.where(picked, router, 0.0), axis=-1, keepdims=True)
    gate_ref[...] = gate
    low = normed.astype(bf16)
    route = (gate * grad_ref[...].astype(f32)).astype(bf16)
    for z in range(4):
        rows_out[z] = jnp.concatenate([low[:, z * width:(z + 1) * width], route[:, z * width:(z + 1) * width]], axis=1)

    def rows_line(k):
        return remote(rows_out.at[me.line[k]], rows_ref.at[gx * 8 + gy], rz_s.at[k], rz_r.at[k], me.on_line(k))

    def rows_plane(z, k, m):
        at = z * 8 + gy
        return remote(rows_ref.at[at], rows_ref.at[at], rc_s.at[m, k], rc_r.at[m, k], me.on_plane(k))

    def rows_pair(z, k, m):
        c = chip if k == 0 else me.chips_from[k - 1]
        at = z * 8 + 2 * c + core
        return remote(rows_ref.at[at], rows_ref.at[at], rp_s.at[m, k], rp_r.at[m, k], me.pair)

    for k in range(3):
        rows_line(k).start()
    rows_ref[gx * 8 + gy] = rows_out[gx]
    zs = [gx] + me.line_from
    for m in range(4):
        if m > 0:
            rows_line(m - 1).wait_recv()
        for k in range(3):
            rows_plane(zs[m], k, m).start()
        rows_pair(zs[m], 0, m).start()
    for m in range(4):
        for k in range(3):
            rows_plane(zs[m], k, m).wait_recv()
            rows_pair(zs[m], k + 1, m).start()
    for m in range(4):
        for k in range(4):
            rows_pair(zs[m], k, m).wait_recv()
    for m in range(4):
        for k in range(4):
            rows_pair(zs[m], k, m).wait_send()
        for k in range(3):
            rows_plane(zs[m], k, m).wait_send()
    for k in range(3):
        rows_line(k).wait_send()
        at_plane(k).wait_send()
        wo_plane(k).wait_send()
        wo_line(k).wait_send()
        sm_line(k).wait_send()
        wq_line(k).wait_send()
        xn_plane(k).wait_send()
    for k in range(4):
        wq_pair(k).wait_send()
        wo_pair(k).wait_send()
        kv_pair(k).wait_send()


def front(x_in, gain1, wqkv, wout, table, small, doc_row, doc_col, choice, grad_out, collective_id):
    local, features = x_in.shape
    width = wqkv.shape[0]
    cols = wqkv.shape[1] // 3
    hd = 2 * cols
    heads = hd // HSIZE
    experts = table.shape[0] if False else EXPERTS
    tokens = 32 * local
    vm = pl.BlockSpec(memory_space=pltpu.VMEM)
    sm = pl.BlockSpec(memory_space=pltpu.SMEM)
    dma = pltpu.SemaphoreType.DMA
    shape = jax.ShapeDtypeStruct
    return pl.pallas_call(
        functools.partial(front_kernel, heads, experts),
        out_shape=(
            shape((32, local, 2 * width), bf16),
            shape((local, features), f32),
            shape((local, features), f32),
            shape((local, experts), f32),
            shape((local, 1), f32),
            shape((4, local, hd), bf16),
            shape((4, local, hd), bf16),
            shape((8, local, 2 * hd), bf16),
            shape((4, heads, local, 128), f32),
            shape((4, local, features), bf16),
            shape((features, 3 * hd), bf16),
            shape((features, features), bf16),
            shape((small.shape[0], features), f32),
            shape((heads, local, 16 * local), f32),
        ),
        in_specs=[vm, vm, vm, vm, sm, vm, vm, vm, vm, vm],
        out_specs=(vm,) * 14,
        scratch_shapes=[
            pltpu.VMEM((2, 4, width, 3 * cols), bf16),
            pltpu.VMEM((8, 4, cols, width), bf16),
            pltpu.VMEM((4, *small.shape), f32),
            pltpu.VMEM((4, local, hd), bf16),
            pltpu.VMEM((4, local, 2 * width), bf16),
        ] + [dma((n,)) for n in (3, 3, 3, 3, 4, 4, 3, 3, 3, 3, 3, 3, 4, 4, 4, 4, 3, 3, 3, 3)]
        + [dma((4, 3)), dma((4, 3)), dma((4, 4)), dma((4, 4))],
        compiler_params=pltpu.CompilerParams(
            collective_id=collective_id, has_side_effects=True, vmem_limit_bytes=60 * 2**20),
        cost_estimate=pl.CostEstimate(flops=4 * 10**9, bytes_accessed=20 * 10**6, transcendentals=2 * 10**6),
    )(x_in, gain1, wqkv, wout, table, small, doc_row, doc_col, choice, grad_out)


HIGH = lax.Precision.HIGHEST


def back_kernel(heads, experts,
                x_ref, gain1_ref, grad_ref, choice_ref, doc_row, doc_col,
                hidden_ref, normed_ref, router_ref, gate_ref, at_ref, q_ref, kv_ref, lse_ref, xn_ref,
                wqkv_all, wout_all, small_all, bias_ref, ret_ref,
                out_ref, gin_ref, wgrad_ref, ograd_ref, small_out, tail_out,
                ag_ref, dq_ref, dk_ref, dv_ref, near_ref, go_ref, fg_ref, top_ref,
                sp_out, sp_in, sc_out, sc_in, sz_out, sz_in,
                kv_out, kv_in, kv_sum, fg_out, fg_in, wp_out, wp_in, wz_out, wz_in,
                op_out, op_in, oz_out, oz_in, tp_out, tp_in, tc_out, tc_in, tz_out, tz_in,
                ag_s, ag_r, sp_s, sp_r, sc_s, sc_r, sz_s, sz_r, kv_s, kv_r, fg_s, fg_r, wp_s, wp_r,
                wz_s, wz_r, op_s, op_r, oz_s, oz_r, tp_s, tp_r, tc_s, tc_r, tz_s, tz_r):
    me = Place()
    gx, gy, core, chip = me.gx, me.gy, me.core, me.chip
    local, features = x_ref.shape
    width = features // 4
    hd = q_ref.shape[2]
    cols = hd // 2
    seq = 8 * local
    hidden = hidden_ref[...]
    r2 = lax.rsqrt(jnp.mean(hidden * hidden, axis=-1, keepdims=True) + epsilon)
    grads = grad_ref[...].astype(f32)
    gate = gate_ref[...]
    routed = jnp.concatenate([ret_ref[z][:, :width] for z in range(4)], axis=1)
    back = jnp.concatenate([ret_ref[z][:, width:] for z in range(4)], axis=1)
    out_ref[...] = hidden + gate * routed
    gate_grad = jnp.sum(grads * routed, axis=-1, keepdims=True)
    router = router_ref[...]
    picked = (choice_ref[...] == lax.broadcasted_iota(jnp.int32, router.shape, 1)).astype(f32)
    logit_grad = router * (gate_grad * picked - gate * gate_grad)
    second = back + jnp.dot(logit_grad, small_all[:experts, :], precision=HIGH, preferred_element_type=f32)
    gained = second * small_all[experts:experts + 1, :]
    dot2 = jnp.sum(gained * hidden, axis=-1, keepdims=True)
    hidden_grad = grads + r2 * gained - hidden * (r2 * r2 * r2) * (dot2 / features)
    ag_ref[chip] = hidden_grad.astype(bf16)
    me.greet_all()

    def ag_plane(k):
        return remote(ag_ref.at[chip], ag_ref.at[chip], ag_s.at[k], ag_r.at[k], me.on_plane(k))

    for k in range(3):
        ag_plane(k).start()

    routed_grad = lax.dot_general(logit_grad, normed_ref[...], (((0,), (0,)), ((), ())), precision=HIGH,
                                  preferred_element_type=f32)
    norm2 = jnp.sum(second * hidden * r2, axis=0, keepdims=True)
    own_small = jnp.concatenate([routed_grad, norm2, jnp.zeros((7, features), f32)], axis=0)
    sp_out[...] = own_small
    small_pair = remote(sp_out, sp_in, sp_s.at[0], sp_r.at[0], me.pair)
    small_pair.start()

    def small_plane(k):
        return remote(sc_out, sc_in.at[k], sc_s.at[k], sc_r.at[k], me.on_plane(k))

    def small_line(k):
        return remote(sz_out.at[me.line[k]], sz_in.at[k], sz_s.at[k], sz_r.at[k], me.on_line(k))

    dk_ref[...] = jnp.zeros_like(dk_ref)
    dv_ref[...] = jnp.zeros_like(dv_ref)
    near_ref[...] = jnp.zeros_like(near_ref)
    go_ref[...] = jnp.zeros_like(go_ref)
    scale = HSIZE ** (-0.5)
    lanes = lax.broadcasted_iota(jnp.int32, (local, hd), 1) // HSIZE

    def attend_block(c):
        block_at = 2 * c + core
        allowed = doc_col[pl.ds(pl.multiple_of(block_at * local, local), local), :] == doc_row[...]
        keys = kv_ref[:, :, :hd].reshape(seq, hd)
        values = kv_ref[:, :, hd:].reshape(seq, hd)
        rows_out = pl.ds(pl.multiple_of(chip * hd, 16), hd)
        att_grad = nt(ag_ref[c], wout_all[rows_out, :]).astype(bf16)
        go_ref[...] += tn(at_ref[c], ag_ref[c])
        q_block = q_ref[c]
        q_turn = jnp.transpose(q_block.astype(f32)).astype(bf16)
        g_turn = jnp.transpose(att_grad.astype(f32)).astype(bf16)
        dq = jnp.zeros((local, hd), f32)
        for h in range(heads):
            scores = unit_scores(q_block, keys, bias_ref, h, block_at, allowed)
            probs = jnp.exp(scores - lse_ref[c, h][:, :1])
            masked = jnp.where(lanes == h, att_grad, jnp.zeros_like(att_grad))
            prob_grad = nt(masked, values)
            weighted = probs * prob_grad
            score_grad = (weighted - probs * jnp.sum(weighted, axis=-1, keepdims=True)).astype(bf16)
            part = slice(h * HSIZE, (h + 1) * HSIZE)
            dv_ref[part, :] += nn(g_turn[part, :], probs.astype(bf16))
            dk_ref[part, :] += nn(q_turn[part, :], score_grad)
            dq = jnp.where(lanes == h, nn(score_grad, keys), dq)
            start = pl.multiple_of(seq - local * block_at, local)
            near_ref[h, :, pl.ds(start, seq)] += score_grad.astype(f32)
        dq_ref[c] = (dq * scale).astype(bf16)

    attend_block(chip)
    small_pair.wait_recv()
    sc_out[...] = own_small + sp_in[...]
    for k in range(3):
        small_plane(k).start()
    for k in range(3):
        ag_plane(k).wait_recv()
        attend_block(me.chips_from[k])
        if k == 0:
            total = sc_out[...]
            for j in range(3):
                small_plane(j).wait_recv()
                total = total + sc_in[j]
            for z in range(4):
                sz_out[z] = total[:, z * width:(z + 1) * width]
            for j in range(3):
                small_line(j).start()

    both = jnp.concatenate([dk_ref[...], dv_ref[...]], axis=0)
    for j in range(8):
        turned = jnp.transpose(both[:, j * local:(j + 1) * local])
        @pl.when(core == j % 2)
        def _():
            kv_sum[j // 2] = turned
        @pl.when(core != j % 2)
        def _():
            kv_out[j // 2] = turned.astype(bf16)
    kv_pair = remote(kv_out, kv_in, kv_s.at[0], kv_r.at[0], me.pair)
    kv_pair.start()

    op_out[...] = go_ref[pl.ds(pl.multiple_of((1 - core) * cols, 16), cols), :].astype(bf16)
    op_pair = remote(op_out, op_in, op_s.at[0], op_r.at[0], me.pair)
    op_pair.start()

    def op_line(k):
        return remote(oz_out.at[me.line[k]], oz_in.at[k], oz_s.at[k], oz_r.at[k], me.on_line(k))

    buckets = near_buckets(local)
    table = jnp.zeros((experts, 128), f32)
    lane = lax.broadcasted_iota(jnp.int32, (experts, 128), 1)
    row = lax.broadcasted_iota(jnp.int32, (experts, 1), 0)
    for h in range(heads):
        close = near_ref[h, :, seq - local:seq + 2 * local]
        for b in range(experts):
            top_ref[b:b + 1, :] = jnp.sum(jnp.where(buckets == b, close, 0.0), axis=0, keepdims=True)
        column = jnp.sum(top_ref[...], axis=1, keepdims=True)
        left = jnp.sum(near_ref[h, :, :seq - local])
        right = jnp.sum(near_ref[h, :, seq + 2 * local:])
        column = column + jnp.where(row == 15, left, 0.0) + jnp.where(row == 31, right, 0.0)
        table = jnp.where(lane == chip * heads + h, column, table)

    kv_pair.wait_recv()
    made = []
    for c in range(4):
        keyval = (kv_sum[c] + kv_in[c].astype(f32)).astype(bf16)
        made.append(jnp.concatenate([dq_ref[c], keyval], axis=1))

    def fg_plane(k):
        return remote(fg_out.at[me.chips[k]], fg_in.at[k], fg_s.at[k], fg_r.at[k], me.on_plane(k))

    for c in range(4):
        fg_ref[c] = nt(made[c], wqkv_all[...])
        fg_out[c] = fg_ref[c].astype(bf16)
    for k in range(3):
        fg_plane(k).start()
    weight_grad = jnp.zeros((features, 3 * hd), f32)
    weight_grad = tn(xn_ref[...].reshape(4 * local, features), jnp.concatenate(made, axis=0))
    halves = [jnp.concatenate([weight_grad[:, n * hd + j * cols:n * hd + (j + 1) * cols] for n in range(3)], axis=1)
              for j in range(2)]
    wp_out[...] = jnp.where(core == 0, halves[1], halves[0]).astype(bf16)
    w_pair = remote(wp_out, wp_in, wp_s.at[0], wp_r.at[0], me.pair)
    w_pair.start()
    own_w = jnp.where(core == 0, halves[0], halves[1])

    def w_line(k):
        return remote(wz_out.at[me.line[k]], wz_in.at[k], wz_s.at[k], wz_r.at[k], me.on_line(k))

    op_pair.wait_recv()
    own_o = go_ref[pl.ds(pl.multiple_of(core * cols, 16), cols), :] + op_in[...].astype(f32)
    for z in range(4):
        oz_out[z] = own_o[:, z * width:(z + 1) * width].astype(bf16)
    for k in range(3):
        op_line(k).start()
    w_pair.wait_recv()
    own_w = own_w + wp_in[...].astype(f32)
    for z in range(4):
        wz_out[z] = own_w[z * width:(z + 1) * width, :].astype(bf16)
    for k in range(3):
        w_line(k).start()

    first = fg_ref[chip]
    for k in range(3):
        fg_plane(k).wait_recv()
        first = first + fg_in[k].astype(f32)
    x = x_ref[...].astype(f32)
    r1 = lax.rsqrt(jnp.mean(x * x, axis=-1, keepdims=True) + epsilon)
    norm1 = jnp.sum(first * x * r1, axis=0, keepdims=True)
    gained1 = first * gain1_ref[...]
    dot1 = jnp.sum(gained1 * x, axis=-1, keepdims=True)
    gin_ref[...] = hidden_grad + r1 * gained1 - x * (r1 * r1 * r1) * (dot1 / features)

    tail = jnp.concatenate([table] + [norm1[:, n * 128:(n + 1) * 128] for n in range(6)] + [jnp.zeros((2, 128), f32)],
                           axis=0)
    tp_out[...] = tail
    t_pair = remote(tp_out, tp_in, tp_s.at[0], tp_r.at[0], me.pair)
    t_pair.start()

    def t_plane(k):
        return remote(tc_out, tc_in.at[k], tc_s.at[k], tc_r.at[k], me.on_plane(k))

    def t_line(k):
        return remote(tz_out, tz_in.at[k], tz_s.at[k], tz_r.at[k], me.on_line(k))

    t_pair.wait_recv()
    tail = jnp.where(core == 0, tail + tp_in[...], tp_in[...] + tail)
    tc_out[...] = tail
    for k in range(3):
        t_plane(k).start()
    for k in range(3):
        t_plane(k).wait_recv()
    tail = jnp.zeros_like(tail)
    for c in range(4):
        part = jnp.where(chip == c, tc_out[...], 0.0)
        for k in range(3):
            part = jnp.where(me.chips_from[k] == c, tc_in[k], part)
        tail = tail + part
    tz_out[...] = tail
    for k in range(3):
        t_line(k).start()

    total = sz_out[gx]
    for k in range(3):
        small_line(k).wait_recv()
        total = total + sz_in[k]
    small_out[...] = total
    total = oz_out[gx].astype(f32)
    for k in range(3):
        op_line(k).wait_recv()
        total = total + oz_in[k].astype(f32)
    ograd_ref[...] = total
    total = wz_out[gx].astype(f32)
    for k in range(3):
        w_line(k).wait_recv()
        total = total + wz_in[k].astype(f32)
    wgrad_ref[...] = total
    for k in range(3):
        t_line(k).wait_recv()
    tail = jnp.zeros_like(tail)
    for z in range(4):
        part = jnp.where(gx == z, tz_out[...], 0.0)
        for k in range(3):
            part = jnp.where(me.line_from[k] == z, tz_in[k], part)
        tail = tail + part
    tail_out[...] = tail
    for copy in (small_pair, kv_pair, op_pair, w_pair, t_pair):
        copy.wait_send()
    for k in range(3):
        for copy in (ag_plane, small_plane, small_line, fg_plane, op_line, w_line, t_plane, t_line):
            copy(k).wait_send()


def back_pass(x_in, gain1, grad_out, choice, doc_row, doc_col, saved, returned, collective_id):
    local, features = x_in.shape
    width = features // 4
    hidden, normed, router, gate, attended, queries, keyvals, lse, xn, wqkv, wout, small, bias = saved
    hd = queries.shape[2]
    cols = hd // 2
    heads = hd // HSIZE
    seq = 8 * local
    rows = small.shape[0]
    vm = pl.BlockSpec(memory_space=pltpu.VMEM)
    dma = pltpu.SemaphoreType.DMA
    shape = jax.ShapeDtypeStruct
    V = pltpu.VMEM
    return pl.pallas_call(
        functools.partial(back_kernel, heads, EXPERTS),
        out_shape=(
            shape((local, features), f32),
            shape((local, features), f32),
            shape((width, 3 * cols), f32),
            shape((cols, width), f32),
            shape((rows, width), f32),
            shape((40, 128), f32),
        ),
        in_specs=[vm] * 20,
        out_specs=(vm,) * 6,
        scratch_shapes=[
            V((4, local, features), bf16), V((4, local, hd), bf16), V((hd, seq), f32), V((hd, seq), f32),
            V((heads, local, 2 * seq), f32), V((hd, features), f32), V((4, local, features), f32),
            V((EXPERTS, 3 * local), f32),
            V((rows, features), f32), V((rows, features), f32), V((rows, features), f32), V((3, rows, features), f32),
            V((4, rows, width), f32), V((3, rows, width), f32),
            V((4, local, 2 * hd), bf16), V((4, local, 2 * hd), bf16), V((4, local, 2 * hd), f32),
            V((4, local, features), bf16), V((3, local, features), bf16),
            V((features, 3 * cols), bf16), V((features, 3 * cols), bf16),
            V((4, width, 3 * cols), bf16), V((3, width, 3 * cols), bf16),
            V((cols, features), bf16), V((cols, features), bf16), V((4, cols, width), bf16), V((3, cols, width), bf16),
            V((40, 128), f32), V((40, 128), f32), V((40, 128), f32), V((3, 40, 128), f32),
            V((40, 128), f32), V((3, 40, 128), f32),
        ] + [dma((n,)) for n in (3, 3, 1, 1, 3, 3, 3, 3, 1, 1, 3, 3, 1, 1, 3, 3, 1, 1, 3, 3, 1, 1, 3, 3, 3, 3)],
        compiler_params=pltpu.CompilerParams(
            collective_id=collective_id, has_side_effects=True, vmem_limit_bytes=60 * 2**20),
        cost_estimate=pl.CostEstimate(flops=6 * 10**9, bytes_accessed=20 * 10**6, transcendentals=2 * 10**6),
    )(x_in, gain1, grad_out, choice, doc_row, doc_col, hidden, normed, router, gate, attended, queries, keyvals, lse, xn,
      wqkv, wout, small, bias, returned)


def fits(mesh):
    return mesh.shape["gx"] == 4 and mesh.shape["gy"] == 8


def expert_slots(expert_choice, experts, capacity):
    all_tokens = expert_choice.shape[0]
    tok_block = 128
    chosen_rows = jnp.arange(experts, dtype=jnp.int32)[:, None] == expert_choice[None, :]
    chosen_low = chosen_rows.astype(jnp.bfloat16).reshape(experts, all_tokens // tok_block, tok_block)
    block_iota = jnp.arange(tok_block, dtype=jnp.int32)
    upper = (block_iota[:, None] <= block_iota[None, :]).astype(jnp.bfloat16)
    inside_count = jnp.einsum("ebi,ij->ebj", chosen_low, upper, preferred_element_type=jnp.float32)
    block_totals = inside_count[:, :, tok_block - 1]
    earlier_blocks = jnp.cumsum(block_totals, axis=1) - block_totals
    counted = (inside_count + earlier_blocks[:, :, None]).reshape(experts, all_tokens)
    position = (jnp.sum(jnp.where(chosen_rows, counted, 0.0), axis=0) - 1.0).astype(jnp.int32)
    return jnp.where(position < capacity, expert_choice * capacity + position, -1)


def fast(
    x_in,
    norm1_gain,
    w_query,
    w_key,
    w_value,
    relative_bias_table,
    w_out,
    norm2_gain,
    w_router,
    w_hidden,
    w_back,
    expert_choice,
    doc_ids,
    grad_out,
):
    token_devs = lax.axis_size("gy")
    member, column = lax.axis_index("gy"), lax.axis_index("gx")
    local_count = x_in.shape[0]
    width_cols, experts = w_router.shape
    all_tokens = expert_choice.shape[0]
    capacity = all_tokens * 5 // (4 * experts)
    head_cols = w_query.shape[1]
    gain_row = norm1_gain[None, :]
    wqkv = jnp.concatenate([w_query, w_key, w_value], axis=1)
    small = jnp.concatenate(
        [w_router.T, norm2_gain[None, :], jnp.zeros((7, width_cols), jnp.float32)], axis=0
    )
    own_choice = lax.dynamic_slice_in_dim(
        expert_choice, (column * token_devs + member) * local_count, local_count, 0
    )[:, None]
    doc_row, doc_col = doc_ids[None, :], doc_ids[:, None]
    slot_all = expert_slots(expert_choice, experts, capacity)
    hidden_weight = jnp.transpose(w_hidden.reshape(width_cols, -1, experts), (2, 0, 1))
    back_weight = jnp.transpose(w_back.reshape(width_cols, -1, experts), (2, 0, 1))
    rows, *saved = front(
        x_in,
        gain_row,
        wqkv,
        w_out,
        relative_bias_table,
        small,
        doc_row,
        doc_col,
        own_choice,
        grad_out,
        2,
    )
    returned, hidden_grads, back_grads = moe(
        rows.reshape(all_tokens, 2 * width_cols),
        slot_all[None, :],
        slot_all[:, None],
        hidden_weight,
        back_weight,
        1,
    )
    grad_hidden = jnp.transpose(hidden_grads, (1, 2, 0)).reshape(width_cols, -1)
    grad_back = jnp.transpose(back_grads, (1, 2, 0)).reshape(width_cols, -1)
    out_rows, input_rows, weight_part, out_part, small_part, tail = back_pass(
        x_in, gain_row, grad_out, own_choice, doc_row, doc_col, saved, returned, 3
    )
    heads = relative_bias_table.shape[1]
    features = x_in.shape[1]
    return (
        out_rows,
        input_rows,
        tail[experts : experts + features // 128].reshape(features),
        weight_part[:, :head_cols],
        weight_part[:, head_cols : 2 * head_cols],
        weight_part[:, 2 * head_cols :],
        tail[:experts, :heads],
        out_part,
        small_part[experts],
        small_part[:experts].T,
        grad_hidden,
        grad_back,
    )


def solution(mesh):
    return jax.shard_map(
        fast if fits(mesh) else local,
        mesh=mesh,
        in_specs=(
            P(("gx", "gy"), None),
            P(),
            P("gx", "gy"),
            P("gx", "gy"),
            P("gx", "gy"),
            P(),
            P("gy", "gx"),
            P("gx"),
            P("gx", None),
            P("gx", "gy"),
            P("gx", "gy"),
            P(),
            P("gx"),
            P(("gx", "gy"), None),
        ),
        out_specs=(
            P(("gx", "gy"), None),
            P(("gx", "gy"), None),
            P(),
            P("gx", "gy"),
            P("gx", "gy"),
            P("gx", "gy"),
            P(),
            P("gy", "gx"),
            P("gx"),
            P("gx", None),
            P("gx", "gy"),
            P("gx", "gy"),
        ),
        check_vma=False,
    )
```

```python
import functools
import math

import jax
import jax.numpy as jnp
from jax import lax
from jax.experimental import pallas as pl
from jax.experimental.pallas import tpu as pltpu
from jax.sharding import PartitionSpec as P

D = 768
HEADS = 12
HSIZE = 64
EXPERTS = 32
WINDOW = 1024


epsilon = 1e-06
far_steps = (12, 16, 23, 32, 46, 64, 91)
highest = lax.Precision.HIGHEST


def passed_along(value, axis, steps):
    count = lax.axis_size(axis)
    first, last = (max(0, -steps), min(count, count - steps))
    return lax.ppermute(value, axis, [(source, source + steps) for source in range(first, last)])


def bucket_ids(offset):
    ahead_part = (offset > 0).astype(jnp.int32) * 16
    distance = jnp.abs(offset)
    far_part = 8 + sum(((distance >= threshold).astype(jnp.int32) for threshold in far_steps))
    return ahead_part + jnp.where(distance < 8, distance, far_part)


def width_total(values):
    return lax.psum(values, "gx")


def token_rows(block_part):
    return lax.all_gather(block_part, "gy", axis=0, tiled=True)


def width_rows(block_part):
    return lax.all_gather(block_part, "gx", axis=0, tiled=True)


def width_sums(term_fn, row_number):
    return lax.psum_scatter(
        term_fn(jnp.int32(0), lax.axis_size("gx") * row_number),
        "gx",
        scatter_dimension=0,
        tiled=True,
    )


def token_sums(term_fn, row_number):
    return lax.psum_scatter(
        term_fn(jnp.int32(0), lax.axis_size("gy") * row_number),
        "gy",
        scatter_dimension=0,
        tiled=True,
    )


def collect_window(own_pair, reach):
    window_parts = []
    for offset_step in range(-reach, reach + 1):
        if offset_step == 0:
            window_parts.append(own_pair)
        else:
            window_parts.append(passed_along(own_pair, "gy", -offset_step))
    return jnp.concatenate(window_parts, axis=0)


def return_window(partials, reach, head_rows):
    combined = partials[reach * head_rows : (reach + 1) * head_rows]
    for offset_step in range(-reach, reach + 1):
        if offset_step != 0:
            start = (offset_step + reach) * head_rows
            combined = combined + passed_along(
                partials[start : start + head_rows], "gy", offset_step
            )
    return combined


def head_scores(query_heads, key_heads, bias_terms, allowed, score_scale):
    raw_scores = jnp.einsum(
        "qhd,khd->hqk", query_heads, key_heads, preferred_element_type=jnp.float32
    )
    return jnp.where(allowed[None], raw_scores * score_scale + bias_terms, -1000000000.0)


def rows_cols(blocks, width_devs, token_devs):
    grid = blocks.reshape(width_devs, token_devs, blocks.shape[1], blocks.shape[2])
    return jnp.transpose(grid, (0, 2, 1, 3)).reshape(
        width_devs * blocks.shape[1], token_devs * blocks.shape[2]
    )


def cols_rows(blocks, width_devs, token_devs):
    grid = blocks.reshape(width_devs, token_devs, blocks.shape[1], blocks.shape[2])
    return jnp.transpose(grid, (1, 2, 0, 3)).reshape(
        token_devs * blocks.shape[1], width_devs * blocks.shape[2]
    )


def grid_rows_cols(complete, width_devs, token_devs):
    row_total, col_total = complete.shape
    grid = complete.reshape(
        width_devs, row_total // width_devs, token_devs, col_total // token_devs
    )
    return jnp.transpose(grid, (0, 2, 1, 3)).reshape(
        width_devs * token_devs, row_total // width_devs, col_total // token_devs
    )


def grid_cols_rows(complete, width_devs, token_devs):
    row_total, col_total = complete.shape
    grid = complete.reshape(
        token_devs, row_total // token_devs, width_devs, col_total // width_devs
    )
    return jnp.transpose(grid, (2, 0, 1, 3)).reshape(
        width_devs * token_devs, row_total // token_devs, col_total // width_devs
    )


def spread_rows(partial_sum, column, group_count):
    picked_row = (jnp.arange(group_count, dtype=jnp.int32) == column).astype(jnp.float32)
    return picked_row.reshape((group_count,) + (1,) * partial_sum.ndim) * partial_sum[None]


def take_rows(table, index):
    return jnp.take(table, index, axis=0, mode="fill", fill_value=0)


def local(
    x_in,
    norm1_gain,
    w_query,
    w_key,
    w_value,
    relative_bias_table,
    w_out,
    norm2_gain,
    w_router,
    w_hidden,
    w_back,
    expert_choice,
    doc_ids,
    grad_out,
):
    token_devs = lax.axis_size("gy")
    width_devs = lax.axis_size("gx")
    member = lax.axis_index("gy")
    column = lax.axis_index("gx")
    local_count = x_in.shape[0]
    width_cols = w_router.shape[0]
    own_rows = local_count * width_devs
    all_tokens = own_rows * token_devs
    seq_len = local_count * token_devs
    experts = EXPERTS
    capacity = all_tokens * 5 // (4 * experts)
    score_scale = HSIZE ** (-0.5)
    reach = min((WINDOW + local_count - 2) // local_count, token_devs - 1)
    key_count = (2 * reach + 1) * local_count
    whole_weights = (
        lax.all_gather(w_query[None], ("gx", "gy"), axis=0, tiled=True),
        lax.all_gather(w_key[None], ("gx", "gy"), axis=0, tiled=True),
        lax.all_gather(w_value[None], ("gx", "gy"), axis=0, tiled=True),
        lax.all_gather(w_out[None], ("gx", "gy"), axis=0, tiled=True),
    )
    qkv_full = jnp.concatenate(
        [
            rows_cols(whole_weights[0], width_devs, token_devs),
            rows_cols(whole_weights[1], width_devs, token_devs),
            rows_cols(whole_weights[2], width_devs, token_devs),
        ],
        axis=1,
    )
    out_full = cols_rows(whole_weights[3], width_devs, token_devs)
    head_width = out_full.shape[0]
    inputs_row = x_in.astype(jnp.float32)
    scale_first = lax.rsqrt(jnp.mean(inputs_row * inputs_row, axis=-1, keepdims=True) + epsilon)
    normed_first = (inputs_row * scale_first * norm1_gain).astype(jnp.bfloat16)
    qkv_rows = jnp.dot(normed_first, qkv_full, preferred_element_type=jnp.float32).astype(
        jnp.bfloat16
    )
    query_heads = qkv_rows[:, :head_width].reshape(local_count, HEADS, HSIZE)
    pair_window = collect_window(
        qkv_rows[:, head_width:].reshape(local_count, 2, head_width), reach
    )
    key_heads = pair_window[:, 0].reshape(key_count, HEADS, HSIZE)
    value_heads = pair_window[:, 1].reshape(key_count, HEADS, HSIZE)
    query_pos = member * local_count + jnp.arange(local_count, dtype=jnp.int32)
    key_pos = (member - reach) * local_count + jnp.arange(key_count, dtype=jnp.int32)
    offset = key_pos[None, :] - query_pos[:, None]
    buckets = bucket_ids(offset)
    bias_terms = jnp.take(jnp.transpose(relative_bias_table), buckets, axis=1)
    no_doc = jnp.full((reach * local_count,), -1, jnp.int32)
    doc_padded = jnp.concatenate([no_doc, doc_ids, no_doc], axis=0)
    key_docs = lax.dynamic_slice_in_dim(doc_padded, member * local_count, key_count, 0)
    query_docs = lax.dynamic_slice_in_dim(doc_ids, member * local_count, local_count, 0)
    allowed = (jnp.abs(offset) < WINDOW) & (query_docs[:, None] == key_docs[None, :])
    attention_scores = head_scores(query_heads, key_heads, bias_terms, allowed, score_scale)
    row_peak = jnp.max(attention_scores, axis=-1, keepdims=True)
    shifted = jnp.exp(attention_scores - row_peak)
    row_sum = jnp.sum(shifted, axis=-1, keepdims=True)
    log_total = row_peak + jnp.log(row_sum)
    weights_reduced_precision = (shifted / row_sum).astype(jnp.bfloat16)
    attended = jnp.einsum(
        "hqk,khd->qhd", weights_reduced_precision, value_heads, preferred_element_type=jnp.float32
    )
    attended_low = attended.reshape(local_count, head_width).astype(jnp.bfloat16)
    attn_low = jnp.dot(attended_low, out_full, preferred_element_type=jnp.float32).astype(
        jnp.bfloat16
    )
    arrived = lax.all_to_all(
        jnp.stack([x_in, attn_low, grad_out], axis=1), "gx", split_axis=2, concat_axis=0, tiled=True
    )
    inputs = arrived[:, 0].astype(jnp.float32)
    grad_rows = arrived[:, 2].astype(jnp.float32)
    hidden_first = inputs + arrived[:, 1].astype(jnp.float32)
    scale_second = lax.rsqrt(
        width_total(jnp.sum(hidden_first * hidden_first, axis=-1)) / D + epsilon
    )[:, None]
    normed_second = hidden_first * scale_second * norm2_gain
    logits = width_total(jnp.dot(normed_second, w_router, precision=highest))
    router = jax.nn.softmax(logits, axis=-1)
    expert_iota = jnp.arange(experts, dtype=jnp.int32)
    tok_block = math.gcd(all_tokens, 128)
    block_count = all_tokens // tok_block
    chosen_rows = expert_iota[:, None] == expert_choice[None, :]
    chosen_low = chosen_rows.astype(jnp.bfloat16).reshape(experts, block_count, tok_block)
    block_iota = jnp.arange(tok_block, dtype=jnp.int32)
    upper = (block_iota[:, None] <= block_iota[None, :]).astype(jnp.bfloat16)
    inside_count = jnp.einsum("ebi,ij->ebj", chosen_low, upper, preferred_element_type=jnp.float32)
    block_totals = inside_count[:, :, tok_block - 1]
    earlier_blocks = jnp.cumsum(block_totals, axis=1) - block_totals
    counted = (inside_count + earlier_blocks[:, :, None]).reshape(experts, all_tokens)
    position = (jnp.sum(jnp.where(chosen_rows, counted, 0.0), axis=0) - 1.0).astype(jnp.int32)
    kept_all = position < capacity
    slot_all = jnp.where(kept_all, expert_choice * capacity + position, experts * capacity)
    source = (
        jnp.full((experts * capacity + 1,), all_tokens, jnp.int32)
        .at[slot_all]
        .set(jnp.arange(all_tokens, dtype=jnp.int32))[: experts * capacity]
    )
    source_seq = source // seq_len
    source_inner = source % seq_len
    source_rows = jnp.where(
        source < all_tokens,
        source_inner // local_count * own_rows
        + source_seq * local_count
        + source_inner % local_count,
        all_tokens,
    )
    row_iota = jnp.arange(all_tokens, dtype=jnp.int32)
    global_of_row = (
        row_iota // local_count % width_devs * seq_len
        + row_iota // own_rows * local_count
        + row_iota % local_count
    )
    slot_rows = jnp.take(slot_all, global_of_row)
    own_global = lax.dynamic_slice_in_dim(global_of_row, member * own_rows, own_rows, 0)
    picked_mine = jnp.take(expert_choice, own_global)[:, None] == expert_iota[None, :]
    gate_value = jnp.sum(jnp.where(picked_mine, router, 0.0), axis=-1)
    second_rows = token_rows(normed_second.astype(jnp.bfloat16))
    hidden_weight = jnp.transpose(w_hidden.reshape(width_cols, -1, experts), (2, 0, 1))
    back_weight = jnp.transpose(w_back.reshape(width_cols, -1, experts), (2, 1, 0))
    expert_rows = experts // width_devs
    slot_in = take_rows(second_rows, source_rows).reshape(experts, capacity, width_cols)

    def hidden_term(first_row, row_count):
        return jnp.einsum(
            "ecd,edf->ecf", slot_in, hidden_weight, preferred_element_type=jnp.float32
        )

    pre_block = width_sums(hidden_term, expert_rows)
    act_rows = width_rows(jax.nn.gelu(pre_block).astype(jnp.bfloat16))
    expert_out = jnp.einsum(
        "ecf,efd->ecd", act_rows, back_weight, preferred_element_type=jnp.float32
    ).reshape(experts * capacity, width_cols)

    def route_term(first_row, row_count):
        return take_rows(expert_out, slot_rows)

    routed = token_sums(route_term, own_rows)
    block_out = hidden_first + gate_value[:, None] * routed
    gate_grad = width_total(jnp.sum(grad_rows * routed, axis=-1))
    route_rows = token_rows((grad_rows * gate_value[:, None]).astype(jnp.bfloat16))
    gelu_pair = jax.vjp(jax.nn.gelu, pre_block)
    slot_grad = take_rows(route_rows, source_rows).reshape(experts, capacity, width_cols)
    back_grads = jnp.einsum("ecf,ecd->efd", act_rows, slot_grad, preferred_element_type=jnp.float32)

    def act_term(first_row, row_count):
        return jnp.einsum(
            "ecd,efd->ecf", slot_grad, back_weight, preferred_element_type=jnp.float32
        )

    act_grad = width_sums(act_term, expert_rows)
    pre_rows = width_rows(gelu_pair[1](act_grad)[0].astype(jnp.bfloat16))
    hidden_gradient_rows = jnp.einsum(
        "ecd,ecf->edf", slot_in, pre_rows, preferred_element_type=jnp.float32
    )
    slot_in_grad = jnp.einsum(
        "ecf,edf->ecd", pre_rows, hidden_weight, preferred_element_type=jnp.float32
    ).reshape(experts * capacity, width_cols)

    def back_route_term(first_row, row_count):
        return take_rows(slot_in_grad, slot_rows)

    back_routed = token_sums(back_route_term, own_rows)
    grad_hidden = jnp.transpose(hidden_gradient_rows, (1, 2, 0)).reshape(width_cols, -1)
    grad_back = jnp.transpose(back_grads, (2, 1, 0)).reshape(width_cols, -1)
    logit_grad = router * (
        gate_grad[:, None] * picked_mine.astype(jnp.float32) - (gate_value * gate_grad)[:, None]
    )
    second_grad = back_routed + jnp.einsum("re,de->rd", logit_grad, w_router, precision=highest)
    router_part = jnp.einsum("rd,re->de", normed_second, logit_grad, precision=highest)
    norm2_part = jnp.sum(second_grad * hidden_first * scale_second, axis=0)
    gained_second = second_grad * norm2_gain
    row_dot_second = width_total(jnp.sum(gained_second * hidden_first, axis=-1))[:, None]
    hidden_grad = (
        grad_rows
        + scale_second * gained_second
        - hidden_first * scale_second**3 * row_dot_second / D
    )
    out_rows, hidden_rows = (
        lax.all_to_all(block_out, "gx", split_axis=0, concat_axis=1, tiled=True),
        lax.all_to_all(hidden_grad, "gx", split_axis=0, concat_axis=1, tiled=True),
    )
    attn_grad = hidden_rows.astype(jnp.bfloat16)
    grad_out_full = jnp.einsum(
        "rf,rd->fd", attended_low, attn_grad, preferred_element_type=jnp.float32
    )
    attended_grad = (
        jnp.einsum("rd,fd->rf", attn_grad, out_full, preferred_element_type=jnp.float32)
        .astype(jnp.bfloat16)
        .reshape(local_count, HEADS, HSIZE)
    )
    scores_again = head_scores(query_heads, key_heads, bias_terms, allowed, score_scale)
    probs_again = jnp.exp(scores_again - log_total)
    value_grad = jnp.einsum(
        "hqk,qhd->khd",
        probs_again.astype(jnp.bfloat16),
        attended_grad,
        preferred_element_type=jnp.float32,
    )
    prob_grad = jnp.einsum(
        "qhd,khd->hqk", attended_grad, value_heads, preferred_element_type=jnp.float32
    )
    score_gradient = (
        probs_again * (prob_grad - jnp.sum(probs_again * prob_grad, axis=-1, keepdims=True))
    ).astype(jnp.bfloat16)
    query_grad = (
        jnp.einsum("hqk,khd->qhd", score_gradient, key_heads, preferred_element_type=jnp.float32)
        * score_scale
    ).astype(jnp.bfloat16)
    key_grad = (
        jnp.einsum("hqk,qhd->khd", score_gradient, query_heads, preferred_element_type=jnp.float32)
        * score_scale
    )
    band_low = max(0, reach * local_count - 90)
    band_high = min(key_count, reach * local_count + local_count + 90)
    bucket_iota = jnp.arange(relative_bias_table.shape[0], dtype=jnp.int32)
    band_onehot = (buckets[None, :, band_low:band_high] == bucket_iota[:, None, None]).astype(
        jnp.bfloat16
    )
    table_near = jnp.einsum(
        "ivt,zvt->zi",
        score_gradient[:, :, band_low:band_high],
        band_onehot,
        preferred_element_type=jnp.float32,
    )
    left_far = jnp.sum(score_gradient[:, :, :band_low].astype(jnp.float32), axis=(1, 2))
    right_far = jnp.sum(score_gradient[:, :, band_high:].astype(jnp.float32), axis=(1, 2))
    table_part = (
        table_near
        + (bucket_iota == 15).astype(jnp.float32)[:, None] * left_far[None, :]
        + (bucket_iota == 31).astype(jnp.float32)[:, None] * right_far[None, :]
    )
    pair_grads = return_window(
        jnp.stack(
            [key_grad.reshape(key_count, head_width), value_grad.reshape(key_count, head_width)],
            axis=1,
        ),
        reach,
        local_count,
    )
    qkv_grad = jnp.concatenate(
        [
            query_grad.reshape(local_count, head_width),
            pair_grads.astype(jnp.bfloat16).reshape(local_count, 2 * head_width),
        ],
        axis=1,
    )
    qkv_grads = jnp.einsum("rd,rc->dc", normed_first, qkv_grad, preferred_element_type=jnp.float32)
    first_grad = jnp.einsum("rc,dc->rd", qkv_grad, qkv_full, preferred_element_type=jnp.float32)
    norm1_part = jnp.sum(first_grad * inputs_row * scale_first, axis=0)
    gained_first = first_grad * norm1_gain
    row_dot_first = jnp.sum(gained_first * inputs_row, axis=-1, keepdims=True)
    input_rows = (
        hidden_rows + scale_first * gained_first - inputs_row * scale_first**3 * row_dot_first / D
    )
    summed = lax.psum(
        (
            norm1_part,
            table_part,
            spread_rows(norm2_part, column, width_devs),
            spread_rows(router_part, column, width_devs),
        ),
        ("gx", "gy"),
    )
    grad_norm1 = summed[0]
    grad_table = summed[1]
    grad_norm2 = lax.dynamic_index_in_dim(summed[2], column, 0, keepdims=False)
    grad_router = lax.dynamic_index_in_dim(summed[3], column, 0, keepdims=False)
    weight_parts = (
        lax.psum_scatter(
            grid_rows_cols(qkv_grads[:, :head_width], width_devs, token_devs),
            ("gx", "gy"),
            scatter_dimension=0,
            tiled=True,
        ),
        lax.psum_scatter(
            grid_rows_cols(qkv_grads[:, head_width : 2 * head_width], width_devs, token_devs),
            ("gx", "gy"),
            scatter_dimension=0,
            tiled=True,
        ),
        lax.psum_scatter(
            grid_rows_cols(qkv_grads[:, 2 * head_width :], width_devs, token_devs),
            ("gx", "gy"),
            scatter_dimension=0,
            tiled=True,
        ),
        lax.psum_scatter(
            grid_cols_rows(grad_out_full, width_devs, token_devs),
            ("gx", "gy"),
            scatter_dimension=0,
            tiled=True,
        ),
    )
    return (
        out_rows,
        input_rows,
        grad_norm1,
        weight_parts[0][0],
        weight_parts[1][0],
        weight_parts[2][0],
        grad_table,
        weight_parts[3][0],
        grad_norm2,
        grad_router,
        grad_hidden,
        grad_back,
    )


MESH = pl.DeviceIdType.MESH
GELU_C = math.sqrt(2.0 / math.pi)
f32, bf16 = jnp.float32, jnp.bfloat16


def nn(a, b):
    return jnp.dot(a, b, preferred_element_type=f32)


def nt(a, b):
    return lax.dot_general(a, b, (((1,), (1,)), ((), ())), preferred_element_type=f32)


def tn(a, b):
    return lax.dot_general(a, b, (((0,), (0,)), ((), ())), preferred_element_type=f32)


def remote(src, dst, send_sem, recv_sem, device):
    return pltpu.make_async_remote_copy(
        src_ref=src, dst_ref=dst, send_sem=send_sem, recv_sem=recv_sem,
        device_id=device, device_id_type=MESH)


class Place:
    def __init__(self):
        self.gx, self.gy = lax.axis_index("gx"), lax.axis_index("gy")
        self.core, self.chip = lax.rem(self.gy, 2), self.gy // 2
        self.pair = (self.gx, self.gy + 1 - 2 * self.core)
        self.line = [lax.rem(self.gx + k, 4) for k in (1, 2, 3)]
        self.chips = [lax.rem(self.chip + k, 4) for k in (1, 2, 3)]
        self.line_from = [lax.rem(self.gx + 4 - k, 4) for k in (1, 2, 3)]
        self.chips_from = [lax.rem(self.chip + 4 - k, 4) for k in (1, 2, 3)]
        self.is_mid = jnp.logical_and(self.gx > 0, self.gx < 3)
        self.is_end = jnp.logical_not(self.is_mid)
        self.mid = (jnp.where(self.gx < 2, 1, 2), self.gy)
        self.other_mid = (jnp.where(self.gx < 2, 2, 1), self.gy)
        self.end = (jnp.where(self.gx < 2, 0, 3), self.gy)

    def on_line(self, k):
        return (self.line[k], self.gy)

    def on_plane(self, k):
        return (self.gx, 2 * self.chips[k] + self.core)

    def greet_all(self):
        devices = [self.on_line(k) for k in range(3)] + [self.on_plane(k) for k in range(3)] + [self.pair]
        barrier = pltpu.get_barrier_semaphore()
        for device in devices:
            pl.semaphore_signal(barrier, inc=1, device_id=device, device_id_type=MESH)
        pl.semaphore_wait(barrier, len(devices))


def as_column(row):
    n = row.shape[1]
    same = lax.broadcasted_iota(jnp.int32, (n, n), 0) == lax.broadcasted_iota(jnp.int32, (n, n), 1)
    return jnp.sum(jnp.where(same, row.astype(f32), 0.0), axis=1, keepdims=True)


def pick_rows(slot_row, base, capacity, rows_ref, tokens):
    kblock = 1024
    ids = lax.broadcasted_iota(jnp.int32, (capacity, kblock), 0) + base
    total = None
    for kb in range(tokens // kblock):
        hot = (slot_row[:, kb * kblock:(kb + 1) * kblock] == ids).astype(f32).astype(bf16)
        part = nn(hot, rows_ref[kb * kblock:(kb + 1) * kblock, :])
        total = part if total is None else total + part
    return total


class LineSum:
    def __init__(self, me, own, got, other, own_sem, got_sem, other_sem, out_sem, experts):
        self.me, self.own, self.got, self.other = me, own, got, other
        self.sems = (own_sem, got_sem, other_sem, out_sem)
        self.ring, self.experts = own.shape[0], experts

    def to_mid(self, e):
        sl = lax.rem(e, self.ring)
        return remote(self.own.at[sl], self.got.at[e], self.sems[0].at[sl], self.sems[1].at[e], self.me.mid)

    def across(self, e):
        sl = lax.rem(e, self.ring)
        return remote(self.own.at[sl], self.other.at[e], self.sems[0].at[sl], self.sems[2].at[e], self.me.other_mid)

    def to_end(self, e):
        return remote(self.got.at[e], self.got.at[e], self.sems[3].at[e], self.sems[1].at[e], self.me.end)

    def slot_free(self, e):
        @pl.when(e >= self.ring)
        def _():
            self.to_mid(e - self.ring).wait_send()

    def put(self, e, value):
        self.own[lax.rem(e, self.ring)] = value

        @pl.when(self.me.is_end)
        def _():
            self.to_mid(e).start()

    def half(self, e):
        @pl.when(jnp.logical_and(self.me.is_mid, jnp.logical_and(e >= 0, e < self.experts)))
        def _():
            sl = lax.rem(e + self.ring, self.ring)
            self.to_mid(e).wait_recv()
            self.own[sl] = (self.own[sl].astype(f32) + self.got[e].astype(f32)).astype(bf16)
            self.across(e).start()

    def whole(self, e):
        @pl.when(jnp.logical_and(self.me.is_mid, jnp.logical_and(e >= 0, e < self.experts)))
        def _():
            sl = lax.rem(e + self.ring, self.ring)
            self.across(e).wait_recv()
            self.got[e] = (self.own[sl].astype(f32) + self.other[e].astype(f32)).astype(bf16)
            self.to_end(e).start()

    def await_total(self, e):
        @pl.when(self.me.is_end)
        def _():
            self.to_end(e).wait_recv()

    def drain(self):
        def sent(e, carry):
            self.to_mid(e).wait_send()
            return carry
        lax.fori_loop(self.experts - self.ring, self.experts, sent, 0)

        @pl.when(self.me.is_mid)
        def _():
            def out(e, carry):
                self.to_end(e).wait_send()
                return carry
            lax.fori_loop(0, self.experts, out, 0)


RING = 8
GROUP = 4
LAG_B, LAG_C, LAG_D = 2, 4, 6


def moe_kernel(experts, capacity, width, units, tokens,
               rows_ref, slot_row, w1_ref, w2_ref, gs_ref, ag_ref,
               out_ref, gh_ref, gb_ref,
               xs_ref, p_ref, got_ref, other_ref, gh_st, gb_st,
               y_own, y_out, y_in, s_out, s_in, yt_ref, line_out, line_in,
               p_sem, got_sem, other_sem, t_sem, gh_sem, gb_sem,
               yo_s, yo_r, so_s, so_r, ya_s, ya_r, yp_s, yp_r, lo_s, lo_r):
    me = Place()
    gx, gy, core, chip = me.gx, me.gy, me.core, me.chip
    half = capacity // 2
    me.greet_all()
    line = LineSum(me, p_ref, got_ref, other_ref, p_sem, got_sem, other_sem, t_sem, experts)
    groups = experts // GROUP

    def grad_copy(stage, target, sems, e):
        return pltpu.make_async_copy(stage.at[lax.rem(e, 2)], target.at[e], sems.at[lax.rem(e, 2)])

    def pair_half(j):
        return remote(y_out.at[j], y_in.at[j], yo_s.at[j], yo_r.at[j], me.pair)

    def to_owner(j, k):
        return remote(s_out.at[j, me.chips[k]], s_in.at[j, k], so_s.at[j, k], so_r.at[j, k], me.on_plane(k))

    own_half = pl.ds(pl.multiple_of(core * half, 16), half)

    def from_owner(j, k):
        at = yt_ref.at[j * GROUP + chip, own_half]
        return remote(at, at, ya_s.at[j, k], ya_r.at[j, k], me.on_plane(k))

    def pair_total(j, k):
        c = chip if k == 0 else me.chips_from[k - 1]
        at = yt_ref.at[j * GROUP + c, own_half]
        return remote(at, at, yp_s.at[j, k], yp_r.at[j, k], me.pair)

    def stage_two(j):
        pair_half(j).wait_recv()
        for m in range(GROUP):
            s_out[j, m] = (y_own[j, m].astype(f32) + y_in[j, m].astype(f32)).astype(bf16)
        for k in range(3):
            to_owner(j, k).start()

    def stage_three(j):
        total = s_out[j, chip].astype(f32)
        for k in range(3):
            to_owner(j, k).wait_recv()
            total = total + s_in[j, k].astype(f32)
        yt_ref[j * GROUP + chip, own_half] = total.astype(bf16)
        for k in range(3):
            from_owner(j, k).start()
        pair_total(j, 0).start()

    def stage_four(j):
        for k in range(3):
            from_owner(j, k).wait_recv()
            pair_total(j, k + 1).start()

    def step(i, carry):
        @pl.when(i < experts)
        def _():
            line.slot_free(i)
            xs = pick_rows(slot_row, i * capacity, capacity, rows_ref, tokens).astype(bf16)
            xs_ref[lax.rem(i, RING)] = xs
            line.put(i, nn(xs[:, :width], w1_ref[i]).astype(bf16))
        line.half(i - LAG_B)
        line.whole(i - LAG_C)
        e = i - LAG_D

        @pl.when(e >= 0)
        def _():
            line.await_total(e)
            xs = xs_ref[lax.rem(e, RING)]
            pieces = xs[:, width:].astype(f32)
            gate = pieces[:, 0:1] + pieces[:, 1:2] + pieces[:, 2:3]
            u = got_ref[e].astype(f32)
            ag = gate * ag_ref[e].astype(f32)
            u2 = u * u
            th = jnp.tanh(GELU_C * (u + 0.044715 * (u2 * u)))
            part = 0.5 * (1.0 + th)
            act = (u * part).astype(bf16)
            dg = part + 0.5 * u * (1.0 - th * th) * (GELU_C * (1.0 + 3 * 0.044715 * u2))
            pg = (ag * dg).astype(bf16)
            y = jnp.concatenate([nt(act, w2_ref[e]), nt(pg, w1_ref[e])], axis=1).astype(bf16)
            j, m = e // GROUP, lax.rem(e, GROUP)

            @pl.when(core == 0)
            def _():
                y_own[j, m] = y[:half]
                y_out[j, m] = y[half:]

            @pl.when(core == 1)
            def _():
                y_own[j, m] = y[half:]
                y_out[j, m] = y[:half]

            @pl.when(e >= 2)
            def _():
                grad_copy(gh_st, gh_ref, gh_sem, e - 2).wait()
                grad_copy(gb_st, gb_ref, gb_sem, e - 2).wait()
            slot_grad = (gate * gs_ref[e].astype(f32)).astype(bf16)
            gh_st[lax.rem(e, 2)] = tn(xs[:, :width], pg).astype(bf16)
            gb_st[lax.rem(e, 2)] = tn(slot_grad, act).astype(bf16)
            grad_copy(gh_st, gh_ref, gh_sem, e).start()
            grad_copy(gb_st, gb_ref, gb_sem, e).start()

            @pl.when(m == GROUP - 1)
            def _():
                pair_half(j).start()

            @pl.when(jnp.logical_and(m == 0, j >= 1))
            def _():
                stage_two(j - 1)

            @pl.when(jnp.logical_and(m == 2, j >= 1))
            def _():
                stage_three(j - 1)

            @pl.when(jnp.logical_and(m == 1, j >= 2))
            def _():
                stage_four(j - 2)
        return carry

    lax.fori_loop(0, experts + LAG_D, step, 0)
    last = groups - 1
    stage_two(last)
    stage_four(last - 1)
    slots = [as_column(slot_row[:, pl.ds(pl.multiple_of((z * 8 + gy) * 128, 128), 128)]) for z in range(4)]
    own_slots = jnp.concatenate(slots, axis=0).astype(jnp.int32)
    many = 8
    cols = lax.broadcasted_iota(jnp.int32, (own_slots.shape[0], many * capacity), 1)

    def picked(b):
        hot = (own_slots == cols + b * many * capacity).astype(f32).astype(bf16)
        return nn(hot, yt_ref[b * many:(b + 1) * many].reshape(many * capacity, 2 * width))

    per = many // GROUP
    stage_three(last)
    total = None
    for b in range(experts // many - 1):
        for j in range(b * per, (b + 1) * per):
            for k in range(4):
                pair_total(j, k).wait_recv()
        part = picked(b)
        total = part if total is None else total + part
    stage_four(last)
    for j in range(groups - per, groups):
        for k in range(4):
            pair_total(j, k).wait_recv()
    total = total + picked(experts // many - 1)
    local = tokens // 32

    def line_copy(k):
        return remote(line_out.at[me.line[k]], line_in.at[k], lo_s.at[k], lo_r.at[k], me.on_line(k))

    for z in range(4):
        line_out[z] = total[z * local:(z + 1) * local].astype(bf16)
    for k in range(3):
        line_copy(k).start()
    out_ref[gx] = line_out[gx].astype(f32)
    for k in range(3):
        line_copy(k).wait_recv()
        out_ref[me.line_from[k]] = line_in[k].astype(f32)
    line.drain()
    for e in (experts - 2, experts - 1):
        grad_copy(gh_st, gh_ref, gh_sem, e).wait()
        grad_copy(gb_st, gb_ref, gb_sem, e).wait()

    def sent(j, carry):
        pair_half(j).wait_send()
        for k in range(3):
            to_owner(j, k).wait_send()
            from_owner(j, k).wait_send()
        for k in range(4):
            pair_total(j, k).wait_send()
        return carry
    lax.fori_loop(0, groups, sent, 0)
    for k in range(3):
        line_copy(k).wait_send()


def moe(rows, slot_row, w1, w2, slot_grads, act_grads, collective_id):
    experts, width, units = w1.shape
    tokens = rows.shape[0]
    capacity = slot_grads.shape[1]
    local = tokens // 32
    groups = experts // GROUP
    half = capacity // 2
    vm = pl.BlockSpec(memory_space=pltpu.VMEM)
    hbm = pl.BlockSpec(memory_space=pl.ANY)
    dma = pltpu.SemaphoreType.DMA
    V = pltpu.VMEM
    return pl.pallas_call(
        functools.partial(moe_kernel, experts, capacity, width, units, tokens),
        out_shape=(jax.ShapeDtypeStruct((4, local, 2 * width), f32),
                   jax.ShapeDtypeStruct((experts, width, units), bf16),
                   jax.ShapeDtypeStruct((experts, width, units), bf16)),
        in_specs=[vm] * 6,
        out_specs=(vm, hbm, hbm),
        scratch_shapes=[
            V((RING, capacity, rows.shape[1]), bf16),
            V((RING, capacity, units), bf16),
            V((experts, capacity, units), bf16),
            V((experts, capacity, units), bf16),
            V((2, width, units), bf16),
            V((2, width, units), bf16),
            V((groups, GROUP, half, 2 * width), bf16),
            V((groups, GROUP, half, 2 * width), bf16),
            V((groups, GROUP, half, 2 * width), bf16),
            V((groups, GROUP, half, 2 * width), bf16),
            V((groups, 3, half, 2 * width), bf16),
            V((experts, capacity, 2 * width), bf16),
            V((4, local, 2 * width), bf16),
            V((3, local, 2 * width), bf16),
            dma((RING,)), dma((experts,)), dma((experts,)), dma((experts,)), dma((2,)), dma((2,)),
            dma((groups,)), dma((groups,)), dma((groups, 3)), dma((groups, 3)), dma((groups, 3)), dma((groups, 3)),
            dma((groups, 4)), dma((groups, 4)), dma((3,)), dma((3,)),
        ],
        compiler_params=pltpu.CompilerParams(
            collective_id=collective_id, has_side_effects=True, vmem_limit_bytes=62 * 2**20),
        cost_estimate=pl.CostEstimate(flops=20 * 10**9, bytes_accessed=50 * 10**6, transcendentals=2 * 10**6),
    )(rows, slot_row, w1, w2, slot_grads, act_grads)


def place_one(lane):
    register, unit, expert = lane // 128, lax.rem(lane // 32, 4), lax.rem(lane, 32)
    return expert // 4 * 128 + lax.rem(expert, 4) * 32 + register * 4 + unit


def place_two(lane):
    register, expert, unit = lane // 128, lax.rem(lane // 32, 4), lax.rem(lane, 32)
    return expert * 128 + register * 32 + unit


def fill_moves(one_ref, two_ref, inward):
    for ref, place in ((one_ref, place_one), (two_ref, place_two)):
        n = ref.shape[0]
        if inward:
            moved = place(lax.broadcasted_iota(jnp.int32, (n, 1), 0))
            ref[...] = (moved == lax.broadcasted_iota(jnp.int32, (n, n), 1)).astype(f32).astype(bf16)
        else:
            moved = place(lax.broadcasted_iota(jnp.int32, (1, n), 1))
            ref[...] = (moved == lax.broadcasted_iota(jnp.int32, (n, n), 0)).astype(f32).astype(bf16)


def near_buckets(rows):
    offset = (
        lax.broadcasted_iota(jnp.int32, (rows, 3 * rows), 1)
        - rows
        - lax.broadcasted_iota(jnp.int32, (rows, 3 * rows), 0)
    )
    return bucket_ids(offset)


def fill_bias(bias_ref, table_ref, chip, heads):
    rows = bias_ref.shape[1]
    span = bias_ref.shape[2]
    mid = span // 2
    buckets = near_buckets(rows)
    for h in range(heads):
        column = chip * heads + h
        near = jnp.zeros(buckets.shape, f32)
        for b in range(table_ref.shape[0]):
            near = jnp.where(buckets == b, table_ref[b, column], near)
        bias_ref[h, :, 0:mid - rows] = jnp.full((rows, mid - rows), table_ref[15, column], f32)
        bias_ref[h, :, mid - rows:mid + 2 * rows] = near
        bias_ref[h, :, mid + 2 * rows:] = jnp.full((rows, span - mid - 2 * rows), table_ref[31, column], f32)


def allowed_pairs(doc_row, block_at, local):
    start = pl.multiple_of(block_at * local, local)
    return as_column(doc_row[:, pl.ds(start, local)]) == doc_row[...].astype(f32)


def unit_scores(q_block, keys, bias_ref, h, block_at, allowed):
    rows = q_block.shape[0]
    seq = keys.shape[0]
    lanes = lax.broadcasted_iota(jnp.int32, q_block.shape, 1) // HSIZE
    masked = jnp.where(lanes == h, q_block, jnp.zeros_like(q_block))
    start = pl.multiple_of(seq - rows * block_at, rows)
    return jnp.where(allowed, nt(masked, keys) + bias_ref[h, :, pl.ds(start, seq)], -1000000000.0)


def fill_slots(slot_ref, choice_row, experts, capacity):
    tokens = choice_row.shape[1]
    expert = lax.broadcasted_iota(jnp.int32, (experts, 128), 0)
    upper = (lax.broadcasted_iota(jnp.int32, (128, 128), 0)
             <= lax.broadcasted_iota(jnp.int32, (128, 128), 1)).astype(f32).astype(bf16)
    before = jnp.zeros((experts, 1), f32)
    for b in range(tokens // 128):
        choice = choice_row[:, b * 128:(b + 1) * 128]
        chosen = (expert == choice).astype(f32)
        count = nn(chosen.astype(bf16), upper)
        place = jnp.sum(chosen * (count + before), axis=0, keepdims=True).astype(jnp.int32) - 1
        slot_ref[:, b * 128:(b + 1) * 128] = jnp.where(place < capacity, choice * capacity + place, -1)
        before = before + count[:, 127:128]


def front_kernel(heads, experts, capacity,
                 x_ref, gain1_ref, wq_ref, wk_ref, wv_ref, wout_ref, table_ref, wr_ref, gain2_ref, doc_row, choice_row,
                 grad_ref, wh_hbm, wb_hbm,
                 rows_ref, slot_ref, w1_hbm, w2_hbm, ag_ref, gs_ref,
                 hidden_ref, normed_ref, router_ref, gate_ref, at_ref, q_ref, kv_ref, lse_ref, xn_ref,
                 wqkv_all, wout_all, small_all,
                 bias_ref, w2_ref, nat_ref, half_ref, one_ref, two_ref, wt_ref, g_ref, g_out, own_ref, other_ref,
                 wq_st, wo_st, sm_st, at_in, rows_out,
                 nat_sem, wt_sem, w2_sem, own_sem, got_sem, other_sem, t_sem,
                 xn_s, xn_r, wq_s, wq_r, wqp_s, wqp_r, sm_s, sm_r, wo_s, wo_r, woc_s, woc_r, wop_s, wop_r,
                 kv_s, kv_r, at_s, at_r, gz_s, gz_r, rz_s, rz_r, gc_s, gc_r, gp_s, gp_r, rc_s, rc_r, rp_s, rp_r):
    me = Place()
    gx, gy, core, chip = me.gx, me.gy, me.core, me.chip
    width, cols = wq_ref.shape
    local = x_ref.shape[0]
    tokens = 32 * local
    units = wh_hbm.shape[1] // experts
    hd = 2 * cols
    seq = 8 * local
    zs = [gx] + me.line_from
    spans = units // 128

    def load_span(source, g, q):
        at = source.at[:, pl.ds(pl.multiple_of(g * 4096 + q * 1024, 1024), 1024)]
        return pltpu.make_async_copy(at, nat_ref.at[q], nat_sem.at[q])

    def turn_span(source, g, put):
        for q in range(4):
            load_span(source, g, q).wait()
            moved = nn(nat_ref[q], one_ref[...]).astype(bf16)
            for r in range(8):
                half_ref[r, :, q * 128:(q + 1) * 128] = moved[:, r * 128:(r + 1) * 128]
        for r in range(8):
            moved = nn(half_ref[r], two_ref[...]).astype(bf16)
            put(r, [moved[:, n * 128:(n + 1) * 128] for n in range(4)])

    def turn_back_weights():
        def body(g, carry):
            lanes = pl.ds(pl.multiple_of(g * 128, 128), 128)

            def put(r, blocks):
                for n, block in enumerate(blocks):
                    w2_ref[4 * r + n, :, lanes] = block
            turn_span(wb_hbm, g, put)

            @pl.when(g + 1 < spans)
            def _():
                for q in range(4):
                    load_span(wb_hbm, g + 1, q).start()
            return carry
        lax.fori_loop(0, spans, body, 0)
        w2_copy().start()

    def w2_copy():
        return pltpu.make_async_copy(w2_ref, w2_hbm, w2_sem.at[0])

    def store_span(g, r):
        lanes = pl.ds(pl.multiple_of(g * 128, 128), 128)
        return pltpu.make_async_copy(wt_ref.at[r], w1_hbm.at[pl.ds(4 * r, 4), :, lanes], wt_sem.at[r])

    def turn_hidden_weights(g):
        def put(r, blocks):
            if g > 0:
                store_span(g - 1, r).wait()
            for n, block in enumerate(blocks):
                wt_ref[r, n] = block
            store_span(g, r).start()
        turn_span(wh_hbm, g, put)
        if g + 1 < spans:
            for q in range(4):
                load_span(wh_hbm, g + 1, q).start()

    def dispatcher(out, dst, zsem_s, zsem_r, csem_s, csem_r, psem_s, psem_r):
        def to_line(k):
            return remote(out.at[me.line[k]], dst.at[gx * 8 + gy], zsem_s.at[k], zsem_r.at[k], me.on_line(k))

        def to_plane(m, k):
            at = dst.at[zs[m] * 8 + gy]
            return remote(at, at, csem_s.at[m, k], csem_r.at[m, k], me.on_plane(k))

        def to_pair(m, k):
            c = chip if k == 0 else me.chips_from[k - 1]
            at = dst.at[zs[m] * 8 + 2 * c + core]
            return remote(at, at, psem_s.at[m, k], psem_r.at[m, k], me.pair)
        return to_line, to_plane, to_pair

    def start_plane(to_line, to_plane, to_pair, m):
        if m > 0:
            to_line(m - 1).wait_recv()
        for k in range(3):
            to_plane(m, k).start()
        to_pair(m, 0).start()

    g_line, g_plane, g_pair = dispatcher(g_out, g_ref, gz_s, gz_r, gc_s, gc_r, gp_s, gp_r)
    r_line, r_plane, r_pair = dispatcher(rows_out, rows_ref, rz_s, rz_r, rc_s, rc_r, rp_s, rp_r)
    acts = LineSum(me, own_ref, ag_ref, other_ref, own_sem, got_sem, other_sem, t_sem, experts)

    def act_step(i, carry):
        @pl.when(i < experts)
        def _():
            acts.slot_free(i)
            gs = pick_rows(slot_ref, i * capacity, capacity, g_ref_rows, tokens).astype(bf16)
            gs_ref[i] = gs
            acts.put(i, nn(gs, w2_ref[i]).astype(bf16))
        acts.half(i - LAG_B)
        acts.whole(i - LAG_C)
        return carry

    class Rows:
        def __getitem__(self, at):
            rows = at[0]
            return g_ref[rows.start // local:rows.stop // local].reshape(rows.stop - rows.start, width)

    g_ref_rows = Rows()

    def act_steps(first, last):
        lax.fori_loop(first, last, act_step, 0)

    for z in range(4):
        g_out[z] = grad_ref[:, z * width:(z + 1) * width]
    x = x_ref[...].astype(f32)
    r1 = lax.rsqrt(jnp.mean(x * x, axis=-1, keepdims=True) + epsilon)
    xn_ref[chip] = (x * r1 * gain1_ref[...]).astype(bf16)
    wq_st[core, gx] = jnp.concatenate([wq_ref[...], wk_ref[...], wv_ref[...]], axis=1)
    wo_st[gy, gx] = wout_ref[...]
    wr_wide = jnp.concatenate([wr_ref[...], jnp.zeros((width, 128 - experts), f32)], axis=1)
    sm_st[gx] = jnp.concatenate([jnp.transpose(wr_wide)[:experts], gain2_ref[...], jnp.zeros((7, width), f32)], axis=0)
    g_ref[gx * 8 + gy] = g_out[gx]
    me.greet_all()

    def wq_line(k):
        at = wq_st.at[core, gx]
        return remote(at, at, wq_s.at[k], wq_r.at[k], me.on_line(k))

    def xn_plane(k):
        return remote(xn_ref.at[chip], xn_ref.at[chip], xn_s.at[k], xn_r.at[k], me.on_plane(k))

    def sm_line(k):
        return remote(sm_st.at[gx], sm_st.at[gx], sm_s.at[k], sm_r.at[k], me.on_line(k))

    def wo_line(k):
        return remote(wo_st.at[gy, gx], wo_st.at[gy, gx], wo_s.at[k], wo_r.at[k], me.on_line(k))

    def wq_pair(k):
        at = wq_st.at[core, zs[k]]
        return remote(at, at, wqp_s.at[k], wqp_r.at[k], me.pair)

    def wo_plane(k):
        return remote(wo_st.at[gy], wo_st.at[gy], woc_s.at[k], woc_r.at[k], me.on_plane(k))

    def wo_pair(k):
        c = chip if k == 0 else me.chips_from[k - 1]
        return remote(wo_st.at[2 * c + core], wo_st.at[2 * c + core], wop_s.at[k], wop_r.at[k], me.pair)

    for k in range(3):
        g_line(k).start()
    for k in range(3):
        wq_line(k).start()
    start_plane(g_line, g_plane, g_pair, 0)
    for k in range(3):
        xn_plane(k).start()
    wq_pair(0).start()
    for k in range(3):
        wo_line(k).start()
        sm_line(k).start()
    for q in range(4):
        load_span(wb_hbm, 0, q).start()
    fill_moves(one_ref, two_ref, True)
    fill_slots(slot_ref, choice_row, experts, capacity)
    fill_bias(bias_ref, table_ref, chip, heads)
    for m in (1, 2, 3):
        start_plane(g_line, g_plane, g_pair, m)
    turn_back_weights()
    for q in range(4):
        load_span(wh_hbm, 0, q).start()
    for m in range(4):
        for k in range(3):
            g_plane(m, k).wait_recv()
            g_pair(m, k + 1).start()
    for k in range(3):
        wq_line(k).wait_recv()
        wq_pair(k + 1).start()
    for k in range(3):
        wo_line(k).wait_recv()
    for k in range(3):
        wo_plane(k).start()
    wo_pair(0).start()
    for m in range(4):
        for k in range(4):
            g_pair(m, k).wait_recv()
    act_steps(0, 4)
    for k in range(4):
        wq_pair(k).wait_recv()
    for z in range(4):
        parts = [wq_st[0, z], wq_st[1, z]]
        wqkv_all[z * width:(z + 1) * width, :] = jnp.concatenate(
            [parts[j][:, n * cols:(n + 1) * cols] for n in range(3) for j in range(2)], axis=1)

    def kv_pair(c):
        return remote(kv_ref.at[2 * c + core], kv_ref.at[2 * c + core], kv_s.at[c], kv_r.at[c], me.pair)

    scale = HSIZE ** (-0.5)
    for k in range(4):
        c = chip if k == 0 else me.chips_from[k - 1]
        if k > 0:
            xn_plane(k - 1).wait_recv()
        made = nn(xn_ref[c], wqkv_all[...])
        q_ref[c] = (made[:, :hd].astype(bf16).astype(f32) * scale).astype(bf16)
        kv_ref[2 * c + core] = made[:, hd:].astype(bf16)
        kv_pair(c).start()
    for k in range(3):
        wo_plane(k).wait_recv()
        wo_pair(k + 1).start()
    act_steps(4, 7)
    for c in range(4):
        kv_pair(c).wait_recv()
    lanes = lax.broadcasted_iota(jnp.int32, (local, hd), 1) // HSIZE

    def at_plane(k):
        return remote(at_ref.at[me.chips[k]], at_in.at[chip], at_s.at[k], at_r.at[k], me.on_plane(k))

    for k in range(4):
        c = me.chips[k] if k < 3 else chip
        block_at = 2 * c + core
        allowed = allowed_pairs(doc_row, block_at, local)
        keys = kv_ref[:, :, :hd].reshape(seq, hd)
        values = kv_ref[:, :, hd:].reshape(seq, hd)
        total = jnp.zeros((local, hd), f32)
        for h in range(heads):
            scores = unit_scores(q_ref[c], keys, bias_ref, h, block_at, allowed)
            peak = jnp.max(scores, axis=-1, keepdims=True)
            shifted = jnp.exp(scores - peak)
            summed = jnp.sum(shifted, axis=-1, keepdims=True)
            lse_ref[c, h] = jnp.broadcast_to(peak + jnp.log(summed), (local, 128))
            low = (shifted * (1.0 / summed)).astype(bf16)
            total = jnp.where(lanes == h, nn(low, values), total)
        at_ref[c] = total.astype(bf16)
        if k < 3:
            at_plane(k).start()
        else:
            at_in[chip] = total.astype(bf16)
        act_steps(7 + 2 * k, 9 + 2 * k)
    for k in range(3):
        sm_line(k).wait_recv()
    small_all[...] = jnp.concatenate([sm_st[z] for z in range(4)], axis=1)
    for k in range(4):
        wo_pair(k).wait_recv()
    for g in range(8):
        wout_all[g * cols:(g + 1) * cols, :] = jnp.concatenate([wo_st[g, z] for z in range(4)], axis=1)
    for k in range(3):
        at_plane(k).wait_recv()
    attended = jnp.concatenate([at_in[c] for c in range(4)], axis=1)
    hidden = x + nn(attended, wout_all[...]).astype(bf16).astype(f32)
    hidden_ref[...] = hidden
    r2 = lax.rsqrt(jnp.mean(hidden * hidden, axis=-1, keepdims=True) + epsilon)
    normed = hidden * r2 * small_all[experts:experts + 1, :]
    normed_ref[...] = normed
    logits = lax.dot_general(normed, small_all[:experts, :], (((1,), (1,)), ((), ())),
                             precision=lax.Precision.HIGHEST, preferred_element_type=f32)
    lifted = jnp.exp(logits - jnp.max(logits, axis=-1, keepdims=True))
    router = lifted / jnp.sum(lifted, axis=-1, keepdims=True)
    router_ref[...] = router
    own_tokens = pl.ds(pl.multiple_of((gx * 8 + gy) * local, local), local)
    picked = as_column(choice_row[:, own_tokens]) == lax.broadcasted_iota(jnp.int32, router.shape, 1).astype(f32)
    gate = jnp.sum(jnp.where(picked, router, 0.0), axis=-1, keepdims=True)
    gate_ref[...] = gate
    first = gate.astype(bf16).astype(f32)
    second = (gate - first).astype(bf16).astype(f32)
    third = gate - first - second
    lane = lax.broadcasted_iota(jnp.int32, (local, 64), 1)
    pieces = jnp.where(lane == 0, first, jnp.where(lane == 1, second, jnp.where(lane == 2, third, 0.0))).astype(bf16)
    low = normed.astype(bf16)
    for z in range(4):
        rows_out[z] = jnp.concatenate([low[:, z * width:(z + 1) * width], pieces], axis=1)
    for k in range(3):
        r_line(k).start()
    rows_ref[gx * 8 + gy] = rows_out[gx]
    start_plane(r_line, r_plane, r_pair, 0)
    act_steps(15, 18)
    for m in (1, 2, 3):
        start_plane(r_line, r_plane, r_pair, m)
    act_steps(18, 21)
    for m in range(4):
        for k in range(3):
            r_plane(m, k).wait_recv()
            r_pair(m, k + 1).start()
    for n in range(spans):
        turn_hidden_weights(n)
        act_steps(21 + 3 * n, 24 + 3 * n)
    act_steps(21 + 3 * spans, experts + LAG_C)
    for m in range(4):
        for k in range(4):
            r_pair(m, k).wait_recv()

    def arrived(e, carry):
        acts.await_total(e)
        return carry
    lax.fori_loop(0, experts, arrived, 0)
    acts.drain()
    for r in range(8):
        store_span(spans - 1, r).wait()
    w2_copy().wait()
    for m in range(4):
        for k in range(4):
            g_pair(m, k).wait_send()
            r_pair(m, k).wait_send()
        for k in range(3):
            g_plane(m, k).wait_send()
            r_plane(m, k).wait_send()
    for k in range(3):
        for copy in (g_line, r_line, at_plane, wo_plane, wo_line, sm_line, wq_line, xn_plane):
            copy(k).wait_send()
    for k in range(4):
        for copy in (wq_pair, wo_pair, kv_pair):
            copy(k).wait_send()


def front(x_in, gain1, wq, wk, wv, wout, table, wr, gain2, doc_row, choice_row, grad_out, w_hidden, w_back,
          collective_id):
    local, features = x_in.shape
    width, cols = wq.shape
    hd = 2 * cols
    heads = hd // HSIZE
    experts = wr.shape[1]
    tokens = choice_row.shape[1]
    capacity = tokens * 5 // (4 * experts)
    units = w_hidden.shape[1] // experts
    vm = pl.BlockSpec(memory_space=pltpu.VMEM)
    sm = pl.BlockSpec(memory_space=pltpu.SMEM)
    hbm = pl.BlockSpec(memory_space=pl.ANY)
    dma = pltpu.SemaphoreType.DMA
    shape = jax.ShapeDtypeStruct
    V = pltpu.VMEM
    ring = 12
    return pl.pallas_call(
        functools.partial(front_kernel, heads, experts, capacity),
        out_shape=(
            shape((32, local, width + 64), bf16),
            shape((1, tokens), jnp.int32),
            shape((experts, width, units), bf16),
            shape((experts, width, units), bf16),
            shape((experts, capacity, units), bf16),
            shape((experts, capacity, width), bf16),
            shape((local, features), f32),
            shape((local, features), f32),
            shape((local, experts), f32),
            shape((local, 1), f32),
            shape((4, local, hd), bf16),
            shape((4, local, hd), bf16),
            shape((8, local, 2 * hd), bf16),
            shape((4, heads, local, 128), f32),
            shape((4, local, features), bf16),
            shape((features, 3 * hd), bf16),
            shape((features, features), bf16),
            shape((experts + 8, features), f32),
        ),
        in_specs=[vm] * 6 + [sm] + [vm] * 5 + [hbm] * 2,
        out_specs=(vm, vm, hbm, hbm) + (vm,) * 14,
        scratch_shapes=[
            V((heads, local, 16 * local), f32),
            V((experts, width, units), bf16),
            V((4, width, 1024), bf16), V((8, width, 512), bf16), V((1024, 1024), bf16), V((512, 512), bf16),
            V((8, 4, width, 128), bf16),
            V((32, local, width), bf16), V((4, local, width), bf16),
            V((ring, capacity, units), bf16), V((experts, capacity, units), bf16),
            V((2, 4, width, 3 * cols), bf16), V((8, 4, cols, width), bf16), V((4, experts + 8, width), f32),
            V((4, local, hd), bf16), V((4, local, width + 64), bf16),
            dma((4,)), dma((8,)), dma((1,)), dma((ring,)), dma((experts,)), dma((experts,)), dma((experts,)),
        ] + [dma((n,)) for n in (3, 3, 3, 3, 4, 4, 3, 3, 3, 3, 3, 3, 4, 4, 4, 4, 3, 3, 3, 3, 3, 3)]
        + [dma((4, 3)), dma((4, 3)), dma((4, 4)), dma((4, 4))] * 2,
        compiler_params=pltpu.CompilerParams(
            collective_id=collective_id, has_side_effects=True, vmem_limit_bytes=62 * 2**20),
        cost_estimate=pl.CostEstimate(flops=4 * 10**9, bytes_accessed=20 * 10**6, transcendentals=2 * 10**6),
    )(x_in, gain1, wq, wk, wv, wout, table, wr, gain2, doc_row, choice_row, grad_out, w_hidden, w_back)


HIGH = lax.Precision.HIGHEST


def back_kernel(heads, experts,
                x_ref, gain1_ref, grad_ref, choice_row, doc_row, table_ref,
                hidden_ref, normed_ref, router_ref, gate_ref, at_ref, q_ref, kv_ref, lse_ref, xn_ref,
                wqkv_all, wout_all, small_all, ret_ref,
                out_ref, gin_ref, wgrad_ref, ograd_ref, small_out, tail_out,
                bias_ref,
                ag_ref, dq_ref, dk_ref, dv_ref, near_ref, go_ref, fg_ref, top_ref,
                sp_out, sp_in, sc_out, sc_in, sz_out, sz_in,
                kv_out, kv_in, kv_sum, fg_out, fg_in, wp_out, wp_in, wz_out, wz_in,
                op_out, op_in, oz_out, oz_in, tp_out, tp_in, tc_out, tc_in, tz_out, tz_in,
                ag_s, ag_r, sp_s, sp_r, sc_s, sc_r, sz_s, sz_r, kv_s, kv_r, fg_s, fg_r, wp_s, wp_r,
                wz_s, wz_r, op_s, op_r, oz_s, oz_r, tp_s, tp_r, tc_s, tc_r, tz_s, tz_r):
    me = Place()
    gx, gy, core, chip = me.gx, me.gy, me.core, me.chip
    local, features = x_ref.shape
    width = features // 4
    hd = q_ref.shape[2]
    cols = hd // 2
    seq = 8 * local
    hidden = hidden_ref[...]
    r2 = lax.rsqrt(jnp.mean(hidden * hidden, axis=-1, keepdims=True) + epsilon)
    grads = grad_ref[...].astype(f32)
    gate = gate_ref[...]
    routed = jnp.concatenate([ret_ref[z][:, :width] for z in range(4)], axis=1)
    back = jnp.concatenate([ret_ref[z][:, width:] for z in range(4)], axis=1)
    out_ref[...] = hidden + gate * routed
    gate_grad = jnp.sum(grads * routed, axis=-1, keepdims=True)
    router = router_ref[...]
    own_tokens = pl.ds(pl.multiple_of((gx * 8 + gy) * local, local), local)
    picked = (as_column(choice_row[:, own_tokens])
              == lax.broadcasted_iota(jnp.int32, router.shape, 1).astype(f32)).astype(f32)
    logit_grad = router * (gate_grad * picked - gate * gate_grad)
    second = back + jnp.dot(logit_grad, small_all[:experts, :], precision=HIGH, preferred_element_type=f32)
    gained = second * small_all[experts:experts + 1, :]
    dot2 = jnp.sum(gained * hidden, axis=-1, keepdims=True)
    hidden_grad = grads + r2 * gained - hidden * (r2 * r2 * r2) * (dot2 / features)
    ag_ref[chip] = hidden_grad.astype(bf16)
    me.greet_all()

    def ag_plane(k):
        return remote(ag_ref.at[chip], ag_ref.at[chip], ag_s.at[k], ag_r.at[k], me.on_plane(k))

    for k in range(3):
        ag_plane(k).start()

    fill_bias(bias_ref, table_ref, chip, heads)

    routed_grad = lax.dot_general(logit_grad, normed_ref[...], (((0,), (0,)), ((), ())), precision=HIGH,
                                  preferred_element_type=f32)
    norm2 = jnp.sum(second * hidden * r2, axis=0, keepdims=True)
    own_small = jnp.concatenate([routed_grad, norm2, jnp.zeros((7, features), f32)], axis=0)
    sp_out[...] = own_small
    small_pair = remote(sp_out, sp_in, sp_s.at[0], sp_r.at[0], me.pair)
    small_pair.start()

    def small_plane(k):
        return remote(sc_out, sc_in.at[k], sc_s.at[k], sc_r.at[k], me.on_plane(k))

    def small_line(k):
        return remote(sz_out.at[me.line[k]], sz_in.at[k], sz_s.at[k], sz_r.at[k], me.on_line(k))

    dk_ref[...] = jnp.zeros_like(dk_ref)
    dv_ref[...] = jnp.zeros_like(dv_ref)
    near_ref[...] = jnp.zeros_like(near_ref)
    go_ref[...] = jnp.zeros_like(go_ref)
    scale = HSIZE ** (-0.5)
    lanes = lax.broadcasted_iota(jnp.int32, (local, hd), 1) // HSIZE

    def attend_block(c):
        block_at = 2 * c + core
        allowed = allowed_pairs(doc_row, block_at, local)
        keys = kv_ref[:, :, :hd].reshape(seq, hd)
        values = kv_ref[:, :, hd:].reshape(seq, hd)
        rows_out = pl.ds(pl.multiple_of(chip * hd, 16), hd)
        att_grad = nt(ag_ref[c], wout_all[rows_out, :]).astype(bf16)
        go_ref[...] += tn(at_ref[c], ag_ref[c])
        q_block = q_ref[c]
        q_turn = jnp.transpose(q_block.astype(f32)).astype(bf16)
        g_turn = jnp.transpose(att_grad.astype(f32)).astype(bf16)
        dq = jnp.zeros((local, hd), f32)
        for h in range(heads):
            scores = unit_scores(q_block, keys, bias_ref, h, block_at, allowed)
            probs = jnp.exp(scores - lse_ref[c, h][:, :1])
            masked = jnp.where(lanes == h, att_grad, jnp.zeros_like(att_grad))
            prob_grad = nt(masked, values)
            weighted = probs * prob_grad
            score_grad = (weighted - probs * jnp.sum(weighted, axis=-1, keepdims=True)).astype(bf16)
            part = slice(h * HSIZE, (h + 1) * HSIZE)
            dv_ref[part, :] += nn(g_turn[part, :], probs.astype(bf16))
            dk_ref[part, :] += nn(q_turn[part, :], score_grad)
            dq = jnp.where(lanes == h, nn(score_grad, keys), dq)
            start = pl.multiple_of(seq - local * block_at, local)
            near_ref[h, :, pl.ds(start, seq)] += score_grad.astype(f32)
        dq_ref[c] = (dq * scale).astype(bf16)

    attend_block(chip)
    small_pair.wait_recv()
    sc_out[...] = own_small + sp_in[...]
    for k in range(3):
        small_plane(k).start()
    for k in range(3):
        ag_plane(k).wait_recv()
        attend_block(me.chips_from[k])
        if k == 0:
            total = sc_out[...]
            for j in range(3):
                small_plane(j).wait_recv()
                total = total + sc_in[j]
            for z in range(4):
                sz_out[z] = total[:, z * width:(z + 1) * width]
            for j in range(3):
                small_line(j).start()

    both = jnp.concatenate([dk_ref[...], dv_ref[...]], axis=0)
    for j in range(8):
        turned = jnp.transpose(both[:, j * local:(j + 1) * local])
        @pl.when(core == j % 2)
        def _():
            kv_sum[j // 2] = turned
        @pl.when(core != j % 2)
        def _():
            kv_out[j // 2] = turned.astype(bf16)
    kv_pair = remote(kv_out, kv_in, kv_s.at[0], kv_r.at[0], me.pair)
    kv_pair.start()

    op_out[...] = go_ref[pl.ds(pl.multiple_of((1 - core) * cols, 16), cols), :].astype(bf16)
    op_pair = remote(op_out, op_in, op_s.at[0], op_r.at[0], me.pair)
    op_pair.start()

    def op_line(k):
        return remote(oz_out.at[me.line[k]], oz_in.at[k], oz_s.at[k], oz_r.at[k], me.on_line(k))

    buckets = near_buckets(local)
    table = jnp.zeros((experts, 128), f32)
    lane = lax.broadcasted_iota(jnp.int32, (experts, 128), 1)
    row = lax.broadcasted_iota(jnp.int32, (experts, 1), 0)
    for h in range(heads):
        close = near_ref[h, :, seq - local:seq + 2 * local]
        for b in range(experts):
            top_ref[b:b + 1, :] = jnp.sum(jnp.where(buckets == b, close, 0.0), axis=0, keepdims=True)
        column = jnp.sum(top_ref[...], axis=1, keepdims=True)
        left = jnp.sum(near_ref[h, :, :seq - local])
        right = jnp.sum(near_ref[h, :, seq + 2 * local:])
        column = column + jnp.where(row == 15, left, 0.0) + jnp.where(row == 31, right, 0.0)
        table = jnp.where(lane == chip * heads + h, column, table)

    kv_pair.wait_recv()
    made = []
    for c in range(4):
        keyval = (kv_sum[c] + kv_in[c].astype(f32)).astype(bf16)
        made.append(jnp.concatenate([dq_ref[c], keyval], axis=1))

    def fg_plane(k):
        return remote(fg_out.at[me.chips[k]], fg_in.at[k], fg_s.at[k], fg_r.at[k], me.on_plane(k))

    for c in range(4):
        fg_ref[c] = nt(made[c], wqkv_all[...])
        fg_out[c] = fg_ref[c].astype(bf16)
    for k in range(3):
        fg_plane(k).start()
    weight_grad = tn(xn_ref[...].reshape(4 * local, features), jnp.concatenate(made, axis=0))
    halves = [jnp.concatenate([weight_grad[:, n * hd + j * cols:n * hd + (j + 1) * cols] for n in range(3)], axis=1)
              for j in range(2)]
    wp_out[...] = jnp.where(core == 0, halves[1], halves[0]).astype(bf16)
    w_pair = remote(wp_out, wp_in, wp_s.at[0], wp_r.at[0], me.pair)
    w_pair.start()
    own_w = jnp.where(core == 0, halves[0], halves[1])

    def w_line(k):
        return remote(wz_out.at[me.line[k]], wz_in.at[k], wz_s.at[k], wz_r.at[k], me.on_line(k))

    op_pair.wait_recv()
    own_o = go_ref[pl.ds(pl.multiple_of(core * cols, 16), cols), :] + op_in[...].astype(f32)
    for z in range(4):
        oz_out[z] = own_o[:, z * width:(z + 1) * width].astype(bf16)
    for k in range(3):
        op_line(k).start()
    w_pair.wait_recv()
    own_w = own_w + wp_in[...].astype(f32)
    for z in range(4):
        wz_out[z] = own_w[z * width:(z + 1) * width, :].astype(bf16)
    for k in range(3):
        w_line(k).start()

    first = fg_ref[chip]
    for k in range(3):
        fg_plane(k).wait_recv()
        first = first + fg_in[k].astype(f32)
    x = x_ref[...].astype(f32)
    r1 = lax.rsqrt(jnp.mean(x * x, axis=-1, keepdims=True) + epsilon)
    norm1 = jnp.sum(first * x * r1, axis=0, keepdims=True)
    gained1 = first * gain1_ref[...]
    dot1 = jnp.sum(gained1 * x, axis=-1, keepdims=True)
    gin_ref[...] = hidden_grad + r1 * gained1 - x * (r1 * r1 * r1) * (dot1 / features)

    tail = jnp.concatenate([table] + [norm1[:, n * 128:(n + 1) * 128] for n in range(6)] + [jnp.zeros((2, 128), f32)],
                           axis=0)
    tp_out[...] = tail
    t_pair = remote(tp_out, tp_in, tp_s.at[0], tp_r.at[0], me.pair)
    t_pair.start()

    def t_plane(k):
        return remote(tc_out, tc_in.at[k], tc_s.at[k], tc_r.at[k], me.on_plane(k))

    def t_line(k):
        return remote(tz_out, tz_in.at[k], tz_s.at[k], tz_r.at[k], me.on_line(k))

    t_pair.wait_recv()
    tail = jnp.where(core == 0, tail + tp_in[...], tp_in[...] + tail)
    tc_out[...] = tail
    for k in range(3):
        t_plane(k).start()
    for k in range(3):
        t_plane(k).wait_recv()
    tail = jnp.zeros_like(tail)
    for c in range(4):
        part = jnp.where(chip == c, tc_out[...], 0.0)
        for k in range(3):
            part = jnp.where(me.chips_from[k] == c, tc_in[k], part)
        tail = tail + part
    tz_out[...] = tail
    for k in range(3):
        t_line(k).start()

    total = sz_out[gx]
    for k in range(3):
        small_line(k).wait_recv()
        total = total + sz_in[k]
    small_out[...] = total
    total = oz_out[gx].astype(f32)
    for k in range(3):
        op_line(k).wait_recv()
        total = total + oz_in[k].astype(f32)
    ograd_ref[...] = total
    total = wz_out[gx].astype(f32)
    for k in range(3):
        w_line(k).wait_recv()
        total = total + wz_in[k].astype(f32)
    wgrad_ref[...] = total
    for k in range(3):
        t_line(k).wait_recv()
    tail = jnp.zeros_like(tail)
    for z in range(4):
        part = jnp.where(gx == z, tz_out[...], 0.0)
        for k in range(3):
            part = jnp.where(me.line_from[k] == z, tz_in[k], part)
        tail = tail + part
    tail_out[...] = tail
    for copy in (small_pair, kv_pair, op_pair, w_pair, t_pair):
        copy.wait_send()
    for k in range(3):
        for copy in (ag_plane, small_plane, small_line, fg_plane, op_line, w_line, t_plane, t_line):
            copy(k).wait_send()


def back_pass(x_in, gain1, grad_out, choice_row, doc_row, table, saved, returned, collective_id):
    local, features = x_in.shape
    width = features // 4
    hidden, normed, router, gate, attended, queries, keyvals, lse, xn, wqkv, wout, small = saved
    hd = queries.shape[2]
    cols = hd // 2
    heads = hd // HSIZE
    seq = 8 * local
    rows = small.shape[0]
    vm = pl.BlockSpec(memory_space=pltpu.VMEM)
    sm = pl.BlockSpec(memory_space=pltpu.SMEM)
    dma = pltpu.SemaphoreType.DMA
    shape = jax.ShapeDtypeStruct
    V = pltpu.VMEM
    return pl.pallas_call(
        functools.partial(back_kernel, heads, EXPERTS),
        out_shape=(
            shape((local, features), f32),
            shape((local, features), f32),
            shape((width, 3 * cols), f32),
            shape((cols, width), f32),
            shape((rows, width), f32),
            shape((40, 128), f32),
        ),
        in_specs=[vm] * 5 + [sm] + [vm] * 13,
        out_specs=(vm,) * 6,
        scratch_shapes=[
            V((heads, local, 16 * local), f32),
            V((4, local, features), bf16), V((4, local, hd), bf16), V((hd, seq), f32), V((hd, seq), f32),
            V((heads, local, 2 * seq), f32), V((hd, features), f32), V((4, local, features), f32),
            V((EXPERTS, 3 * local), f32),
            V((rows, features), f32), V((rows, features), f32), V((rows, features), f32), V((3, rows, features), f32),
            V((4, rows, width), f32), V((3, rows, width), f32),
            V((4, local, 2 * hd), bf16), V((4, local, 2 * hd), bf16), V((4, local, 2 * hd), f32),
            V((4, local, features), bf16), V((3, local, features), bf16),
            V((features, 3 * cols), bf16), V((features, 3 * cols), bf16),
            V((4, width, 3 * cols), bf16), V((3, width, 3 * cols), bf16),
            V((cols, features), bf16), V((cols, features), bf16), V((4, cols, width), bf16), V((3, cols, width), bf16),
            V((40, 128), f32), V((40, 128), f32), V((40, 128), f32), V((3, 40, 128), f32),
            V((40, 128), f32), V((3, 40, 128), f32),
        ] + [dma((n,)) for n in (3, 3, 1, 1, 3, 3, 3, 3, 1, 1, 3, 3, 1, 1, 3, 3, 1, 1, 3, 3, 1, 1, 3, 3, 3, 3)],
        compiler_params=pltpu.CompilerParams(
            collective_id=collective_id, has_side_effects=True, vmem_limit_bytes=60 * 2**20),
        cost_estimate=pl.CostEstimate(flops=6 * 10**9, bytes_accessed=20 * 10**6, transcendentals=2 * 10**6),
    )(x_in, gain1, grad_out, choice_row, doc_row, table, hidden, normed, router, gate, attended, queries, keyvals, lse, xn,
      wqkv, wout, small, returned)


def finish_kernel(heads, experts,
                  out_ref, gin_ref, wgrad_ref, ograd_ref, small_ref, tail_ref, gh_hbm, gb_hbm,
                  out_to, gin_to, norm1_to, query_to, key_to, value_to, table_to, proj_to, norm2_to, router_to,
                  hidden_to, back_to,
                  one_ref, two_ref, in_ref, half_ref, nat_ref, in_sem, nat_sem):
    width, cols = query_to.shape
    spans = gh_hbm.shape[2] // 128

    def load(source, g, slot):
        at = source.at[:, :, pl.ds(pl.multiple_of(g * 128, 128), 128)]
        return pltpu.make_async_copy(at, in_ref.at[slot], in_sem.at[slot])

    def store(target, g, q):
        at = target.at[:, pl.ds(pl.multiple_of(g * 4096 + q * 1024, 1024), 1024)]
        return pltpu.make_async_copy(nat_ref.at[q], at, nat_sem.at[q])

    work = [(gh_hbm, hidden_to, g) for g in range(spans)] + [(gb_hbm, back_to, g) for g in range(spans)]
    load(work[0][0], work[0][2], 0).start()
    fill_moves(one_ref, two_ref, False)
    for i, (source, target, g) in enumerate(work):
        slot = i % 2
        if i + 1 < len(work):
            load(work[i + 1][0], work[i + 1][2], 1 - slot).start()
        load(source, g, slot).wait()
        for r in range(8):
            block = jnp.concatenate([in_ref[slot, 4 * r + n] for n in range(4)], axis=1)
            moved = nn(block, two_ref[...]).astype(bf16)
            for q in range(4):
                half_ref[q, :, r * 128:(r + 1) * 128] = moved[:, q * 128:(q + 1) * 128]
        for q in range(4):
            if i > 0:
                store(work[i - 1][1], work[i - 1][2], q).wait()
            nat_ref[q] = nn(half_ref[q], one_ref[...])
            store(target, g, q).start()
    out_to[...] = out_ref[...]
    gin_to[...] = gin_ref[...]
    for n in range(6):
        norm1_to[:, n * 128:(n + 1) * 128] = tail_ref[experts + n:experts + n + 1, :]
    query_to[...] = wgrad_ref[:, :cols]
    key_to[...] = wgrad_ref[:, cols:2 * cols]
    value_to[...] = wgrad_ref[:, 2 * cols:]
    table_to[...] = tail_ref[:experts, :heads]
    proj_to[...] = ograd_ref[...]
    norm2_to[...] = small_ref[experts:experts + 1, :]
    router_to[...] = jnp.transpose(small_ref[...])[:, :experts]
    for q in range(4):
        store(work[-1][1], work[-1][2], q).wait()


def finish(out_rows, gin, wgrad, ograd, small, tail, gh, gb, heads):
    experts, width, units = gh.shape
    features = out_rows.shape[1]
    cols = wgrad.shape[1] // 3
    vm = pl.BlockSpec(memory_space=pltpu.VMEM)
    hbm = pl.BlockSpec(memory_space=pl.ANY)
    dma = pltpu.SemaphoreType.DMA
    shape = lambda *dims: jax.ShapeDtypeStruct(dims, f32)
    V = pltpu.VMEM
    return pl.pallas_call(
        functools.partial(finish_kernel, heads, experts),
        out_shape=(
            shape(*out_rows.shape), shape(*gin.shape), shape(1, features),
            shape(width, cols), shape(width, cols), shape(width, cols), shape(experts, heads), shape(*ograd.shape),
            shape(1, width), shape(width, experts), shape(width, experts * units), shape(width, experts * units),
        ),
        in_specs=[vm] * 6 + [hbm] * 2,
        out_specs=(vm,) * 10 + (hbm,) * 2,
        scratch_shapes=[
            V((1024, 1024), bf16), V((512, 512), bf16), V((2, experts, width, 128), bf16), V((4, width, 1024), bf16),
            V((4, width, 1024), f32), dma((2,)), dma((4,)),
        ],
        compiler_params=pltpu.CompilerParams(vmem_limit_bytes=48 * 2**20),
        cost_estimate=pl.CostEstimate(flops=15 * 10**9, bytes_accessed=30 * 10**6, transcendentals=0),
    )(out_rows, gin, wgrad, ograd, small, tail, gh, gb)


def fits(mesh):
    return mesh.shape["gx"] == 4 and mesh.shape["gy"] == 8


def fast(
    x_in,
    norm1_gain,
    w_query,
    w_key,
    w_value,
    relative_bias_table,
    w_out,
    norm2_gain,
    w_router,
    w_hidden,
    w_back,
    expert_choice,
    doc_ids,
    grad_out,
):
    all_tokens = expert_choice.shape[0]
    gain_row = norm1_gain[None, :]
    choice_row, doc_row = expert_choice[None, :], doc_ids[None, :]
    rows, slots, w1, w2, act_grads, slot_grads, *saved = front(
        x_in,
        gain_row,
        w_query,
        w_key,
        w_value,
        w_out,
        relative_bias_table,
        w_router,
        norm2_gain[None, :],
        doc_row,
        choice_row,
        grad_out,
        w_hidden,
        w_back,
        2,
    )
    returned, hidden_grads, back_grads = moe(
        rows.reshape(all_tokens, rows.shape[2]), slots, w1, w2, slot_grads, act_grads, 1
    )
    results = back_pass(
        x_in, gain_row, grad_out, choice_row, doc_row, relative_bias_table, saved, returned, 3
    )
    (
        out_rows,
        input_rows,
        grad_norm1,
        grad_query,
        grad_key,
        grad_value,
        grad_table,
        grad_out_proj,
        grad_norm2,
        grad_router,
        grad_hidden,
        grad_back,
    ) = finish(*results, hidden_grads, back_grads, relative_bias_table.shape[1])
    return (
        out_rows,
        input_rows,
        grad_norm1[0],
        grad_query,
        grad_key,
        grad_value,
        grad_table,
        grad_out_proj,
        grad_norm2[0],
        grad_router,
        grad_hidden,
        grad_back,
    )


def solution(mesh):
    return jax.shard_map(
        fast if fits(mesh) else local,
        mesh=mesh,
        in_specs=(
            P(("gx", "gy"), None),
            P(),
            P("gx", "gy"),
            P("gx", "gy"),
            P("gx", "gy"),
            P(),
            P("gy", "gx"),
            P("gx"),
            P("gx", None),
            P("gx", "gy"),
            P("gx", "gy"),
            P(),
            P("gx"),
            P(("gx", "gy"), None),
        ),
        out_specs=(
            P(("gx", "gy"), None),
            P(("gx", "gy"), None),
            P(),
            P("gx", "gy"),
            P("gx", "gy"),
            P("gx", "gy"),
            P(),
            P("gy", "gx"),
            P("gx"),
            P("gx", None),
            P("gx", "gy"),
            P("gx", "gy"),
        ),
        check_vma=False,
    )
```

```python
import functools
import math

import jax
import jax.numpy as jnp
from jax import lax
from jax.experimental import pallas as pl
from jax.experimental.pallas import tpu as pltpu
from jax.sharding import PartitionSpec as P

D = 768
HEADS = 12
HSIZE = 64
EXPERTS = 32
WINDOW = 1024


epsilon = 1e-06
far_steps = (12, 16, 23, 32, 46, 64, 91)
highest = lax.Precision.HIGHEST


def passed_along(value, axis, steps):
    count = lax.axis_size(axis)
    first, last = (max(0, -steps), min(count, count - steps))
    return lax.ppermute(value, axis, [(source, source + steps) for source in range(first, last)])


def bucket_ids(offset):
    ahead_part = (offset > 0).astype(jnp.int32) * 16
    distance = jnp.abs(offset)
    far_part = 8 + sum(((distance >= threshold).astype(jnp.int32) for threshold in far_steps))
    return ahead_part + jnp.where(distance < 8, distance, far_part)


def width_total(values):
    return lax.psum(values, "gx")


def token_rows(block_part):
    return lax.all_gather(block_part, "gy", axis=0, tiled=True)


def width_rows(block_part):
    return lax.all_gather(block_part, "gx", axis=0, tiled=True)


def width_sums(term_fn, row_number):
    return lax.psum_scatter(
        term_fn(jnp.int32(0), lax.axis_size("gx") * row_number),
        "gx",
        scatter_dimension=0,
        tiled=True,
    )


def token_sums(term_fn, row_number):
    return lax.psum_scatter(
        term_fn(jnp.int32(0), lax.axis_size("gy") * row_number),
        "gy",
        scatter_dimension=0,
        tiled=True,
    )


def collect_window(own_pair, reach):
    window_parts = []
    for offset_step in range(-reach, reach + 1):
        if offset_step == 0:
            window_parts.append(own_pair)
        else:
            window_parts.append(passed_along(own_pair, "gy", -offset_step))
    return jnp.concatenate(window_parts, axis=0)


def return_window(partials, reach, head_rows):
    combined = partials[reach * head_rows : (reach + 1) * head_rows]
    for offset_step in range(-reach, reach + 1):
        if offset_step != 0:
            start = (offset_step + reach) * head_rows
            combined = combined + passed_along(
                partials[start : start + head_rows], "gy", offset_step
            )
    return combined


def head_scores(query_heads, key_heads, bias_terms, allowed, score_scale):
    raw_scores = jnp.einsum(
        "qhd,khd->hqk", query_heads, key_heads, preferred_element_type=jnp.float32
    )
    return jnp.where(allowed[None], raw_scores * score_scale + bias_terms, -1000000000.0)


def rows_cols(blocks, width_devs, token_devs):
    grid = blocks.reshape(width_devs, token_devs, blocks.shape[1], blocks.shape[2])
    return jnp.transpose(grid, (0, 2, 1, 3)).reshape(
        width_devs * blocks.shape[1], token_devs * blocks.shape[2]
    )


def cols_rows(blocks, width_devs, token_devs):
    grid = blocks.reshape(width_devs, token_devs, blocks.shape[1], blocks.shape[2])
    return jnp.transpose(grid, (1, 2, 0, 3)).reshape(
        token_devs * blocks.shape[1], width_devs * blocks.shape[2]
    )


def grid_rows_cols(complete, width_devs, token_devs):
    row_total, col_total = complete.shape
    grid = complete.reshape(
        width_devs, row_total // width_devs, token_devs, col_total // token_devs
    )
    return jnp.transpose(grid, (0, 2, 1, 3)).reshape(
        width_devs * token_devs, row_total // width_devs, col_total // token_devs
    )


def grid_cols_rows(complete, width_devs, token_devs):
    row_total, col_total = complete.shape
    grid = complete.reshape(
        token_devs, row_total // token_devs, width_devs, col_total // width_devs
    )
    return jnp.transpose(grid, (2, 0, 1, 3)).reshape(
        width_devs * token_devs, row_total // token_devs, col_total // width_devs
    )


def spread_rows(partial_sum, column, group_count):
    picked_row = (jnp.arange(group_count, dtype=jnp.int32) == column).astype(jnp.float32)
    return picked_row.reshape((group_count,) + (1,) * partial_sum.ndim) * partial_sum[None]


def take_rows(table, index):
    return jnp.take(table, index, axis=0, mode="fill", fill_value=0)


def local(
    x_in,
    norm1_gain,
    w_query,
    w_key,
    w_value,
    relative_bias_table,
    w_out,
    norm2_gain,
    w_router,
    w_hidden,
    w_back,
    expert_choice,
    doc_ids,
    grad_out,
):
    token_devs = lax.axis_size("gy")
    width_devs = lax.axis_size("gx")
    member = lax.axis_index("gy")
    column = lax.axis_index("gx")
    local_count = x_in.shape[0]
    width_cols = w_router.shape[0]
    own_rows = local_count * width_devs
    all_tokens = own_rows * token_devs
    seq_len = local_count * token_devs
    experts = EXPERTS
    capacity = all_tokens * 5 // (4 * experts)
    score_scale = HSIZE ** (-0.5)
    reach = min((WINDOW + local_count - 2) // local_count, token_devs - 1)
    key_count = (2 * reach + 1) * local_count
    whole_weights = (
        lax.all_gather(w_query[None], ("gx", "gy"), axis=0, tiled=True),
        lax.all_gather(w_key[None], ("gx", "gy"), axis=0, tiled=True),
        lax.all_gather(w_value[None], ("gx", "gy"), axis=0, tiled=True),
        lax.all_gather(w_out[None], ("gx", "gy"), axis=0, tiled=True),
    )
    qkv_full = jnp.concatenate(
        [
            rows_cols(whole_weights[0], width_devs, token_devs),
            rows_cols(whole_weights[1], width_devs, token_devs),
            rows_cols(whole_weights[2], width_devs, token_devs),
        ],
        axis=1,
    )
    out_full = cols_rows(whole_weights[3], width_devs, token_devs)
    head_width = out_full.shape[0]
    inputs_row = x_in.astype(jnp.float32)
    scale_first = lax.rsqrt(jnp.mean(inputs_row * inputs_row, axis=-1, keepdims=True) + epsilon)
    normed_first = (inputs_row * scale_first * norm1_gain).astype(jnp.bfloat16)
    qkv_rows = jnp.dot(normed_first, qkv_full, preferred_element_type=jnp.float32).astype(
        jnp.bfloat16
    )
    query_heads = qkv_rows[:, :head_width].reshape(local_count, HEADS, HSIZE)
    pair_window = collect_window(
        qkv_rows[:, head_width:].reshape(local_count, 2, head_width), reach
    )
    key_heads = pair_window[:, 0].reshape(key_count, HEADS, HSIZE)
    value_heads = pair_window[:, 1].reshape(key_count, HEADS, HSIZE)
    query_pos = member * local_count + jnp.arange(local_count, dtype=jnp.int32)
    key_pos = (member - reach) * local_count + jnp.arange(key_count, dtype=jnp.int32)
    offset = key_pos[None, :] - query_pos[:, None]
    buckets = bucket_ids(offset)
    bias_terms = jnp.take(jnp.transpose(relative_bias_table), buckets, axis=1)
    no_doc = jnp.full((reach * local_count,), -1, jnp.int32)
    doc_padded = jnp.concatenate([no_doc, doc_ids, no_doc], axis=0)
    key_docs = lax.dynamic_slice_in_dim(doc_padded, member * local_count, key_count, 0)
    query_docs = lax.dynamic_slice_in_dim(doc_ids, member * local_count, local_count, 0)
    allowed = (jnp.abs(offset) < WINDOW) & (query_docs[:, None] == key_docs[None, :])
    attention_scores = head_scores(query_heads, key_heads, bias_terms, allowed, score_scale)
    row_peak = jnp.max(attention_scores, axis=-1, keepdims=True)
    shifted = jnp.exp(attention_scores - row_peak)
    row_sum = jnp.sum(shifted, axis=-1, keepdims=True)
    log_total = row_peak + jnp.log(row_sum)
    weights_reduced_precision = (shifted / row_sum).astype(jnp.bfloat16)
    attended = jnp.einsum(
        "hqk,khd->qhd", weights_reduced_precision, value_heads, preferred_element_type=jnp.float32
    )
    attended_low = attended.reshape(local_count, head_width).astype(jnp.bfloat16)
    attn_low = jnp.dot(attended_low, out_full, preferred_element_type=jnp.float32).astype(
        jnp.bfloat16
    )
    arrived = lax.all_to_all(
        jnp.stack([x_in, attn_low, grad_out], axis=1), "gx", split_axis=2, concat_axis=0, tiled=True
    )
    inputs = arrived[:, 0].astype(jnp.float32)
    grad_rows = arrived[:, 2].astype(jnp.float32)
    hidden_first = inputs + arrived[:, 1].astype(jnp.float32)
    scale_second = lax.rsqrt(
        width_total(jnp.sum(hidden_first * hidden_first, axis=-1)) / D + epsilon
    )[:, None]
    normed_second = hidden_first * scale_second * norm2_gain
    logits = width_total(jnp.dot(normed_second, w_router, precision=highest))
    router = jax.nn.softmax(logits, axis=-1)
    expert_iota = jnp.arange(experts, dtype=jnp.int32)
    tok_block = math.gcd(all_tokens, 128)
    block_count = all_tokens // tok_block
    chosen_rows = expert_iota[:, None] == expert_choice[None, :]
    chosen_low = chosen_rows.astype(jnp.bfloat16).reshape(experts, block_count, tok_block)
    block_iota = jnp.arange(tok_block, dtype=jnp.int32)
    upper = (block_iota[:, None] <= block_iota[None, :]).astype(jnp.bfloat16)
    inside_count = jnp.einsum("ebi,ij->ebj", chosen_low, upper, preferred_element_type=jnp.float32)
    block_totals = inside_count[:, :, tok_block - 1]
    earlier_blocks = jnp.cumsum(block_totals, axis=1) - block_totals
    counted = (inside_count + earlier_blocks[:, :, None]).reshape(experts, all_tokens)
    position = (jnp.sum(jnp.where(chosen_rows, counted, 0.0), axis=0) - 1.0).astype(jnp.int32)
    kept_all = position < capacity
    slot_all = jnp.where(kept_all, expert_choice * capacity + position, experts * capacity)
    source = (
        jnp.full((experts * capacity + 1,), all_tokens, jnp.int32)
        .at[slot_all]
        .set(jnp.arange(all_tokens, dtype=jnp.int32))[: experts * capacity]
    )
    source_seq = source // seq_len
    source_inner = source % seq_len
    source_rows = jnp.where(
        source < all_tokens,
        source_inner // local_count * own_rows
        + source_seq * local_count
        + source_inner % local_count,
        all_tokens,
    )
    row_iota = jnp.arange(all_tokens, dtype=jnp.int32)
    global_of_row = (
        row_iota // local_count % width_devs * seq_len
        + row_iota // own_rows * local_count
        + row_iota % local_count
    )
    slot_rows = jnp.take(slot_all, global_of_row)
    own_global = lax.dynamic_slice_in_dim(global_of_row, member * own_rows, own_rows, 0)
    picked_mine = jnp.take(expert_choice, own_global)[:, None] == expert_iota[None, :]
    gate_value = jnp.sum(jnp.where(picked_mine, router, 0.0), axis=-1)
    second_rows = token_rows(normed_second.astype(jnp.bfloat16))
    hidden_weight = jnp.transpose(w_hidden.reshape(width_cols, -1, experts), (2, 0, 1))
    back_weight = jnp.transpose(w_back.reshape(width_cols, -1, experts), (2, 1, 0))
    expert_rows = experts // width_devs
    slot_in = take_rows(second_rows, source_rows).reshape(experts, capacity, width_cols)

    def hidden_term(first_row, row_count):
        return jnp.einsum(
            "ecd,edf->ecf", slot_in, hidden_weight, preferred_element_type=jnp.float32
        )

    pre_block = width_sums(hidden_term, expert_rows)
    act_rows = width_rows(jax.nn.gelu(pre_block).astype(jnp.bfloat16))
    expert_out = jnp.einsum(
        "ecf,efd->ecd", act_rows, back_weight, preferred_element_type=jnp.float32
    ).reshape(experts * capacity, width_cols)

    def route_term(first_row, row_count):
        return take_rows(expert_out, slot_rows)

    routed = token_sums(route_term, own_rows)
    block_out = hidden_first + gate_value[:, None] * routed
    gate_grad = width_total(jnp.sum(grad_rows * routed, axis=-1))
    route_rows = token_rows((grad_rows * gate_value[:, None]).astype(jnp.bfloat16))
    gelu_pair = jax.vjp(jax.nn.gelu, pre_block)
    slot_grad = take_rows(route_rows, source_rows).reshape(experts, capacity, width_cols)
    back_grads = jnp.einsum("ecf,ecd->efd", act_rows, slot_grad, preferred_element_type=jnp.float32)

    def act_term(first_row, row_count):
        return jnp.einsum(
            "ecd,efd->ecf", slot_grad, back_weight, preferred_element_type=jnp.float32
        )

    act_grad = width_sums(act_term, expert_rows)
    pre_rows = width_rows(gelu_pair[1](act_grad)[0].astype(jnp.bfloat16))
    hidden_gradient_rows = jnp.einsum(
        "ecd,ecf->edf", slot_in, pre_rows, preferred_element_type=jnp.float32
    )
    slot_in_grad = jnp.einsum(
        "ecf,edf->ecd", pre_rows, hidden_weight, preferred_element_type=jnp.float32
    ).reshape(experts * capacity, width_cols)

    def back_route_term(first_row, row_count):
        return take_rows(slot_in_grad, slot_rows)

    back_routed = token_sums(back_route_term, own_rows)
    grad_hidden = jnp.transpose(hidden_gradient_rows, (1, 2, 0)).reshape(width_cols, -1)
    grad_back = jnp.transpose(back_grads, (2, 1, 0)).reshape(width_cols, -1)
    logit_grad = router * (
        gate_grad[:, None] * picked_mine.astype(jnp.float32) - (gate_value * gate_grad)[:, None]
    )
    second_grad = back_routed + jnp.einsum("re,de->rd", logit_grad, w_router, precision=highest)
    router_part = jnp.einsum("rd,re->de", normed_second, logit_grad, precision=highest)
    norm2_part = jnp.sum(second_grad * hidden_first * scale_second, axis=0)
    gained_second = second_grad * norm2_gain
    row_dot_second = width_total(jnp.sum(gained_second * hidden_first, axis=-1))[:, None]
    hidden_grad = (
        grad_rows
        + scale_second * gained_second
        - hidden_first * scale_second**3 * row_dot_second / D
    )
    out_rows, hidden_rows = (
        lax.all_to_all(block_out, "gx", split_axis=0, concat_axis=1, tiled=True),
        lax.all_to_all(hidden_grad, "gx", split_axis=0, concat_axis=1, tiled=True),
    )
    attn_grad = hidden_rows.astype(jnp.bfloat16)
    grad_out_full = jnp.einsum(
        "rf,rd->fd", attended_low, attn_grad, preferred_element_type=jnp.float32
    )
    attended_grad = (
        jnp.einsum("rd,fd->rf", attn_grad, out_full, preferred_element_type=jnp.float32)
        .astype(jnp.bfloat16)
        .reshape(local_count, HEADS, HSIZE)
    )
    scores_again = head_scores(query_heads, key_heads, bias_terms, allowed, score_scale)
    probs_again = jnp.exp(scores_again - log_total)
    value_grad = jnp.einsum(
        "hqk,qhd->khd",
        probs_again.astype(jnp.bfloat16),
        attended_grad,
        preferred_element_type=jnp.float32,
    )
    prob_grad = jnp.einsum(
        "qhd,khd->hqk", attended_grad, value_heads, preferred_element_type=jnp.float32
    )
    score_gradient = (
        probs_again * (prob_grad - jnp.sum(probs_again * prob_grad, axis=-1, keepdims=True))
    ).astype(jnp.bfloat16)
    query_grad = (
        jnp.einsum("hqk,khd->qhd", score_gradient, key_heads, preferred_element_type=jnp.float32)
        * score_scale
    ).astype(jnp.bfloat16)
    key_grad = (
        jnp.einsum("hqk,qhd->khd", score_gradient, query_heads, preferred_element_type=jnp.float32)
        * score_scale
    )
    band_low = max(0, reach * local_count - 90)
    band_high = min(key_count, reach * local_count + local_count + 90)
    bucket_iota = jnp.arange(relative_bias_table.shape[0], dtype=jnp.int32)
    band_onehot = (buckets[None, :, band_low:band_high] == bucket_iota[:, None, None]).astype(
        jnp.bfloat16
    )
    table_near = jnp.einsum(
        "ivt,zvt->zi",
        score_gradient[:, :, band_low:band_high],
        band_onehot,
        preferred_element_type=jnp.float32,
    )
    left_far = jnp.sum(score_gradient[:, :, :band_low].astype(jnp.float32), axis=(1, 2))
    right_far = jnp.sum(score_gradient[:, :, band_high:].astype(jnp.float32), axis=(1, 2))
    table_part = (
        table_near
        + (bucket_iota == 15).astype(jnp.float32)[:, None] * left_far[None, :]
        + (bucket_iota == 31).astype(jnp.float32)[:, None] * right_far[None, :]
    )
    pair_grads = return_window(
        jnp.stack(
            [key_grad.reshape(key_count, head_width), value_grad.reshape(key_count, head_width)],
            axis=1,
        ),
        reach,
        local_count,
    )
    qkv_grad = jnp.concatenate(
        [
            query_grad.reshape(local_count, head_width),
            pair_grads.astype(jnp.bfloat16).reshape(local_count, 2 * head_width),
        ],
        axis=1,
    )
    qkv_grads = jnp.einsum("rd,rc->dc", normed_first, qkv_grad, preferred_element_type=jnp.float32)
    first_grad = jnp.einsum("rc,dc->rd", qkv_grad, qkv_full, preferred_element_type=jnp.float32)
    norm1_part = jnp.sum(first_grad * inputs_row * scale_first, axis=0)
    gained_first = first_grad * norm1_gain
    row_dot_first = jnp.sum(gained_first * inputs_row, axis=-1, keepdims=True)
    input_rows = (
        hidden_rows + scale_first * gained_first - inputs_row * scale_first**3 * row_dot_first / D
    )
    summed = lax.psum(
        (
            norm1_part,
            table_part,
            spread_rows(norm2_part, column, width_devs),
            spread_rows(router_part, column, width_devs),
        ),
        ("gx", "gy"),
    )
    grad_norm1 = summed[0]
    grad_table = summed[1]
    grad_norm2 = lax.dynamic_index_in_dim(summed[2], column, 0, keepdims=False)
    grad_router = lax.dynamic_index_in_dim(summed[3], column, 0, keepdims=False)
    weight_parts = (
        lax.psum_scatter(
            grid_rows_cols(qkv_grads[:, :head_width], width_devs, token_devs),
            ("gx", "gy"),
            scatter_dimension=0,
            tiled=True,
        ),
        lax.psum_scatter(
            grid_rows_cols(qkv_grads[:, head_width : 2 * head_width], width_devs, token_devs),
            ("gx", "gy"),
            scatter_dimension=0,
            tiled=True,
        ),
        lax.psum_scatter(
            grid_rows_cols(qkv_grads[:, 2 * head_width :], width_devs, token_devs),
            ("gx", "gy"),
            scatter_dimension=0,
            tiled=True,
        ),
        lax.psum_scatter(
            grid_cols_rows(grad_out_full, width_devs, token_devs),
            ("gx", "gy"),
            scatter_dimension=0,
            tiled=True,
        ),
    )
    return (
        out_rows,
        input_rows,
        grad_norm1,
        weight_parts[0][0],
        weight_parts[1][0],
        weight_parts[2][0],
        grad_table,
        weight_parts[3][0],
        grad_norm2,
        grad_router,
        grad_hidden,
        grad_back,
    )


MESH = pl.DeviceIdType.MESH
GELU_C = math.sqrt(2.0 / math.pi)
f32, bf16 = jnp.float32, jnp.bfloat16


def nn(a, b):
    return jnp.dot(a, b, preferred_element_type=f32)


def nt(a, b):
    return lax.dot_general(a, b, (((1,), (1,)), ((), ())), preferred_element_type=f32)


def tn(a, b):
    return lax.dot_general(a, b, (((0,), (0,)), ((), ())), preferred_element_type=f32)


def remote(src, dst, send_sem, recv_sem, device):
    return pltpu.make_async_remote_copy(
        src_ref=src, dst_ref=dst, send_sem=send_sem, recv_sem=recv_sem,
        device_id=device, device_id_type=MESH)


class Place:
    def __init__(self):
        self.gx, self.gy = lax.axis_index("gx"), lax.axis_index("gy")
        self.core, self.chip = lax.rem(self.gy, 2), self.gy // 2
        self.pair = (self.gx, self.gy + 1 - 2 * self.core)
        self.line = [lax.rem(self.gx + k, 4) for k in (1, 2, 3)]
        self.chips = [lax.rem(self.chip + k, 4) for k in (1, 2, 3)]
        self.line_from = [lax.rem(self.gx + 4 - k, 4) for k in (1, 2, 3)]
        self.chips_from = [lax.rem(self.chip + 4 - k, 4) for k in (1, 2, 3)]
        self.is_mid = jnp.logical_and(self.gx > 0, self.gx < 3)
        self.is_end = jnp.logical_not(self.is_mid)
        self.mid = (jnp.where(self.gx < 2, 1, 2), self.gy)
        self.other_mid = (jnp.where(self.gx < 2, 2, 1), self.gy)
        self.end = (jnp.where(self.gx < 2, 0, 3), self.gy)

    def on_line(self, k):
        return (self.line[k], self.gy)

    def on_plane(self, k):
        return (self.gx, 2 * self.chips[k] + self.core)

    def greet_all(self):
        devices = [self.on_line(k) for k in range(3)] + [self.on_plane(k) for k in range(3)] + [self.pair]
        barrier = pltpu.get_barrier_semaphore()
        for device in devices:
            pl.semaphore_signal(barrier, inc=1, device_id=device, device_id_type=MESH)
        pl.semaphore_wait(barrier, len(devices))


def as_column(row):
    n = row.shape[1]
    same = lax.broadcasted_iota(jnp.int32, (n, n), 0) == lax.broadcasted_iota(jnp.int32, (n, n), 1)
    return jnp.sum(jnp.where(same, row.astype(f32), 0.0), axis=1, keepdims=True)


def pick_rows(slot_row, base, capacity, rows_ref, tokens):
    kblock = 1024
    ids = lax.broadcasted_iota(jnp.int32, (capacity, kblock), 0) + base
    total = None
    for kb in range(tokens // kblock):
        hot = (slot_row[:, kb * kblock:(kb + 1) * kblock] == ids).astype(f32).astype(bf16)
        part = nn(hot, rows_ref[kb * kblock:(kb + 1) * kblock, :])
        total = part if total is None else total + part
    return total


class LineSum:
    def __init__(self, me, own, got, other, own_sem, got_sem, other_sem, out_sem, experts):
        self.me, self.own, self.got, self.other = me, own, got, other
        self.sems = (own_sem, got_sem, other_sem, out_sem)
        self.ring, self.experts = own.shape[0], experts

    def to_mid(self, e):
        sl = lax.rem(e, self.ring)
        return remote(self.own.at[sl], self.got.at[e], self.sems[0].at[sl], self.sems[1].at[e], self.me.mid)

    def across(self, e):
        sl = lax.rem(e, self.ring)
        return remote(self.own.at[sl], self.other.at[e], self.sems[0].at[sl], self.sems[2].at[e], self.me.other_mid)

    def to_end(self, e):
        return remote(self.got.at[e], self.got.at[e], self.sems[3].at[e], self.sems[1].at[e], self.me.end)

    def slot_free(self, e):
        @pl.when(e >= self.ring)
        def _():
            self.to_mid(e - self.ring).wait_send()

    def put(self, e, value):
        self.own[lax.rem(e, self.ring)] = value

        @pl.when(self.me.is_end)
        def _():
            self.to_mid(e).start()

    def half(self, e):
        @pl.when(jnp.logical_and(self.me.is_mid, jnp.logical_and(e >= 0, e < self.experts)))
        def _():
            sl = lax.rem(e + self.ring, self.ring)
            self.to_mid(e).wait_recv()
            self.own[sl] = (self.own[sl].astype(f32) + self.got[e].astype(f32)).astype(bf16)
            self.across(e).start()

    def whole(self, e):
        @pl.when(jnp.logical_and(self.me.is_mid, jnp.logical_and(e >= 0, e < self.experts)))
        def _():
            sl = lax.rem(e + self.ring, self.ring)
            self.across(e).wait_recv()
            self.got[e] = (self.own[sl].astype(f32) + self.other[e].astype(f32)).astype(bf16)
            self.to_end(e).start()

    def await_total(self, e):
        @pl.when(self.me.is_end)
        def _():
            self.to_end(e).wait_recv()

    def drain(self):
        def sent(e, carry):
            self.to_mid(e).wait_send()
            return carry
        lax.fori_loop(self.experts - self.ring, self.experts, sent, 0)

        @pl.when(self.me.is_mid)
        def _():
            def out(e, carry):
                self.to_end(e).wait_send()
                return carry
            lax.fori_loop(0, self.experts, out, 0)


RING = 8
GROUP = 4
LAG_B, LAG_C, LAG_D = 2, 4, 6


class LineGather:
    def __init__(self, me, slot, right_s, right_r, left_s, left_r):
        self.me, self.slot = me, slot
        self.sems = (right_s, right_r, left_s, left_r)

    def right(self, h):
        at = self.slot(jnp.maximum(self.me.gx - h, 0))
        return remote(at, at, self.sems[0].at[h], self.sems[1].at[h], (jnp.minimum(self.me.gx + 1, 3), self.me.gy))

    def left(self, h):
        at = self.slot(jnp.minimum(self.me.gx + h, 3))
        return remote(at, at, self.sems[2].at[h], self.sems[3].at[h], (jnp.maximum(self.me.gx - 1, 0), self.me.gy))

    def from_left(self, h):
        at = self.slot(jnp.maximum(self.me.gx - 1 - h, 0))
        return remote(at, at, self.sems[0].at[h], self.sems[1].at[h], (jnp.maximum(self.me.gx - 1, 0), self.me.gy))

    def from_right(self, h):
        at = self.slot(jnp.minimum(self.me.gx + 1 + h, 3))
        return remote(at, at, self.sems[2].at[h], self.sems[3].at[h], (jnp.minimum(self.me.gx + 1, 3), self.me.gy))

    def sends(self, h):
        gx = self.me.gx
        return jnp.logical_and(gx < 3, gx >= h), jnp.logical_and(gx > 0, gx + h <= 3)

    def start(self):
        self.pass_on(0)

    def pass_on(self, h):
        go_right, go_left = self.sends(h)

        @pl.when(go_right)
        def _():
            self.right(h).start()

        @pl.when(go_left)
        def _():
            self.left(h).start()

    def receive(self, h):
        @pl.when(self.me.gx >= h + 1)
        def _():
            self.from_left(h).wait_recv()

        @pl.when(self.me.gx + h + 1 <= 3)
        def _():
            self.from_right(h).wait_recv()
        if h < 2:
            self.pass_on(h + 1)

    def drain(self):
        for h in range(3):
            go_right, go_left = self.sends(h)

            @pl.when(go_right)
            def _():
                self.right(h).wait_send()

            @pl.when(go_left)
            def _():
                self.left(h).wait_send()


def place_one(lane):
    register, unit, expert = lane // 128, lax.rem(lane // 32, 4), lax.rem(lane, 32)
    return expert // 4 * 128 + lax.rem(expert, 4) * 32 + register * 4 + unit


def place_two(lane):
    register, expert, unit = lane // 128, lax.rem(lane // 32, 4), lax.rem(lane, 32)
    return expert * 128 + register * 32 + unit


def fill_moves(one_ref, two_ref, inward):
    for ref, place in ((one_ref, place_one), (two_ref, place_two)):
        n = ref.shape[0]
        if inward:
            moved = place(lax.broadcasted_iota(jnp.int32, (n, 1), 0))
            ref[...] = (moved == lax.broadcasted_iota(jnp.int32, (n, n), 1)).astype(f32).astype(bf16)
        else:
            moved = place(lax.broadcasted_iota(jnp.int32, (1, n), 1))
            ref[...] = (moved == lax.broadcasted_iota(jnp.int32, (n, n), 0)).astype(f32).astype(bf16)


def near_buckets(rows):
    offset = (
        lax.broadcasted_iota(jnp.int32, (rows, 3 * rows), 1)
        - rows
        - lax.broadcasted_iota(jnp.int32, (rows, 3 * rows), 0)
    )
    return bucket_ids(offset)


def fill_bias(bias_ref, table_ref, chip, heads):
    rows = bias_ref.shape[1]
    span = bias_ref.shape[2]
    mid = span // 2
    buckets = near_buckets(rows)
    for h in range(heads):
        column = chip * heads + h
        near = jnp.zeros(buckets.shape, f32)
        for b in range(table_ref.shape[1]):
            near = jnp.where(buckets == b, table_ref[column, b], near)
        bias_ref[h, :, 0:mid - rows] = jnp.full((rows, mid - rows), table_ref[column, 15], f32)
        bias_ref[h, :, mid - rows:mid + 2 * rows] = near
        bias_ref[h, :, mid + 2 * rows:] = jnp.full((rows, span - mid - 2 * rows), table_ref[column, 31], f32)


def allowed_pairs(doc_row, block_at, local):
    start = pl.multiple_of(block_at * local, local)
    return as_column(doc_row[:, pl.ds(start, local)]) == doc_row[...].astype(f32)


def unit_scores(q_block, keys, bias_ref, h, block_at, allowed):
    rows = q_block.shape[0]
    seq = keys.shape[0]
    lanes = lax.broadcasted_iota(jnp.int32, q_block.shape, 1) // HSIZE
    masked = jnp.where(lanes == h, q_block, jnp.zeros_like(q_block))
    start = pl.multiple_of(seq - rows * block_at, rows)
    return jnp.where(allowed, nt(masked, keys) + bias_ref[h, :, pl.ds(start, seq)], -1000000000.0)


def fill_slots(slot_ref, choice_row, experts, capacity):
    tokens = choice_row.shape[1]
    expert = lax.broadcasted_iota(jnp.int32, (experts, 128), 0)
    upper = (lax.broadcasted_iota(jnp.int32, (128, 128), 0)
             <= lax.broadcasted_iota(jnp.int32, (128, 128), 1)).astype(f32).astype(bf16)
    before = jnp.zeros((experts, 1), f32)
    for b in range(tokens // 128):
        choice = choice_row[:, b * 128:(b + 1) * 128]
        chosen = (expert == choice).astype(f32)
        count = nn(chosen.astype(bf16), upper)
        place = jnp.sum(chosen * (count + before), axis=0, keepdims=True).astype(jnp.int32) - 1
        slot_ref[:, b * 128:(b + 1) * 128] = jnp.where(place < capacity, choice * capacity + place, -1)
        before = before + count[:, 127:128]


class BlockRows:
    def __init__(self, ref):
        self.ref = ref

    def __getitem__(self, at):
        rows = at[0]
        size = self.ref.shape[1]
        part = self.ref[rows.start // size:rows.stop // size]
        return part.reshape(rows.stop - rows.start, self.ref.shape[2])


class Dispatch:
    def __init__(self, me, out, dst, line_s, line_r, plane_s, plane_r, pair_s, pair_r):
        self.me, self.out, self.dst = me, out, dst
        self.sems = (line_s, line_r, plane_s, plane_r, pair_s, pair_r)
        self.zs = [me.gx] + me.line_from

    def line(self, k):
        at = self.dst.at[self.me.gx * 8 + self.me.gy]
        return remote(self.out.at[self.me.line[k]], at, self.sems[0].at[k], self.sems[1].at[k], self.me.on_line(k))

    def plane(self, m, k):
        at = self.dst.at[self.zs[m] * 8 + self.me.gy]
        return remote(at, at, self.sems[2].at[m, k], self.sems[3].at[m, k], self.me.on_plane(k))

    def pair(self, m, k):
        c = self.me.chip if k == 0 else self.me.chips_from[k - 1]
        at = self.dst.at[self.zs[m] * 8 + 2 * c + self.me.core]
        return remote(at, at, self.sems[4].at[m, k], self.sems[5].at[m, k], self.me.pair)

    def start(self):
        for k in range(3):
            self.line(k).start()

    def spread(self, m):
        if m > 0:
            self.line(m - 1).wait_recv()
        for k in range(3):
            self.plane(m, k).start()
        self.pair(m, 0).start()

    def share(self, m):
        for k in range(3):
            self.plane(m, k).wait_recv()
            self.pair(m, k + 1).start()

    def arrive(self):
        for m in range(4):
            for k in range(4):
                self.pair(m, k).wait_recv()

    def drain(self):
        for m in range(4):
            for k in range(4):
                self.pair(m, k).wait_send()
            for k in range(3):
                self.plane(m, k).wait_send()
        for k in range(3):
            self.line(k).wait_send()


def forward_kernel(heads, experts, capacity,
                   x_ref, gain1_ref, wq_ref, wk_ref, wv_ref, wout_ref, table_ref, wr_ref, gain2_ref, doc_row,
                   choice_row, grad_ref, wh_hbm, wb_hbm,
                   out_ref, gh_hbm, gb_hbm,
                   hidden_ref, normed_ref, router_ref, gate_ref, at_ref, q_ref, kv_ref, lse_ref, xb_ref,
                   wqkv_all, wout_all, small_all,
                   slot_ref, w1_ref, w2_ref, g_ref, g_out, rows_ref, rows_out, gs_ref,
                   own_ref, ag_ref, other_ref, xs_ref, p_ref, got_ref, other2_ref,
                   wq_st, wo_st, sm_st, at_in, y_in, s_in, line_out, line_in,
                   nat_sem, own_sem, got_sem, other_sem, t_sem, p_sem, got2_sem, other2_sem, t2_sem, gh_sem, gb_sem,
                   wqr_s, wqr_r, wql_s, wql_r, smr_s, smr_r, sml_s, sml_r,
                   xb_s, xb_r, wqp_s, wqp_r, woc_s, woc_r, wop_s, wop_r, kv_s, kv_r, at_s, at_r,
                   gz_s, gz_r, rz_s, rz_r, lo_s, lo_r, gc_s, gc_r, gp_s, gp_r, rc_s, rc_r, rp_s, rp_r,
                   yo_s, yo_r, so_s, so_r, ya_s, ya_r, yp_s, yp_r):
    me = Place()
    gx, gy, core, chip = me.gx, me.gy, me.core, me.chip
    width, cols = wq_ref.shape
    local = x_ref.shape[0]
    tokens = 32 * local
    units = wh_hbm.shape[1] // experts
    hd = 2 * cols
    seq = 8 * local
    zs = [gx] + me.line_from
    spans = units // 128
    scale = HSIZE ** (-0.5)
    half = capacity // 2
    groups = experts // GROUP
    yt_ref = other_ref

    give = Dispatch(me, g_out, g_ref, gz_s, gz_r, gc_s, gc_r, gp_s, gp_r)
    rows = Dispatch(me, rows_out, rows_ref, rz_s, rz_r, rc_s, rc_r, rp_s, rp_r)
    acts = LineSum(me, own_ref, ag_ref, other_ref, own_sem, got_sem, other_sem, t_sem, experts)
    pres = LineSum(me, p_ref, got_ref, other2_ref, p_sem, got2_sem, other2_sem, t2_sem, experts)
    weights = LineGather(me, lambda z: wq_st.at[core, z], wqr_s, wqr_r, wql_s, wql_r)
    smalls = LineGather(me, lambda z: sm_st.at[z], smr_s, smr_r, sml_s, sml_r)

    def act_step(i, carry):
        @pl.when(i < experts)
        def _():
            acts.slot_free(i)
            gs = pick_rows(slot_ref, i * capacity, capacity, BlockRows(g_ref), tokens).astype(bf16)
            gs_ref[i] = gs
            acts.put(i, nn(gs, w2_ref[i]).astype(bf16))
        acts.half(i - LAG_B)
        acts.whole(i - LAG_C)
        return carry

    done = [0]

    def act_steps(count):
        lax.fori_loop(done[0], done[0] + count, act_step, 0)
        done[0] += count

    def xb_plane(k):
        return remote(xb_ref.at[chip], xb_ref.at[chip], xb_s.at[k], xb_r.at[k], me.on_plane(k))

    def wq_pair(k):
        at = wq_st.at[core, zs[k]]
        return remote(at, at, wqp_s.at[k], wqp_r.at[k], me.pair)

    def wo_plane(k):
        return remote(wo_st.at[gy], wo_st.at[gy], woc_s.at[k], woc_r.at[k], me.on_plane(k))

    def wo_pair(k):
        c = me.chips_from[k]
        return remote(wo_st.at[2 * c + core], wo_st.at[2 * c + core], wop_s.at[k], wop_r.at[k], me.pair)

    def kv_pair(c):
        return remote(kv_ref.at[2 * c + core], kv_ref.at[2 * c + core], kv_s.at[c], kv_r.at[c], me.pair)

    def at_plane(k):
        return remote(at_ref.at[me.chips[k]], at_in.at[chip], at_s.at[k], at_r.at[k], me.on_plane(k))

    barrier = pltpu.get_barrier_semaphore()
    friends = [me.on_line(k) for k in range(3)] + [me.on_plane(k) for k in range(3)] + [me.pair]
    for device in friends:
        pl.semaphore_signal(barrier, inc=1, device_id=device, device_id_type=MESH)

    for z in range(4):
        g_out[z] = grad_ref[:, z * width:(z + 1) * width]
    xb_ref[chip] = x_ref[...]
    wq_st[core, gx] = jnp.concatenate(
        [wq_ref[...], wk_ref[...], wv_ref[...], jnp.transpose(wout_ref[...].astype(f32)).astype(bf16)], axis=1)
    sm_st[gx] = jnp.concatenate([wr_ref[...], gain2_ref[...], jnp.zeros((7, width), f32)], axis=0)
    g_ref[gx * 8 + gy] = g_out[gx]
    pl.semaphore_wait(barrier, len(friends))
    give.start()
    weights.start()
    give.spread(0)
    for k in range(3):
        xb_plane(k).start()
    wq_pair(0).start()
    smalls.start()

    def front(bias_ref, nat_ref, half_ref, one_ref, two_ref):
        def load_span(source, g, q):
            at = source.at[:, pl.ds(pl.multiple_of(g * 4096 + q * 1024, 1024), 1024)]
            return pltpu.make_async_copy(at, nat_ref.at[q], nat_sem.at[q])

        def load_spans(source, g):
            for q in range(4):
                load_span(source, g, q).start()

        def turn_span(source, target, g, following):
            lanes = pl.ds(pl.multiple_of(g * 128, 128), 128)
            for q in range(4):
                load_span(source, g, q).wait()
                moved = nn(nat_ref[q], one_ref[...]).astype(bf16)
                for r in range(8):
                    half_ref[r, :, q * 128:(q + 1) * 128] = moved[:, r * 128:(r + 1) * 128]
            following()
            for r in range(8):
                moved = nn(half_ref[r], two_ref[...]).astype(bf16)
                for n in range(4):
                    target[4 * r + n, :, lanes] = moved[:, n * 128:(n + 1) * 128]

        load_spans(wb_hbm, 0)
        fill_moves(one_ref, two_ref, True)
        fill_slots(slot_ref, choice_row, experts, capacity)
        fill_bias(bias_ref, table_ref, chip, heads)
        for m in (1, 2, 3):
            give.spread(m)
        for h in range(3):
            weights.receive(h)
            smalls.receive(h)

        def back_body(g, carry):
            def following():
                @pl.when(g + 1 < spans)
                def _():
                    load_spans(wb_hbm, g + 1)
            turn_span(wb_hbm, w2_ref, g, following)
            return carry
        lax.fori_loop(0, spans, back_body, 0)
        load_spans(wh_hbm, 0)
        for k in (1, 2, 3):
            wq_pair(k).start()
        for z in range(4):
            wo_st[gy, z] = wq_st[core, z][:, 3 * cols:]
        for k in range(3):
            wo_plane(k).start()
        for m in range(4):
            give.share(m)
        give.arrive()
        act_steps(4)
        for k in range(4):
            wq_pair(k).wait_recv()
        for z in range(4):
            parts = [wq_st[0, z], wq_st[1, z]]
            wqkv_all[z * width:(z + 1) * width, :] = jnp.concatenate(
                [parts[j][:, n * cols:(n + 1) * cols] for n in range(3) for j in range(2)], axis=1)
            wo_st[gy + 1 - 2 * core, z] = wq_st[1 - core, z][:, 3 * cols:]

        for k in range(4):
            c = chip if k == 0 else me.chips_from[k - 1]
            if k > 0:
                xb_plane(k - 1).wait_recv()
            xc = xb_ref[c].astype(f32)
            r1 = lax.rsqrt(jnp.mean(xc * xc, axis=-1, keepdims=True) + epsilon)
            xn = (xc * r1 * gain1_ref[...]).astype(bf16)
            made = nn(xn, wqkv_all[...])
            q_ref[c] = (made[:, :hd].astype(bf16).astype(f32) * scale).astype(bf16)
            kv_ref[2 * c + core] = made[:, hd:].astype(bf16)
            kv_pair(c).start()
        for k in range(3):
            wo_plane(k).wait_recv()
            wo_pair(k).start()
        act_steps(2)
        for c in range(4):
            kv_pair(c).wait_recv()
        lanes = lax.broadcasted_iota(jnp.int32, (local, hd), 1) // HSIZE
        for k in range(4):
            c = me.chips[k] if k < 3 else chip
            block_at = 2 * c + core
            allowed = allowed_pairs(doc_row, block_at, local)
            keys = kv_ref[:, :, :hd].reshape(seq, hd)
            values = kv_ref[:, :, hd:].reshape(seq, hd)
            total = jnp.zeros((local, hd), f32)
            for h in range(heads):
                scores = unit_scores(q_ref[c], keys, bias_ref, h, block_at, allowed)
                peak = jnp.max(scores, axis=-1, keepdims=True)
                shifted = jnp.exp(scores - peak)
                summed = jnp.sum(shifted, axis=-1, keepdims=True)
                lse_ref[c, h] = jnp.broadcast_to(peak + jnp.log(summed), (local, 128))
                low = (shifted * (1.0 / summed)).astype(bf16)
                total = jnp.where(lanes == h, nn(low, values), total)
            at_ref[c] = total.astype(bf16)
            if k < 3:
                at_plane(k).start()
            else:
                at_in[chip] = total.astype(bf16)
            act_steps(3)
        small_all[...] = jnp.concatenate([sm_st[z] for z in range(4)], axis=1)
        for k in range(3):
            wo_pair(k).wait_recv()
        for z in range(4):
            wout_all[z * width:(z + 1) * width, :] = jnp.concatenate([wo_st[g, z] for g in range(8)], axis=1)
        for k in range(3):
            at_plane(k).wait_recv()
        attended = jnp.concatenate([at_in[c] for c in range(4)], axis=1)
        hidden = x_ref[...].astype(f32) + nt(attended, wout_all[...]).astype(bf16).astype(f32)
        hidden_ref[...] = hidden
        r2 = lax.rsqrt(jnp.mean(hidden * hidden, axis=-1, keepdims=True) + epsilon)
        normed = hidden * r2 * small_all[experts:experts + 1, :]
        normed_ref[...] = normed
        logits = lax.dot_general(normed, small_all[:experts, :], (((1,), (1,)), ((), ())),
                                 precision=lax.Precision.HIGHEST, preferred_element_type=f32)
        lifted = jnp.exp(logits - jnp.max(logits, axis=-1, keepdims=True))
        router = lifted / jnp.sum(lifted, axis=-1, keepdims=True)
        router_ref[...] = router
        own_tokens = pl.ds(pl.multiple_of((gx * 8 + gy) * local, local), local)
        picked = as_column(choice_row[:, own_tokens]) == lax.broadcasted_iota(jnp.int32, router.shape, 1).astype(f32)
        gate = jnp.sum(jnp.where(picked, router, 0.0), axis=-1, keepdims=True)
        gate_ref[...] = gate
        first = gate.astype(bf16).astype(f32)
        second = (gate - first).astype(bf16).astype(f32)
        third = gate - first - second
        lane = lax.broadcasted_iota(jnp.int32, (local, 64), 1)
        pieces = jnp.where(lane == 0, first, jnp.where(lane == 1, second, jnp.where(lane == 2, third, 0.0)))
        pieces = pieces.astype(bf16)
        low = normed.astype(bf16)
        for z in range(4):
            rows_out[z] = jnp.concatenate([low[:, z * width:(z + 1) * width], pieces], axis=1)
        rows.start()
        rows_ref[gx * 8 + gy] = rows_out[gx]
        rows.spread(0)
        act_steps(2)
        turn_span(wh_hbm, w1_ref, 0, lambda: load_spans(wh_hbm, 1))
        for m in (1, 2, 3):
            rows.spread(m)
        act_steps(2)
        for n in range(1, spans):
            turn_span(wh_hbm, w1_ref, n, lambda: load_spans(wh_hbm, n + 1) if n + 1 < spans else None)
            act_steps(1)
        for m in range(4):
            rows.share(m)
        act_steps(1)
        rows.arrive()

    V = pltpu.VMEM
    pl.run_scoped(front, V((heads, local, 16 * local), f32), V((4, width, 1024), bf16), V((8, width, 512), bf16),
                  V((1024, 1024), bf16), V((512, 512), bf16))
    first_left = done[0]
    per_step = -(-(experts + LAG_C - first_left) // LAG_D)

    def experts_part(y_own, y_out, s_out, gh_st, gb_st):
        def grad_copy(stage, target, sems, e):
            return pltpu.make_async_copy(stage.at[lax.rem(e, 2)], target.at[e], sems.at[lax.rem(e, 2)])

        def pair_half(j):
            return remote(y_out.at[j], y_in.at[j], yo_s.at[j], yo_r.at[j], me.pair)

        def to_owner(j, k):
            return remote(s_out.at[j, me.chips[k]], s_in.at[j, k], so_s.at[j, k], so_r.at[j, k], me.on_plane(k))

        own_half = pl.ds(pl.multiple_of(core * half, 16), half)

        def from_owner(j, k):
            at = yt_ref.at[j * GROUP + chip, own_half]
            return remote(at, at, ya_s.at[j, k], ya_r.at[j, k], me.on_plane(k))

        def pair_total(j, k):
            c = chip if k == 0 else me.chips_from[k - 1]
            at = yt_ref.at[j * GROUP + c, own_half]
            return remote(at, at, yp_s.at[j, k], yp_r.at[j, k], me.pair)

        def stage_two(j):
            pair_half(j).wait_recv()
            for m in range(GROUP):
                s_out[j, m] = (y_own[j, m].astype(f32) + y_in[j, m].astype(f32)).astype(bf16)
            for k in range(3):
                to_owner(j, k).start()

        def stage_three(j):
            total = s_out[j, chip].astype(f32)
            for k in range(3):
                to_owner(j, k).wait_recv()
                total = total + s_in[j, k].astype(f32)
            yt_ref[j * GROUP + chip, own_half] = total.astype(bf16)
            for k in range(3):
                from_owner(j, k).start()
            pair_total(j, 0).start()

        def stage_four(j):
            for k in range(3):
                from_owner(j, k).wait_recv()
                pair_total(j, k + 1).start()

        def step(i, carry):
            @pl.when(i < LAG_D)
            def _():
                for n in range(per_step):
                    act_step(first_left + per_step * i + n, 0)

            @pl.when(i < experts)
            def _():
                pres.slot_free(i)
                xs = pick_rows(slot_ref, i * capacity, capacity, BlockRows(rows_ref), tokens).astype(bf16)
                xs_ref[lax.rem(i, RING)] = xs
                pres.put(i, nn(xs[:, :width], w1_ref[i]).astype(bf16))
            pres.half(i - LAG_B)
            pres.whole(i - LAG_C)
            e = i - LAG_D

            @pl.when(e >= 0)
            def _():
                acts.await_total(e)
                pres.await_total(e)
                xs = xs_ref[lax.rem(e, RING)]
                pieces = xs[:, width:].astype(f32)
                gate = pieces[:, 0:1] + pieces[:, 1:2] + pieces[:, 2:3]
                u = got_ref[e].astype(f32)
                ag = gate * ag_ref[e].astype(f32)
                u2 = u * u
                th = jnp.tanh(GELU_C * (u + 0.044715 * (u2 * u)))
                part = 0.5 * (1.0 + th)
                act = (u * part).astype(bf16)
                dg = part + 0.5 * u * (1.0 - th * th) * (GELU_C * (1.0 + 3 * 0.044715 * u2))
                pg = (ag * dg).astype(bf16)
                y = jnp.concatenate([nt(act, w2_ref[e]), nt(pg, w1_ref[e])], axis=1).astype(bf16)
                j, m = e // GROUP, lax.rem(e, GROUP)

                @pl.when(core == 0)
                def _():
                    y_own[j, m] = y[:half]
                    y_out[j, m] = y[half:]

                @pl.when(core == 1)
                def _():
                    y_own[j, m] = y[half:]
                    y_out[j, m] = y[:half]

                @pl.when(m == GROUP - 1)
                def _():
                    pair_half(j).start()

                @pl.when(e >= 2)
                def _():
                    grad_copy(gh_st, gh_hbm, gh_sem, e - 2).wait()
                    grad_copy(gb_st, gb_hbm, gb_sem, e - 2).wait()
                slot_grad = (gate * gs_ref[e].astype(f32)).astype(bf16)
                gh_st[lax.rem(e, 2)] = tn(xs[:, :width], pg).astype(bf16)
                gb_st[lax.rem(e, 2)] = tn(slot_grad, act).astype(bf16)
                grad_copy(gh_st, gh_hbm, gh_sem, e).start()
                grad_copy(gb_st, gb_hbm, gb_sem, e).start()

                @pl.when(jnp.logical_and(m == 0, j >= 1))
                def _():
                    stage_two(j - 1)

                @pl.when(jnp.logical_and(m == 2, j >= 1))
                def _():
                    stage_three(j - 1)

                @pl.when(jnp.logical_and(m == 1, j >= 2))
                def _():
                    stage_four(j - 2)
            return carry

        lax.fori_loop(0, experts + LAG_D, step, 0)
        last = groups - 1
        stage_two(last)
        stage_four(last - 1)
        slots = [as_column(slot_ref[:, pl.ds(pl.multiple_of((z * 8 + gy) * 128, 128), 128)]) for z in range(4)]
        own_slots = jnp.concatenate(slots, axis=0).astype(jnp.int32)
        many = 8
        per = many // GROUP
        places = lax.broadcasted_iota(jnp.int32, (own_slots.shape[0], many * capacity), 1)

        def picked(b):
            hot = (own_slots == places + b * many * capacity).astype(f32).astype(bf16)
            return nn(hot, yt_ref[b * many:(b + 1) * many].reshape(many * capacity, 2 * width))

        total = None
        for b in range(experts // many - 1):
            for j in range(b * per, (b + 1) * per):
                for k in range(4):
                    pair_total(j, k).wait_recv()
            if b == 0:
                stage_three(last)
            part = picked(b)
            total = part if total is None else total + part
        stage_four(last)
        for j in range(groups - per, groups):
            for k in range(4):
                pair_total(j, k).wait_recv()
        total = total + picked(experts // many - 1)

        def line_copy(k):
            return remote(line_out.at[me.line[k]], line_in.at[k], lo_s.at[k], lo_r.at[k], me.on_line(k))

        for z in range(4):
            line_out[z] = total[z * local:(z + 1) * local].astype(bf16)
        for k in range(3):
            line_copy(k).start()
        out_ref[gx] = line_out[gx].astype(f32)
        acts.drain()
        pres.drain()
        for e in (experts - 2, experts - 1):
            grad_copy(gh_st, gh_hbm, gh_sem, e).wait()
            grad_copy(gb_st, gb_hbm, gb_sem, e).wait()

        def sent(j, carry):
            pair_half(j).wait_send()
            for k in range(3):
                to_owner(j, k).wait_send()
                from_owner(j, k).wait_send()
            for k in range(4):
                pair_total(j, k).wait_send()
            return carry
        lax.fori_loop(0, groups, sent, 0)
        give.drain()
        rows.drain()
        weights.drain()
        smalls.drain()
        for k in range(3):
            for copy in (xb_plane, wo_plane, wo_pair, at_plane):
                copy(k).wait_send()
        for k in range(4):
            for copy in (wq_pair, kv_pair):
                copy(k).wait_send()
        for k in range(3):
            line_copy(k).wait_recv()
            out_ref[me.line_from[k]] = line_in[k].astype(f32)
        for k in range(3):
            line_copy(k).wait_send()

    block = (groups, GROUP, half, 2 * width)
    pl.run_scoped(experts_part, V(block, bf16), V(block, bf16), V(block, bf16),
                  V((2, width, units), bf16), V((2, width, units), bf16))


def forward_pass(x_in, gain1, wq, wk, wv, wout, table, wr, gain2, doc_row, choice_row, grad_out, w_hidden, w_back,
                 collective_id):
    local, features = x_in.shape
    width, cols = wq.shape
    hd = 2 * cols
    heads = hd // HSIZE
    experts = wr.shape[0]
    tokens = choice_row.shape[1]
    capacity = tokens * 5 // (4 * experts)
    units = w_hidden.shape[1] // experts
    half = capacity // 2
    groups = experts // GROUP
    vm = pl.BlockSpec(memory_space=pltpu.VMEM)
    sm = pl.BlockSpec(memory_space=pltpu.SMEM)
    hbm = pl.BlockSpec(memory_space=pl.ANY)
    dma = pltpu.SemaphoreType.DMA
    shape = jax.ShapeDtypeStruct
    V = pltpu.VMEM
    ring = 8
    return pl.pallas_call(
        functools.partial(forward_kernel, heads, experts, capacity),
        out_shape=(
            shape((4, local, 2 * width), f32),
            shape((experts, width, units), bf16),
            shape((experts, width, units), bf16),
            shape((local, features), f32),
            shape((local, features), f32),
            shape((local, experts), f32),
            shape((local, 1), f32),
            shape((4, local, hd), bf16),
            shape((4, local, hd), bf16),
            shape((8, local, 2 * hd), bf16),
            shape((4, heads, local, 128), f32),
            shape((4, local, features), bf16),
            shape((features, 3 * hd), bf16),
            shape((features, features), bf16),
            shape((experts + 8, features), f32),
        ),
        in_specs=[vm] * 6 + [sm] + [vm] * 5 + [hbm] * 2,
        out_specs=(vm, hbm, hbm) + (vm,) * 12,
        scratch_shapes=[
            V((1, tokens), jnp.int32),
            V((experts, width, units), bf16), V((experts, width, units), bf16),
            V((32, local, width), bf16), V((4, local, width), bf16),
            V((32, local, width + 64), bf16), V((4, local, width + 64), bf16),
            V((experts, capacity, width), bf16),
            V((ring, capacity, units), bf16), V((experts, capacity, units), bf16), V((experts, capacity, units), bf16),
            V((RING, capacity, width + 64), bf16),
            V((RING, capacity, units), bf16), V((experts, capacity, units), bf16), V((experts, capacity, units), bf16),
            V((2, 4, width, 4 * cols), bf16), V((8, 4, width, cols), bf16), V((4, experts + 8, width), f32),
            V((4, local, hd), bf16),
            V((groups, GROUP, half, 2 * width), bf16), V((groups, 3, half, 2 * width), bf16),
            V((4, local, 2 * width), bf16), V((3, local, 2 * width), bf16),
        ] + [dma((n,)) for n in (4, ring, experts, experts, experts, RING, experts, experts, experts, 2, 2)]
        + [dma((3,))] * 8
        + [dma((n,)) for n in (3, 3, 4, 4, 3, 3, 3, 3, 4, 4, 3, 3, 3, 3, 3, 3, 3, 3)]
        + [dma((4, 3)), dma((4, 3)), dma((4, 4)), dma((4, 4))] * 2
        + [dma((groups,)), dma((groups,)), dma((groups, 3)), dma((groups, 3)), dma((groups, 3)), dma((groups, 3)),
           dma((groups, 4)), dma((groups, 4))],
        compiler_params=pltpu.CompilerParams(
            collective_id=collective_id, has_side_effects=True, vmem_limit_bytes=64 * 2**20),
        cost_estimate=pl.CostEstimate(flops=25 * 10**9, bytes_accessed=50 * 10**6, transcendentals=4 * 10**6),
    )(x_in, gain1, wq, wk, wv, wout, table, wr, gain2, doc_row, choice_row, grad_out, w_hidden, w_back)


HIGH = lax.Precision.HIGHEST


def back_kernel(heads, experts,
                x_ref, gain1_ref, grad_ref, choice_row, doc_row, table_ref,
                hidden_ref, normed_ref, router_ref, gate_ref, at_ref, q_ref, kv_ref, lse_ref, xb_ref,
                wqkv_all, wout_all, small_all, ret_ref, gh_hbm, gb_hbm,
                out_ref, gin_ref, wgrad_ref, small_out, tail_out, nh_hbm, nb_hbm,
                bias_ref, ag_ref, dq_ref, dk_ref, dv_ref, near_ref, go_ref, fg_ref, top_ref,
                one_ref, two_ref, in_ref, half_ref, nat_ref,
                sp_out, sp_in, sc_out, sc_in, sz_out, sz_in,
                kv_out, kv_in, kv_sum, fg_out, fg_in, wp_out, wp_in, wz_out, wz_in,
                tp_out, tp_in, tc_out, tc_in, tz_out, tz_in,
                in_sem, nat_sem,
                ag_s, ag_r, sp_s, sp_r, sc_s, sc_r, sz_s, sz_r, kv_s, kv_r, fg_s, fg_r, wp_s, wp_r,
                tp_s, tp_r, tc_s, tc_r, tz_s, tz_r, wz_s, wz_r):
    me = Place()
    gx, gy, core, chip = me.gx, me.gy, me.core, me.chip
    local, features = x_ref.shape
    width = features // 4
    hd = q_ref.shape[2]
    cols = hd // 2
    seq = 8 * local
    spans = gh_hbm.shape[2] // 128

    barrier = pltpu.get_barrier_semaphore()
    friends = [me.on_line(k) for k in range(3)] + [me.on_plane(k) for k in range(3)] + [me.pair]
    for device in friends:
        pl.semaphore_signal(barrier, inc=1, device_id=device, device_id_type=MESH)

    work = [(gh_hbm, nh_hbm, g) for g in range(spans)] + [(gb_hbm, nb_hbm, g) for g in range(spans)]

    def load(i):
        at = work[i][0].at[:, :, work[i][2] * 128:(work[i][2] + 1) * 128]
        return pltpu.make_async_copy(at, in_ref, in_sem.at[0])

    def store(i, q):
        at = work[i][1].at[:, work[i][2] * 4096 + q * 1024:work[i][2] * 4096 + (q + 1) * 1024]
        return pltpu.make_async_copy(nat_ref.at[q], at, nat_sem.at[q])

    def turn_span(i):
        load(i).wait()
        for r in range(8):
            block = jnp.concatenate([in_ref[4 * r + n] for n in range(4)], axis=1)
            moved = nn(block, two_ref[...]).astype(bf16)
            for q in range(4):
                half_ref[q, :, r * 128:(r + 1) * 128] = moved[:, q * 128:(q + 1) * 128]
        if i + 1 < len(work):
            load(i + 1).start()
        for q in range(4):
            if i > 0:
                store(i - 1, q).wait()
            nat_ref[q] = nn(half_ref[q], one_ref[...]).astype(bf16)
            store(i, q).start()

    load(0).start()
    hidden = hidden_ref[...]
    r2 = lax.rsqrt(jnp.mean(hidden * hidden, axis=-1, keepdims=True) + epsilon)
    grads = grad_ref[...].astype(f32)
    gate = gate_ref[...]
    routed = jnp.concatenate([ret_ref[z][:, :width] for z in range(4)], axis=1)
    back = jnp.concatenate([ret_ref[z][:, width:] for z in range(4)], axis=1)
    out_ref[...] = hidden + gate * routed
    gate_grad = jnp.sum(grads * routed, axis=-1, keepdims=True)
    router = router_ref[...]
    own_tokens = pl.ds(pl.multiple_of((gx * 8 + gy) * local, local), local)
    picked = (as_column(choice_row[:, own_tokens])
              == lax.broadcasted_iota(jnp.int32, router.shape, 1).astype(f32)).astype(f32)
    logit_grad = router * (gate_grad * picked - gate * gate_grad)
    second = back + jnp.dot(logit_grad, small_all[:experts, :], precision=HIGH, preferred_element_type=f32)
    gained = second * small_all[experts:experts + 1, :]
    dot2 = jnp.sum(gained * hidden, axis=-1, keepdims=True)
    hidden_grad = grads + r2 * gained - hidden * (r2 * r2 * r2) * (dot2 / features)
    gin_ref[...] = hidden_grad
    ag_ref[chip] = hidden_grad.astype(bf16)
    pl.semaphore_wait(barrier, len(friends))

    def ag_plane(k):
        return remote(ag_ref.at[chip], ag_ref.at[chip], ag_s.at[k], ag_r.at[k], me.on_plane(k))

    for k in range(3):
        ag_plane(k).start()

    routed_grad = lax.dot_general(logit_grad, normed_ref[...], (((0,), (0,)), ((), ())), precision=HIGH,
                                  preferred_element_type=f32)
    norm2 = jnp.sum(second * hidden * r2, axis=0, keepdims=True)
    sp_out[...] = jnp.concatenate([routed_grad, norm2, jnp.zeros((7, features), f32)], axis=0)
    small_pair = remote(sp_out, sp_in, sp_s.at[0], sp_r.at[0], me.pair)
    small_pair.start()

    def small_plane(k):
        return remote(sc_out, sc_in.at[k], sc_s.at[k], sc_r.at[k], me.on_plane(k))

    def small_line(k):
        return remote(sz_out.at[me.line[k]], sz_in.at[k], sz_s.at[k], sz_r.at[k], me.on_line(k))

    fill_bias(bias_ref, table_ref, chip, heads)
    dk_ref[...] = jnp.zeros_like(dk_ref)
    dv_ref[...] = jnp.zeros_like(dv_ref)
    near_ref[...] = jnp.zeros_like(near_ref)
    scale = HSIZE ** (-0.5)
    lanes = lax.broadcasted_iota(jnp.int32, (local, hd), 1) // HSIZE

    def attend_block(c, fresh):
        block_at = 2 * c + core
        allowed = allowed_pairs(doc_row, block_at, local)
        keys = kv_ref[:, :, :hd].reshape(seq, hd)
        values = kv_ref[:, :, hd:].reshape(seq, hd)
        att_grad = nn(ag_ref[c], wout_own).astype(bf16)
        part_o = tn(at_ref[c], ag_ref[c])
        go_ref[...] = part_o if fresh else go_ref[...] + part_o
        q_block = q_ref[c]
        q_turn = jnp.transpose(q_block.astype(f32)).astype(bf16)
        g_turn = jnp.transpose(att_grad.astype(f32)).astype(bf16)
        dq = jnp.zeros((local, hd), f32)
        for h in range(heads):
            scores = unit_scores(q_block, keys, bias_ref, h, block_at, allowed)
            probs = jnp.exp(scores - lse_ref[c, h][:, :1])
            masked = jnp.where(lanes == h, att_grad, jnp.zeros_like(att_grad))
            prob_grad = nt(masked, values)
            weighted = probs * prob_grad
            score_grad = (weighted - probs * jnp.sum(weighted, axis=-1, keepdims=True)).astype(bf16)
            part = slice(h * HSIZE, (h + 1) * HSIZE)
            dv_ref[part, :] += nn(g_turn[part, :], probs.astype(bf16))
            dk_ref[part, :] += nn(q_turn[part, :], score_grad)
            dq = jnp.where(lanes == h, nn(score_grad, keys), dq)
            start = pl.multiple_of(seq - local * block_at, local)
            near_ref[h, :, pl.ds(start, seq)] += score_grad.astype(f32)
        dq_ref[c] = (dq * scale).astype(bf16)

    own_pieces = [wout_all[:, n * hd:(n + 1) * hd] for n in range(4)]
    wout_own = own_pieces[3]
    for n in range(3):
        wout_own = jnp.where(chip == n, own_pieces[n], wout_own)

    attend_block(chip, True)
    small_pair.wait_recv()
    sc_out[...] = sp_out[...] + sp_in[...]
    for k in range(3):
        small_plane(k).start()
    fill_moves(one_ref, two_ref, False)
    for k in range(3):
        ag_plane(k).wait_recv()
        attend_block(me.chips_from[k], False)
        if k == 0:
            total = sc_out[...]
            for j in range(3):
                small_plane(j).wait_recv()
                total = total + sc_in[j]
            for z in range(4):
                sz_out[z] = total[:, z * width:(z + 1) * width]
            for j in range(3):
                small_line(j).start()

    both = jnp.concatenate([dk_ref[...], dv_ref[...]], axis=0)
    for j in range(8):
        turned = jnp.transpose(both[:, j * local:(j + 1) * local])

        @pl.when(core == j % 2)
        def _():
            kv_sum[j // 2] = turned

        @pl.when(core != j % 2)
        def _():
            kv_out[j // 2] = turned.astype(bf16)
    kv_pair = remote(kv_out, kv_in, kv_s.at[0], kv_r.at[0], me.pair)
    kv_pair.start()

    def xn_block(c):
        xc = xb_ref[c].astype(f32)
        return xc * lax.rsqrt(jnp.mean(xc * xc, axis=-1, keepdims=True) + epsilon)

    xr = [xn_block(c) for c in range(4)]
    xn = jnp.concatenate([(v * gain1_ref[...]).astype(bf16) for v in xr], axis=0)

    def packed(value, z):
        top, mid, bottom = z * width, z * width + width // 2, (z + 1) * width
        return jnp.concatenate([value[top:mid], value[mid:bottom]], axis=1)

    def w_pair(p):
        return remote(wp_out.at[p], wp_in.at[p], wp_s.at[p], wp_r.at[p], me.pair)

    def w_line(p, k):
        return remote(wz_out.at[p, me.line[k]], wz_in.at[p, k], wz_s.at[p, k], wz_r.at[p, k], me.on_line(k))

    def weight_part(p, a, b):
        halves = [jnp.concatenate([a[:, j * cols:(j + 1) * cols], b[:, j * cols:(j + 1) * cols]], axis=1)
                  for j in range(2)]
        other = jnp.where(core == 0, halves[1], halves[0]).astype(bf16)
        own = jnp.where(core == 0, halves[0], halves[1])
        for z in range(4):
            wp_out[p, z] = packed(other, z)
        w_pair(p).start()
        return own

    def weight_line(p, own):
        w_pair(p).wait_recv()
        for z in range(4):
            wz_out[p, z] = (packed(own, z) + wp_in[p, z].astype(f32)).astype(bf16)
        for k in range(3):
            w_line(p, k).start()

    queries = jnp.concatenate([dq_ref[c] for c in range(4)], axis=0)
    own_0 = weight_part(0, tn(xn, queries), jnp.transpose(go_ref[...]))
    kv_pair.wait_recv()
    keyval = [(kv_sum[c] + kv_in[c].astype(f32)).astype(bf16) for c in range(4)]

    def fg_plane(k):
        return remote(fg_out.at[me.chips[k]], fg_in.at[k], fg_s.at[k], fg_r.at[k], me.on_plane(k))

    norm1 = jnp.zeros((1, features), f32)
    for k in range(4):
        c = me.chips[k] if k < 3 else chip
        both = jnp.concatenate([dq_ref[c], (kv_sum[c] + kv_in[c].astype(f32)).astype(bf16)], axis=1)
        part = nt(both, wqkv_all[...])
        xc = xb_ref[c].astype(f32)
        r1 = lax.rsqrt(jnp.mean(xc * xc, axis=-1, keepdims=True) + epsilon)
        norm1 = norm1 + jnp.sum(part * (xc * r1), axis=0, keepdims=True)
        if k < 3:
            fg_out[c] = part.astype(bf16)
            fg_plane(k).start()
        else:
            fg_ref[...] = part
    weight_line(0, own_0)

    buckets = near_buckets(local)
    table = jnp.zeros((experts, 128), f32)
    lane = lax.broadcasted_iota(jnp.int32, (experts, 128), 1)
    row = lax.broadcasted_iota(jnp.int32, (experts, 1), 0)
    for h in range(heads):
        close = near_ref[h, :, seq - local:seq + 2 * local]
        for b in range(experts):
            top_ref[b:b + 1, :] = jnp.sum(jnp.where(buckets == b, close, 0.0), axis=0, keepdims=True)
        column = jnp.sum(top_ref[...], axis=1, keepdims=True)
        left = jnp.sum(near_ref[h, :, :seq - local])
        right = jnp.sum(near_ref[h, :, seq + 2 * local:])
        column = column + jnp.where(row == 15, left, 0.0) + jnp.where(row == 31, right, 0.0)
        table = jnp.where(lane == chip * heads + h, column, table)

    tp_out[...] = jnp.concatenate(
        [table] + [norm1[:, n * 128:(n + 1) * 128] for n in range(6)] + [jnp.zeros((2, 128), f32)], axis=0)
    t_pair = remote(tp_out, tp_in, tp_s.at[0], tp_r.at[0], me.pair)
    t_pair.start()

    def t_plane(k):
        return remote(tc_out, tc_in.at[k], tc_s.at[k], tc_r.at[k], me.on_plane(k))

    def t_line(k):
        return remote(tz_out, tz_in.at[k], tz_s.at[k], tz_r.at[k], me.on_line(k))

    keyvals = jnp.concatenate(keyval, axis=0)
    grads_kv = tn(xn, keyvals)
    own_1 = weight_part(1, grads_kv[:, :hd], grads_kv[:, hd:])
    t_pair.wait_recv()
    tc_out[...] = tp_out[...] + tp_in[...]
    for k in range(3):
        t_plane(k).start()
    weight_line(1, own_1)
    turn_span(0)
    turn_span(1)
    for k in range(3):
        t_plane(k).wait_recv()
    tail = jnp.zeros((40, 128), f32)
    for c in range(4):
        part = jnp.where(chip == c, tc_out[...], 0.0)
        for k in range(3):
            part = jnp.where(me.chips_from[k] == c, tc_in[k], part)
        tail = tail + part
    tz_out[...] = tail
    for k in range(3):
        t_line(k).start()
    turn_span(2)
    turn_span(3)

    first = fg_ref[...]
    for k in range(3):
        fg_plane(k).wait_recv()
        first = first + fg_in[k].astype(f32)
    x = x_ref[...].astype(f32)
    r1 = lax.rsqrt(jnp.mean(x * x, axis=-1, keepdims=True) + epsilon)
    gained1 = first * gain1_ref[...]
    dot1 = jnp.sum(gained1 * x, axis=-1, keepdims=True)
    gin_ref[...] = gin_ref[...] + r1 * gained1 - x * (r1 * r1 * r1) * (dot1 / features)

    total = sz_out[gx]
    for k in range(3):
        small_line(k).wait_recv()
        total = total + sz_in[k]
    small_out[...] = total
    turn_span(4)
    turn_span(5)
    for p in range(2):
        total = wz_out[p, gx].astype(f32)
        for k in range(3):
            w_line(p, k).wait_recv()
            total = total + wz_in[p, k].astype(f32)
        wgrad_ref[p] = total
    for k in range(3):
        t_line(k).wait_recv()
    tail = jnp.zeros((40, 128), f32)
    for z in range(4):
        part = jnp.where(gx == z, tz_out[...], 0.0)
        for k in range(3):
            part = jnp.where(me.line_from[k] == z, tz_in[k], part)
        tail = tail + part
    tail_out[...] = tail
    for q in range(4):
        store(len(work) - 1, q).wait()
    for copy in (small_pair, kv_pair, t_pair):
        copy.wait_send()
    for p in range(2):
        w_pair(p).wait_send()
        for k in range(3):
            w_line(p, k).wait_send()
    for k in range(3):
        for copy in (ag_plane, small_plane, small_line, fg_plane, t_plane, t_line):
            copy(k).wait_send()


def back_pass(x_in, gain1, grad_out, choice_row, doc_row, table, saved, returned, gh, gb, collective_id):
    local, features = x_in.shape
    width = features // 4
    hidden, normed, router, gate, attended, queries, keyvals, lse, xb, wqkv, wout, small = saved
    experts, _, units = gh.shape
    hd = queries.shape[2]
    cols = hd // 2
    heads = hd // HSIZE
    seq = 8 * local
    rows = small.shape[0]
    vm = pl.BlockSpec(memory_space=pltpu.VMEM)
    sm = pl.BlockSpec(memory_space=pltpu.SMEM)
    hbm = pl.BlockSpec(memory_space=pl.ANY)
    dma = pltpu.SemaphoreType.DMA
    shape = jax.ShapeDtypeStruct
    V = pltpu.VMEM
    return pl.pallas_call(
        functools.partial(back_kernel, heads, experts),
        out_shape=(
            shape((local, features), f32),
            shape((local, features), f32),
            shape((2, width // 2, 4 * cols), f32),
            shape((rows, width), f32),
            shape((40, 128), f32),
            shape((width, experts * units), bf16),
            shape((width, experts * units), bf16),
        ),
        in_specs=[vm] * 5 + [sm] + [vm] * 13 + [hbm] * 2,
        out_specs=(vm,) * 5 + (hbm,) * 2,
        scratch_shapes=[
            V((heads, local, 16 * local), f32),
            V((4, local, features), bf16), V((4, local, hd), bf16), V((hd, seq), f32), V((hd, seq), f32),
            V((heads, local, 2 * seq), f32), V((hd, features), f32), V((local, features), f32),
            V((experts, 3 * local), f32),
            V((1024, 1024), bf16), V((512, 512), bf16), V((experts, width, 128), bf16), V((4, width, 1024), bf16),
            V((4, width, 1024), bf16),
            V((rows, features), f32), V((rows, features), f32), V((rows, features), f32), V((3, rows, features), f32),
            V((4, rows, width), f32), V((3, rows, width), f32),
            V((4, local, 2 * hd), bf16), V((4, local, 2 * hd), bf16), V((4, local, 2 * hd), f32),
            V((4, local, features), bf16), V((3, local, features), bf16),
            V((2, 4, width // 2, 4 * cols), bf16), V((2, 4, width // 2, 4 * cols), bf16),
            V((2, 4, width // 2, 4 * cols), bf16), V((2, 3, width // 2, 4 * cols), bf16),
            V((40, 128), f32), V((40, 128), f32), V((40, 128), f32), V((3, 40, 128), f32),
            V((40, 128), f32), V((3, 40, 128), f32),
        ] + [dma((n,)) for n in (1, 4, 3, 3, 1, 1, 3, 3, 3, 3, 1, 1, 3, 3, 2, 2, 1, 1, 3, 3, 3, 3)]
        + [dma((2, 3)), dma((2, 3))],
        compiler_params=pltpu.CompilerParams(
            collective_id=collective_id, has_side_effects=True, vmem_limit_bytes=62 * 2**20),
        cost_estimate=pl.CostEstimate(flops=20 * 10**9, bytes_accessed=40 * 10**6, transcendentals=2 * 10**6),
    )(x_in, gain1, grad_out, choice_row, doc_row, table, hidden, normed, router, gate, attended, queries, keyvals, lse,
      xb, wqkv, wout, small, returned, gh, gb)


def finish_kernel(heads, experts,
                  out_ref, gin_ref, wgrad_ref, small_ref, tail_ref, nh_hbm, nb_hbm,
                  out_to, gin_to, norm1_to, query_to, key_to, value_to, table_to, proj_to, norm2_to, router_to,
                  hidden_to, back_to,
                  in_ref, nat_ref, in_sem, nat_sem):
    width, cols = query_to.shape
    span = in_ref.shape[2]
    count = nh_hbm.shape[1] // span
    work = [(nh_hbm, hidden_to, g) for g in range(count)] + [(nb_hbm, back_to, g) for g in range(count)]
    ring = in_ref.shape[0]

    def load(i):
        source, _, g = work[i]
        return pltpu.make_async_copy(source.at[:, g * span:(g + 1) * span], in_ref.at[i % ring], in_sem.at[i % ring])

    def store(i):
        _, target, g = work[i]
        return pltpu.make_async_copy(nat_ref.at[i % ring], target.at[:, g * span:(g + 1) * span], nat_sem.at[i % ring])

    for i in range(ring):
        load(i).start()
    out_to[...] = out_ref[...]
    gin_to[...] = gin_ref[...]
    for n in range(6):
        norm1_to[:, n * 128:(n + 1) * 128] = tail_ref[experts + n:experts + n + 1, :]
    parts = []
    for p in range(2):
        rows = wgrad_ref[p]
        parts.append(jnp.concatenate([rows[:, :2 * cols], rows[:, 2 * cols:]], axis=0))
    query_to[...] = parts[0][:, :cols]
    proj_to[...] = jnp.transpose(parts[0])[cols:]
    key_to[...] = parts[1][:, :cols]
    value_to[...] = parts[1][:, cols:]
    table_to[...] = jnp.transpose(jnp.concatenate([tail_ref[:experts, :], jnp.zeros((128 - experts, 128), f32)], axis=0)
                                  )[:heads, :experts]
    norm2_to[...] = small_ref[experts:experts + 1, :]
    router_to[...] = small_ref[:experts, :]
    for i in range(len(work)):
        load(i).wait()
        if i >= ring:
            store(i - ring).wait()
        nat_ref[i % ring] = in_ref[i % ring].astype(f32)
        store(i).start()
        if i + ring < len(work):
            load(i + ring).start()
    for i in range(len(work) - ring, len(work)):
        store(i).wait()


def finish(out_rows, gin, wgrad, small, tail, nh, nb, heads):
    width, natural = nh.shape
    local, features = out_rows.shape
    cols = wgrad.shape[2] // 4
    experts = EXPERTS
    vm = pl.BlockSpec(memory_space=pltpu.VMEM)
    hbm = pl.BlockSpec(memory_space=pl.ANY)
    dma = pltpu.SemaphoreType.DMA
    shape = lambda *dims: jax.ShapeDtypeStruct(dims, f32)
    V = pltpu.VMEM
    ring, span = 4, 2048
    return pl.pallas_call(
        functools.partial(finish_kernel, heads, experts),
        out_shape=(
            shape(local, features), shape(local, features), shape(1, features),
            shape(width, cols), shape(width, cols), shape(width, cols), shape(heads, experts), shape(cols, width),
            shape(1, width), shape(experts, width), shape(width, natural), shape(width, natural),
        ),
        in_specs=[vm] * 5 + [hbm] * 2,
        out_specs=(vm,) * 10 + (hbm,) * 2,
        scratch_shapes=[V((ring, width, span), bf16), V((ring, width, span), f32), dma((ring,)), dma((ring,))],
        compiler_params=pltpu.CompilerParams(vmem_limit_bytes=63 * 2**20),
        cost_estimate=pl.CostEstimate(flops=10**7, bytes_accessed=30 * 10**6, transcendentals=0),
    )(out_rows, gin, wgrad, small, tail, nh, nb)


def fits(mesh):
    return mesh.shape["gx"] == 4 and mesh.shape["gy"] == 8


def fast(
    x_in,
    norm1_gain,
    w_query,
    w_key,
    w_value,
    relative_bias_table,
    w_out,
    norm2_gain,
    w_router,
    w_hidden,
    w_back,
    expert_choice,
    doc_ids,
    grad_out,
):
    gain_row = norm1_gain[None, :]
    choice_row, doc_row = expert_choice[None, :], doc_ids[None, :]
    table = relative_bias_table.T
    returned, hidden_grads, back_grads, *saved = forward_pass(
        x_in,
        gain_row,
        w_query,
        w_key,
        w_value,
        w_out,
        table,
        w_router.T,
        norm2_gain[None, :],
        doc_row,
        choice_row,
        grad_out,
        w_hidden,
        w_back,
        1,
    )
    results = back_pass(
        x_in,
        gain_row,
        grad_out,
        choice_row,
        doc_row,
        table,
        saved,
        returned,
        hidden_grads,
        back_grads,
        2,
    )
    (
        out_rows,
        input_rows,
        grad_norm1,
        grad_query,
        grad_key,
        grad_value,
        grad_table,
        grad_out_proj,
        grad_norm2,
        grad_router,
        grad_hidden,
        grad_back,
    ) = finish(*results, table.shape[0])
    return (
        out_rows,
        input_rows,
        grad_norm1[0],
        grad_query,
        grad_key,
        grad_value,
        grad_table.T,
        grad_out_proj,
        grad_norm2[0],
        grad_router.T,
        grad_hidden,
        grad_back,
    )


def solution(mesh):
    return jax.shard_map(
        fast if fits(mesh) else local,
        mesh=mesh,
        in_specs=(
            P(("gx", "gy"), None),
            P(),
            P("gx", "gy"),
            P("gx", "gy"),
            P("gx", "gy"),
            P(),
            P("gy", "gx"),
            P("gx"),
            P("gx", None),
            P("gx", "gy"),
            P("gx", "gy"),
            P(),
            P("gx"),
            P(("gx", "gy"), None),
        ),
        out_specs=(
            P(("gx", "gy"), None),
            P(("gx", "gy"), None),
            P(),
            P("gx", "gy"),
            P("gx", "gy"),
            P("gx", "gy"),
            P(),
            P("gy", "gx"),
            P("gx"),
            P("gx", None),
            P("gx", "gy"),
            P("gx", "gy"),
        ),
        check_vma=False,
    )
```

```python
import functools
import math

import jax
import jax.numpy as jnp
from jax import lax
from jax.experimental import pallas as pl
from jax.experimental.pallas import tpu as pltpu
from jax.sharding import PartitionSpec as P

D = 768
HEADS = 12
HSIZE = 64
EXPERTS = 32
WINDOW = 1024


epsilon = 1e-06
far_steps = (12, 16, 23, 32, 46, 64, 91)
highest = lax.Precision.HIGHEST


def passed_along(value, axis, steps):
    count = lax.axis_size(axis)
    first, last = (max(0, -steps), min(count, count - steps))
    return lax.ppermute(value, axis, [(source, source + steps) for source in range(first, last)])


def bucket_ids(offset):
    ahead_part = (offset > 0).astype(jnp.int32) * 16
    distance = jnp.abs(offset)
    far_part = 8 + sum(((distance >= threshold).astype(jnp.int32) for threshold in far_steps))
    return ahead_part + jnp.where(distance < 8, distance, far_part)


def width_total(values):
    return lax.psum(values, "gx")


def token_rows(block_part):
    return lax.all_gather(block_part, "gy", axis=0, tiled=True)


def width_rows(block_part):
    return lax.all_gather(block_part, "gx", axis=0, tiled=True)


def width_sums(term_fn, row_number):
    return lax.psum_scatter(
        term_fn(jnp.int32(0), lax.axis_size("gx") * row_number),
        "gx",
        scatter_dimension=0,
        tiled=True,
    )


def token_sums(term_fn, row_number):
    return lax.psum_scatter(
        term_fn(jnp.int32(0), lax.axis_size("gy") * row_number),
        "gy",
        scatter_dimension=0,
        tiled=True,
    )


def collect_window(own_pair, reach):
    window_parts = []
    for offset_step in range(-reach, reach + 1):
        if offset_step == 0:
            window_parts.append(own_pair)
        else:
            window_parts.append(passed_along(own_pair, "gy", -offset_step))
    return jnp.concatenate(window_parts, axis=0)


def return_window(partials, reach, head_rows):
    combined = partials[reach * head_rows : (reach + 1) * head_rows]
    for offset_step in range(-reach, reach + 1):
        if offset_step != 0:
            start = (offset_step + reach) * head_rows
            combined = combined + passed_along(
                partials[start : start + head_rows], "gy", offset_step
            )
    return combined


def head_scores(query_heads, key_heads, bias_terms, allowed, score_scale):
    raw_scores = jnp.einsum(
        "qhd,khd->hqk", query_heads, key_heads, preferred_element_type=jnp.float32
    )
    return jnp.where(allowed[None], raw_scores * score_scale + bias_terms, -1000000000.0)


def rows_cols(blocks, width_devs, token_devs):
    grid = blocks.reshape(width_devs, token_devs, blocks.shape[1], blocks.shape[2])
    return jnp.transpose(grid, (0, 2, 1, 3)).reshape(
        width_devs * blocks.shape[1], token_devs * blocks.shape[2]
    )


def cols_rows(blocks, width_devs, token_devs):
    grid = blocks.reshape(width_devs, token_devs, blocks.shape[1], blocks.shape[2])
    return jnp.transpose(grid, (1, 2, 0, 3)).reshape(
        token_devs * blocks.shape[1], width_devs * blocks.shape[2]
    )


def grid_rows_cols(complete, width_devs, token_devs):
    row_total, col_total = complete.shape
    grid = complete.reshape(
        width_devs, row_total // width_devs, token_devs, col_total // token_devs
    )
    return jnp.transpose(grid, (0, 2, 1, 3)).reshape(
        width_devs * token_devs, row_total // width_devs, col_total // token_devs
    )


def grid_cols_rows(complete, width_devs, token_devs):
    row_total, col_total = complete.shape
    grid = complete.reshape(
        token_devs, row_total // token_devs, width_devs, col_total // width_devs
    )
    return jnp.transpose(grid, (2, 0, 1, 3)).reshape(
        width_devs * token_devs, row_total // token_devs, col_total // width_devs
    )


def spread_rows(partial_sum, column, group_count):
    picked_row = (jnp.arange(group_count, dtype=jnp.int32) == column).astype(jnp.float32)
    return picked_row.reshape((group_count,) + (1,) * partial_sum.ndim) * partial_sum[None]


def take_rows(table, index):
    return jnp.take(table, index, axis=0, mode="fill", fill_value=0)


def local(
    x_in,
    norm1_gain,
    w_query,
    w_key,
    w_value,
    relative_bias_table,
    w_out,
    norm2_gain,
    w_router,
    w_hidden,
    w_back,
    expert_choice,
    doc_ids,
    grad_out,
):
    token_devs = lax.axis_size("gy")
    width_devs = lax.axis_size("gx")
    member = lax.axis_index("gy")
    column = lax.axis_index("gx")
    local_count = x_in.shape[0]
    width_cols = w_router.shape[0]
    own_rows = local_count * width_devs
    all_tokens = own_rows * token_devs
    seq_len = local_count * token_devs
    experts = EXPERTS
    capacity = all_tokens * 5 // (4 * experts)
    score_scale = HSIZE ** (-0.5)
    reach = min((WINDOW + local_count - 2) // local_count, token_devs - 1)
    key_count = (2 * reach + 1) * local_count
    whole_weights = (
        lax.all_gather(w_query[None], ("gx", "gy"), axis=0, tiled=True),
        lax.all_gather(w_key[None], ("gx", "gy"), axis=0, tiled=True),
        lax.all_gather(w_value[None], ("gx", "gy"), axis=0, tiled=True),
        lax.all_gather(w_out[None], ("gx", "gy"), axis=0, tiled=True),
    )
    qkv_full = jnp.concatenate(
        [
            rows_cols(whole_weights[0], width_devs, token_devs),
            rows_cols(whole_weights[1], width_devs, token_devs),
            rows_cols(whole_weights[2], width_devs, token_devs),
        ],
        axis=1,
    )
    out_full = cols_rows(whole_weights[3], width_devs, token_devs)
    head_width = out_full.shape[0]
    inputs_row = x_in.astype(jnp.float32)
    scale_first = lax.rsqrt(jnp.mean(inputs_row * inputs_row, axis=-1, keepdims=True) + epsilon)
    normed_first = (inputs_row * scale_first * norm1_gain).astype(jnp.bfloat16)
    qkv_rows = jnp.dot(normed_first, qkv_full, preferred_element_type=jnp.float32).astype(
        jnp.bfloat16
    )
    query_heads = qkv_rows[:, :head_width].reshape(local_count, HEADS, HSIZE)
    pair_window = collect_window(
        qkv_rows[:, head_width:].reshape(local_count, 2, head_width), reach
    )
    key_heads = pair_window[:, 0].reshape(key_count, HEADS, HSIZE)
    value_heads = pair_window[:, 1].reshape(key_count, HEADS, HSIZE)
    query_pos = member * local_count + jnp.arange(local_count, dtype=jnp.int32)
    key_pos = (member - reach) * local_count + jnp.arange(key_count, dtype=jnp.int32)
    offset = key_pos[None, :] - query_pos[:, None]
    buckets = bucket_ids(offset)
    bias_terms = jnp.take(jnp.transpose(relative_bias_table), buckets, axis=1)
    no_doc = jnp.full((reach * local_count,), -1, jnp.int32)
    doc_padded = jnp.concatenate([no_doc, doc_ids, no_doc], axis=0)
    key_docs = lax.dynamic_slice_in_dim(doc_padded, member * local_count, key_count, 0)
    query_docs = lax.dynamic_slice_in_dim(doc_ids, member * local_count, local_count, 0)
    allowed = (jnp.abs(offset) < WINDOW) & (query_docs[:, None] == key_docs[None, :])
    attention_scores = head_scores(query_heads, key_heads, bias_terms, allowed, score_scale)
    row_peak = jnp.max(attention_scores, axis=-1, keepdims=True)
    shifted = jnp.exp(attention_scores - row_peak)
    row_sum = jnp.sum(shifted, axis=-1, keepdims=True)
    log_total = row_peak + jnp.log(row_sum)
    weights_reduced_precision = (shifted / row_sum).astype(jnp.bfloat16)
    attended = jnp.einsum(
        "hqk,khd->qhd", weights_reduced_precision, value_heads, preferred_element_type=jnp.float32
    )
    attended_low = attended.reshape(local_count, head_width).astype(jnp.bfloat16)
    attn_low = jnp.dot(attended_low, out_full, preferred_element_type=jnp.float32).astype(
        jnp.bfloat16
    )
    arrived = lax.all_to_all(
        jnp.stack([x_in, attn_low, grad_out], axis=1), "gx", split_axis=2, concat_axis=0, tiled=True
    )
    inputs = arrived[:, 0].astype(jnp.float32)
    grad_rows = arrived[:, 2].astype(jnp.float32)
    hidden_first = inputs + arrived[:, 1].astype(jnp.float32)
    scale_second = lax.rsqrt(
        width_total(jnp.sum(hidden_first * hidden_first, axis=-1)) / D + epsilon
    )[:, None]
    normed_second = hidden_first * scale_second * norm2_gain
    logits = width_total(jnp.dot(normed_second, w_router, precision=highest))
    router = jax.nn.softmax(logits, axis=-1)
    expert_iota = jnp.arange(experts, dtype=jnp.int32)
    tok_block = math.gcd(all_tokens, 128)
    block_count = all_tokens // tok_block
    chosen_rows = expert_iota[:, None] == expert_choice[None, :]
    chosen_low = chosen_rows.astype(jnp.bfloat16).reshape(experts, block_count, tok_block)
    block_iota = jnp.arange(tok_block, dtype=jnp.int32)
    upper = (block_iota[:, None] <= block_iota[None, :]).astype(jnp.bfloat16)
    inside_count = jnp.einsum("ebi,ij->ebj", chosen_low, upper, preferred_element_type=jnp.float32)
    block_totals = inside_count[:, :, tok_block - 1]
    earlier_blocks = jnp.cumsum(block_totals, axis=1) - block_totals
    counted = (inside_count + earlier_blocks[:, :, None]).reshape(experts, all_tokens)
    position = (jnp.sum(jnp.where(chosen_rows, counted, 0.0), axis=0) - 1.0).astype(jnp.int32)
    kept_all = position < capacity
    slot_all = jnp.where(kept_all, expert_choice * capacity + position, experts * capacity)
    source = (
        jnp.full((experts * capacity + 1,), all_tokens, jnp.int32)
        .at[slot_all]
        .set(jnp.arange(all_tokens, dtype=jnp.int32))[: experts * capacity]
    )
    source_seq = source // seq_len
    source_inner = source % seq_len
    source_rows = jnp.where(
        source < all_tokens,
        source_inner // local_count * own_rows
        + source_seq * local_count
        + source_inner % local_count,
        all_tokens,
    )
    row_iota = jnp.arange(all_tokens, dtype=jnp.int32)
    global_of_row = (
        row_iota // local_count % width_devs * seq_len
        + row_iota // own_rows * local_count
        + row_iota % local_count
    )
    slot_rows = jnp.take(slot_all, global_of_row)
    own_global = lax.dynamic_slice_in_dim(global_of_row, member * own_rows, own_rows, 0)
    picked_mine = jnp.take(expert_choice, own_global)[:, None] == expert_iota[None, :]
    gate_value = jnp.sum(jnp.where(picked_mine, router, 0.0), axis=-1)
    second_rows = token_rows(normed_second.astype(jnp.bfloat16))
    hidden_weight = jnp.transpose(w_hidden.reshape(width_cols, -1, experts), (2, 0, 1))
    back_weight = jnp.transpose(w_back.reshape(width_cols, -1, experts), (2, 1, 0))
    expert_rows = experts // width_devs
    slot_in = take_rows(second_rows, source_rows).reshape(experts, capacity, width_cols)

    def hidden_term(first_row, row_count):
        return jnp.einsum(
            "ecd,edf->ecf", slot_in, hidden_weight, preferred_element_type=jnp.float32
        )

    pre_block = width_sums(hidden_term, expert_rows)
    act_rows = width_rows(jax.nn.gelu(pre_block).astype(jnp.bfloat16))
    expert_out = jnp.einsum(
        "ecf,efd->ecd", act_rows, back_weight, preferred_element_type=jnp.float32
    ).reshape(experts * capacity, width_cols)

    def route_term(first_row, row_count):
        return take_rows(expert_out, slot_rows)

    routed = token_sums(route_term, own_rows)
    block_out = hidden_first + gate_value[:, None] * routed
    gate_grad = width_total(jnp.sum(grad_rows * routed, axis=-1))
    route_rows = token_rows((grad_rows * gate_value[:, None]).astype(jnp.bfloat16))
    gelu_pair = jax.vjp(jax.nn.gelu, pre_block)
    slot_grad = take_rows(route_rows, source_rows).reshape(experts, capacity, width_cols)
    back_grads = jnp.einsum("ecf,ecd->efd", act_rows, slot_grad, preferred_element_type=jnp.float32)

    def act_term(first_row, row_count):
        return jnp.einsum(
            "ecd,efd->ecf", slot_grad, back_weight, preferred_element_type=jnp.float32
        )

    act_grad = width_sums(act_term, expert_rows)
    pre_rows = width_rows(gelu_pair[1](act_grad)[0].astype(jnp.bfloat16))
    hidden_gradient_rows = jnp.einsum(
        "ecd,ecf->edf", slot_in, pre_rows, preferred_element_type=jnp.float32
    )
    slot_in_grad = jnp.einsum(
        "ecf,edf->ecd", pre_rows, hidden_weight, preferred_element_type=jnp.float32
    ).reshape(experts * capacity, width_cols)

    def back_route_term(first_row, row_count):
        return take_rows(slot_in_grad, slot_rows)

    back_routed = token_sums(back_route_term, own_rows)
    grad_hidden = jnp.transpose(hidden_gradient_rows, (1, 2, 0)).reshape(width_cols, -1)
    grad_back = jnp.transpose(back_grads, (2, 1, 0)).reshape(width_cols, -1)
    logit_grad = router * (
        gate_grad[:, None] * picked_mine.astype(jnp.float32) - (gate_value * gate_grad)[:, None]
    )
    second_grad = back_routed + jnp.einsum("re,de->rd", logit_grad, w_router, precision=highest)
    router_part = jnp.einsum("rd,re->de", normed_second, logit_grad, precision=highest)
    norm2_part = jnp.sum(second_grad * hidden_first * scale_second, axis=0)
    gained_second = second_grad * norm2_gain
    row_dot_second = width_total(jnp.sum(gained_second * hidden_first, axis=-1))[:, None]
    hidden_grad = (
        grad_rows
        + scale_second * gained_second
        - hidden_first * scale_second**3 * row_dot_second / D
    )
    out_rows, hidden_rows = (
        lax.all_to_all(block_out, "gx", split_axis=0, concat_axis=1, tiled=True),
        lax.all_to_all(hidden_grad, "gx", split_axis=0, concat_axis=1, tiled=True),
    )
    attn_grad = hidden_rows.astype(jnp.bfloat16)
    grad_out_full = jnp.einsum(
        "rf,rd->fd", attended_low, attn_grad, preferred_element_type=jnp.float32
    )
    attended_grad = (
        jnp.einsum("rd,fd->rf", attn_grad, out_full, preferred_element_type=jnp.float32)
        .astype(jnp.bfloat16)
        .reshape(local_count, HEADS, HSIZE)
    )
    scores_again = head_scores(query_heads, key_heads, bias_terms, allowed, score_scale)
    probs_again = jnp.exp(scores_again - log_total)
    value_grad = jnp.einsum(
        "hqk,qhd->khd",
        probs_again.astype(jnp.bfloat16),
        attended_grad,
        preferred_element_type=jnp.float32,
    )
    prob_grad = jnp.einsum(
        "qhd,khd->hqk", attended_grad, value_heads, preferred_element_type=jnp.float32
    )
    score_gradient = (
        probs_again * (prob_grad - jnp.sum(probs_again * prob_grad, axis=-1, keepdims=True))
    ).astype(jnp.bfloat16)
    query_grad = (
        jnp.einsum("hqk,khd->qhd", score_gradient, key_heads, preferred_element_type=jnp.float32)
        * score_scale
    ).astype(jnp.bfloat16)
    key_grad = (
        jnp.einsum("hqk,qhd->khd", score_gradient, query_heads, preferred_element_type=jnp.float32)
        * score_scale
    )
    band_low = max(0, reach * local_count - 90)
    band_high = min(key_count, reach * local_count + local_count + 90)
    bucket_iota = jnp.arange(relative_bias_table.shape[0], dtype=jnp.int32)
    band_onehot = (buckets[None, :, band_low:band_high] == bucket_iota[:, None, None]).astype(
        jnp.bfloat16
    )
    table_near = jnp.einsum(
        "ivt,zvt->zi",
        score_gradient[:, :, band_low:band_high],
        band_onehot,
        preferred_element_type=jnp.float32,
    )
    left_far = jnp.sum(score_gradient[:, :, :band_low].astype(jnp.float32), axis=(1, 2))
    right_far = jnp.sum(score_gradient[:, :, band_high:].astype(jnp.float32), axis=(1, 2))
    table_part = (
        table_near
        + (bucket_iota == 15).astype(jnp.float32)[:, None] * left_far[None, :]
        + (bucket_iota == 31).astype(jnp.float32)[:, None] * right_far[None, :]
    )
    pair_grads = return_window(
        jnp.stack(
            [key_grad.reshape(key_count, head_width), value_grad.reshape(key_count, head_width)],
            axis=1,
        ),
        reach,
        local_count,
    )
    qkv_grad = jnp.concatenate(
        [
            query_grad.reshape(local_count, head_width),
            pair_grads.astype(jnp.bfloat16).reshape(local_count, 2 * head_width),
        ],
        axis=1,
    )
    qkv_grads = jnp.einsum("rd,rc->dc", normed_first, qkv_grad, preferred_element_type=jnp.float32)
    first_grad = jnp.einsum("rc,dc->rd", qkv_grad, qkv_full, preferred_element_type=jnp.float32)
    norm1_part = jnp.sum(first_grad * inputs_row * scale_first, axis=0)
    gained_first = first_grad * norm1_gain
    row_dot_first = jnp.sum(gained_first * inputs_row, axis=-1, keepdims=True)
    input_rows = (
        hidden_rows + scale_first * gained_first - inputs_row * scale_first**3 * row_dot_first / D
    )
    summed = lax.psum(
        (
            norm1_part,
            table_part,
            spread_rows(norm2_part, column, width_devs),
            spread_rows(router_part, column, width_devs),
        ),
        ("gx", "gy"),
    )
    grad_norm1 = summed[0]
    grad_table = summed[1]
    grad_norm2 = lax.dynamic_index_in_dim(summed[2], column, 0, keepdims=False)
    grad_router = lax.dynamic_index_in_dim(summed[3], column, 0, keepdims=False)
    weight_parts = (
        lax.psum_scatter(
            grid_rows_cols(qkv_grads[:, :head_width], width_devs, token_devs),
            ("gx", "gy"),
            scatter_dimension=0,
            tiled=True,
        ),
        lax.psum_scatter(
            grid_rows_cols(qkv_grads[:, head_width : 2 * head_width], width_devs, token_devs),
            ("gx", "gy"),
            scatter_dimension=0,
            tiled=True,
        ),
        lax.psum_scatter(
            grid_rows_cols(qkv_grads[:, 2 * head_width :], width_devs, token_devs),
            ("gx", "gy"),
            scatter_dimension=0,
            tiled=True,
        ),
        lax.psum_scatter(
            grid_cols_rows(grad_out_full, width_devs, token_devs),
            ("gx", "gy"),
            scatter_dimension=0,
            tiled=True,
        ),
    )
    return (
        out_rows,
        input_rows,
        grad_norm1,
        weight_parts[0][0],
        weight_parts[1][0],
        weight_parts[2][0],
        grad_table,
        weight_parts[3][0],
        grad_norm2,
        grad_router,
        grad_hidden,
        grad_back,
    )


MESH = pl.DeviceIdType.MESH
GELU_C = math.sqrt(2.0 / math.pi)
f32, bf16 = jnp.float32, jnp.bfloat16


def nn(a, b):
    return jnp.dot(a, b, preferred_element_type=f32)


def nt(a, b):
    return lax.dot_general(a, b, (((1,), (1,)), ((), ())), preferred_element_type=f32)


def tn(a, b):
    return lax.dot_general(a, b, (((0,), (0,)), ((), ())), preferred_element_type=f32)


def remote(src, dst, send_sem, recv_sem, device):
    return pltpu.make_async_remote_copy(
        src_ref=src, dst_ref=dst, send_sem=send_sem, recv_sem=recv_sem,
        device_id=device, device_id_type=MESH)


class Place:
    def __init__(self):
        self.gx, self.gy = lax.axis_index("gx"), lax.axis_index("gy")
        self.core, self.chip = lax.rem(self.gy, 2), self.gy // 2
        self.pair = (self.gx, self.gy + 1 - 2 * self.core)
        self.line = [lax.rem(self.gx + k, 4) for k in (1, 2, 3)]
        self.chips = [lax.rem(self.chip + k, 4) for k in (1, 2, 3)]
        self.line_from = [lax.rem(self.gx + 4 - k, 4) for k in (1, 2, 3)]
        self.chips_from = [lax.rem(self.chip + 4 - k, 4) for k in (1, 2, 3)]
        self.is_mid = jnp.logical_and(self.gx > 0, self.gx < 3)
        self.is_end = jnp.logical_not(self.is_mid)
        self.mid = (jnp.where(self.gx < 2, 1, 2), self.gy)
        self.other_mid = (jnp.where(self.gx < 2, 2, 1), self.gy)
        self.end = (jnp.where(self.gx < 2, 0, 3), self.gy)

    def on_line(self, k):
        return (self.line[k], self.gy)

    def on_plane(self, k):
        return (self.gx, 2 * self.chips[k] + self.core)

    def greet_all(self):
        devices = [self.on_line(k) for k in range(3)] + [self.on_plane(k) for k in range(3)] + [self.pair]
        barrier = pltpu.get_barrier_semaphore()
        for device in devices:
            pl.semaphore_signal(barrier, inc=1, device_id=device, device_id_type=MESH)
        pl.semaphore_wait(barrier, len(devices))


def as_column(row):
    n = row.shape[1]
    same = lax.broadcasted_iota(jnp.int32, (n, n), 0) == lax.broadcasted_iota(jnp.int32, (n, n), 1)
    return jnp.sum(jnp.where(same, row.astype(f32), 0.0), axis=1, keepdims=True)


def pick_rows(slot_row, base, capacity, rows_ref, tokens):
    kblock = 1024
    ids = lax.broadcasted_iota(jnp.int32, (capacity, kblock), 0) + base
    total = None
    for kb in range(tokens // kblock):
        hot = (slot_row[:, kb * kblock:(kb + 1) * kblock] == ids).astype(f32).astype(bf16)
        part = nn(hot, rows_ref[kb * kblock:(kb + 1) * kblock, :])
        total = part if total is None else total + part
    return total


class LineSum:
    def __init__(self, me, own, got, other, own_sem, got_sem, other_sem, out_sem, experts):
        self.me, self.own, self.got, self.other = me, own, got, other
        self.sems = (own_sem, got_sem, other_sem, out_sem)
        self.ring, self.experts = own.shape[0], experts

    def to_mid(self, e):
        sl = lax.rem(e, self.ring)
        return remote(self.own.at[sl], self.got.at[e], self.sems[0].at[sl], self.sems[1].at[e], self.me.mid)

    def across(self, e):
        sl = lax.rem(e, self.ring)
        return remote(self.own.at[sl], self.other.at[e], self.sems[0].at[sl], self.sems[2].at[e], self.me.other_mid)

    def to_end(self, e):
        return remote(self.got.at[e], self.got.at[e], self.sems[3].at[e], self.sems[1].at[e], self.me.end)

    def put(self, e, value):
        self.own[lax.rem(e, self.ring)] = value

    def valid(self, e):
        return jnp.logical_and(e >= 0, e < self.experts)

    def send(self, e):
        @pl.when(jnp.logical_and(self.me.is_end, self.valid(e)))
        def _():
            @pl.when(e >= PACE)
            def _():
                self.to_mid(e - PACE).wait_send()
            self.to_mid(e).start()

    def half(self, e):
        @pl.when(jnp.logical_and(self.me.is_mid, self.valid(e)))
        def _():
            sl = lax.rem(e + self.ring, self.ring)
            self.to_mid(e).wait_recv()
            self.own[sl] = (self.own[sl].astype(f32) + self.got[e].astype(f32)).astype(bf16)

            @pl.when(e >= PACE)
            def _():
                self.across(e - PACE).wait_send()
            self.across(e).start()

    def whole(self, e):
        @pl.when(jnp.logical_and(self.me.is_mid, self.valid(e)))
        def _():
            sl = lax.rem(e + self.ring, self.ring)
            self.across(e).wait_recv()
            self.got[e] = (self.own[sl].astype(f32) + self.other[e].astype(f32)).astype(bf16)

            @pl.when(e >= PACE)
            def _():
                self.to_end(e - PACE).wait_send()
            self.to_end(e).start()

    def tick(self, t):
        self.send(t)
        self.half(t - LAG_B)
        self.whole(t - LAG_C)

    def await_total(self, e):
        @pl.when(self.me.is_end)
        def _():
            self.to_end(e).wait_recv()

    def drain(self):
        for e in range(self.experts - PACE, self.experts):
            @pl.when(self.me.is_end)
            def _():
                self.to_mid(e).wait_send()

            @pl.when(self.me.is_mid)
            def _():
                self.across(e).wait_send()
                self.to_end(e).wait_send()


RING = 8
GROUP = 4
LAG_B, LAG_C, LAG_D = 2, 4, 6
PACE = 2


class LineGather:
    def __init__(self, me, slot, right_s, right_r, left_s, left_r):
        self.me, self.slot = me, slot
        self.sems = (right_s, right_r, left_s, left_r)

    def right(self, h):
        at = self.slot(jnp.maximum(self.me.gx - h, 0))
        return remote(at, at, self.sems[0].at[h], self.sems[1].at[h], (jnp.minimum(self.me.gx + 1, 3), self.me.gy))

    def left(self, h):
        at = self.slot(jnp.minimum(self.me.gx + h, 3))
        return remote(at, at, self.sems[2].at[h], self.sems[3].at[h], (jnp.maximum(self.me.gx - 1, 0), self.me.gy))

    def from_left(self, h):
        at = self.slot(jnp.maximum(self.me.gx - 1 - h, 0))
        return remote(at, at, self.sems[0].at[h], self.sems[1].at[h], (jnp.maximum(self.me.gx - 1, 0), self.me.gy))

    def from_right(self, h):
        at = self.slot(jnp.minimum(self.me.gx + 1 + h, 3))
        return remote(at, at, self.sems[2].at[h], self.sems[3].at[h], (jnp.minimum(self.me.gx + 1, 3), self.me.gy))

    def sends(self, h):
        gx = self.me.gx
        return jnp.logical_and(gx < 3, gx >= h), jnp.logical_and(gx > 0, gx + h <= 3)

    def start(self):
        self.pass_on(0)

    def pass_on(self, h):
        go_right, go_left = self.sends(h)

        @pl.when(go_right)
        def _():
            self.right(h).start()

        @pl.when(go_left)
        def _():
            self.left(h).start()

    def receive(self, h):
        @pl.when(self.me.gx >= h + 1)
        def _():
            self.from_left(h).wait_recv()

        @pl.when(self.me.gx + h + 1 <= 3)
        def _():
            self.from_right(h).wait_recv()
        if h < 2:
            self.pass_on(h + 1)

    def drain(self):
        for h in range(3):
            go_right, go_left = self.sends(h)

            @pl.when(go_right)
            def _():
                self.right(h).wait_send()

            @pl.when(go_left)
            def _():
                self.left(h).wait_send()


def place_one(lane):
    register, unit, expert = lane // 128, lax.rem(lane // 32, 4), lax.rem(lane, 32)
    return expert // 4 * 128 + lax.rem(expert, 4) * 32 + register * 4 + unit


def place_two(lane):
    register, expert, unit = lane // 128, lax.rem(lane // 32, 4), lax.rem(lane, 32)
    return expert * 128 + register * 32 + unit


def fill_moves(one_ref, two_ref, inward):
    for ref, place in ((one_ref, place_one), (two_ref, place_two)):
        n = ref.shape[0]
        if inward:
            moved = place(lax.broadcasted_iota(jnp.int32, (n, 1), 0))
            ref[...] = (moved == lax.broadcasted_iota(jnp.int32, (n, n), 1)).astype(f32).astype(bf16)
        else:
            moved = place(lax.broadcasted_iota(jnp.int32, (1, n), 1))
            ref[...] = (moved == lax.broadcasted_iota(jnp.int32, (n, n), 0)).astype(f32).astype(bf16)


def near_buckets(rows):
    offset = (
        lax.broadcasted_iota(jnp.int32, (rows, 3 * rows), 1)
        - rows
        - lax.broadcasted_iota(jnp.int32, (rows, 3 * rows), 0)
    )
    return bucket_ids(offset)


def fill_bias(bias_ref, table_ref, chip, heads):
    rows = bias_ref.shape[1]
    span = bias_ref.shape[2]
    mid = span // 2
    buckets = near_buckets(rows)
    for h in range(heads):
        column = chip * heads + h
        near = jnp.zeros(buckets.shape, f32)
        for b in range(table_ref.shape[1]):
            near = jnp.where(buckets == b, table_ref[column, b], near)
        bias_ref[h, :, 0:mid - rows] = jnp.full((rows, mid - rows), table_ref[column, 15], f32)
        bias_ref[h, :, mid - rows:mid + 2 * rows] = near
        bias_ref[h, :, mid + 2 * rows:] = jnp.full((rows, span - mid - 2 * rows), table_ref[column, 31], f32)


def allowed_pairs(doc_row, block_at, local):
    start = pl.multiple_of(block_at * local, local)
    return as_column(doc_row[:, pl.ds(start, local)]) == doc_row[...].astype(f32)


def unit_scores(q_block, keys, bias_ref, h, block_at, allowed):
    rows = q_block.shape[0]
    seq = keys.shape[0]
    lanes = lax.broadcasted_iota(jnp.int32, q_block.shape, 1) // HSIZE
    masked = jnp.where(lanes == h, q_block, jnp.zeros_like(q_block))
    start = pl.multiple_of(seq - rows * block_at, rows)
    return jnp.where(allowed, nt(masked, keys) + bias_ref[h, :, pl.ds(start, seq)], -1000000000.0)


def fill_slots(slot_ref, choice_row, experts, capacity):
    tokens = choice_row.shape[1]
    expert = lax.broadcasted_iota(jnp.int32, (experts, 128), 0)
    upper = (lax.broadcasted_iota(jnp.int32, (128, 128), 0)
             <= lax.broadcasted_iota(jnp.int32, (128, 128), 1)).astype(f32).astype(bf16)
    before = jnp.zeros((experts, 1), f32)
    for b in range(tokens // 128):
        choice = choice_row[:, b * 128:(b + 1) * 128]
        chosen = (expert == choice).astype(f32)
        count = nn(chosen.astype(bf16), upper)
        place = jnp.sum(chosen * (count + before), axis=0, keepdims=True).astype(jnp.int32) - 1
        slot_ref[:, b * 128:(b + 1) * 128] = jnp.where(place < capacity, choice * capacity + place, -1)
        before = before + count[:, 127:128]


POINTS = (2, 2, 2, 2, 2, 0, 2, 2, 2, 4, 1)
AHEAD = 4
KEEP = 12


class BlockRows:
    def __init__(self, ref):
        self.ref = ref

    def __getitem__(self, at):
        rows = at[0]
        size = self.ref.shape[1]
        part = self.ref[rows.start // size:rows.stop // size]
        return part.reshape(rows.stop - rows.start, self.ref.shape[2])


class Dispatch:
    def __init__(self, me, out, dst, line_s, line_r, plane_s, plane_r, pair_s, pair_r):
        self.me, self.out, self.dst = me, out, dst
        self.sems = (line_s, line_r, plane_s, plane_r, pair_s, pair_r)
        self.zs = [me.gx] + me.line_from

    def line(self, k):
        at = self.dst.at[self.me.gx * 8 + self.me.gy]
        return remote(self.out.at[self.me.line[k]], at, self.sems[0].at[k], self.sems[1].at[k], self.me.on_line(k))

    def plane(self, m, k):
        at = self.dst.at[self.zs[m] * 8 + self.me.gy]
        return remote(at, at, self.sems[2].at[m, k], self.sems[3].at[m, k], self.me.on_plane(k))

    def pair(self, m, k):
        c = self.me.chip if k == 0 else self.me.chips_from[k - 1]
        at = self.dst.at[self.zs[m] * 8 + 2 * c + self.me.core]
        return remote(at, at, self.sems[4].at[m, k], self.sems[5].at[m, k], self.me.pair)

    def start(self):
        for k in range(3):
            self.line(k).start()

    def spread(self, m):
        if m > 0:
            self.line(m - 1).wait_recv()
        for k in range(3):
            self.plane(m, k).start()
        self.pair(m, 0).start()

    def share(self, m):
        for k in range(3):
            self.plane(m, k).wait_recv()
            self.pair(m, k + 1).start()

    def arrive(self):
        for m in range(4):
            for k in range(4):
                self.pair(m, k).wait_recv()

    def drain(self):
        for m in range(4):
            for k in range(4):
                self.pair(m, k).wait_send()
            for k in range(3):
                self.plane(m, k).wait_send()
        for k in range(3):
            self.line(k).wait_send()


def forward_kernel(heads, experts, capacity,
                   x_ref, gain1_ref, wq_ref, wk_ref, wv_ref, wout_ref, table_ref, wr_ref, gain2_ref, doc_row,
                   choice_row, grad_ref, wh_hbm, wb_hbm,
                   out_ref, gh_hbm, gb_hbm, nh_hbm,
                   hidden_ref, normed_ref, router_ref, gate_ref, at_ref, q_ref, kv_ref, lse_ref, xb_ref,
                   wqkv_all, wout_all, small_all,
                   slot_ref, w1_ref, w2_ref, g_ref, g_out, rows_ref, rows_out, gs_ref,
                   own_ref, ag_ref, other_ref, xs_ref, got_ref, other2_ref,
                   wq_st, wo_st, sm_st, at_in, y_in, s_in, line_out, line_in,
                   nat_sem, own_sem, got_sem, other_sem, t_sem, p_sem, got2_sem, other2_sem, t2_sem, gh_sem, gb_sem,
                   wqr_s, wqr_r, wql_s, wql_r, smr_s, smr_r, sml_s, sml_r,
                   xb_s, xb_r, wqp_s, wqp_r, woc_s, woc_r, wop_s, wop_r, kv_s, kv_r, at_s, at_r,
                   gz_s, gz_r, rz_s, rz_r, lo_s, lo_r, gc_s, gc_r, gp_s, gp_r, rc_s, rc_r, rp_s, rp_r,
                   yo_s, yo_r, so_s, so_r, ya_s, ya_r, yp_s, yp_r):
    me = Place()
    gx, gy, core, chip = me.gx, me.gy, me.core, me.chip
    width, cols = wq_ref.shape
    local = x_ref.shape[0]
    tokens = 32 * local
    units = wh_hbm.shape[1] // experts
    hd = 2 * cols
    seq = 8 * local
    zs = [gx] + me.line_from
    spans = units // 128
    scale = HSIZE ** (-0.5)
    half = capacity // 2
    groups = experts // GROUP
    yt_ref = other_ref

    give = Dispatch(me, g_out, g_ref, gz_s, gz_r, gc_s, gc_r, gp_s, gp_r)
    rows = Dispatch(me, rows_out, rows_ref, rz_s, rz_r, rc_s, rc_r, rp_s, rp_r)
    acts = LineSum(me, own_ref, ag_ref, other_ref, own_sem, got_sem, other_sem, t_sem, experts)
    pres = LineSum(me, own_ref, got_ref, other2_ref, p_sem, got2_sem, other2_sem, t2_sem, experts)
    weights = LineGather(me, lambda z: wq_st.at[core, z], wqr_s, wqr_r, wql_s, wql_r)
    smalls = LineGather(me, lambda z: sm_st.at[z], smr_s, smr_r, sml_s, sml_r)

    def act_step(t):
        @pl.when(t < experts)
        def _():
            gs = pick_rows(slot_ref, t * capacity, capacity, BlockRows(g_ref), tokens).astype(bf16)
            gs_ref[t] = gs
            acts.put(t, nn(gs, w2_ref[t]).astype(bf16))
        acts.tick(t)

    done = [0]

    def ticks(count):
        def body(t, carry):
            act_step(t)
            return carry
        if count:
            lax.fori_loop(done[0], done[0] + count, body, 0)
        done[0] += count

    def xb_plane(k):
        return remote(xb_ref.at[chip], xb_ref.at[chip], xb_s.at[k], xb_r.at[k], me.on_plane(k))

    def wq_pair(k):
        at = wq_st.at[core, zs[k]]
        return remote(at, at, wqp_s.at[k], wqp_r.at[k], me.pair)

    def wo_plane(k):
        return remote(wo_st.at[gy], wo_st.at[gy], woc_s.at[k], woc_r.at[k], me.on_plane(k))

    def wo_pair(k):
        c = me.chips_from[k]
        return remote(wo_st.at[2 * c + core], wo_st.at[2 * c + core], wop_s.at[k], wop_r.at[k], me.pair)

    def kv_pair(c):
        return remote(kv_ref.at[2 * c + core], kv_ref.at[2 * c + core], kv_s.at[c], kv_r.at[c], me.pair)

    def at_plane(k):
        return remote(at_ref.at[me.chips[k]], at_in.at[chip], at_s.at[k], at_r.at[k], me.on_plane(k))

    def line_copy(k):
        return remote(line_out.at[me.line[k]], line_in.at[k], lo_s.at[k], lo_r.at[k], me.on_line(k))

    barrier = pltpu.get_barrier_semaphore()
    friends = [me.on_line(k) for k in range(3)] + [me.on_plane(k) for k in range(3)] + [me.pair]
    for device in friends:
        pl.semaphore_signal(barrier, inc=1, device_id=device, device_id_type=MESH)

    for z in range(4):
        g_out[z] = grad_ref[:, z * width:(z + 1) * width]
    xb_ref[chip] = x_ref[...]
    wq_st[core, gx] = jnp.concatenate(
        [wq_ref[...], wk_ref[...], wv_ref[...], jnp.transpose(wout_ref[...].astype(f32)).astype(bf16)], axis=1)
    sm_st[gx] = jnp.concatenate([wr_ref[...], gain2_ref[...], jnp.zeros((7, width), f32)], axis=0)
    g_ref[gx * 8 + gy] = g_out[gx]
    pl.semaphore_wait(barrier, len(friends))
    give.start()
    give.spread(0)
    for k in range(3):
        xb_plane(k).start()
    wq_pair(0).start()

    def front(bias_ref, nat_ref, half_ref, one_ref, two_ref):
        def load_span(source, g, q):
            at = source.at[:, pl.ds(pl.multiple_of(g * 4096 + q * 1024, 1024), 1024)]
            return pltpu.make_async_copy(at, nat_ref.at[q], nat_sem.at[q])

        def load_spans(source, g):
            for q in range(4):
                load_span(source, g, q).start()

        def turn_span(source, target, g, following):
            lanes = pl.ds(pl.multiple_of(g * 128, 128), 128)
            for q in range(4):
                load_span(source, g, q).wait()
                moved = nn(nat_ref[q], one_ref[...]).astype(bf16)
                for r in range(8):
                    half_ref[r, :, q * 128:(q + 1) * 128] = moved[:, r * 128:(r + 1) * 128]
            following()
            for r in range(8):
                moved = nn(half_ref[r], two_ref[...]).astype(bf16)
                for n in range(4):
                    target[4 * r + n, :, lanes] = moved[:, n * 128:(n + 1) * 128]

        load_spans(wb_hbm, 0)
        fill_moves(one_ref, two_ref, True)
        fill_slots(slot_ref, choice_row, experts, capacity)
        fill_bias(bias_ref, table_ref, chip, heads)
        for m in (1, 2, 3):
            give.spread(m)
        weights.start()
        smalls.start()
        for g in range(spans):
            turn_span(wb_hbm, w2_ref, g, lambda: load_spans(wb_hbm, g + 1) if g + 1 < spans else None)
            if g > 0:
                weights.receive(g - 1)
                smalls.receive(g - 1)
        give.share(0)
        for h in range(spans - 1, 3):
            weights.receive(h)
            smalls.receive(h)
        load_spans(wh_hbm, 0)
        for k in (1, 2, 3):
            wq_pair(k).start()
        for z in range(4):
            wo_st[gy, z] = wq_st[core, z][:, 3 * cols:]
        for m in (1, 2, 3):
            give.share(m)
        give.arrive()
        for k in range(3):
            wo_plane(k).start()
        ticks(POINTS[9])
        for k in range(4):
            wq_pair(k).wait_recv()
        for z in range(4):
            parts = [wq_st[0, z], wq_st[1, z]]
            wqkv_all[z * width:(z + 1) * width, :] = jnp.concatenate(
                [parts[j][:, n * cols:(n + 1) * cols] for n in range(3) for j in range(2)], axis=1)
            wo_st[gy + 1 - 2 * core, z] = wq_st[1 - core, z][:, 3 * cols:]

        for k in range(4):
            c = chip if k == 0 else me.chips_from[k - 1]
            if k > 0:
                xb_plane(k - 1).wait_recv()
            xc = xb_ref[c].astype(f32)
            r1 = lax.rsqrt(jnp.mean(xc * xc, axis=-1, keepdims=True) + epsilon)
            xn = (xc * r1 * gain1_ref[...]).astype(bf16)
            made = nn(xn, wqkv_all[...])
            q_ref[c] = (made[:, :hd].astype(bf16).astype(f32) * scale).astype(bf16)
            kv_ref[2 * c + core] = made[:, hd:].astype(bf16)
            kv_pair(c).start()
        ticks(POINTS[0])
        for c in range(4):
            kv_pair(c).wait_recv()
        lanes = lax.broadcasted_iota(jnp.int32, (local, hd), 1) // HSIZE
        for k in range(4):
            c = me.chips[k] if k < 3 else chip
            block_at = 2 * c + core
            allowed = allowed_pairs(doc_row, block_at, local)
            keys = kv_ref[:, :, :hd].reshape(seq, hd)
            values = kv_ref[:, :, hd:].reshape(seq, hd)
            total = jnp.zeros((local, hd), f32)
            for h in range(heads):
                scores = unit_scores(q_ref[c], keys, bias_ref, h, block_at, allowed)
                peak = jnp.max(scores, axis=-1, keepdims=True)
                shifted = jnp.exp(scores - peak)
                summed = jnp.sum(shifted, axis=-1, keepdims=True)
                lse_ref[c, h] = jnp.broadcast_to(peak + jnp.log(summed), (local, 128))
                low = (shifted * (1.0 / summed)).astype(bf16)
                total = jnp.where(lanes == h, nn(low, values), total)
            at_ref[c] = total.astype(bf16)
            if k < 3:
                at_plane(k).start()
            else:
                at_in[chip] = total.astype(bf16)
            ticks(POINTS[1 + k])
        for k in range(3):
            wo_plane(k).wait_recv()
            wo_pair(k).start()
        small_all[...] = jnp.concatenate([sm_st[z] for z in range(4)], axis=1)
        for k in range(3):
            wo_pair(k).wait_recv()
        for z in range(4):
            wout_all[z * width:(z + 1) * width, :] = jnp.concatenate([wo_st[g, z] for g in range(8)], axis=1)
        ticks(POINTS[10])
        for k in range(3):
            at_plane(k).wait_recv()
        attended = jnp.concatenate([at_in[c] for c in range(4)], axis=1)
        hidden = x_ref[...].astype(f32) + nt(attended, wout_all[...]).astype(bf16).astype(f32)
        hidden_ref[...] = hidden
        r2 = lax.rsqrt(jnp.mean(hidden * hidden, axis=-1, keepdims=True) + epsilon)
        normed = hidden * r2 * small_all[experts:experts + 1, :]
        normed_ref[...] = normed
        logits = lax.dot_general(normed, small_all[:experts, :], (((1,), (1,)), ((), ())),
                                 precision=lax.Precision.HIGHEST, preferred_element_type=f32)
        lifted = jnp.exp(logits - jnp.max(logits, axis=-1, keepdims=True))
        router = lifted / jnp.sum(lifted, axis=-1, keepdims=True)
        router_ref[...] = router
        own_tokens = pl.ds(pl.multiple_of((gx * 8 + gy) * local, local), local)
        picked = as_column(choice_row[:, own_tokens]) == lax.broadcasted_iota(jnp.int32, router.shape, 1).astype(f32)
        gate = jnp.sum(jnp.where(picked, router, 0.0), axis=-1, keepdims=True)
        gate_ref[...] = gate
        first = gate.astype(bf16).astype(f32)
        second = (gate - first).astype(bf16).astype(f32)
        third = gate - first - second
        lane = lax.broadcasted_iota(jnp.int32, (local, 64), 1)
        pieces = jnp.where(lane == 0, first, jnp.where(lane == 1, second, jnp.where(lane == 2, third, 0.0)))
        pieces = pieces.astype(bf16)
        low = normed.astype(bf16)
        for z in range(4):
            rows_out[z] = jnp.concatenate([low[:, z * width:(z + 1) * width], pieces], axis=1)
        rows.start()
        rows_ref[gx * 8 + gy] = rows_out[gx]
        rows.spread(0)
        ticks(POINTS[5])
        turn_span(wh_hbm, w1_ref, 0, lambda: load_spans(wh_hbm, 1))
        for m in (1, 2, 3):
            rows.spread(m)
        ticks(POINTS[6])
        for n in range(1, spans):
            turn_span(wh_hbm, w1_ref, n, lambda: load_spans(wh_hbm, n + 1) if n + 1 < spans else None)
            ticks(POINTS[7])
        for m in range(4):
            rows.share(m)
        ticks(POINTS[8])
        rows.arrive()

    V = pltpu.VMEM
    pl.run_scoped(front, V((heads, local, 16 * local), f32), V((4, width, 1024), bf16), V((8, width, 512), bf16),
                  V((1024, 1024), bf16), V((512, 512), bf16))
    first_left = done[0]

    def experts_part(y_own, y_out, s_out, gh_st, gb_st):
        def grad_copy(stage, target, sems, e):
            return pltpu.make_async_copy(stage.at[lax.rem(e, 2)], target.at[e], sems.at[lax.rem(e, 2)])

        def pair_half(j):
            return remote(y_out.at[j], y_in.at[j], yo_s.at[j], yo_r.at[j], me.pair)

        def to_owner(j, k):
            return remote(s_out.at[j, me.chips[k]], s_in.at[j, k], so_s.at[j, k], so_r.at[j, k], me.on_plane(k))

        own_half = pl.ds(pl.multiple_of(core * half, 16), half)

        def from_owner(j, k):
            at = yt_ref.at[j * GROUP + chip, own_half]
            return remote(at, at, ya_s.at[j, k], ya_r.at[j, k], me.on_plane(k))

        def pair_total(j, k):
            c = chip if k == 0 else me.chips_from[k - 1]
            at = yt_ref.at[j * GROUP + c, own_half]
            return remote(at, at, yp_s.at[j, k], yp_r.at[j, k], me.pair)

        def stage_two(j):
            pair_half(j).wait_recv()
            for m in range(GROUP):
                s_out[j, m] = (y_own[j, m].astype(f32) + y_in[j, m].astype(f32)).astype(bf16)
            for k in range(3):
                to_owner(j, k).start()

        def stage_three(j):
            total = s_out[j, chip].astype(f32)
            for k in range(3):
                to_owner(j, k).wait_recv()
                total = total + s_in[j, k].astype(f32)
            yt_ref[j * GROUP + chip, own_half] = total.astype(bf16)
            for k in range(3):
                from_owner(j, k).start()
            pair_total(j, 0).start()

        def stage_four(j):
            for k in range(3):
                from_owner(j, k).wait_recv()
                pair_total(j, k + 1).start()

        def step(t, carry):
            i = t - experts + AHEAD

            @pl.when(i == experts - PACE)
            def _():
                acts.drain()

            @pl.when(jnp.logical_and(i >= 0, i < experts))
            def _():
                xs = pick_rows(slot_ref, i * capacity, capacity, BlockRows(rows_ref), tokens).astype(bf16)
                xs_ref[lax.rem(i, KEEP)] = xs
                pres.put(i, nn(xs[:, :width], w1_ref[i]).astype(bf16))
            act_step(t)
            pres.tick(t - experts)
            e = t - experts - LAG_D

            @pl.when(e >= 0)
            def _():
                acts.await_total(e)
                pres.await_total(e)
                xs = xs_ref[lax.rem(e, KEEP)]
                pieces = xs[:, width:].astype(f32)
                gate = pieces[:, 0:1] + pieces[:, 1:2] + pieces[:, 2:3]
                u = got_ref[e].astype(f32)
                ag = gate * ag_ref[e].astype(f32)
                u2 = u * u
                th = jnp.tanh(GELU_C * (u + 0.044715 * (u2 * u)))
                part = 0.5 * (1.0 + th)
                act = (u * part).astype(bf16)
                dg = part + 0.5 * u * (1.0 - th * th) * (GELU_C * (1.0 + 3 * 0.044715 * u2))
                pg = (ag * dg).astype(bf16)
                y = jnp.concatenate([nt(act, w2_ref[e]), nt(pg, w1_ref[e])], axis=1).astype(bf16)
                j, m = e // GROUP, lax.rem(e, GROUP)

                @pl.when(core == 0)
                def _():
                    y_own[j, m] = y[:half]
                    y_out[j, m] = y[half:]

                @pl.when(core == 1)
                def _():
                    y_own[j, m] = y[half:]
                    y_out[j, m] = y[:half]

                @pl.when(m == GROUP - 1)
                def _():
                    pair_half(j).start()

                @pl.when(e >= 2)
                def _():
                    grad_copy(gh_st, gh_hbm, gh_sem, e - 2).wait()
                    grad_copy(gb_st, gb_hbm, gb_sem, e - 2).wait()
                slot_grad = (gate * gs_ref[e].astype(f32)).astype(bf16)
                gh_st[lax.rem(e, 2)] = tn(xs[:, :width], pg).astype(bf16)
                gb_st[lax.rem(e, 2)] = tn(slot_grad, act).astype(bf16)
                grad_copy(gh_st, gh_hbm, gh_sem, e).start()
                grad_copy(gb_st, gb_hbm, gb_sem, e).start()

                @pl.when(jnp.logical_and(m == 0, j >= 1))
                def _():
                    stage_two(j - 1)

                @pl.when(jnp.logical_and(m == 2, j >= 1))
                def _():
                    stage_three(j - 1)

                @pl.when(jnp.logical_and(m == 1, j >= 2))
                def _():
                    stage_four(j - 2)
            return carry

        lax.fori_loop(first_left, 2 * experts + LAG_D, step, 0)
        last = groups - 1
        stage_two(last)
        stage_four(last - 1)
        slots = [as_column(slot_ref[:, pl.ds(pl.multiple_of((z * 8 + gy) * 128, 128), 128)]) for z in range(4)]
        own_slots = jnp.concatenate(slots, axis=0).astype(jnp.int32)
        many = 8
        per = many // GROUP
        places = lax.broadcasted_iota(jnp.int32, (own_slots.shape[0], many * capacity), 1)

        def picked(b):
            hot = (own_slots == places + b * many * capacity).astype(f32).astype(bf16)
            return nn(hot, yt_ref[b * many:(b + 1) * many].reshape(many * capacity, 2 * width))

        total = None
        for b in range(experts // many - 1):
            for j in range(b * per, (b + 1) * per):
                for k in range(4):
                    pair_total(j, k).wait_recv()
            if b == 0:
                stage_three(last)
            part = picked(b)
            total = part if total is None else total + part
        stage_four(last)
        for j in range(groups - per, groups):
            for k in range(4):
                pair_total(j, k).wait_recv()
        total = total + picked(experts // many - 1)

        for z in range(4):
            line_out[z] = total[z * local:(z + 1) * local].astype(bf16)
        for k in range(3):
            line_copy(k).start()
        out_ref[gx] = line_out[gx].astype(f32)
        pres.drain()
        for e in (experts - 2, experts - 1):
            grad_copy(gh_st, gh_hbm, gh_sem, e).wait()
            grad_copy(gb_st, gb_hbm, gb_sem, e).wait()

        def sent(j, carry):
            pair_half(j).wait_send()
            for k in range(3):
                to_owner(j, k).wait_send()
                from_owner(j, k).wait_send()
            for k in range(4):
                pair_total(j, k).wait_send()
            return carry
        lax.fori_loop(0, groups, sent, 0)
        give.drain()
        rows.drain()
        weights.drain()
        smalls.drain()
        for k in range(3):
            for copy in (xb_plane, wo_plane, wo_pair, at_plane):
                copy(k).wait_send()
        for k in range(4):
            for copy in (wq_pair, kv_pair):
                copy(k).wait_send()

    def turn_part(one_ref, two_ref, in_ref, half_ref, nat_ref):
        def load(g):
            return pltpu.make_async_copy(gh_hbm.at[:, :, g * 128:(g + 1) * 128], in_ref, gh_sem.at[0])

        def store(g, q):
            at = nh_hbm.at[:, g * 4096 + q * 1024:g * 4096 + (q + 1) * 1024]
            return pltpu.make_async_copy(nat_ref.at[q], at, nat_sem.at[q])

        load(0).start()
        fill_moves(one_ref, two_ref, False)
        for g in range(spans):
            load(g).wait()
            for r in range(8):
                gathered = jnp.concatenate([in_ref[4 * r + n] for n in range(4)], axis=1)
                moved = nn(gathered, two_ref[...]).astype(bf16)
                for q in range(4):
                    half_ref[q, :, r * 128:(r + 1) * 128] = moved[:, q * 128:(q + 1) * 128]
            if g + 1 < spans:
                load(g + 1).start()
            for q in range(4):
                if g > 0:
                    store(g - 1, q).wait()
                nat_ref[q] = nn(half_ref[q], one_ref[...]).astype(bf16)
                store(g, q).start()
        for k in range(3):
            line_copy(k).wait_recv()
            out_ref[me.line_from[k]] = line_in[k].astype(f32)
        for k in range(3):
            line_copy(k).wait_send()
        for q in range(4):
            store(spans - 1, q).wait()

    block = (groups, GROUP, half, 2 * width)
    pl.run_scoped(experts_part, V(block, bf16), V(block, bf16), V(block, bf16),
                  V((2, width, units), bf16), V((2, width, units), bf16))
    pl.run_scoped(turn_part, V((1024, 1024), bf16), V((512, 512), bf16), V((experts, width, 128), bf16),
                  V((4, width, 1024), bf16), V((4, width, 1024), bf16))


def forward_pass(x_in, gain1, wq, wk, wv, wout, table, wr, gain2, doc_row, choice_row, grad_out, w_hidden, w_back,
                 collective_id):
    local, features = x_in.shape
    width, cols = wq.shape
    hd = 2 * cols
    heads = hd // HSIZE
    experts = wr.shape[0]
    tokens = choice_row.shape[1]
    capacity = tokens * 5 // (4 * experts)
    units = w_hidden.shape[1] // experts
    half = capacity // 2
    groups = experts // GROUP
    vm = pl.BlockSpec(memory_space=pltpu.VMEM)
    sm = pl.BlockSpec(memory_space=pltpu.SMEM)
    hbm = pl.BlockSpec(memory_space=pl.ANY)
    dma = pltpu.SemaphoreType.DMA
    shape = jax.ShapeDtypeStruct
    V = pltpu.VMEM
    return pl.pallas_call(
        functools.partial(forward_kernel, heads, experts, capacity),
        out_shape=(
            shape((4, local, 2 * width), f32),
            shape((experts, width, units), bf16),
            shape((experts, width, units), bf16),
            shape((width, experts * units), bf16),
            shape((local, features), f32),
            shape((local, features), f32),
            shape((local, experts), f32),
            shape((local, 1), f32),
            shape((4, local, hd), bf16),
            shape((4, local, hd), bf16),
            shape((8, local, 2 * hd), bf16),
            shape((4, heads, local, 128), f32),
            shape((4, local, features), bf16),
            shape((features, 3 * hd), bf16),
            shape((features, features), bf16),
            shape((experts + 8, features), f32),
        ),
        in_specs=[vm] * 6 + [sm] + [vm] * 5 + [hbm] * 2,
        out_specs=(vm, hbm, hbm, hbm) + (vm,) * 12,
        scratch_shapes=[
            V((1, tokens), jnp.int32),
            V((experts, width, units), bf16), V((experts, width, units), bf16),
            V((32, local, width), bf16), V((4, local, width), bf16),
            V((32, local, width + 64), bf16), V((4, local, width + 64), bf16),
            V((experts, capacity, width), bf16),
            V((experts, capacity, units), bf16), V((experts, capacity, units), bf16), V((experts, capacity, units), bf16),
            V((KEEP, capacity, width + 64), bf16),
            V((experts, capacity, units), bf16), V((experts, capacity, units), bf16),
            V((2, 4, width, 4 * cols), bf16), V((8, 4, width, cols), bf16), V((4, experts + 8, width), f32),
            V((4, local, hd), bf16),
            V((groups, GROUP, half, 2 * width), bf16), V((groups, 3, half, 2 * width), bf16),
            V((4, local, 2 * width), bf16), V((3, local, 2 * width), bf16),
        ] + [dma((n,)) for n in (4, experts, experts, experts, experts, experts, experts, experts, experts, 2, 2)]
        + [dma((3,))] * 8
        + [dma((n,)) for n in (3, 3, 4, 4, 3, 3, 3, 3, 4, 4, 3, 3, 3, 3, 3, 3, 3, 3)]
        + [dma((4, 3)), dma((4, 3)), dma((4, 4)), dma((4, 4))] * 2
        + [dma((groups,)), dma((groups,)), dma((groups, 3)), dma((groups, 3)), dma((groups, 3)), dma((groups, 3)),
           dma((groups, 4)), dma((groups, 4))],
        compiler_params=pltpu.CompilerParams(
            collective_id=collective_id, has_side_effects=True, vmem_limit_bytes=64 * 2**20),
        cost_estimate=pl.CostEstimate(flops=25 * 10**9, bytes_accessed=50 * 10**6, transcendentals=4 * 10**6),
    )(x_in, gain1, wq, wk, wv, wout, table, wr, gain2, doc_row, choice_row, grad_out, w_hidden, w_back)


HIGH = lax.Precision.HIGHEST


def back_kernel(heads, experts,
                x_ref, gain1_ref, grad_ref, choice_row, doc_row, table_ref,
                hidden_ref, normed_ref, router_ref, gate_ref, at_ref, q_ref, kv_ref, lse_ref, xb_ref,
                wqkv_all, wout_all, small_all, ret_ref, gb_hbm,
                out_ref, gin_ref, wgrad_ref, small_out, tail_out, nb_hbm,
                bias_ref, ag_ref, dq_ref, dk_ref, dv_ref, near_ref, go_ref, fg_ref, top_ref,
                one_ref, two_ref, in_ref, half_ref, nat_ref,
                sp_out, sp_in, sc_out, sc_in, sz_out, sz_in,
                kv_out, kv_in, kv_sum, fg_out, fg_in, wp_out, wp_in, wz_out, wz_in,
                tp_out, tp_in, tc_out, tc_in, tz_out, tz_in,
                in_sem, nat_sem,
                ag_s, ag_r, sp_s, sp_r, sc_s, sc_r, sz_s, sz_r, kv_s, kv_r, fg_s, fg_r, wp_s, wp_r,
                tp_s, tp_r, tc_s, tc_r, tz_s, tz_r, wz_s, wz_r):
    me = Place()
    gx, gy, core, chip = me.gx, me.gy, me.core, me.chip
    local, features = x_ref.shape
    width = features // 4
    hd = q_ref.shape[2]
    cols = hd // 2
    seq = 8 * local
    spans = gb_hbm.shape[2] // 128

    barrier = pltpu.get_barrier_semaphore()
    friends = [me.on_line(k) for k in range(3)] + [me.on_plane(k) for k in range(3)] + [me.pair]
    for device in friends:
        pl.semaphore_signal(barrier, inc=1, device_id=device, device_id_type=MESH)

    work = [(gb_hbm, nb_hbm, g) for g in range(spans)]

    def load(i):
        at = work[i][0].at[:, :, work[i][2] * 128:(work[i][2] + 1) * 128]
        return pltpu.make_async_copy(at, in_ref, in_sem.at[0])

    def store(i, q):
        at = work[i][1].at[:, work[i][2] * 4096 + q * 1024:work[i][2] * 4096 + (q + 1) * 1024]
        return pltpu.make_async_copy(nat_ref.at[q], at, nat_sem.at[q])

    def turn_span(i):
        load(i).wait()
        for r in range(8):
            block = jnp.concatenate([in_ref[4 * r + n] for n in range(4)], axis=1)
            moved = nn(block, two_ref[...]).astype(bf16)
            for q in range(4):
                half_ref[q, :, r * 128:(r + 1) * 128] = moved[:, q * 128:(q + 1) * 128]
        if i + 1 < len(work):
            load(i + 1).start()
        for q in range(4):
            if i > 0:
                store(i - 1, q).wait()
            nat_ref[q] = nn(half_ref[q], one_ref[...]).astype(bf16)
            store(i, q).start()

    load(0).start()
    hidden = hidden_ref[...]
    r2 = lax.rsqrt(jnp.mean(hidden * hidden, axis=-1, keepdims=True) + epsilon)
    grads = grad_ref[...].astype(f32)
    gate = gate_ref[...]
    routed = jnp.concatenate([ret_ref[z][:, :width] for z in range(4)], axis=1)
    back = jnp.concatenate([ret_ref[z][:, width:] for z in range(4)], axis=1)
    out_ref[...] = hidden + gate * routed
    gate_grad = jnp.sum(grads * routed, axis=-1, keepdims=True)
    router = router_ref[...]
    own_tokens = pl.ds(pl.multiple_of((gx * 8 + gy) * local, local), local)
    picked = (as_column(choice_row[:, own_tokens])
              == lax.broadcasted_iota(jnp.int32, router.shape, 1).astype(f32)).astype(f32)
    logit_grad = router * (gate_grad * picked - gate * gate_grad)
    second = back + jnp.dot(logit_grad, small_all[:experts, :], precision=HIGH, preferred_element_type=f32)
    gained = second * small_all[experts:experts + 1, :]
    dot2 = jnp.sum(gained * hidden, axis=-1, keepdims=True)
    hidden_grad = grads + r2 * gained - hidden * (r2 * r2 * r2) * (dot2 / features)
    gin_ref[...] = hidden_grad
    ag_ref[chip] = hidden_grad.astype(bf16)
    pl.semaphore_wait(barrier, len(friends))

    def ag_plane(k):
        return remote(ag_ref.at[chip], ag_ref.at[chip], ag_s.at[k], ag_r.at[k], me.on_plane(k))

    for k in range(3):
        ag_plane(k).start()

    routed_grad = lax.dot_general(logit_grad, normed_ref[...], (((0,), (0,)), ((), ())), precision=HIGH,
                                  preferred_element_type=f32)
    norm2 = jnp.sum(second * hidden * r2, axis=0, keepdims=True)
    sp_out[...] = jnp.concatenate([routed_grad, norm2, jnp.zeros((7, features), f32)], axis=0)
    small_pair = remote(sp_out, sp_in, sp_s.at[0], sp_r.at[0], me.pair)
    small_pair.start()

    def small_plane(k):
        return remote(sc_out, sc_in.at[k], sc_s.at[k], sc_r.at[k], me.on_plane(k))

    def small_line(k):
        return remote(sz_out.at[me.line[k]], sz_in.at[k], sz_s.at[k], sz_r.at[k], me.on_line(k))

    fill_bias(bias_ref, table_ref, chip, heads)
    dk_ref[...] = jnp.zeros_like(dk_ref)
    dv_ref[...] = jnp.zeros_like(dv_ref)
    near_ref[...] = jnp.zeros_like(near_ref)
    scale = HSIZE ** (-0.5)
    lanes = lax.broadcasted_iota(jnp.int32, (local, hd), 1) // HSIZE

    def attend_block(c, fresh):
        block_at = 2 * c + core
        allowed = allowed_pairs(doc_row, block_at, local)
        keys = kv_ref[:, :, :hd].reshape(seq, hd)
        values = kv_ref[:, :, hd:].reshape(seq, hd)
        att_grad = nn(ag_ref[c], wout_own).astype(bf16)
        part_o = tn(at_ref[c], ag_ref[c])
        go_ref[...] = part_o if fresh else go_ref[...] + part_o
        q_block = q_ref[c]
        q_turn = jnp.transpose(q_block.astype(f32)).astype(bf16)
        g_turn = jnp.transpose(att_grad.astype(f32)).astype(bf16)
        dq = jnp.zeros((local, hd), f32)
        for h in range(heads):
            scores = unit_scores(q_block, keys, bias_ref, h, block_at, allowed)
            probs = jnp.exp(scores - lse_ref[c, h][:, :1])
            masked = jnp.where(lanes == h, att_grad, jnp.zeros_like(att_grad))
            prob_grad = nt(masked, values)
            weighted = probs * prob_grad
            score_grad = (weighted - probs * jnp.sum(weighted, axis=-1, keepdims=True)).astype(bf16)
            part = slice(h * HSIZE, (h + 1) * HSIZE)
            dv_ref[part, :] += nn(g_turn[part, :], probs.astype(bf16))
            dk_ref[part, :] += nn(q_turn[part, :], score_grad)
            dq = jnp.where(lanes == h, nn(score_grad, keys), dq)
            start = pl.multiple_of(seq - local * block_at, local)
            near_ref[h, :, pl.ds(start, seq)] += score_grad.astype(f32)
        dq_ref[c] = (dq * scale).astype(bf16)

    own_pieces = [wout_all[:, n * hd:(n + 1) * hd] for n in range(4)]
    wout_own = own_pieces[3]
    for n in range(3):
        wout_own = jnp.where(chip == n, own_pieces[n], wout_own)

    attend_block(chip, True)
    small_pair.wait_recv()
    sc_out[...] = sp_out[...] + sp_in[...]
    for k in range(3):
        small_plane(k).start()
    fill_moves(one_ref, two_ref, False)
    for k in range(3):
        ag_plane(k).wait_recv()
        attend_block(me.chips_from[k], False)
        if k == 0:
            total = sc_out[...]
            for j in range(3):
                small_plane(j).wait_recv()
                total = total + sc_in[j]
            for z in range(4):
                sz_out[z] = total[:, z * width:(z + 1) * width]
            for j in range(3):
                small_line(j).start()

    both = jnp.concatenate([dk_ref[...], dv_ref[...]], axis=0)
    for j in range(8):
        turned = jnp.transpose(both[:, j * local:(j + 1) * local])

        @pl.when(core == j % 2)
        def _():
            kv_sum[j // 2] = turned

        @pl.when(core != j % 2)
        def _():
            kv_out[j // 2] = turned.astype(bf16)
    kv_pair = remote(kv_out, kv_in, kv_s.at[0], kv_r.at[0], me.pair)
    kv_pair.start()

    def xn_block(c):
        xc = xb_ref[c].astype(f32)
        return xc * lax.rsqrt(jnp.mean(xc * xc, axis=-1, keepdims=True) + epsilon)

    xr = [xn_block(c) for c in range(4)]
    xn = jnp.concatenate([(v * gain1_ref[...]).astype(bf16) for v in xr], axis=0)

    def packed(value, z):
        top, mid, bottom = z * width, z * width + width // 2, (z + 1) * width
        return jnp.concatenate([value[top:mid], value[mid:bottom]], axis=1)

    def w_pair(p):
        return remote(wp_out.at[p], wp_in.at[p], wp_s.at[p], wp_r.at[p], me.pair)

    def w_line(p, k):
        return remote(wz_out.at[p, me.line[k]], wz_in.at[p, k], wz_s.at[p, k], wz_r.at[p, k], me.on_line(k))

    def weight_part(p, a, b):
        halves = [jnp.concatenate([a[:, j * cols:(j + 1) * cols], b[:, j * cols:(j + 1) * cols]], axis=1)
                  for j in range(2)]
        other = jnp.where(core == 0, halves[1], halves[0]).astype(bf16)
        own = jnp.where(core == 0, halves[0], halves[1])
        for z in range(4):
            wp_out[p, z] = packed(other, z)
        w_pair(p).start()
        return own

    def weight_line(p, own):
        w_pair(p).wait_recv()
        for z in range(4):
            wz_out[p, z] = (packed(own, z) + wp_in[p, z].astype(f32)).astype(bf16)
        for k in range(3):
            w_line(p, k).start()

    queries = jnp.concatenate([dq_ref[c] for c in range(4)], axis=0)
    own_0 = weight_part(0, tn(xn, queries), jnp.transpose(go_ref[...]))
    kv_pair.wait_recv()
    keyval = [(kv_sum[c] + kv_in[c].astype(f32)).astype(bf16) for c in range(4)]

    def fg_plane(k):
        return remote(fg_out.at[me.chips[k]], fg_in.at[k], fg_s.at[k], fg_r.at[k], me.on_plane(k))

    norm1 = jnp.zeros((1, features), f32)
    for k in range(4):
        c = me.chips[k] if k < 3 else chip
        both = jnp.concatenate([dq_ref[c], (kv_sum[c] + kv_in[c].astype(f32)).astype(bf16)], axis=1)
        part = nt(both, wqkv_all[...])
        xc = xb_ref[c].astype(f32)
        r1 = lax.rsqrt(jnp.mean(xc * xc, axis=-1, keepdims=True) + epsilon)
        norm1 = norm1 + jnp.sum(part * (xc * r1), axis=0, keepdims=True)
        if k < 3:
            fg_out[c] = part.astype(bf16)
            fg_plane(k).start()
        else:
            fg_ref[...] = part
    weight_line(0, own_0)

    buckets = near_buckets(local)
    table = jnp.zeros((experts, 128), f32)
    lane = lax.broadcasted_iota(jnp.int32, (experts, 128), 1)
    row = lax.broadcasted_iota(jnp.int32, (experts, 1), 0)
    for h in range(heads):
        close = near_ref[h, :, seq - local:seq + 2 * local]
        for b in range(experts):
            top_ref[b:b + 1, :] = jnp.sum(jnp.where(buckets == b, close, 0.0), axis=0, keepdims=True)
        column = jnp.sum(top_ref[...], axis=1, keepdims=True)
        left = jnp.sum(near_ref[h, :, :seq - local])
        right = jnp.sum(near_ref[h, :, seq + 2 * local:])
        column = column + jnp.where(row == 15, left, 0.0) + jnp.where(row == 31, right, 0.0)
        table = jnp.where(lane == chip * heads + h, column, table)

    tp_out[...] = jnp.concatenate(
        [table] + [norm1[:, n * 128:(n + 1) * 128] for n in range(6)] + [jnp.zeros((2, 128), f32)], axis=0)
    t_pair = remote(tp_out, tp_in, tp_s.at[0], tp_r.at[0], me.pair)
    t_pair.start()

    def t_plane(k):
        return remote(tc_out, tc_in.at[k], tc_s.at[k], tc_r.at[k], me.on_plane(k))

    def t_line(k):
        return remote(tz_out, tz_in.at[k], tz_s.at[k], tz_r.at[k], me.on_line(k))

    keyvals = jnp.concatenate(keyval, axis=0)
    grads_kv = tn(xn, keyvals)
    own_1 = weight_part(1, grads_kv[:, :hd], grads_kv[:, hd:])
    t_pair.wait_recv()
    tc_out[...] = tp_out[...] + tp_in[...]
    for k in range(3):
        t_plane(k).start()
    weight_line(1, own_1)
    turn_span(0)
    for k in range(3):
        t_plane(k).wait_recv()
    tail = jnp.zeros((40, 128), f32)
    for c in range(4):
        part = jnp.where(chip == c, tc_out[...], 0.0)
        for k in range(3):
            part = jnp.where(me.chips_from[k] == c, tc_in[k], part)
        tail = tail + part
    tz_out[...] = tail
    for k in range(3):
        t_line(k).start()
    turn_span(1)

    first = fg_ref[...]
    for k in range(3):
        fg_plane(k).wait_recv()
        first = first + fg_in[k].astype(f32)
    x = x_ref[...].astype(f32)
    r1 = lax.rsqrt(jnp.mean(x * x, axis=-1, keepdims=True) + epsilon)
    gained1 = first * gain1_ref[...]
    dot1 = jnp.sum(gained1 * x, axis=-1, keepdims=True)
    gin_ref[...] = gin_ref[...] + r1 * gained1 - x * (r1 * r1 * r1) * (dot1 / features)

    total = sz_out[gx]
    for k in range(3):
        small_line(k).wait_recv()
        total = total + sz_in[k]
    small_out[...] = total
    turn_span(2)
    for p in range(2):
        total = wz_out[p, gx].astype(f32)
        for k in range(3):
            w_line(p, k).wait_recv()
            total = total + wz_in[p, k].astype(f32)
        wgrad_ref[p] = total
    for k in range(3):
        t_line(k).wait_recv()
    tail = jnp.zeros((40, 128), f32)
    for z in range(4):
        part = jnp.where(gx == z, tz_out[...], 0.0)
        for k in range(3):
            part = jnp.where(me.line_from[k] == z, tz_in[k], part)
        tail = tail + part
    tail_out[...] = tail
    for q in range(4):
        store(len(work) - 1, q).wait()
    for copy in (small_pair, kv_pair, t_pair):
        copy.wait_send()
    for p in range(2):
        w_pair(p).wait_send()
        for k in range(3):
            w_line(p, k).wait_send()
    for k in range(3):
        for copy in (ag_plane, small_plane, small_line, fg_plane, t_plane, t_line):
            copy(k).wait_send()


def back_pass(x_in, gain1, grad_out, choice_row, doc_row, table, saved, returned, gb, collective_id):
    local, features = x_in.shape
    width = features // 4
    hidden, normed, router, gate, attended, queries, keyvals, lse, xb, wqkv, wout, small = saved
    experts, _, units = gb.shape
    hd = queries.shape[2]
    cols = hd // 2
    heads = hd // HSIZE
    seq = 8 * local
    rows = small.shape[0]
    vm = pl.BlockSpec(memory_space=pltpu.VMEM)
    sm = pl.BlockSpec(memory_space=pltpu.SMEM)
    hbm = pl.BlockSpec(memory_space=pl.ANY)
    dma = pltpu.SemaphoreType.DMA
    shape = jax.ShapeDtypeStruct
    V = pltpu.VMEM
    return pl.pallas_call(
        functools.partial(back_kernel, heads, experts),
        out_shape=(
            shape((local, features), f32),
            shape((local, features), f32),
            shape((2, width // 2, 4 * cols), f32),
            shape((rows, width), f32),
            shape((40, 128), f32),
            shape((width, experts * units), bf16),
        ),
        in_specs=[vm] * 5 + [sm] + [vm] * 13 + [hbm],
        out_specs=(vm,) * 5 + (hbm,),
        scratch_shapes=[
            V((heads, local, 16 * local), f32),
            V((4, local, features), bf16), V((4, local, hd), bf16), V((hd, seq), f32), V((hd, seq), f32),
            V((heads, local, 2 * seq), f32), V((hd, features), f32), V((local, features), f32),
            V((experts, 3 * local), f32),
            V((1024, 1024), bf16), V((512, 512), bf16), V((experts, width, 128), bf16), V((4, width, 1024), bf16),
            V((4, width, 1024), bf16),
            V((rows, features), f32), V((rows, features), f32), V((rows, features), f32), V((3, rows, features), f32),
            V((4, rows, width), f32), V((3, rows, width), f32),
            V((4, local, 2 * hd), bf16), V((4, local, 2 * hd), bf16), V((4, local, 2 * hd), f32),
            V((4, local, features), bf16), V((3, local, features), bf16),
            V((2, 4, width // 2, 4 * cols), bf16), V((2, 4, width // 2, 4 * cols), bf16),
            V((2, 4, width // 2, 4 * cols), bf16), V((2, 3, width // 2, 4 * cols), bf16),
            V((40, 128), f32), V((40, 128), f32), V((40, 128), f32), V((3, 40, 128), f32),
            V((40, 128), f32), V((3, 40, 128), f32),
        ] + [dma((n,)) for n in (1, 4, 3, 3, 1, 1, 3, 3, 3, 3, 1, 1, 3, 3, 2, 2, 1, 1, 3, 3, 3, 3)]
        + [dma((2, 3)), dma((2, 3))],
        compiler_params=pltpu.CompilerParams(
            collective_id=collective_id, has_side_effects=True, vmem_limit_bytes=62 * 2**20),
        cost_estimate=pl.CostEstimate(flops=20 * 10**9, bytes_accessed=40 * 10**6, transcendentals=2 * 10**6),
    )(x_in, gain1, grad_out, choice_row, doc_row, table, hidden, normed, router, gate, attended, queries, keyvals, lse,
      xb, wqkv, wout, small, returned, gb)


def finish_kernel(heads, experts,
                  out_ref, gin_ref, wgrad_ref, small_ref, tail_ref, nh_hbm, nb_hbm,
                  out_to, gin_to, norm1_to, query_to, key_to, value_to, table_to, proj_to, norm2_to, router_to,
                  hidden_to, back_to,
                  in_ref, nat_ref, in_sem, nat_sem):
    width, cols = query_to.shape
    span = in_ref.shape[2]
    count = nh_hbm.shape[1] // span
    work = [(nh_hbm, hidden_to, g) for g in range(count)] + [(nb_hbm, back_to, g) for g in range(count)]
    ring = in_ref.shape[0]

    def load(i):
        source, _, g = work[i]
        return pltpu.make_async_copy(source.at[:, g * span:(g + 1) * span], in_ref.at[i % ring], in_sem.at[i % ring])

    def store(i):
        _, target, g = work[i]
        return pltpu.make_async_copy(nat_ref.at[i % ring], target.at[:, g * span:(g + 1) * span], nat_sem.at[i % ring])

    for i in range(ring):
        load(i).start()
    out_to[...] = out_ref[...]
    gin_to[...] = gin_ref[...]
    for n in range(6):
        norm1_to[:, n * 128:(n + 1) * 128] = tail_ref[experts + n:experts + n + 1, :]
    parts = []
    for p in range(2):
        rows = wgrad_ref[p]
        parts.append(jnp.concatenate([rows[:, :2 * cols], rows[:, 2 * cols:]], axis=0))
    query_to[...] = parts[0][:, :cols]
    proj_to[...] = jnp.transpose(parts[0])[cols:]
    key_to[...] = parts[1][:, :cols]
    value_to[...] = parts[1][:, cols:]
    table_to[...] = jnp.transpose(jnp.concatenate([tail_ref[:experts, :], jnp.zeros((128 - experts, 128), f32)], axis=0)
                                  )[:heads, :experts]
    norm2_to[...] = small_ref[experts:experts + 1, :]
    router_to[...] = small_ref[:experts, :]
    for i in range(len(work)):
        load(i).wait()
        if i >= ring:
            store(i - ring).wait()
        nat_ref[i % ring] = in_ref[i % ring].astype(f32)
        store(i).start()
        if i + ring < len(work):
            load(i + ring).start()
    for i in range(len(work) - ring, len(work)):
        store(i).wait()


def finish(out_rows, gin, wgrad, small, tail, nh, nb, heads):
    width, natural = nh.shape
    local, features = out_rows.shape
    cols = wgrad.shape[2] // 4
    experts = EXPERTS
    vm = pl.BlockSpec(memory_space=pltpu.VMEM)
    hbm = pl.BlockSpec(memory_space=pl.ANY)
    dma = pltpu.SemaphoreType.DMA
    shape = lambda *dims: jax.ShapeDtypeStruct(dims, f32)
    V = pltpu.VMEM
    ring, span = 4, 2048
    return pl.pallas_call(
        functools.partial(finish_kernel, heads, experts),
        out_shape=(
            shape(local, features), shape(local, features), shape(1, features),
            shape(width, cols), shape(width, cols), shape(width, cols), shape(heads, experts), shape(cols, width),
            shape(1, width), shape(experts, width), shape(width, natural), shape(width, natural),
        ),
        in_specs=[vm] * 5 + [hbm] * 2,
        out_specs=(vm,) * 10 + (hbm,) * 2,
        scratch_shapes=[V((ring, width, span), bf16), V((ring, width, span), f32), dma((ring,)), dma((ring,))],
        compiler_params=pltpu.CompilerParams(vmem_limit_bytes=63 * 2**20),
        cost_estimate=pl.CostEstimate(flops=10**7, bytes_accessed=30 * 10**6, transcendentals=0),
    )(out_rows, gin, wgrad, small, tail, nh, nb)


def fits(mesh):
    return mesh.shape["gx"] == 4 and mesh.shape["gy"] == 8


def fast(
    x_in,
    norm1_gain,
    w_query,
    w_key,
    w_value,
    relative_bias_table,
    w_out,
    norm2_gain,
    w_router,
    w_hidden,
    w_back,
    expert_choice,
    doc_ids,
    grad_out,
):
    gain_row = norm1_gain[None, :]
    choice_row, doc_row = expert_choice[None, :], doc_ids[None, :]
    table = relative_bias_table.T
    returned, _, back_grads, natural_hidden, *saved = forward_pass(
        x_in,
        gain_row,
        w_query,
        w_key,
        w_value,
        w_out,
        table,
        w_router.T,
        norm2_gain[None, :],
        doc_row,
        choice_row,
        grad_out,
        w_hidden,
        w_back,
        1,
    )
    *results, natural_back = back_pass(
        x_in,
        gain_row,
        grad_out,
        choice_row,
        doc_row,
        table,
        saved,
        returned,
        back_grads,
        2,
    )
    (
        out_rows,
        input_rows,
        grad_norm1,
        grad_query,
        grad_key,
        grad_value,
        grad_table,
        grad_out_proj,
        grad_norm2,
        grad_router,
        grad_hidden,
        grad_back,
    ) = finish(*results, natural_hidden, natural_back, table.shape[0])
    return (
        out_rows,
        input_rows,
        grad_norm1[0],
        grad_query,
        grad_key,
        grad_value,
        grad_table.T,
        grad_out_proj,
        grad_norm2[0],
        grad_router.T,
        grad_hidden,
        grad_back,
    )


def solution(mesh):
    return jax.shard_map(
        fast if fits(mesh) else local,
        mesh=mesh,
        in_specs=(
            P(("gx", "gy"), None),
            P(),
            P("gx", "gy"),
            P("gx", "gy"),
            P("gx", "gy"),
            P(),
            P("gy", "gx"),
            P("gx"),
            P("gx", None),
            P("gx", "gy"),
            P("gx", "gy"),
            P(),
            P("gx"),
            P(("gx", "gy"), None),
        ),
        out_specs=(
            P(("gx", "gy"), None),
            P(("gx", "gy"), None),
            P(),
            P("gx", "gy"),
            P("gx", "gy"),
            P("gx", "gy"),
            P(),
            P("gy", "gx"),
            P("gx"),
            P("gx", None),
            P("gx", "gy"),
            P("gx", "gy"),
        ),
        check_vma=False,
    )
```

```python
import functools
import math

import jax
import jax.numpy as jnp
from jax import lax
from jax.experimental import pallas as pl
from jax.experimental.pallas import tpu as pltpu
from jax.sharding import PartitionSpec as P

D = 768
HEADS = 12
HSIZE = 64
EXPERTS = 32
WINDOW = 1024


epsilon = 1e-06
far_steps = (12, 16, 23, 32, 46, 64, 91)
highest = lax.Precision.HIGHEST


def passed_along(value, axis, steps):
    count = lax.axis_size(axis)
    first, last = (max(0, -steps), min(count, count - steps))
    return lax.ppermute(value, axis, [(source, source + steps) for source in range(first, last)])


def bucket_ids(offset):
    ahead_part = (offset > 0).astype(jnp.int32) * 16
    distance = jnp.abs(offset)
    far_part = 8 + sum(((distance >= threshold).astype(jnp.int32) for threshold in far_steps))
    return ahead_part + jnp.where(distance < 8, distance, far_part)


def width_total(values):
    return lax.psum(values, "gx")


def token_rows(block_part):
    return lax.all_gather(block_part, "gy", axis=0, tiled=True)


def width_rows(block_part):
    return lax.all_gather(block_part, "gx", axis=0, tiled=True)


def width_sums(term_fn, row_number):
    return lax.psum_scatter(
        term_fn(jnp.int32(0), lax.axis_size("gx") * row_number),
        "gx",
        scatter_dimension=0,
        tiled=True,
    )


def token_sums(term_fn, row_number):
    return lax.psum_scatter(
        term_fn(jnp.int32(0), lax.axis_size("gy") * row_number),
        "gy",
        scatter_dimension=0,
        tiled=True,
    )


def collect_window(own_pair, reach):
    window_parts = []
    for offset_step in range(-reach, reach + 1):
        if offset_step == 0:
            window_parts.append(own_pair)
        else:
            window_parts.append(passed_along(own_pair, "gy", -offset_step))
    return jnp.concatenate(window_parts, axis=0)


def return_window(partials, reach, head_rows):
    combined = partials[reach * head_rows : (reach + 1) * head_rows]
    for offset_step in range(-reach, reach + 1):
        if offset_step != 0:
            start = (offset_step + reach) * head_rows
            combined = combined + passed_along(
                partials[start : start + head_rows], "gy", offset_step
            )
    return combined


def head_scores(query_heads, key_heads, bias_terms, allowed, score_scale):
    raw_scores = jnp.einsum(
        "qhd,khd->hqk", query_heads, key_heads, preferred_element_type=jnp.float32
    )
    return jnp.where(allowed[None], raw_scores * score_scale + bias_terms, -1000000000.0)


def rows_cols(blocks, width_devs, token_devs):
    grid = blocks.reshape(width_devs, token_devs, blocks.shape[1], blocks.shape[2])
    return jnp.transpose(grid, (0, 2, 1, 3)).reshape(
        width_devs * blocks.shape[1], token_devs * blocks.shape[2]
    )


def cols_rows(blocks, width_devs, token_devs):
    grid = blocks.reshape(width_devs, token_devs, blocks.shape[1], blocks.shape[2])
    return jnp.transpose(grid, (1, 2, 0, 3)).reshape(
        token_devs * blocks.shape[1], width_devs * blocks.shape[2]
    )


def grid_rows_cols(complete, width_devs, token_devs):
    row_total, col_total = complete.shape
    grid = complete.reshape(
        width_devs, row_total // width_devs, token_devs, col_total // token_devs
    )
    return jnp.transpose(grid, (0, 2, 1, 3)).reshape(
        width_devs * token_devs, row_total // width_devs, col_total // token_devs
    )


def grid_cols_rows(complete, width_devs, token_devs):
    row_total, col_total = complete.shape
    grid = complete.reshape(
        token_devs, row_total // token_devs, width_devs, col_total // width_devs
    )
    return jnp.transpose(grid, (2, 0, 1, 3)).reshape(
        width_devs * token_devs, row_total // token_devs, col_total // width_devs
    )


def spread_rows(partial_sum, column, group_count):
    picked_row = (jnp.arange(group_count, dtype=jnp.int32) == column).astype(jnp.float32)
    return picked_row.reshape((group_count,) + (1,) * partial_sum.ndim) * partial_sum[None]


def take_rows(table, index):
    return jnp.take(table, index, axis=0, mode="fill", fill_value=0)


def local(
    x_in,
    norm1_gain,
    w_query,
    w_key,
    w_value,
    relative_bias_table,
    w_out,
    norm2_gain,
    w_router,
    w_hidden,
    w_back,
    expert_choice,
    doc_ids,
    grad_out,
):
    token_devs = lax.axis_size("gy")
    width_devs = lax.axis_size("gx")
    member = lax.axis_index("gy")
    column = lax.axis_index("gx")
    local_count = x_in.shape[0]
    width_cols = w_router.shape[0]
    own_rows = local_count * width_devs
    all_tokens = own_rows * token_devs
    seq_len = local_count * token_devs
    experts = EXPERTS
    capacity = all_tokens * 5 // (4 * experts)
    score_scale = HSIZE ** (-0.5)
    reach = min((WINDOW + local_count - 2) // local_count, token_devs - 1)
    key_count = (2 * reach + 1) * local_count
    whole_weights = (
        lax.all_gather(w_query[None], ("gx", "gy"), axis=0, tiled=True),
        lax.all_gather(w_key[None], ("gx", "gy"), axis=0, tiled=True),
        lax.all_gather(w_value[None], ("gx", "gy"), axis=0, tiled=True),
        lax.all_gather(w_out[None], ("gx", "gy"), axis=0, tiled=True),
    )
    qkv_full = jnp.concatenate(
        [
            rows_cols(whole_weights[0], width_devs, token_devs),
            rows_cols(whole_weights[1], width_devs, token_devs),
            rows_cols(whole_weights[2], width_devs, token_devs),
        ],
        axis=1,
    )
    out_full = cols_rows(whole_weights[3], width_devs, token_devs)
    head_width = out_full.shape[0]
    inputs_row = x_in.astype(jnp.float32)
    scale_first = lax.rsqrt(jnp.mean(inputs_row * inputs_row, axis=-1, keepdims=True) + epsilon)
    normed_first = (inputs_row * scale_first * norm1_gain).astype(jnp.bfloat16)
    qkv_rows = jnp.dot(normed_first, qkv_full, preferred_element_type=jnp.float32).astype(
        jnp.bfloat16
    )
    query_heads = qkv_rows[:, :head_width].reshape(local_count, HEADS, HSIZE)
    pair_window = collect_window(
        qkv_rows[:, head_width:].reshape(local_count, 2, head_width), reach
    )
    key_heads = pair_window[:, 0].reshape(key_count, HEADS, HSIZE)
    value_heads = pair_window[:, 1].reshape(key_count, HEADS, HSIZE)
    query_pos = member * local_count + jnp.arange(local_count, dtype=jnp.int32)
    key_pos = (member - reach) * local_count + jnp.arange(key_count, dtype=jnp.int32)
    offset = key_pos[None, :] - query_pos[:, None]
    buckets = bucket_ids(offset)
    bias_terms = jnp.take(jnp.transpose(relative_bias_table), buckets, axis=1)
    no_doc = jnp.full((reach * local_count,), -1, jnp.int32)
    doc_padded = jnp.concatenate([no_doc, doc_ids, no_doc], axis=0)
    key_docs = lax.dynamic_slice_in_dim(doc_padded, member * local_count, key_count, 0)
    query_docs = lax.dynamic_slice_in_dim(doc_ids, member * local_count, local_count, 0)
    allowed = (jnp.abs(offset) < WINDOW) & (query_docs[:, None] == key_docs[None, :])
    attention_scores = head_scores(query_heads, key_heads, bias_terms, allowed, score_scale)
    row_peak = jnp.max(attention_scores, axis=-1, keepdims=True)
    shifted = jnp.exp(attention_scores - row_peak)
    row_sum = jnp.sum(shifted, axis=-1, keepdims=True)
    log_total = row_peak + jnp.log(row_sum)
    weights_reduced_precision = (shifted / row_sum).astype(jnp.bfloat16)
    attended = jnp.einsum(
        "hqk,khd->qhd", weights_reduced_precision, value_heads, preferred_element_type=jnp.float32
    )
    attended_low = attended.reshape(local_count, head_width).astype(jnp.bfloat16)
    attn_low = jnp.dot(attended_low, out_full, preferred_element_type=jnp.float32).astype(
        jnp.bfloat16
    )
    arrived = lax.all_to_all(
        jnp.stack([x_in, attn_low, grad_out], axis=1), "gx", split_axis=2, concat_axis=0, tiled=True
    )
    inputs = arrived[:, 0].astype(jnp.float32)
    grad_rows = arrived[:, 2].astype(jnp.float32)
    hidden_first = inputs + arrived[:, 1].astype(jnp.float32)
    scale_second = lax.rsqrt(
        width_total(jnp.sum(hidden_first * hidden_first, axis=-1)) / D + epsilon
    )[:, None]
    normed_second = hidden_first * scale_second * norm2_gain
    logits = width_total(jnp.dot(normed_second, w_router, precision=highest))
    router = jax.nn.softmax(logits, axis=-1)
    expert_iota = jnp.arange(experts, dtype=jnp.int32)
    tok_block = math.gcd(all_tokens, 128)
    block_count = all_tokens // tok_block
    chosen_rows = expert_iota[:, None] == expert_choice[None, :]
    chosen_low = chosen_rows.astype(jnp.bfloat16).reshape(experts, block_count, tok_block)
    block_iota = jnp.arange(tok_block, dtype=jnp.int32)
    upper = (block_iota[:, None] <= block_iota[None, :]).astype(jnp.bfloat16)
    inside_count = jnp.einsum("ebi,ij->ebj", chosen_low, upper, preferred_element_type=jnp.float32)
    block_totals = inside_count[:, :, tok_block - 1]
    earlier_blocks = jnp.cumsum(block_totals, axis=1) - block_totals
    counted = (inside_count + earlier_blocks[:, :, None]).reshape(experts, all_tokens)
    position = (jnp.sum(jnp.where(chosen_rows, counted, 0.0), axis=0) - 1.0).astype(jnp.int32)
    kept_all = position < capacity
    slot_all = jnp.where(kept_all, expert_choice * capacity + position, experts * capacity)
    source = (
        jnp.full((experts * capacity + 1,), all_tokens, jnp.int32)
        .at[slot_all]
        .set(jnp.arange(all_tokens, dtype=jnp.int32))[: experts * capacity]
    )
    source_seq = source // seq_len
    source_inner = source % seq_len
    source_rows = jnp.where(
        source < all_tokens,
        source_inner // local_count * own_rows
        + source_seq * local_count
        + source_inner % local_count,
        all_tokens,
    )
    row_iota = jnp.arange(all_tokens, dtype=jnp.int32)
    global_of_row = (
        row_iota // local_count % width_devs * seq_len
        + row_iota // own_rows * local_count
        + row_iota % local_count
    )
    slot_rows = jnp.take(slot_all, global_of_row)
    own_global = lax.dynamic_slice_in_dim(global_of_row, member * own_rows, own_rows, 0)
    picked_mine = jnp.take(expert_choice, own_global)[:, None] == expert_iota[None, :]
    gate_value = jnp.sum(jnp.where(picked_mine, router, 0.0), axis=-1)
    second_rows = token_rows(normed_second.astype(jnp.bfloat16))
    hidden_weight = jnp.transpose(w_hidden.reshape(width_cols, -1, experts), (2, 0, 1))
    back_weight = jnp.transpose(w_back.reshape(width_cols, -1, experts), (2, 1, 0))
    expert_rows = experts // width_devs
    slot_in = take_rows(second_rows, source_rows).reshape(experts, capacity, width_cols)

    def hidden_term(first_row, row_count):
        return jnp.einsum(
            "ecd,edf->ecf", slot_in, hidden_weight, preferred_element_type=jnp.float32
        )

    pre_block = width_sums(hidden_term, expert_rows)
    act_rows = width_rows(jax.nn.gelu(pre_block).astype(jnp.bfloat16))
    expert_out = jnp.einsum(
        "ecf,efd->ecd", act_rows, back_weight, preferred_element_type=jnp.float32
    ).reshape(experts * capacity, width_cols)

    def route_term(first_row, row_count):
        return take_rows(expert_out, slot_rows)

    routed = token_sums(route_term, own_rows)
    block_out = hidden_first + gate_value[:, None] * routed
    gate_grad = width_total(jnp.sum(grad_rows * routed, axis=-1))
    route_rows = token_rows((grad_rows * gate_value[:, None]).astype(jnp.bfloat16))
    gelu_pair = jax.vjp(jax.nn.gelu, pre_block)
    slot_grad = take_rows(route_rows, source_rows).reshape(experts, capacity, width_cols)
    back_grads = jnp.einsum("ecf,ecd->efd", act_rows, slot_grad, preferred_element_type=jnp.float32)

    def act_term(first_row, row_count):
        return jnp.einsum(
            "ecd,efd->ecf", slot_grad, back_weight, preferred_element_type=jnp.float32
        )

    act_grad = width_sums(act_term, expert_rows)
    pre_rows = width_rows(gelu_pair[1](act_grad)[0].astype(jnp.bfloat16))
    hidden_gradient_rows = jnp.einsum(
        "ecd,ecf->edf", slot_in, pre_rows, preferred_element_type=jnp.float32
    )
    slot_in_grad = jnp.einsum(
        "ecf,edf->ecd", pre_rows, hidden_weight, preferred_element_type=jnp.float32
    ).reshape(experts * capacity, width_cols)

    def back_route_term(first_row, row_count):
        return take_rows(slot_in_grad, slot_rows)

    back_routed = token_sums(back_route_term, own_rows)
    grad_hidden = jnp.transpose(hidden_gradient_rows, (1, 2, 0)).reshape(width_cols, -1)
    grad_back = jnp.transpose(back_grads, (2, 1, 0)).reshape(width_cols, -1)
    logit_grad = router * (
        gate_grad[:, None] * picked_mine.astype(jnp.float32) - (gate_value * gate_grad)[:, None]
    )
    second_grad = back_routed + jnp.einsum("re,de->rd", logit_grad, w_router, precision=highest)
    router_part = jnp.einsum("rd,re->de", normed_second, logit_grad, precision=highest)
    norm2_part = jnp.sum(second_grad * hidden_first * scale_second, axis=0)
    gained_second = second_grad * norm2_gain
    row_dot_second = width_total(jnp.sum(gained_second * hidden_first, axis=-1))[:, None]
    hidden_grad = (
        grad_rows
        + scale_second * gained_second
        - hidden_first * scale_second**3 * row_dot_second / D
    )
    out_rows, hidden_rows = (
        lax.all_to_all(block_out, "gx", split_axis=0, concat_axis=1, tiled=True),
        lax.all_to_all(hidden_grad, "gx", split_axis=0, concat_axis=1, tiled=True),
    )
    attn_grad = hidden_rows.astype(jnp.bfloat16)
    grad_out_full = jnp.einsum(
        "rf,rd->fd", attended_low, attn_grad, preferred_element_type=jnp.float32
    )
    attended_grad = (
        jnp.einsum("rd,fd->rf", attn_grad, out_full, preferred_element_type=jnp.float32)
        .astype(jnp.bfloat16)
        .reshape(local_count, HEADS, HSIZE)
    )
    scores_again = head_scores(query_heads, key_heads, bias_terms, allowed, score_scale)
    probs_again = jnp.exp(scores_again - log_total)
    value_grad = jnp.einsum(
        "hqk,qhd->khd",
        probs_again.astype(jnp.bfloat16),
        attended_grad,
        preferred_element_type=jnp.float32,
    )
    prob_grad = jnp.einsum(
        "qhd,khd->hqk", attended_grad, value_heads, preferred_element_type=jnp.float32
    )
    score_gradient = (
        probs_again * (prob_grad - jnp.sum(probs_again * prob_grad, axis=-1, keepdims=True))
    ).astype(jnp.bfloat16)
    query_grad = (
        jnp.einsum("hqk,khd->qhd", score_gradient, key_heads, preferred_element_type=jnp.float32)
        * score_scale
    ).astype(jnp.bfloat16)
    key_grad = (
        jnp.einsum("hqk,qhd->khd", score_gradient, query_heads, preferred_element_type=jnp.float32)
        * score_scale
    )
    band_low = max(0, reach * local_count - 90)
    band_high = min(key_count, reach * local_count + local_count + 90)
    bucket_iota = jnp.arange(relative_bias_table.shape[0], dtype=jnp.int32)
    band_onehot = (buckets[None, :, band_low:band_high] == bucket_iota[:, None, None]).astype(
        jnp.bfloat16
    )
    table_near = jnp.einsum(
        "ivt,zvt->zi",
        score_gradient[:, :, band_low:band_high],
        band_onehot,
        preferred_element_type=jnp.float32,
    )
    left_far = jnp.sum(score_gradient[:, :, :band_low].astype(jnp.float32), axis=(1, 2))
    right_far = jnp.sum(score_gradient[:, :, band_high:].astype(jnp.float32), axis=(1, 2))
    table_part = (
        table_near
        + (bucket_iota == 15).astype(jnp.float32)[:, None] * left_far[None, :]
        + (bucket_iota == 31).astype(jnp.float32)[:, None] * right_far[None, :]
    )
    pair_grads = return_window(
        jnp.stack(
            [key_grad.reshape(key_count, head_width), value_grad.reshape(key_count, head_width)],
            axis=1,
        ),
        reach,
        local_count,
    )
    qkv_grad = jnp.concatenate(
        [
            query_grad.reshape(local_count, head_width),
            pair_grads.astype(jnp.bfloat16).reshape(local_count, 2 * head_width),
        ],
        axis=1,
    )
    qkv_grads = jnp.einsum("rd,rc->dc", normed_first, qkv_grad, preferred_element_type=jnp.float32)
    first_grad = jnp.einsum("rc,dc->rd", qkv_grad, qkv_full, preferred_element_type=jnp.float32)
    norm1_part = jnp.sum(first_grad * inputs_row * scale_first, axis=0)
    gained_first = first_grad * norm1_gain
    row_dot_first = jnp.sum(gained_first * inputs_row, axis=-1, keepdims=True)
    input_rows = (
        hidden_rows + scale_first * gained_first - inputs_row * scale_first**3 * row_dot_first / D
    )
    summed = lax.psum(
        (
            norm1_part,
            table_part,
            spread_rows(norm2_part, column, width_devs),
            spread_rows(router_part, column, width_devs),
        ),
        ("gx", "gy"),
    )
    grad_norm1 = summed[0]
    grad_table = summed[1]
    grad_norm2 = lax.dynamic_index_in_dim(summed[2], column, 0, keepdims=False)
    grad_router = lax.dynamic_index_in_dim(summed[3], column, 0, keepdims=False)
    weight_parts = (
        lax.psum_scatter(
            grid_rows_cols(qkv_grads[:, :head_width], width_devs, token_devs),
            ("gx", "gy"),
            scatter_dimension=0,
            tiled=True,
        ),
        lax.psum_scatter(
            grid_rows_cols(qkv_grads[:, head_width : 2 * head_width], width_devs, token_devs),
            ("gx", "gy"),
            scatter_dimension=0,
            tiled=True,
        ),
        lax.psum_scatter(
            grid_rows_cols(qkv_grads[:, 2 * head_width :], width_devs, token_devs),
            ("gx", "gy"),
            scatter_dimension=0,
            tiled=True,
        ),
        lax.psum_scatter(
            grid_cols_rows(grad_out_full, width_devs, token_devs),
            ("gx", "gy"),
            scatter_dimension=0,
            tiled=True,
        ),
    )
    return (
        out_rows,
        input_rows,
        grad_norm1,
        weight_parts[0][0],
        weight_parts[1][0],
        weight_parts[2][0],
        grad_table,
        weight_parts[3][0],
        grad_norm2,
        grad_router,
        grad_hidden,
        grad_back,
    )


MESH = pl.DeviceIdType.MESH
GELU_C = math.sqrt(2.0 / math.pi)
f32, bf16 = jnp.float32, jnp.bfloat16


def nn(a, b):
    return jnp.dot(a, b, preferred_element_type=f32)


def nt(a, b):
    return lax.dot_general(a, b, (((1,), (1,)), ((), ())), preferred_element_type=f32)


def tn(a, b):
    return lax.dot_general(a, b, (((0,), (0,)), ((), ())), preferred_element_type=f32)


def remote(src, dst, send_sem, recv_sem, device):
    return pltpu.make_async_remote_copy(
        src_ref=src, dst_ref=dst, send_sem=send_sem, recv_sem=recv_sem,
        device_id=device, device_id_type=MESH)


class Place:
    def __init__(self):
        self.gx, self.gy = lax.axis_index("gx"), lax.axis_index("gy")
        self.core, self.chip = lax.rem(self.gy, 2), self.gy // 2
        self.pair = (self.gx, self.gy + 1 - 2 * self.core)
        self.line = [lax.rem(self.gx + k, 4) for k in (1, 2, 3)]
        self.chips = [lax.rem(self.chip + k, 4) for k in (1, 2, 3)]
        self.line_from = [lax.rem(self.gx + 4 - k, 4) for k in (1, 2, 3)]
        self.chips_from = [lax.rem(self.chip + 4 - k, 4) for k in (1, 2, 3)]
        self.is_mid = jnp.logical_and(self.gx > 0, self.gx < 3)
        self.is_end = jnp.logical_not(self.is_mid)
        self.mid = (jnp.where(self.gx < 2, 1, 2), self.gy)
        self.other_mid = (jnp.where(self.gx < 2, 2, 1), self.gy)
        self.end = (jnp.where(self.gx < 2, 0, 3), self.gy)

    def on_line(self, k):
        return (self.line[k], self.gy)

    def on_plane(self, k):
        return (self.gx, 2 * self.chips[k] + self.core)

    def greet_all(self):
        devices = [self.on_line(k) for k in range(3)] + [self.on_plane(k) for k in range(3)] + [self.pair]
        barrier = pltpu.get_barrier_semaphore()
        for device in devices:
            pl.semaphore_signal(barrier, inc=1, device_id=device, device_id_type=MESH)
        pl.semaphore_wait(barrier, len(devices))


def as_column(row):
    n = row.shape[1]
    same = lax.broadcasted_iota(jnp.int32, (n, n), 0) == lax.broadcasted_iota(jnp.int32, (n, n), 1)
    return jnp.sum(jnp.where(same, row.astype(f32), 0.0), axis=1, keepdims=True)


def pick_rows(slot_row, base, capacity, rows_ref, tokens):
    kblock = 1024
    ids = lax.broadcasted_iota(jnp.int32, (capacity, kblock), 0) + base
    total = None
    for kb in range(tokens // kblock):
        hot = (slot_row[:, kb * kblock:(kb + 1) * kblock] == ids).astype(f32).astype(bf16)
        part = nn(hot, rows_ref[kb * kblock:(kb + 1) * kblock, :])
        total = part if total is None else total + part
    return total


class LineSum:
    def __init__(self, me, own, got, other, own_sem, got_sem, other_sem, out_sem, experts):
        self.me, self.own, self.got, self.other = me, own, got, other
        self.sems = (own_sem, got_sem, other_sem, out_sem)
        self.ring, self.experts = own.shape[0], experts

    def to_mid(self, e):
        sl = lax.rem(e, self.ring)
        return remote(self.own.at[sl], self.got.at[e], self.sems[0].at[sl], self.sems[1].at[e], self.me.mid)

    def across(self, e):
        sl = lax.rem(e, self.ring)
        return remote(self.own.at[sl], self.other.at[e], self.sems[0].at[sl], self.sems[2].at[e], self.me.other_mid)

    def to_end(self, e):
        return remote(self.got.at[e], self.got.at[e], self.sems[3].at[e], self.sems[1].at[e], self.me.end)

    def put(self, e, value):
        self.own[lax.rem(e, self.ring)] = value

    def valid(self, e):
        return jnp.logical_and(e >= 0, e < self.experts)

    def send(self, e):
        @pl.when(jnp.logical_and(self.me.is_end, self.valid(e)))
        def _():
            @pl.when(e >= PACE)
            def _():
                self.to_mid(e - PACE).wait_send()
            self.to_mid(e).start()

    def half(self, e):
        @pl.when(jnp.logical_and(self.me.is_mid, self.valid(e)))
        def _():
            sl = lax.rem(e + self.ring, self.ring)
            self.to_mid(e).wait_recv()
            self.own[sl] = (self.own[sl].astype(f32) + self.got[e].astype(f32)).astype(bf16)

            @pl.when(e >= PACE)
            def _():
                self.across(e - PACE).wait_send()
            self.across(e).start()

    def whole(self, e):
        @pl.when(jnp.logical_and(self.me.is_mid, self.valid(e)))
        def _():
            sl = lax.rem(e + self.ring, self.ring)
            self.across(e).wait_recv()
            self.got[e] = (self.own[sl].astype(f32) + self.other[e].astype(f32)).astype(bf16)

            @pl.when(e >= PACE)
            def _():
                self.to_end(e - PACE).wait_send()
            self.to_end(e).start()

    def tick(self, t):
        self.send(t)
        self.half(t - LAG_B)
        self.whole(t - LAG_C)

    def await_total(self, e):
        @pl.when(self.me.is_end)
        def _():
            self.to_end(e).wait_recv()

    def drain(self):
        for e in range(self.experts - PACE, self.experts):
            @pl.when(self.me.is_end)
            def _():
                self.to_mid(e).wait_send()

            @pl.when(self.me.is_mid)
            def _():
                self.across(e).wait_send()
                self.to_end(e).wait_send()


RING = 8
GROUP = 4
LAG_B, LAG_C, LAG_D = 2, 4, 6
PACE = 2


class LineGather:
    def __init__(self, me, slot, right_s, right_r, left_s, left_r):
        self.me, self.slot = me, slot
        self.sems = (right_s, right_r, left_s, left_r)

    def right(self, h):
        at = self.slot(jnp.maximum(self.me.gx - h, 0))
        return remote(at, at, self.sems[0].at[h], self.sems[1].at[h], (jnp.minimum(self.me.gx + 1, 3), self.me.gy))

    def left(self, h):
        at = self.slot(jnp.minimum(self.me.gx + h, 3))
        return remote(at, at, self.sems[2].at[h], self.sems[3].at[h], (jnp.maximum(self.me.gx - 1, 0), self.me.gy))

    def from_left(self, h):
        at = self.slot(jnp.maximum(self.me.gx - 1 - h, 0))
        return remote(at, at, self.sems[0].at[h], self.sems[1].at[h], (jnp.maximum(self.me.gx - 1, 0), self.me.gy))

    def from_right(self, h):
        at = self.slot(jnp.minimum(self.me.gx + 1 + h, 3))
        return remote(at, at, self.sems[2].at[h], self.sems[3].at[h], (jnp.minimum(self.me.gx + 1, 3), self.me.gy))

    def sends(self, h):
        gx = self.me.gx
        return jnp.logical_and(gx < 3, gx >= h), jnp.logical_and(gx > 0, gx + h <= 3)

    def start(self):
        self.pass_on(0)

    def pass_on(self, h):
        go_right, go_left = self.sends(h)

        @pl.when(go_right)
        def _():
            self.right(h).start()

        @pl.when(go_left)
        def _():
            self.left(h).start()

    def receive(self, h):
        @pl.when(self.me.gx >= h + 1)
        def _():
            self.from_left(h).wait_recv()

        @pl.when(self.me.gx + h + 1 <= 3)
        def _():
            self.from_right(h).wait_recv()
        if h < 2:
            self.pass_on(h + 1)

    def drain(self):
        for h in range(3):
            go_right, go_left = self.sends(h)

            @pl.when(go_right)
            def _():
                self.right(h).wait_send()

            @pl.when(go_left)
            def _():
                self.left(h).wait_send()


def place_one(lane):
    register, unit, expert = lane // 128, lax.rem(lane // 32, 4), lax.rem(lane, 32)
    return expert // 4 * 128 + lax.rem(expert, 4) * 32 + register * 4 + unit


def place_two(lane):
    register, expert, unit = lane // 128, lax.rem(lane // 32, 4), lax.rem(lane, 32)
    return expert * 128 + register * 32 + unit


def fill_moves(one_ref, two_ref, inward):
    for ref, place in ((one_ref, place_one), (two_ref, place_two)):
        n = ref.shape[0]
        if inward:
            moved = place(lax.broadcasted_iota(jnp.int32, (n, 1), 0))
            ref[...] = (moved == lax.broadcasted_iota(jnp.int32, (n, n), 1)).astype(f32).astype(bf16)
        else:
            moved = place(lax.broadcasted_iota(jnp.int32, (1, n), 1))
            ref[...] = (moved == lax.broadcasted_iota(jnp.int32, (n, n), 0)).astype(f32).astype(bf16)


def near_buckets(rows):
    offset = (
        lax.broadcasted_iota(jnp.int32, (rows, 3 * rows), 1)
        - rows
        - lax.broadcasted_iota(jnp.int32, (rows, 3 * rows), 0)
    )
    return bucket_ids(offset)


def fill_bias(bias_ref, table_ref, chip, heads):
    rows = bias_ref.shape[1]
    span = bias_ref.shape[2]
    mid = span // 2
    buckets = near_buckets(rows)
    for h in range(heads):
        column = chip * heads + h
        near = jnp.zeros(buckets.shape, f32)
        for b in range(table_ref.shape[1]):
            near = jnp.where(buckets == b, table_ref[column, b], near)
        bias_ref[h, :, 0:mid - rows] = jnp.full((rows, mid - rows), table_ref[column, 15], f32)
        bias_ref[h, :, mid - rows:mid + 2 * rows] = near
        bias_ref[h, :, mid + 2 * rows:] = jnp.full((rows, span - mid - 2 * rows), table_ref[column, 31], f32)


def allowed_pairs(doc_row, block_at, local):
    start = pl.multiple_of(block_at * local, local)
    return as_column(doc_row[:, pl.ds(start, local)]) == doc_row[...].astype(f32)


def unit_scores(q_block, keys, bias_ref, h, block_at, allowed):
    rows = q_block.shape[0]
    seq = keys.shape[0]
    lanes = lax.broadcasted_iota(jnp.int32, q_block.shape, 1) // HSIZE
    masked = jnp.where(lanes == h, q_block, jnp.zeros_like(q_block))
    start = pl.multiple_of(seq - rows * block_at, rows)
    return jnp.where(allowed, nt(masked, keys) + bias_ref[h, :, pl.ds(start, seq)], -1000000000.0)


def fill_slots(slot_ref, choice_row, experts, capacity):
    tokens = choice_row.shape[1]
    expert = lax.broadcasted_iota(jnp.int32, (experts, 128), 0)
    upper = (lax.broadcasted_iota(jnp.int32, (128, 128), 0)
             <= lax.broadcasted_iota(jnp.int32, (128, 128), 1)).astype(f32).astype(bf16)
    before = jnp.zeros((experts, 1), f32)
    for b in range(tokens // 128):
        choice = choice_row[:, b * 128:(b + 1) * 128]
        chosen = (expert == choice).astype(f32)
        count = nn(chosen.astype(bf16), upper)
        place = jnp.sum(chosen * (count + before), axis=0, keepdims=True).astype(jnp.int32) - 1
        slot_ref[:, b * 128:(b + 1) * 128] = jnp.where(place < capacity, choice * capacity + place, -1)
        before = before + count[:, 127:128]


POINTS = (2, 2, 2, 2, 2, 0, 2, 2, 2, 4, 1)
AHEAD = 4
KEEP = 12


class BlockRows:
    def __init__(self, ref):
        self.ref = ref

    def __getitem__(self, at):
        rows = at[0]
        size = self.ref.shape[1]
        part = self.ref[rows.start // size:rows.stop // size]
        return part.reshape(rows.stop - rows.start, self.ref.shape[2])


class Dispatch:
    def __init__(self, me, out, dst, line_s, line_r, plane_s, plane_r, pair_s, pair_r):
        self.me, self.out, self.dst = me, out, dst
        self.sems = (line_s, line_r, plane_s, plane_r, pair_s, pair_r)
        self.zs = [me.gx] + me.line_from

    def line(self, k):
        at = self.dst.at[self.me.gx * 8 + self.me.gy]
        return remote(self.out.at[self.me.line[k]], at, self.sems[0].at[k], self.sems[1].at[k], self.me.on_line(k))

    def plane(self, m, k):
        at = self.dst.at[self.zs[m] * 8 + self.me.gy]
        return remote(at, at, self.sems[2].at[m, k], self.sems[3].at[m, k], self.me.on_plane(k))

    def pair(self, m, k):
        c = self.me.chip if k == 0 else self.me.chips_from[k - 1]
        at = self.dst.at[self.zs[m] * 8 + 2 * c + self.me.core]
        return remote(at, at, self.sems[4].at[m, k], self.sems[5].at[m, k], self.me.pair)

    def start(self):
        for k in range(3):
            self.line(k).start()

    def spread(self, m):
        if m > 0:
            self.line(m - 1).wait_recv()
        for k in range(3):
            self.plane(m, k).start()
        self.pair(m, 0).start()

    def share(self, m):
        for k in range(3):
            self.plane(m, k).wait_recv()
            self.pair(m, k + 1).start()

    def arrive(self):
        for m in range(4):
            for k in range(4):
                self.pair(m, k).wait_recv()

    def drain(self):
        for m in range(4):
            for k in range(4):
                self.pair(m, k).wait_send()
            for k in range(3):
                self.plane(m, k).wait_send()
        for k in range(3):
            self.line(k).wait_send()


def forward_kernel(heads, experts, capacity,
                   x_ref, gain1_ref, wq_ref, wk_ref, wv_ref, wout_ref, table_ref, wr_ref, gain2_ref, doc_row,
                   choice_row, grad_ref, wh_hbm, wb_hbm,
                   out_ref, gh_hbm, gb_hbm, nh_hbm,
                   hidden_ref, normed_ref, router_ref, gate_ref, at_ref, q_ref, kv_ref, lse_ref, xb_ref,
                   wqkv_all, wout_all, small_all,
                   slot_ref, w1_ref, w2_ref, g_ref, g_out, rows_ref, rows_out, gs_ref,
                   own_ref, ag_ref, other_ref, xs_ref, got_ref, other2_ref,
                   wq_st, wo_st, sm_st, at_in, y_in, s_in, line_out, line_in,
                   nat_sem, own_sem, got_sem, other_sem, t_sem, p_sem, got2_sem, other2_sem, t2_sem, gh_sem, gb_sem,
                   wqr_s, wqr_r, wql_s, wql_r, smr_s, smr_r, sml_s, sml_r,
                   xb_s, xb_r, wqp_s, wqp_r, woc_s, woc_r, wop_s, wop_r, kv_s, kv_r, at_s, at_r,
                   gz_s, gz_r, rz_s, rz_r, lo_s, lo_r, gc_s, gc_r, gp_s, gp_r, rc_s, rc_r, rp_s, rp_r,
                   yo_s, yo_r, so_s, so_r, ya_s, ya_r, yp_s, yp_r):
    me = Place()
    gx, gy, core, chip = me.gx, me.gy, me.core, me.chip
    width, cols = wq_ref.shape
    local = x_ref.shape[0]
    tokens = 32 * local
    units = wh_hbm.shape[1] // experts
    hd = 2 * cols
    seq = 8 * local
    zs = [gx] + me.line_from
    spans = units // 128
    scale = HSIZE ** (-0.5)
    half = capacity // 2
    groups = experts // GROUP
    yt_ref = other_ref

    give = Dispatch(me, g_out, g_ref, gz_s, gz_r, gc_s, gc_r, gp_s, gp_r)
    rows = Dispatch(me, rows_out, rows_ref, rz_s, rz_r, rc_s, rc_r, rp_s, rp_r)
    acts = LineSum(me, own_ref, ag_ref, other_ref, own_sem, got_sem, other_sem, t_sem, experts)
    pres = LineSum(me, own_ref, got_ref, other2_ref, p_sem, got2_sem, other2_sem, t2_sem, experts)
    weights = LineGather(me, lambda z: wq_st.at[core, z], wqr_s, wqr_r, wql_s, wql_r)
    smalls = LineGather(me, lambda z: sm_st.at[z], smr_s, smr_r, sml_s, sml_r)

    def act_step(t):
        @pl.when(t < experts)
        def _():
            gs = pick_rows(slot_ref, t * capacity, capacity, BlockRows(g_ref), tokens).astype(bf16)
            gs_ref[t] = gs
            acts.put(t, nn(gs, w2_ref[t]).astype(bf16))
        acts.tick(t)

    done = [0]

    def ticks(count):
        def body(t, carry):
            act_step(t)
            return carry
        if count:
            lax.fori_loop(done[0], done[0] + count, body, 0)
        done[0] += count

    def xb_plane(k):
        return remote(xb_ref.at[chip], xb_ref.at[chip], xb_s.at[k], xb_r.at[k], me.on_plane(k))

    def wq_pair(k):
        at = wq_st.at[core, zs[k]]
        return remote(at, at, wqp_s.at[k], wqp_r.at[k], me.pair)

    def wo_plane(k):
        return remote(wo_st.at[gy], wo_st.at[gy], woc_s.at[k], woc_r.at[k], me.on_plane(k))

    def wo_pair(k):
        c = me.chips_from[k]
        return remote(wo_st.at[2 * c + core], wo_st.at[2 * c + core], wop_s.at[k], wop_r.at[k], me.pair)

    def kv_pair(c):
        return remote(kv_ref.at[2 * c + core], kv_ref.at[2 * c + core], kv_s.at[c], kv_r.at[c], me.pair)

    def at_plane(k):
        return remote(at_ref.at[me.chips[k]], at_in.at[chip], at_s.at[k], at_r.at[k], me.on_plane(k))

    def line_copy(k):
        return remote(line_out.at[me.line[k]], line_in.at[k], lo_s.at[k], lo_r.at[k], me.on_line(k))

    barrier = pltpu.get_barrier_semaphore()
    friends = [me.on_line(k) for k in range(3)] + [me.on_plane(k) for k in range(3)] + [me.pair]
    for device in friends:
        pl.semaphore_signal(barrier, inc=1, device_id=device, device_id_type=MESH)

    for z in range(4):
        g_out[z] = grad_ref[:, z * width:(z + 1) * width]
    xb_ref[chip] = x_ref[...]
    wq_st[core, gx] = jnp.concatenate(
        [wq_ref[...], wk_ref[...], wv_ref[...], jnp.transpose(wout_ref[...].astype(f32)).astype(bf16)], axis=1)
    sm_st[gx] = jnp.concatenate([wr_ref[...], gain2_ref[...], jnp.zeros((7, width), f32)], axis=0)
    g_ref[gx * 8 + gy] = g_out[gx]
    pl.semaphore_wait(barrier, len(friends))
    give.start()
    give.spread(0)
    for k in range(3):
        xb_plane(k).start()
    wq_pair(0).start()

    def front(bias_ref, nat_ref, half_ref, one_ref, two_ref):
        def load_span(source, g, q):
            at = source.at[:, pl.ds(pl.multiple_of(g * 4096 + q * 1024, 1024), 1024)]
            return pltpu.make_async_copy(at, nat_ref.at[q], nat_sem.at[q])

        def load_spans(source, g):
            for q in range(4):
                load_span(source, g, q).start()

        def turn_span(source, target, g, following):
            lanes = pl.ds(pl.multiple_of(g * 128, 128), 128)
            for q in range(4):
                load_span(source, g, q).wait()
                moved = nn(nat_ref[q], one_ref[...]).astype(bf16)
                for r in range(8):
                    half_ref[r, :, q * 128:(q + 1) * 128] = moved[:, r * 128:(r + 1) * 128]
            following()
            for r in range(8):
                moved = nn(half_ref[r], two_ref[...]).astype(bf16)
                for n in range(4):
                    target[4 * r + n, :, lanes] = moved[:, n * 128:(n + 1) * 128]

        load_spans(wb_hbm, 0)
        fill_moves(one_ref, two_ref, True)
        fill_slots(slot_ref, choice_row, experts, capacity)
        fill_bias(bias_ref, table_ref, chip, heads)
        for m in (1, 2, 3):
            give.spread(m)
        weights.start()
        smalls.start()
        for g in range(spans):
            turn_span(wb_hbm, w2_ref, g, lambda: load_spans(wb_hbm, g + 1) if g + 1 < spans else None)
            if g > 0:
                weights.receive(g - 1)
                smalls.receive(g - 1)
        give.share(0)
        for h in range(spans - 1, 3):
            weights.receive(h)
            smalls.receive(h)
        load_spans(wh_hbm, 0)
        for k in (1, 2, 3):
            wq_pair(k).start()
        for z in range(4):
            wo_st[gy, z] = wq_st[core, z][:, 3 * cols:]
        for m in (1, 2, 3):
            give.share(m)
        give.arrive()
        for k in range(3):
            wo_plane(k).start()
        ticks(POINTS[9])
        for k in range(4):
            wq_pair(k).wait_recv()
        for z in range(4):
            parts = [wq_st[0, z], wq_st[1, z]]
            wqkv_all[z * width:(z + 1) * width, :] = jnp.concatenate(
                [parts[j][:, n * cols:(n + 1) * cols] for n in range(3) for j in range(2)], axis=1)
            wo_st[gy + 1 - 2 * core, z] = wq_st[1 - core, z][:, 3 * cols:]

        for k in range(4):
            c = chip if k == 0 else me.chips_from[k - 1]
            if k > 0:
                xb_plane(k - 1).wait_recv()
            xc = xb_ref[c].astype(f32)
            r1 = lax.rsqrt(jnp.mean(xc * xc, axis=-1, keepdims=True) + epsilon)
            xn = (xc * r1 * gain1_ref[...].reshape(1, x_ref.shape[1])).astype(bf16)
            made = nn(xn, wqkv_all[...])
            q_ref[c] = (made[:, :hd].astype(bf16).astype(f32) * scale).astype(bf16)
            kv_ref[2 * c + core] = made[:, hd:].astype(bf16)
            kv_pair(c).start()
        ticks(POINTS[0])
        for c in range(4):
            kv_pair(c).wait_recv()
        lanes = lax.broadcasted_iota(jnp.int32, (local, hd), 1) // HSIZE
        for k in range(4):
            c = me.chips[k] if k < 3 else chip
            block_at = 2 * c + core
            allowed = allowed_pairs(doc_row, block_at, local)
            keys = kv_ref[:, :, :hd].reshape(seq, hd)
            values = kv_ref[:, :, hd:].reshape(seq, hd)
            total = jnp.zeros((local, hd), f32)
            for h in range(heads):
                scores = unit_scores(q_ref[c], keys, bias_ref, h, block_at, allowed)
                peak = jnp.max(scores, axis=-1, keepdims=True)
                shifted = jnp.exp(scores - peak)
                summed = jnp.sum(shifted, axis=-1, keepdims=True)
                lse_ref[c, h] = jnp.broadcast_to(peak + jnp.log(summed), (local, 128))
                low = (shifted * (1.0 / summed)).astype(bf16)
                total = jnp.where(lanes == h, nn(low, values), total)
            at_ref[c] = total.astype(bf16)
            if k < 3:
                at_plane(k).start()
            else:
                at_in[chip] = total.astype(bf16)
            ticks(POINTS[1 + k])
        for k in range(3):
            wo_plane(k).wait_recv()
            wo_pair(k).start()
        small_all[...] = jnp.concatenate([sm_st[z] for z in range(4)], axis=1)
        for k in range(3):
            wo_pair(k).wait_recv()
        for z in range(4):
            wout_all[z * width:(z + 1) * width, :] = jnp.concatenate([wo_st[g, z] for g in range(8)], axis=1)
        ticks(POINTS[10])
        for k in range(3):
            at_plane(k).wait_recv()
        attended = jnp.concatenate([at_in[c] for c in range(4)], axis=1)
        hidden = x_ref[...].astype(f32) + nt(attended, wout_all[...]).astype(bf16).astype(f32)
        hidden_ref[...] = hidden
        r2 = lax.rsqrt(jnp.mean(hidden * hidden, axis=-1, keepdims=True) + epsilon)
        normed = hidden * r2 * small_all[experts:experts + 1, :]
        normed_ref[...] = normed
        logits = lax.dot_general(normed, small_all[:experts, :], (((1,), (1,)), ((), ())),
                                 precision=lax.Precision.HIGHEST, preferred_element_type=f32)
        lifted = jnp.exp(logits - jnp.max(logits, axis=-1, keepdims=True))
        router = lifted / jnp.sum(lifted, axis=-1, keepdims=True)
        router_ref[...] = router
        own_tokens = pl.ds(pl.multiple_of((gx * 8 + gy) * local, local), local)
        picked = as_column(choice_row[:, own_tokens]) == lax.broadcasted_iota(jnp.int32, router.shape, 1).astype(f32)
        gate = jnp.sum(jnp.where(picked, router, 0.0), axis=-1, keepdims=True)
        gate_ref[...] = gate
        first = gate.astype(bf16).astype(f32)
        second = (gate - first).astype(bf16).astype(f32)
        third = gate - first - second
        lane = lax.broadcasted_iota(jnp.int32, (local, 64), 1)
        pieces = jnp.where(lane == 0, first, jnp.where(lane == 1, second, jnp.where(lane == 2, third, 0.0)))
        pieces = pieces.astype(bf16)
        low = normed.astype(bf16)
        for z in range(4):
            rows_out[z] = jnp.concatenate([low[:, z * width:(z + 1) * width], pieces], axis=1)
        rows.start()
        rows_ref[gx * 8 + gy] = rows_out[gx]
        rows.spread(0)
        ticks(POINTS[5])
        turn_span(wh_hbm, w1_ref, 0, lambda: load_spans(wh_hbm, 1))
        for m in (1, 2, 3):
            rows.spread(m)
        ticks(POINTS[6])
        for n in range(1, spans):
            turn_span(wh_hbm, w1_ref, n, lambda: load_spans(wh_hbm, n + 1) if n + 1 < spans else None)
            ticks(POINTS[7])
        for m in range(4):
            rows.share(m)
        ticks(POINTS[8])
        rows.arrive()

    V = pltpu.VMEM
    pl.run_scoped(front, V((heads, local, 16 * local), f32), V((4, width, 1024), bf16), V((8, width, 512), bf16),
                  V((1024, 1024), bf16), V((512, 512), bf16))
    first_left = done[0]

    def experts_part(y_own, y_out, s_out, gh_st, gb_st):
        def grad_copy(stage, target, sems, e):
            return pltpu.make_async_copy(stage.at[lax.rem(e, 2)], target.at[e], sems.at[lax.rem(e, 2)])

        def pair_half(j):
            return remote(y_out.at[j], y_in.at[j], yo_s.at[j], yo_r.at[j], me.pair)

        def to_owner(j, k):
            return remote(s_out.at[j, me.chips[k]], s_in.at[j, k], so_s.at[j, k], so_r.at[j, k], me.on_plane(k))

        own_half = pl.ds(pl.multiple_of(core * half, 16), half)

        def from_owner(j, k):
            at = yt_ref.at[j * GROUP + chip, own_half]
            return remote(at, at, ya_s.at[j, k], ya_r.at[j, k], me.on_plane(k))

        def pair_total(j, k):
            c = chip if k == 0 else me.chips_from[k - 1]
            at = yt_ref.at[j * GROUP + c, own_half]
            return remote(at, at, yp_s.at[j, k], yp_r.at[j, k], me.pair)

        def stage_two(j):
            pair_half(j).wait_recv()
            for m in range(GROUP):
                s_out[j, m] = (y_own[j, m].astype(f32) + y_in[j, m].astype(f32)).astype(bf16)
            for k in range(3):
                to_owner(j, k).start()

        def stage_three(j):
            total = s_out[j, chip].astype(f32)
            for k in range(3):
                to_owner(j, k).wait_recv()
                total = total + s_in[j, k].astype(f32)
            yt_ref[j * GROUP + chip, own_half] = total.astype(bf16)
            for k in range(3):
                from_owner(j, k).start()
            pair_total(j, 0).start()

        def stage_four(j):
            for k in range(3):
                from_owner(j, k).wait_recv()
                pair_total(j, k + 1).start()

        def step(t, carry):
            i = t - experts + AHEAD

            @pl.when(i == experts - PACE)
            def _():
                acts.drain()

            @pl.when(jnp.logical_and(i >= 0, i < experts))
            def _():
                xs = pick_rows(slot_ref, i * capacity, capacity, BlockRows(rows_ref), tokens).astype(bf16)
                xs_ref[lax.rem(i, KEEP)] = xs
                pres.put(i, nn(xs[:, :width], w1_ref[i]).astype(bf16))
            act_step(t)
            pres.tick(t - experts)
            e = t - experts - LAG_D

            @pl.when(e >= 0)
            def _():
                acts.await_total(e)
                pres.await_total(e)
                xs = xs_ref[lax.rem(e, KEEP)]
                pieces = xs[:, width:].astype(f32)
                gate = pieces[:, 0:1] + pieces[:, 1:2] + pieces[:, 2:3]
                u = got_ref[e].astype(f32)
                ag = gate * ag_ref[e].astype(f32)
                u2 = u * u
                th = jnp.tanh(GELU_C * (u + 0.044715 * (u2 * u)))
                part = 0.5 * (1.0 + th)
                act = (u * part).astype(bf16)
                dg = part + 0.5 * u * (1.0 - th * th) * (GELU_C * (1.0 + 3 * 0.044715 * u2))
                pg = (ag * dg).astype(bf16)
                y = jnp.concatenate([nt(act, w2_ref[e]), nt(pg, w1_ref[e])], axis=1).astype(bf16)
                j, m = e // GROUP, lax.rem(e, GROUP)

                @pl.when(core == 0)
                def _():
                    y_own[j, m] = y[:half]
                    y_out[j, m] = y[half:]

                @pl.when(core == 1)
                def _():
                    y_own[j, m] = y[half:]
                    y_out[j, m] = y[:half]

                @pl.when(m == GROUP - 1)
                def _():
                    pair_half(j).start()

                @pl.when(e >= 2)
                def _():
                    grad_copy(gh_st, gh_hbm, gh_sem, e - 2).wait()
                    grad_copy(gb_st, gb_hbm, gb_sem, e - 2).wait()
                slot_grad = (gate * gs_ref[e].astype(f32)).astype(bf16)
                gh_st[lax.rem(e, 2)] = tn(xs[:, :width], pg).astype(bf16)
                gb_st[lax.rem(e, 2)] = tn(slot_grad, act).astype(bf16)
                grad_copy(gh_st, gh_hbm, gh_sem, e).start()
                grad_copy(gb_st, gb_hbm, gb_sem, e).start()

                @pl.when(jnp.logical_and(m == 0, j >= 1))
                def _():
                    stage_two(j - 1)

                @pl.when(jnp.logical_and(m == 2, j >= 1))
                def _():
                    stage_three(j - 1)

                @pl.when(jnp.logical_and(m == 1, j >= 2))
                def _():
                    stage_four(j - 2)
            return carry

        lax.fori_loop(first_left, 2 * experts + LAG_D, step, 0)
        last = groups - 1
        stage_two(last)
        stage_four(last - 1)
        slots = [as_column(slot_ref[:, pl.ds(pl.multiple_of((z * 8 + gy) * 128, 128), 128)]) for z in range(4)]
        own_slots = jnp.concatenate(slots, axis=0).astype(jnp.int32)
        many = 8
        per = many // GROUP
        places = lax.broadcasted_iota(jnp.int32, (own_slots.shape[0], many * capacity), 1)

        def picked(b):
            hot = (own_slots == places + b * many * capacity).astype(f32).astype(bf16)
            return nn(hot, yt_ref[b * many:(b + 1) * many].reshape(many * capacity, 2 * width))

        total = None
        for b in range(experts // many - 1):
            for j in range(b * per, (b + 1) * per):
                for k in range(4):
                    pair_total(j, k).wait_recv()
            if b == 0:
                stage_three(last)
            part = picked(b)
            total = part if total is None else total + part
        stage_four(last)
        for j in range(groups - per, groups):
            for k in range(4):
                pair_total(j, k).wait_recv()
        total = total + picked(experts // many - 1)

        for z in range(4):
            line_out[z] = total[z * local:(z + 1) * local].astype(bf16)
        for k in range(3):
            line_copy(k).start()
        out_ref[gx] = line_out[gx].astype(f32)
        pres.drain()
        for e in (experts - 2, experts - 1):
            grad_copy(gh_st, gh_hbm, gh_sem, e).wait()
            grad_copy(gb_st, gb_hbm, gb_sem, e).wait()

        def sent(j, carry):
            pair_half(j).wait_send()
            for k in range(3):
                to_owner(j, k).wait_send()
                from_owner(j, k).wait_send()
            for k in range(4):
                pair_total(j, k).wait_send()
            return carry
        lax.fori_loop(0, groups, sent, 0)
        give.drain()
        rows.drain()
        weights.drain()
        smalls.drain()
        for k in range(3):
            for copy in (xb_plane, wo_plane, wo_pair, at_plane):
                copy(k).wait_send()
        for k in range(4):
            for copy in (wq_pair, kv_pair):
                copy(k).wait_send()

    def turn_part(one_ref, two_ref, in_ref, half_ref, nat_ref):
        def load(g):
            return pltpu.make_async_copy(gh_hbm.at[:, :, g * 128:(g + 1) * 128], in_ref, gh_sem.at[0])

        def store(g, q):
            at = nh_hbm.at[:, g * 4096 + q * 1024:g * 4096 + (q + 1) * 1024]
            return pltpu.make_async_copy(nat_ref.at[q], at, nat_sem.at[q])

        load(0).start()
        fill_moves(one_ref, two_ref, False)
        for g in range(spans):
            load(g).wait()
            for r in range(8):
                gathered = jnp.concatenate([in_ref[4 * r + n] for n in range(4)], axis=1)
                moved = nn(gathered, two_ref[...]).astype(bf16)
                for q in range(4):
                    half_ref[q, :, r * 128:(r + 1) * 128] = moved[:, q * 128:(q + 1) * 128]
            if g + 1 < spans:
                load(g + 1).start()
            for q in range(4):
                if g > 0:
                    store(g - 1, q).wait()
                nat_ref[q] = nn(half_ref[q], one_ref[...]).astype(bf16)
                store(g, q).start()
        for k in range(3):
            line_copy(k).wait_recv()
            out_ref[me.line_from[k]] = line_in[k].astype(f32)
        for k in range(3):
            line_copy(k).wait_send()
        for q in range(4):
            store(spans - 1, q).wait()

    block = (groups, GROUP, half, 2 * width)
    pl.run_scoped(experts_part, V(block, bf16), V(block, bf16), V(block, bf16),
                  V((2, width, units), bf16), V((2, width, units), bf16))
    pl.run_scoped(turn_part, V((1024, 1024), bf16), V((512, 512), bf16), V((experts, width, 128), bf16),
                  V((4, width, 1024), bf16), V((4, width, 1024), bf16))


def forward_pass(x_in, gain1, wq, wk, wv, wout, table, wr, gain2, doc_row, choice_row, grad_out, w_hidden, w_back,
                 collective_id):
    local, features = x_in.shape
    width, cols = wq.shape
    hd = 2 * cols
    heads = hd // HSIZE
    experts = wr.shape[0]
    tokens = choice_row.shape[1]
    capacity = tokens * 5 // (4 * experts)
    units = w_hidden.shape[1] // experts
    half = capacity // 2
    groups = experts // GROUP
    vm = pl.BlockSpec(memory_space=pltpu.VMEM)
    sm = pl.BlockSpec(memory_space=pltpu.SMEM)
    hbm = pl.BlockSpec(memory_space=pl.ANY)
    dma = pltpu.SemaphoreType.DMA
    shape = jax.ShapeDtypeStruct
    V = pltpu.VMEM
    return pl.pallas_call(
        functools.partial(forward_kernel, heads, experts, capacity),
        out_shape=(
            shape((4, local, 2 * width), f32),
            shape((experts, width, units), bf16),
            shape((experts, width, units), bf16),
            shape((width, experts * units), bf16),
            shape((local, features), f32),
            shape((local, features), f32),
            shape((local, experts), f32),
            shape((local, 1), f32),
            shape((4, local, hd), bf16),
            shape((4, local, hd), bf16),
            shape((8, local, 2 * hd), bf16),
            shape((4, heads, local, 128), f32),
            shape((4, local, features), bf16),
            shape((features, 3 * hd), bf16),
            shape((features, features), bf16),
            shape((experts + 8, features), f32),
        ),
        in_specs=[vm] * 6 + [sm] + [vm] * 5 + [hbm] * 2,
        out_specs=(vm, hbm, hbm, hbm) + (vm,) * 12,
        scratch_shapes=[
            V((1, tokens), jnp.int32),
            V((experts, width, units), bf16), V((experts, width, units), bf16),
            V((32, local, width), bf16), V((4, local, width), bf16),
            V((32, local, width + 64), bf16), V((4, local, width + 64), bf16),
            V((experts, capacity, width), bf16),
            V((experts, capacity, units), bf16), V((experts, capacity, units), bf16), V((experts, capacity, units), bf16),
            V((KEEP, capacity, width + 64), bf16),
            V((experts, capacity, units), bf16), V((experts, capacity, units), bf16),
            V((2, 4, width, 4 * cols), bf16), V((8, 4, width, cols), bf16), V((4, experts + 8, width), f32),
            V((4, local, hd), bf16),
            V((groups, GROUP, half, 2 * width), bf16), V((groups, 3, half, 2 * width), bf16),
            V((4, local, 2 * width), bf16), V((3, local, 2 * width), bf16),
        ] + [dma((n,)) for n in (4, experts, experts, experts, experts, experts, experts, experts, experts, 2, 2)]
        + [dma((3,))] * 8
        + [dma((n,)) for n in (3, 3, 4, 4, 3, 3, 3, 3, 4, 4, 3, 3, 3, 3, 3, 3, 3, 3)]
        + [dma((4, 3)), dma((4, 3)), dma((4, 4)), dma((4, 4))] * 2
        + [dma((groups,)), dma((groups,)), dma((groups, 3)), dma((groups, 3)), dma((groups, 3)), dma((groups, 3)),
           dma((groups, 4)), dma((groups, 4))],
        compiler_params=pltpu.CompilerParams(
            collective_id=collective_id, has_side_effects=True, vmem_limit_bytes=64 * 2**20),
        cost_estimate=pl.CostEstimate(flops=25 * 10**9, bytes_accessed=50 * 10**6, transcendentals=4 * 10**6),
    )(x_in, gain1, wq, wk, wv, wout, table, wr, gain2, doc_row, choice_row, grad_out, w_hidden, w_back)


HIGH = lax.Precision.HIGHEST


def back_kernel(heads, experts,
                x_ref, gain1_ref, grad_ref, choice_row, doc_row, table_ref,
                hidden_ref, normed_ref, router_ref, gate_ref, at_ref, q_ref, kv_ref, lse_ref, xb_ref,
                wqkv_all, wout_all, small_all, ret_ref, gb_hbm,
                out_ref, gin_ref, wgrad_ref, small_out, tail_out, nb_hbm,
                bias_ref, ag_ref, dq_ref, dk_ref, dv_ref, near_ref, go_ref, fg_ref, top_ref,
                one_ref, two_ref, in_ref, half_ref, nat_ref,
                sp_out, sp_in, sc_out, sc_in, sz_out, sz_in,
                kv_out, kv_in, kv_sum, fg_out, fg_in, wp_out, wp_in, wz_out, wz_in,
                tp_out, tp_in, tc_out, tc_in, tz_out, tz_in,
                in_sem, nat_sem,
                ag_s, ag_r, sp_s, sp_r, sc_s, sc_r, sz_s, sz_r, kv_s, kv_r, fg_s, fg_r, wp_s, wp_r,
                tp_s, tp_r, tc_s, tc_r, tz_s, tz_r, wz_s, wz_r):
    me = Place()
    gx, gy, core, chip = me.gx, me.gy, me.core, me.chip
    local, features = x_ref.shape
    width = features // 4
    hd = q_ref.shape[2]
    cols = hd // 2
    seq = 8 * local
    spans = gb_hbm.shape[2] // 128

    barrier = pltpu.get_barrier_semaphore()
    friends = [me.on_line(k) for k in range(3)] + [me.on_plane(k) for k in range(3)] + [me.pair]
    for device in friends:
        pl.semaphore_signal(barrier, inc=1, device_id=device, device_id_type=MESH)

    work = [(gb_hbm, nb_hbm, g) for g in range(spans)]

    def load(i):
        at = work[i][0].at[:, :, work[i][2] * 128:(work[i][2] + 1) * 128]
        return pltpu.make_async_copy(at, in_ref, in_sem.at[0])

    def store(i, q):
        at = work[i][1].at[:, work[i][2] * 4096 + q * 1024:work[i][2] * 4096 + (q + 1) * 1024]
        return pltpu.make_async_copy(nat_ref.at[q], at, nat_sem.at[q])

    def turn_span(i):
        load(i).wait()
        for r in range(8):
            block = jnp.concatenate([in_ref[4 * r + n] for n in range(4)], axis=1)
            moved = nn(block, two_ref[...]).astype(bf16)
            for q in range(4):
                half_ref[q, :, r * 128:(r + 1) * 128] = moved[:, q * 128:(q + 1) * 128]
        if i + 1 < len(work):
            load(i + 1).start()
        for q in range(4):
            if i > 0:
                store(i - 1, q).wait()
            nat_ref[q] = nn(half_ref[q], one_ref[...]).astype(bf16)
            store(i, q).start()

    load(0).start()
    hidden = hidden_ref[...]
    r2 = lax.rsqrt(jnp.mean(hidden * hidden, axis=-1, keepdims=True) + epsilon)
    grads = grad_ref[...].astype(f32)
    gate = gate_ref[...]
    routed = jnp.concatenate([ret_ref[z][:, :width] for z in range(4)], axis=1)
    back = jnp.concatenate([ret_ref[z][:, width:] for z in range(4)], axis=1)
    out_ref[...] = hidden + gate * routed
    gate_grad = jnp.sum(grads * routed, axis=-1, keepdims=True)
    router = router_ref[...]
    own_tokens = pl.ds(pl.multiple_of((gx * 8 + gy) * local, local), local)
    picked = (as_column(choice_row[:, own_tokens])
              == lax.broadcasted_iota(jnp.int32, router.shape, 1).astype(f32)).astype(f32)
    logit_grad = router * (gate_grad * picked - gate * gate_grad)
    second = back + jnp.dot(logit_grad, small_all[:experts, :], precision=HIGH, preferred_element_type=f32)
    gained = second * small_all[experts:experts + 1, :]
    dot2 = jnp.sum(gained * hidden, axis=-1, keepdims=True)
    hidden_grad = grads + r2 * gained - hidden * (r2 * r2 * r2) * (dot2 / features)
    gin_ref[...] = hidden_grad
    ag_ref[chip] = hidden_grad.astype(bf16)
    pl.semaphore_wait(barrier, len(friends))

    def ag_plane(k):
        return remote(ag_ref.at[chip], ag_ref.at[chip], ag_s.at[k], ag_r.at[k], me.on_plane(k))

    for k in range(3):
        ag_plane(k).start()

    routed_grad = lax.dot_general(logit_grad, normed_ref[...], (((0,), (0,)), ((), ())), precision=HIGH,
                                  preferred_element_type=f32)
    norm2 = jnp.sum(second * hidden * r2, axis=0, keepdims=True)
    sp_out[...] = jnp.concatenate([routed_grad, norm2, jnp.zeros((7, features), f32)], axis=0)
    small_pair = remote(sp_out, sp_in, sp_s.at[0], sp_r.at[0], me.pair)
    small_pair.start()

    def small_plane(k):
        return remote(sc_out, sc_in.at[k], sc_s.at[k], sc_r.at[k], me.on_plane(k))

    def small_line(k):
        return remote(sz_out.at[me.line[k]], sz_in.at[k], sz_s.at[k], sz_r.at[k], me.on_line(k))

    fill_bias(bias_ref, table_ref, chip, heads)
    dk_ref[...] = jnp.zeros_like(dk_ref)
    dv_ref[...] = jnp.zeros_like(dv_ref)
    near_ref[...] = jnp.zeros_like(near_ref)
    scale = HSIZE ** (-0.5)
    lanes = lax.broadcasted_iota(jnp.int32, (local, hd), 1) // HSIZE

    def attend_block(c, fresh):
        block_at = 2 * c + core
        allowed = allowed_pairs(doc_row, block_at, local)
        keys = kv_ref[:, :, :hd].reshape(seq, hd)
        values = kv_ref[:, :, hd:].reshape(seq, hd)
        att_grad = nn(ag_ref[c], wout_own).astype(bf16)
        part_o = tn(at_ref[c], ag_ref[c])
        go_ref[...] = part_o if fresh else go_ref[...] + part_o
        q_block = q_ref[c]
        q_turn = jnp.transpose(q_block.astype(f32)).astype(bf16)
        g_turn = jnp.transpose(att_grad.astype(f32)).astype(bf16)
        dq = jnp.zeros((local, hd), f32)
        for h in range(heads):
            scores = unit_scores(q_block, keys, bias_ref, h, block_at, allowed)
            probs = jnp.exp(scores - lse_ref[c, h][:, :1])
            masked = jnp.where(lanes == h, att_grad, jnp.zeros_like(att_grad))
            prob_grad = nt(masked, values)
            weighted = probs * prob_grad
            score_grad = (weighted - probs * jnp.sum(weighted, axis=-1, keepdims=True)).astype(bf16)
            part = slice(h * HSIZE, (h + 1) * HSIZE)
            dv_ref[part, :] += nn(g_turn[part, :], probs.astype(bf16))
            dk_ref[part, :] += nn(q_turn[part, :], score_grad)
            dq = jnp.where(lanes == h, nn(score_grad, keys), dq)
            start = pl.multiple_of(seq - local * block_at, local)
            near_ref[h, :, pl.ds(start, seq)] += score_grad.astype(f32)
        dq_ref[c] = (dq * scale).astype(bf16)

    own_pieces = [wout_all[:, n * hd:(n + 1) * hd] for n in range(4)]
    wout_own = own_pieces[3]
    for n in range(3):
        wout_own = jnp.where(chip == n, own_pieces[n], wout_own)

    attend_block(chip, True)
    small_pair.wait_recv()
    sc_out[...] = sp_out[...] + sp_in[...]
    for k in range(3):
        small_plane(k).start()
    fill_moves(one_ref, two_ref, False)
    for k in range(3):
        ag_plane(k).wait_recv()
        attend_block(me.chips_from[k], False)
        if k == 0:
            total = sc_out[...]
            for j in range(3):
                small_plane(j).wait_recv()
                total = total + sc_in[j]
            for z in range(4):
                sz_out[z] = total[:, z * width:(z + 1) * width]
            for j in range(3):
                small_line(j).start()

    both = jnp.concatenate([dk_ref[...], dv_ref[...]], axis=0)
    for j in range(8):
        turned = jnp.transpose(both[:, j * local:(j + 1) * local])

        @pl.when(core == j % 2)
        def _():
            kv_sum[j // 2] = turned

        @pl.when(core != j % 2)
        def _():
            kv_out[j // 2] = turned.astype(bf16)
    kv_pair = remote(kv_out, kv_in, kv_s.at[0], kv_r.at[0], me.pair)
    kv_pair.start()

    def xn_block(c):
        xc = xb_ref[c].astype(f32)
        return xc * lax.rsqrt(jnp.mean(xc * xc, axis=-1, keepdims=True) + epsilon)

    xr = [xn_block(c) for c in range(4)]
    xn = jnp.concatenate([(v * gain1_ref[...].reshape(1, features)).astype(bf16) for v in xr], axis=0)

    def packed(value, z):
        top, mid, bottom = z * width, z * width + width // 2, (z + 1) * width
        return jnp.concatenate([value[top:mid], value[mid:bottom]], axis=1)

    def w_pair(p):
        return remote(wp_out.at[p], wp_in.at[p], wp_s.at[p], wp_r.at[p], me.pair)

    def w_line(p, k):
        return remote(wz_out.at[p, me.line[k]], wz_in.at[p, k], wz_s.at[p, k], wz_r.at[p, k], me.on_line(k))

    def weight_part(p, a, b):
        halves = [jnp.concatenate([a[:, j * cols:(j + 1) * cols], b[:, j * cols:(j + 1) * cols]], axis=1)
                  for j in range(2)]
        other = jnp.where(core == 0, halves[1], halves[0]).astype(bf16)
        own = jnp.where(core == 0, halves[0], halves[1])
        for z in range(4):
            wp_out[p, z] = packed(other, z)
        w_pair(p).start()
        return own

    def weight_line(p, own):
        w_pair(p).wait_recv()
        for z in range(4):
            wz_out[p, z] = (packed(own, z) + wp_in[p, z].astype(f32)).astype(bf16)
        for k in range(3):
            w_line(p, k).start()

    queries = jnp.concatenate([dq_ref[c] for c in range(4)], axis=0)
    own_0 = weight_part(0, tn(xn, queries), jnp.transpose(go_ref[...]))
    kv_pair.wait_recv()
    keyval = [(kv_sum[c] + kv_in[c].astype(f32)).astype(bf16) for c in range(4)]

    def fg_plane(k):
        return remote(fg_out.at[me.chips[k]], fg_in.at[k], fg_s.at[k], fg_r.at[k], me.on_plane(k))

    norm1 = jnp.zeros((1, features), f32)
    for k in range(4):
        c = me.chips[k] if k < 3 else chip
        both = jnp.concatenate([dq_ref[c], (kv_sum[c] + kv_in[c].astype(f32)).astype(bf16)], axis=1)
        part = nt(both, wqkv_all[...])
        xc = xb_ref[c].astype(f32)
        r1 = lax.rsqrt(jnp.mean(xc * xc, axis=-1, keepdims=True) + epsilon)
        norm1 = norm1 + jnp.sum(part * (xc * r1), axis=0, keepdims=True)
        if k < 3:
            fg_out[c] = part.astype(bf16)
            fg_plane(k).start()
        else:
            fg_ref[...] = part
    weight_line(0, own_0)

    buckets = near_buckets(local)
    table = jnp.zeros((experts, 128), f32)
    lane = lax.broadcasted_iota(jnp.int32, (experts, 128), 1)
    row = lax.broadcasted_iota(jnp.int32, (experts, 1), 0)
    for h in range(heads):
        close = near_ref[h, :, seq - local:seq + 2 * local]
        for b in range(experts):
            top_ref[b:b + 1, :] = jnp.sum(jnp.where(buckets == b, close, 0.0), axis=0, keepdims=True)
        column = jnp.sum(top_ref[...], axis=1, keepdims=True)
        left = jnp.sum(near_ref[h, :, :seq - local])
        right = jnp.sum(near_ref[h, :, seq + 2 * local:])
        column = column + jnp.where(row == 15, left, 0.0) + jnp.where(row == 31, right, 0.0)
        table = jnp.where(lane == chip * heads + h, column, table)

    tp_out[...] = jnp.concatenate(
        [table] + [norm1[:, n * 128:(n + 1) * 128] for n in range(6)] + [jnp.zeros((2, 128), f32)], axis=0)
    t_pair = remote(tp_out, tp_in, tp_s.at[0], tp_r.at[0], me.pair)
    t_pair.start()

    def t_plane(k):
        return remote(tc_out, tc_in.at[k], tc_s.at[k], tc_r.at[k], me.on_plane(k))

    def t_line(k):
        return remote(tz_out, tz_in.at[k], tz_s.at[k], tz_r.at[k], me.on_line(k))

    keyvals = jnp.concatenate(keyval, axis=0)
    grads_kv = tn(xn, keyvals)
    own_1 = weight_part(1, grads_kv[:, :hd], grads_kv[:, hd:])
    t_pair.wait_recv()
    tc_out[...] = tp_out[...] + tp_in[...]
    for k in range(3):
        t_plane(k).start()
    weight_line(1, own_1)
    turn_span(0)
    for k in range(3):
        t_plane(k).wait_recv()
    tail = jnp.zeros((40, 128), f32)
    for c in range(4):
        part = jnp.where(chip == c, tc_out[...], 0.0)
        for k in range(3):
            part = jnp.where(me.chips_from[k] == c, tc_in[k], part)
        tail = tail + part
    tz_out[...] = tail
    for k in range(3):
        t_line(k).start()
    turn_span(1)

    first = fg_ref[...]
    for k in range(3):
        fg_plane(k).wait_recv()
        first = first + fg_in[k].astype(f32)
    x = x_ref[...].astype(f32)
    r1 = lax.rsqrt(jnp.mean(x * x, axis=-1, keepdims=True) + epsilon)
    gained1 = first * gain1_ref[...].reshape(1, features)
    dot1 = jnp.sum(gained1 * x, axis=-1, keepdims=True)
    gin_ref[...] = gin_ref[...] + r1 * gained1 - x * (r1 * r1 * r1) * (dot1 / features)

    total = sz_out[gx]
    for k in range(3):
        small_line(k).wait_recv()
        total = total + sz_in[k]
    small_out[...] = total
    turn_span(2)
    for p in range(2):
        total = wz_out[p, gx].astype(f32)
        for k in range(3):
            w_line(p, k).wait_recv()
            total = total + wz_in[p, k].astype(f32)
        wgrad_ref[p] = total
    for k in range(3):
        t_line(k).wait_recv()
    tail = jnp.zeros((40, 128), f32)
    for z in range(4):
        part = jnp.where(gx == z, tz_out[...], 0.0)
        for k in range(3):
            part = jnp.where(me.line_from[k] == z, tz_in[k], part)
        tail = tail + part
    tail_out[...] = tail
    for q in range(4):
        store(len(work) - 1, q).wait()
    for copy in (small_pair, kv_pair, t_pair):
        copy.wait_send()
    for p in range(2):
        w_pair(p).wait_send()
        for k in range(3):
            w_line(p, k).wait_send()
    for k in range(3):
        for copy in (ag_plane, small_plane, small_line, fg_plane, t_plane, t_line):
            copy(k).wait_send()


def back_pass(x_in, gain1, grad_out, choice_row, doc_row, table, saved, returned, gb, collective_id):
    local, features = x_in.shape
    width = features // 4
    hidden, normed, router, gate, attended, queries, keyvals, lse, xb, wqkv, wout, small = saved
    experts, _, units = gb.shape
    hd = queries.shape[2]
    cols = hd // 2
    heads = hd // HSIZE
    seq = 8 * local
    rows = small.shape[0]
    vm = pl.BlockSpec(memory_space=pltpu.VMEM)
    sm = pl.BlockSpec(memory_space=pltpu.SMEM)
    hbm = pl.BlockSpec(memory_space=pl.ANY)
    dma = pltpu.SemaphoreType.DMA
    shape = jax.ShapeDtypeStruct
    V = pltpu.VMEM
    return pl.pallas_call(
        functools.partial(back_kernel, heads, experts),
        out_shape=(
            shape((local, features), f32),
            shape((local, features), f32),
            shape((2, width // 2, 4 * cols), f32),
            shape((rows, width), f32),
            shape((40, 128), f32),
            shape((width, experts * units), bf16),
        ),
        in_specs=[vm] * 5 + [sm] + [vm] * 13 + [hbm],
        out_specs=(vm,) * 5 + (hbm,),
        scratch_shapes=[
            V((heads, local, 16 * local), f32),
            V((4, local, features), bf16), V((4, local, hd), bf16), V((hd, seq), f32), V((hd, seq), f32),
            V((heads, local, 2 * seq), f32), V((hd, features), f32), V((local, features), f32),
            V((experts, 3 * local), f32),
            V((1024, 1024), bf16), V((512, 512), bf16), V((experts, width, 128), bf16), V((4, width, 1024), bf16),
            V((4, width, 1024), bf16),
            V((rows, features), f32), V((rows, features), f32), V((rows, features), f32), V((3, rows, features), f32),
            V((4, rows, width), f32), V((3, rows, width), f32),
            V((4, local, 2 * hd), bf16), V((4, local, 2 * hd), bf16), V((4, local, 2 * hd), f32),
            V((4, local, features), bf16), V((3, local, features), bf16),
            V((2, 4, width // 2, 4 * cols), bf16), V((2, 4, width // 2, 4 * cols), bf16),
            V((2, 4, width // 2, 4 * cols), bf16), V((2, 3, width // 2, 4 * cols), bf16),
            V((40, 128), f32), V((40, 128), f32), V((40, 128), f32), V((3, 40, 128), f32),
            V((40, 128), f32), V((3, 40, 128), f32),
        ] + [dma((n,)) for n in (1, 4, 3, 3, 1, 1, 3, 3, 3, 3, 1, 1, 3, 3, 2, 2, 1, 1, 3, 3, 3, 3)]
        + [dma((2, 3)), dma((2, 3))],
        compiler_params=pltpu.CompilerParams(
            collective_id=collective_id, has_side_effects=True, vmem_limit_bytes=62 * 2**20),
        cost_estimate=pl.CostEstimate(flops=20 * 10**9, bytes_accessed=40 * 10**6, transcendentals=2 * 10**6),
    )(x_in, gain1, grad_out, choice_row, doc_row, table, hidden, normed, router, gate, attended, queries, keyvals, lse,
      xb, wqkv, wout, small, returned, gb)


def finish_kernel(heads, experts,
                  out_ref, gin_ref, wgrad_ref, small_ref, tail_ref, nh_hbm, nb_hbm,
                  out_to, gin_to, norm1_to, query_to, key_to, value_to, table_to, proj_to, norm2_to, router_to,
                  hidden_to, back_to,
                  in_ref, nat_ref, in_sem, nat_sem):
    width, cols = query_to.shape
    span = in_ref.shape[2]
    count = nh_hbm.shape[1] // span
    work = [(nh_hbm, hidden_to, g) for g in range(count)] + [(nb_hbm, back_to, g) for g in range(count)]
    ring = in_ref.shape[0]

    def load(i):
        source, _, g = work[i]
        return pltpu.make_async_copy(source.at[:, g * span:(g + 1) * span], in_ref.at[i % ring], in_sem.at[i % ring])

    def store(i):
        _, target, g = work[i]
        return pltpu.make_async_copy(nat_ref.at[i % ring], target.at[:, g * span:(g + 1) * span], nat_sem.at[i % ring])

    for i in range(ring):
        load(i).start()
    out_to[...] = out_ref[...]
    gin_to[...] = gin_ref[...]
    for n in range(6):
        norm1_to[n * 128:(n + 1) * 128] = tail_ref[experts + n, :]
    parts = []
    for p in range(2):
        rows = wgrad_ref[p]
        parts.append(jnp.concatenate([rows[:, :2 * cols], rows[:, 2 * cols:]], axis=0))
    query_to[...] = parts[0][:, :cols]
    proj_to[...] = jnp.transpose(parts[0])[cols:]
    key_to[...] = parts[1][:, :cols]
    value_to[...] = parts[1][:, cols:]
    table_to[...] = jnp.transpose(jnp.concatenate([tail_ref[:experts, :], jnp.zeros((128 - experts, 128), f32)], axis=0)
                                  )[:heads, :experts]
    norm2_to[...] = small_ref[experts:experts + 1, :]
    router_to[...] = small_ref[:experts, :]
    for i in range(len(work)):
        load(i).wait()
        if i >= ring:
            store(i - ring).wait()
        nat_ref[i % ring] = in_ref[i % ring].astype(f32)
        store(i).start()
        if i + ring < len(work):
            load(i + ring).start()
    for i in range(len(work) - ring, len(work)):
        store(i).wait()


def finish(out_rows, gin, wgrad, small, tail, nh, nb, heads):
    width, natural = nh.shape
    local, features = out_rows.shape
    cols = wgrad.shape[2] // 4
    experts = EXPERTS
    vm = pl.BlockSpec(memory_space=pltpu.VMEM)
    hbm = pl.BlockSpec(memory_space=pl.ANY)
    dma = pltpu.SemaphoreType.DMA
    shape = lambda *dims: jax.ShapeDtypeStruct(dims, f32)
    V = pltpu.VMEM
    ring, span = 4, 2048
    return pl.pallas_call(
        functools.partial(finish_kernel, heads, experts),
        out_shape=(
            shape(local, features), shape(local, features), shape(features),
            shape(width, cols), shape(width, cols), shape(width, cols), shape(heads, experts), shape(cols, width),
            shape(1, width), shape(experts, width), shape(width, natural), shape(width, natural),
        ),
        in_specs=[vm] * 5 + [hbm] * 2,
        out_specs=(vm,) * 10 + (hbm,) * 2,
        scratch_shapes=[V((ring, width, span), bf16), V((ring, width, span), f32), dma((ring,)), dma((ring,))],
        compiler_params=pltpu.CompilerParams(vmem_limit_bytes=63 * 2**20),
        cost_estimate=pl.CostEstimate(flops=10**7, bytes_accessed=30 * 10**6, transcendentals=0),
    )(out_rows, gin, wgrad, small, tail, nh, nb)


def fits(mesh):
    return mesh.shape["gx"] == 4 and mesh.shape["gy"] == 8


def fast(
    x_in,
    norm1_gain,
    w_query,
    w_key,
    w_value,
    relative_bias_table,
    w_out,
    norm2_gain,
    w_router,
    w_hidden,
    w_back,
    expert_choice,
    doc_ids,
    grad_out,
):
    choice_row, doc_row = expert_choice[None, :], doc_ids[None, :]
    table = relative_bias_table.T
    returned, _, back_grads, natural_hidden, *saved = forward_pass(
        x_in,
        norm1_gain,
        w_query,
        w_key,
        w_value,
        w_out,
        table,
        w_router.T,
        norm2_gain[None, :],
        doc_row,
        choice_row,
        grad_out,
        w_hidden,
        w_back,
        1,
    )
    *results, natural_back = back_pass(
        x_in,
        norm1_gain,
        grad_out,
        choice_row,
        doc_row,
        table,
        saved,
        returned,
        back_grads,
        2,
    )
    (
        out_rows,
        input_rows,
        grad_norm1,
        grad_query,
        grad_key,
        grad_value,
        grad_table,
        grad_out_proj,
        grad_norm2,
        grad_router,
        grad_hidden,
        grad_back,
    ) = finish(*results, natural_hidden, natural_back, table.shape[0])
    return (
        out_rows,
        input_rows,
        grad_norm1,
        grad_query,
        grad_key,
        grad_value,
        grad_table.T,
        grad_out_proj,
        grad_norm2[0],
        grad_router.T,
        grad_hidden,
        grad_back,
    )


def solution(mesh):
    return jax.shard_map(
        fast if fits(mesh) else local,
        mesh=mesh,
        in_specs=(
            P(("gx", "gy"), None),
            P(),
            P("gx", "gy"),
            P("gx", "gy"),
            P("gx", "gy"),
            P(),
            P("gy", "gx"),
            P("gx"),
            P("gx", None),
            P("gx", "gy"),
            P("gx", "gy"),
            P(),
            P("gx"),
            P(("gx", "gy"), None),
        ),
        out_specs=(
            P(("gx", "gy"), None),
            P(("gx", "gy"), None),
            P(),
            P("gx", "gy"),
            P("gx", "gy"),
            P("gx", "gy"),
            P(),
            P("gy", "gx"),
            P("gx"),
            P("gx", None),
            P("gx", "gy"),
            P("gx", "gy"),
        ),
        check_vma=False,
    )
```
